32 devices in a mesh: dp: 2 (over core), fsdp: 16 (over z, y, x).
Axes of the slice: x: 2, y: 2, z: 4, core: 2. Of those that a mesh axis runs over, the one named last changes fastest.
Arguments:
- chars: int32 [2, 64, 35, 21], P(None, ('dp', 'fsdp')), may hold values from 0 to 50
- lengths: int32 [2, 64, 35], P(None, ('dp', 'fsdp')), may hold values from 1 to 21
- targets: int32 [2, 64, 35], P(None, ('dp', 'fsdp')), may hold values from 0 to 9999
- resets: int32 [2, 64, 35], P(None, ('dp', 'fsdp')), may hold values 0 or 1
- init_state: float32 [2, 64, 2, 650], P(None, ('dp', 'fsdp')), may hold values from -3 to 3
- window_grad: float32 [2, 64], P(None, ('dp', 'fsdp')), may hold values from -6 to 6
- char_table: bfloat16 [51, 15], replicated, may hold values from -6 to 6
- conv_weight: bfloat16 [105, 1100], replicated, may hold values from -0.875 to 0.875
- conv_bias: bfloat16 [1100], replicated, may hold values from -3 to 3
- highway_flat: bfloat16 [37856, 128], P('fsdp'), may hold values from -6 to 6
- lstm_flat: bfloat16 [35584, 128], P('fsdp'), may hold values from -6 to 6
- soft_flat: bfloat16 [50880, 128], P('fsdp'), may hold values from -6 to 6
Outputs:
- window_loss: float32 [2, 64], P(None, ('dp', 'fsdp'))
- table_grad: float32 [51, 15], replicated
- conv_weight_grad: float32 [105, 1100], replicated
- conv_bias_grad: float32 [1100], replicated
- highway_grad: float32 [37856, 128], P(('dp', 'fsdp'))
- lstm_grad: float32 [35584, 128], P(('dp', 'fsdp'))
- soft_grad: float32 [50880, 128], P(('dp', 'fsdp'))
The draws below stay inside these ranges and needn't reach their ends.
All inputs are finite; a program needn't handle non-finite values. No bound on the sum of `resets` on one device may be relied on, other than what follows from the above.
Results may differ from the reference program's by a relative error of at most 0.0099.
Values may be sent and summed in bfloat16 or wider, within the bound.
A program may use at most 320 MiB of HBM per device.

```python
import math
import jax
import jax.numpy as jnp
import numpy as np
from jax import lax

CE = 15
CHARV = 51
FILT = 1100
H = 650
V = 10000
KMAX = 7
WLEN = 21
STEPS = 35
MICRO = 2
STREAMS = 64
HW_ROWS = 37856
LSTM_ROWS = 35584
SOFT_ROWS = 50880
N_DP = 2
N_FSDP = 16


def draw_highway_flat(key, part):
    key = jax.random.fold_in(key, 11)
    entries = HW_ROWS * 128
    position = jnp.arange(entries, dtype=jnp.int32)
    normal_draw = jnp.clip(jax.random.normal(key, (entries,), jnp.float32), -6.0, 6.0)
    square = FILT * FILT
    period = 2 * square + 2 * FILT
    in_layer = position % period
    spread = jnp.where(in_layer < square, 2.0 / FILT ** 0.5, jnp.where(in_layer < square + FILT, 0.3, jnp.where(in_layer < 2 * square + FILT, 2.0 / FILT ** 0.5, 0.5)))
    centre = jnp.where(in_layer >= 2 * square + FILT, -1.0, 0.0)
    values = centre + spread * normal_draw
    values = jnp.where(position < 2 * period, values, normal_draw)
    return values.reshape(HW_ROWS, 128).astype(jnp.bfloat16)


def draw_lstm_flat(key, part):
    key = jax.random.fold_in(key, 23)
    entries = LSTM_ROWS * 128
    position = jnp.arange(entries, dtype=jnp.int32)
    normal_draw = jnp.clip(jax.random.normal(key, (entries,), jnp.float32), -6.0, 6.0)
    first_end = FILT * 4 * H
    second_end = first_end + 4 * H * H
    spread = jnp.where(position < first_end, 2.0 / FILT ** 0.5, jnp.where(position < second_end, 1.0 / H ** 0.5, 0.5))
    in_bias = position - second_end
    centre = jnp.where((in_bias >= H) & (in_bias < 2 * H), 1.0, 0.0)
    values = centre + spread * normal_draw
    values = jnp.where(position < second_end + 4 * H, values, normal_draw)
    return values.reshape(LSTM_ROWS, 128).astype(jnp.bfloat16)


def draw_soft_flat(key, part):
    key = jax.random.fold_in(key, 37)
    entries = SOFT_ROWS * 128
    position = jnp.arange(entries, dtype=jnp.int32)
    normal_draw = jnp.clip(jax.random.normal(key, (entries,), jnp.float32), -6.0, 6.0)
    spread = jnp.where(position < H * V, 4.0 / H ** 0.5, 1.0)
    values = jnp.where(position < H * V + V, spread * normal_draw, normal_draw)
    return values.reshape(SOFT_ROWS, 128).astype(jnp.bfloat16)


def set_ends(values, rng, least, high):
    longest = values.shape.index(max(values.shape))
    spots = []
    for shift in (0, 1):
        where = [jax.random.randint(jax.random.fold_in(rng, axis), (), 0, length) for axis, length in enumerate(values.shape)]
        where[longest] = (where[longest] + shift) % values.shape[longest]
        spots.append(tuple(where))
    return values.at[spots[0]].set(least).at[spots[1]].set(high)


def shard_levels(rng, shape, cuts, smallest, top_value):
    loudness, own = 1.0, jax.random.fold_in(rng, 6)
    for dim, shards_of in cuts:
        draws = jnp.exp(jax.random.uniform(jax.random.fold_in(own, dim), (shards_of,), jnp.float32, smallest / len(cuts), top_value / len(cuts)))
        loudness = loudness * jnp.repeat(draws, shape[dim] // shards_of).reshape([-1 if axis == dim else 1 for axis in range(len(shape))])
    return loudness


def rank_table(number_of, lean):
    weights = [(1 << 20) // math.isqrt(standing ** lean) + 1 for standing in range(1, number_of + 1)]
    scale = 1 + sum(weights) // (1 << 30)
    return np.cumsum(np.array([max(1, weight // scale) for weight in weights]))


def ranked_ids(rng, shape, count, slope):
    grid = rank_table(count, slope)
    pick = jax.random.randint(jax.random.fold_in(rng, 1), shape, 0, int(grid[count - 1]))
    standing = jnp.searchsorted(jnp.asarray(grid, jnp.int32), pick, side="right")
    return jax.random.permutation(jax.random.fold_in(rng, 2), count)[standing].astype(jnp.int32)


def bell_draw(key, extent, deviation, bound, cuts=(), held_as=jnp.bfloat16):
    result = deviation * jax.random.normal(key, extent, jnp.float32)
    if cuts:
        result = result * shard_levels(key, extent, cuts, -0.22, 0.18)
    return jnp.clip(result, -bound, bound).astype(held_as)


def setup_inputs(seed: int = 0) -> dict:
    key_list = jax.random.split(jax.random.key(seed), 13)
    chars = set_ends(jax.random.randint(key_list[0], (MICRO, STREAMS, STEPS, WLEN), 0, CHARV), jax.random.fold_in(key_list[0], 1), 0, CHARV - 1).astype(jnp.int32)
    lengths = set_ends(jax.random.randint(key_list[1], (MICRO, STREAMS, STEPS), 1, WLEN + 1), jax.random.fold_in(key_list[1], 1), 1, WLEN).astype(jnp.int32)
    targets = set_ends(ranked_ids(key_list[2], (MICRO, STREAMS, STEPS), V, 2), jax.random.fold_in(key_list[2], 3), 0, V - 1).astype(jnp.int32)
    resets = set_ends((jax.random.randint(key_list[3], (MICRO, STREAMS, STEPS), 0, 16) < 1).astype(jnp.int32), jax.random.fold_in(key_list[3], 1), 0, 1)
    init_state = bell_draw(key_list[4], (MICRO, STREAMS, 2, H), 0.5, 3.0, ((1, 32),), jnp.float32)
    window_grad = bell_draw(key_list[5], (MICRO, STREAMS), 1.0, 6.0, ((1, 32),), jnp.float32)
    char_table = bell_draw(key_list[6], (CHARV, CE), 1.0, 6.0)
    conv_weight = bell_draw(key_list[7], (KMAX * CE, FILT), (3 * CE) ** -0.5, 0.875)
    conv_bias = bell_draw(key_list[8], (FILT,), 0.5, 3.0)
    highway_flat = draw_highway_flat(jax.random.fold_in(key_list[12], 71), 0)
    lstm_flat = draw_lstm_flat(jax.random.fold_in(key_list[12], 71), 0)
    soft_flat = draw_soft_flat(jax.random.fold_in(key_list[12], 71), 0)
    return {"chars": chars, "lengths": lengths, "targets": targets, "resets": resets, "init_state": init_state, "window_grad": window_grad, "char_table": char_table, "conv_weight": conv_weight, "conv_bias": conv_bias, "highway_flat": highway_flat, "lstm_flat": lstm_flat, "soft_flat": soft_flat}


FILTER_CUTS = (1, 3, 6, 10, 14, 18)

@jax.custom_vjp
def low(v):
    return lax.optimization_barrier(v.astype(jnp.bfloat16)).astype(jnp.float32)

@jax.custom_vjp
def low_back(v):
    return v

def low_keep(v):
    return (low(v), None)

def low_pass(kept, grad):
    return (grad,)

def back_keep(v):
    return (v, None)

def back_low(kept, grad):
    return (low(grad),)
low.defvjp(low_keep, low_pass)
low_back.defvjp(back_keep, back_low)

def filter_widths():
    column = jnp.arange(FILT, dtype=jnp.int32)
    widths = jnp.ones((FILT,), jnp.int32)
    for cut_at in FILTER_CUTS:
        widths = widths + (column >= FILT * cut_at // 22).astype(jnp.int32)
    return widths

def product(left, right):
    return jnp.dot(left, right, precision=lax.Precision.HIGHEST, preferred_element_type=jnp.float32)

def split_highway(gathered):
    flat_all = gathered.reshape(-1)
    square = FILT * FILT
    layers = []
    for layer_no in range(2):
        offset = layer_no * (2 * square + 2 * FILT)
        w_trans = flat_all[offset:offset + square].reshape(FILT, FILT)
        b_trans = flat_all[offset + square:offset + square + FILT]
        w_gate = flat_all[offset + square + FILT:offset + 2 * square + FILT].reshape(FILT, FILT)
        b_gate = flat_all[offset + 2 * square + FILT:offset + 2 * square + 2 * FILT]
        layers.append((w_trans, b_trans, w_gate, b_gate))
    return layers

def split_lstm(gathered):
    flat_all = gathered.reshape(-1)
    first_end = FILT * 4 * H
    second_end = first_end + 4 * H * H
    return (flat_all[:first_end].reshape(FILT, 4 * H), flat_all[first_end:second_end].reshape(H, 4 * H), flat_all[second_end:second_end + 4 * H])

def split_soft(gathered):
    flat_all = gathered.reshape(-1)
    return (flat_all[:H * V].reshape(H, V), flat_all[H * V:H * V + V])

def forward(char_table, conv_weight, conv_bias, highway_flat, lstm_flat, soft_flat, chars, lengths, targets, resets, init_state):
    block_rows = chars.shape[0]
    widths = filter_widths()
    positions = jnp.arange(WLEN, dtype=jnp.int32)
    present = positions[None, None, :] < lengths[:, :, None]
    embedded = jnp.where(present[..., None], char_table[chars], 0.0)
    padded = jnp.pad(embedded, ((0, 0), (0, 0), (0, KMAX - 1), (0, 0)))
    windows = jnp.concatenate([padded[:, :, shift_by:shift_by + WLEN, :] for shift_by in range(KMAX)], axis=3)
    kernel_mask = jnp.arange(KMAX * CE, dtype=jnp.int32)[:, None] // CE < widths[None, :]
    kernel = jnp.where(kernel_mask, conv_weight, 0.0)
    pre_conv = low_back(jnp.einsum('bswk,kf->bswf', windows, kernel, precision=lax.Precision.HIGHEST) + conv_bias)
    activated = jnp.tanh(pre_conv)
    counts = jnp.maximum(lengths[..., None] - widths[None, None, :] + 1, 1)
    inside = positions[None, None, :, None] < counts[:, :, None, :]
    totals = lax.optimization_barrier(jnp.sum(jnp.where(inside, jnp.exp(activated), 0.0), axis=2))
    pooled = jnp.log(totals) - jnp.log(counts.astype(jnp.float32))
    feature = low(pooled.reshape(block_rows * STEPS, FILT))
    for w_trans, b_trans, w_gate, b_gate in split_highway(highway_flat):
        trans_pre = low_back(product(feature, w_trans) + b_trans)
        gate_now = jax.nn.sigmoid(low_back(product(feature, w_gate) + b_gate))
        feature = low(gate_now * jax.nn.silu(trans_pre) + (1.0 - gate_now) * feature)
    w_input, w_recur, b_lstm = split_lstm(lstm_flat)
    from_input = (product(feature, w_input) + b_lstm).reshape(block_rows, STEPS, 4 * H)
    keep_all = 1.0 - resets.astype(jnp.float32)

    def lstm_step(carried, slices):
        hidden, cell_state = carried
        input_now, keep_now = slices
        hidden = hidden * keep_now[:, None]
        cell_state = cell_state * keep_now[:, None]
        gate_sums = low_back(input_now + product(hidden, w_recur))
        gate_in = jax.nn.sigmoid(gate_sums[:, :H])
        gate_forget = jax.nn.sigmoid(gate_sums[:, H:2 * H])
        gate_update = jnp.tanh(gate_sums[:, 2 * H:3 * H])
        gate_out = jax.nn.sigmoid(gate_sums[:, 3 * H:])
        cell_now = gate_forget * cell_state + gate_in * gate_update
        hidden_now = low(gate_out * jnp.tanh(cell_now))
        return ((hidden_now, cell_now), hidden_now)
    start_state = (low(init_state[:, 0, :]), init_state[:, 1, :])
    _, hiddens = lax.scan(lstm_step, start_state, (jnp.swapaxes(from_input, 0, 1), keep_all.T))
    hidden_rows = jnp.swapaxes(hiddens, 0, 1).reshape(block_rows * STEPS, H)
    w_soft, b_soft = split_soft(soft_flat)
    logits = low_back(product(hidden_rows, w_soft) + b_soft)
    log_total = jax.nn.logsumexp(logits, axis=1)
    picked = jnp.take_along_axis(logits, targets.reshape(-1, 1).astype(jnp.int32), axis=1)[:, 0]
    return lax.optimization_barrier(jnp.mean((log_total - picked).reshape(block_rows, STEPS), axis=1))

def reference(chars, lengths, targets, resets, init_state, window_grad, char_table, conv_weight, conv_bias, highway_flat, lstm_flat, soft_flat):
    params = tuple((each_param.astype(jnp.float32) for each_param in (char_table, conv_weight, conv_bias, highway_flat, lstm_flat, soft_flat)))
    groups = MICRO * N_DP * N_FSDP // 8

    def regroup(array_in):
        return array_in.reshape((groups, -1) + array_in.shape[2:])
    inputs_all = tuple((regroup(array_in) for array_in in (chars, lengths, targets, resets, init_state, window_grad)))

    def block_step(totals, pieces):
        chars_now, lengths_now, targets_now, resets_now, state_now, grad_now = pieces

        def loss_of(*weights):
            return forward(*weights, chars_now, lengths_now, targets_now, resets_now, state_now)
        losses, pull_back = jax.vjp(loss_of, *params)
        grads_now = pull_back(grad_now)
        return (tuple((total_now + add_now for total_now, add_now in zip(totals, grads_now))), losses)
    zeros_all = tuple((jnp.zeros_like(each_param) for each_param in params))
    totals, losses = lax.scan(block_step, zeros_all, inputs_all)
    window_loss = losses.reshape(MICRO, -1)
    return (window_loss, totals[0], totals[1], totals[2], totals[3], totals[4], totals[5])
```

```python
import functools

import jax
import jax.numpy as jnp
import numpy as np
from jax import lax
from jax.experimental import pallas as pl
from jax.experimental.pallas import tpu as pltpu
from jax.sharding import PartitionSpec as P

H = 650
V = 10000
KMAX = 7
LANE = 128
HP = 768
SLOTS = 24
HOT = 384
FILTER_CUTS = (1, 3, 6, 10, 14, 18)
MESH = pl.DeviceIdType.MESH
BF = jnp.bfloat16
F32 = jnp.float32


def up_to(value, unit):
    return -(-value // unit) * unit


def dot(left, right):
    return jnp.dot(left, right, preferred_element_type=F32)


def dot_rows(left, right):
    return lax.dot_general(left, right, (((0,), (0,)), ((), ())), preferred_element_type=F32)


def dot_cols(left, right):
    return lax.dot_general(left, right, (((1,), (1,)), ((), ())), preferred_element_type=F32)


class Windows:
    def __init__(self, flat_rows, width, used, fsdp, dp, by_rows):
        owners = fsdp * dp
        self.width, self.by_rows, self.fsdp, self.dp = width, by_rows, fsdp, dp
        self.entries = flat_rows * LANE // owners
        starts = [o * self.entries // width for o in range(owners)]
        spans = [
            (o * self.entries % width + self.entries - 1) // width + 1 for o in range(owners)
        ]
        rows = max(spans)
        while (dp * rows) % 16 or (by_rows and (dp // 2 * rows) % 16):
            rows += 1
        self.rows = rows
        self.columns = up_to(width, LANE) if by_rows else 2 * up_to(-(-width // 2), LANE)
        self.block = (
            (dp // 2 * rows, self.columns) if by_rows else (dp * rows, self.columns // 2)
        )
        self.shape = (fsdp, 2) + self.block if by_rows else (2, fsdp) + self.block

        def row_map(order):
            rows_of = [
                [starts[o] + i if i < spans[o] and starts[o] + i < used else -1 for i in range(rows)]
                for o in order
            ]
            return np.array(rows_of, np.int32).reshape(-1)

        self.gathered = row_map(range(owners))
        if by_rows:
            order = [
                (2 * jj + h) * fsdp + f
                for f in range(fsdp)
                for h in range(2)
                for jj in range(dp // 2)
            ]
        else:
            order = [d * fsdp + f for f in range(fsdp) for d in range(dp)]
        self.reduced = row_map(order)

    def pick(self, ref, half, slot):
        return ref.at[slot, half] if self.by_rows else ref.at[half, slot]

    def from_flat(self, shard, fsdp_at):
        parts = []
        flat = shard.reshape(-1)
        for j in range(self.dp):
            shift = lax.rem((fsdp_at * self.dp + j) * self.entries, self.width)
            piece = lax.dynamic_update_slice(
                jnp.zeros((self.rows * self.width,), BF),
                flat[j * self.entries : (j + 1) * self.entries],
                (shift,),
            ).reshape(self.rows, self.width)
            parts.append(jnp.pad(piece, ((0, 0), (0, self.columns - self.width))))
        joined = jnp.concatenate(parts, axis=0)
        if self.by_rows:
            return joined.reshape((2,) + self.block)
        half = self.columns // 2
        return jnp.stack([joined[:, :half], joined[:, half:]])

    def to_flat(self, window, dp_at, fsdp_at):
        shift = lax.rem((dp_at * self.fsdp + fsdp_at) * self.entries, self.width)
        flat = window[:, : self.width].reshape(-1)
        return lax.dynamic_slice(flat, (shift,), (self.entries,)).reshape(-1, LANE)


def one_hot_map(rows, row_map):
    return (
        lax.broadcasted_iota(jnp.int32, (rows, row_map.shape[0]), 0) == jnp.asarray(row_map)[None, :]
    ).astype(BF)


def compress(spread, mapping):
    high = lax.reduce_precision(spread, 8, 7)
    both = jnp.concatenate([high.astype(BF), (spread - high).astype(BF)], axis=0)
    product = dot_cols(both, mapping)
    count = spread.shape[0]
    return product[:count] + product[count:]


def place(fsdp, dp):
    d, f = lax.axis_index("dp"), lax.axis_index("fsdp")
    c = lax.rem(d, 2)
    x, y, z = lax.rem(f, 2), lax.rem(f // 2, 2), f // 4
    first, last = x + c * (y - x), y + c * (x - y)
    return d, f, c, z, first, last, 1 + c, 2 - c


def gather_kernel(plans, *refs):
    count = len(plans)
    ins, outs, sems = refs[:count], refs[count : 2 * count], refs[2 * count]
    n, dp = plans[0].fsdp, plans[0].dp
    lengthwise = n // 4
    d, f, c, z, first, last, stride1, stride3 = place(n, dp)
    partner1 = f + stride1 * (1 - 2 * first)
    partner3 = f + stride3 * (1 - 2 * last)
    sibling = (d + 1 - 2 * c, f)
    flip1 = stride1 * (1 - 2 * first)
    flip3 = stride3 * (1 - 2 * last)
    RECV, SIB_RECV, ONE, UP, DOWN, LAST, SIB, LOCAL = range(8)

    def sem(kind, a, block):
        return sems.at[(kind * count + a) * n + block]

    barrier = pltpu.get_barrier_semaphore()
    for target in ((d, partner1), (d, partner3), sibling):
        pl.semaphore_signal(barrier, inc=1, device_id=target, device_id_type=MESH)

    @pl.when(z > 0)
    def _():
        pl.semaphore_signal(barrier, inc=1, device_id=(d, f - 4), device_id_type=MESH)

    @pl.when(z < lengthwise - 1)
    def _():
        pl.semaphore_signal(barrier, inc=1, device_id=(d, f + 4), device_id_type=MESH)

    has_down = (z > 0).astype(jnp.int32)
    has_up = (z < lengthwise - 1).astype(jnp.int32)
    pl.semaphore_wait(barrier, 3 + has_down + has_up)

    def copy(kind, a, block, target, own=False):
        here = plans[a].pick(outs[a], c, block)
        return pltpu.make_async_remote_copy(
            src_ref=ins[a].at[c] if own else here,
            dst_ref=here,
            send_sem=sem(kind, a, block),
            recv_sem=sem(SIB_RECV if kind == SIB else RECV, a, block),
            device_id=target,
            device_id_type=MESH,
        )

    def arrived(a, block, kind=RECV):
        here = plans[a].pick(outs[a], 1 - c if kind == SIB_RECV else c, block)
        pltpu.make_async_remote_copy(
            src_ref=here,
            dst_ref=here,
            send_sem=sem(SIB, a, block),
            recv_sem=sem(kind, a, block),
            device_id=sibling,
            device_id_type=MESH,
        ).wait_recv()

    def sent(kind, a, block):
        copy(kind, a, block, sibling).wait_send()

    def local(a, half):
        return pltpu.make_async_copy(
            ins[a].at[half], plans[a].pick(outs[a], half, f), sem(LOCAL, a, half)
        )

    def send_up(a, block, own=False):
        @pl.when(z < lengthwise - 1)
        def _():
            copy(UP, a, block, (d, f + 4), own).start()

    def send_down(a, block, own=False):
        @pl.when(z > 0)
        def _():
            copy(DOWN, a, block, (d, f - 4), own).start()

    for a in range(count):
        copy(ONE, a, f, (d, partner1), True).start()
        send_up(a, f, True)
        send_down(a, f, True)
        copy(LAST, a, f, (d, partner3), True).start()
    for a in range(count):
        for half in (0, 1):
            local(a, half).start()
    for a in range(count):
        block = partner1
        arrived(a, block)
        send_up(a, block)
        send_down(a, block)
        copy(LAST, a, block, (d, partner3)).start()
        copy(SIB, a, block, sibling).start()

    def across(distance, a):
        for sign in (1,) if distance == 0 else (1, -1):
            at = z - sign * distance

            def take(at=at):
                for flip in (0, 1):
                    block = f + 4 * (at - z) + flip * flip1 + flip3
                    arrived(a, block)
                    copy(SIB, a, block, sibling).start()

            pl.when((at >= 0) & (at < lengthwise))(take)

    for distance in range(1, lengthwise):
        for a in range(count):
            for sign in (1, -1):
                at = z - sign * distance

                def take(at=at, sign=sign):
                    for flip in (0, 1):
                        block = f + 4 * (at - z) + flip * flip1
                        arrived(a, block)
                        (send_up if sign == 1 else send_down)(a, block)
                        copy(LAST, a, block, (d, partner3)).start()
                        copy(SIB, a, block, sibling).start()

                pl.when((at >= 0) & (at < lengthwise))(take)
        for a in range(count):
            across(distance - 1, a)
    for a in range(count):
        across(lengthwise - 1, a)

    for a in range(count):

        def finish(block, _, a=a):
            at = block // 4
            mine = block == f
            bit_x, bit_y = lax.rem(block, 2), lax.rem(block // 2, 2)
            in_plane = bit_y + c * (bit_x - bit_y) == last

            @pl.when(jnp.logical_not(mine))
            def _():
                arrived(a, block, SIB_RECV)
                sent(SIB, a, block)

            @pl.when(in_plane)
            def _():
                sent(LAST, a, block)

                @pl.when((at <= z) & (z < lengthwise - 1))
                def _():
                    sent(UP, a, block)

                @pl.when((at >= z) & (z > 0))
                def _():
                    sent(DOWN, a, block)

            return 0

        lax.fori_loop(0, n, finish, 0)
        sent(ONE, a, f)
        for half in (0, 1):
            local(a, half).wait()


def gather(plans, shards, collective_id):
    n = plans[0].fsdp
    count = len(plans)
    return pl.pallas_call(
        functools.partial(gather_kernel, plans),
        out_shape=[jax.ShapeDtypeStruct(plan.shape, BF) for plan in plans],
        in_specs=[pl.BlockSpec(memory_space=pl.ANY)] * count,
        out_specs=[pl.BlockSpec(memory_space=pl.ANY)] * count,
        scratch_shapes=[pltpu.SemaphoreType.DMA((8 * count * n,))],
        compiler_params=pltpu.CompilerParams(collective_id=collective_id, has_side_effects=True),
    )(*shards)


def reduce_kernel(plans, *refs):
    count = len(plans)
    ins, outs = refs[:count], refs[count : 2 * count]
    scratch = refs[2 * count :]
    held, landed, flow_up, flow_down, near, cross = (
        scratch[k * count : (k + 1) * count] for k in range(6)
    )
    sems = scratch[6 * count]
    n, dp = plans[0].fsdp, plans[0].dp
    lengthwise = n // 4
    d, f, c, z, first, last, stride1, stride3 = place(n, dp)
    partner1 = f + stride1 * (1 - 2 * first)
    partner3 = f + stride3 * (1 - 2 * last)
    sibling = (d + 1 - 2 * c, f)
    SIB, SIB_RECV, LOAD, NEAR, NEAR_RECV, UP, UP_RECV, DOWN, DOWN_RECV, END = range(10)

    def sem(kind, a, block):
        return sems.at[(kind * count + a) * n + block]

    def slot(at, b1, b3):
        return 4 * at + stride1 * b1 + stride3 * b3

    def order(step):
        half = step // 2
        return jnp.where(lax.rem(step, 2) == 0, half, lengthwise - 1 - half)

    barrier = pltpu.get_barrier_semaphore()
    for target in ((d, partner1), (d, partner3), sibling):
        pl.semaphore_signal(barrier, inc=1, device_id=target, device_id_type=MESH)

    @pl.when(z > 0)
    def _():
        pl.semaphore_signal(barrier, inc=1, device_id=(d, f - 4), device_id_type=MESH)

    @pl.when(z < lengthwise - 1)
    def _():
        pl.semaphore_signal(barrier, inc=1, device_id=(d, f + 4), device_id_type=MESH)

    has_down = (z > 0).astype(jnp.int32)
    has_up = (z < lengthwise - 1).astype(jnp.int32)
    pl.semaphore_wait(barrier, 3 + has_down + has_up)

    def remote(src, dst, send, recv, target):
        return pltpu.make_async_remote_copy(
            src_ref=src,
            dst_ref=dst,
            send_sem=send,
            recv_sem=recv,
            device_id=target,
            device_id_type=MESH,
        )

    def to_sibling(a, block):
        return remote(
            plans[a].pick(ins[a], 1 - c, block),
            landed[a].at[block],
            sem(SIB, a, block),
            sem(SIB_RECV, a, block),
            sibling,
        )

    def load(a, block):
        return pltpu.make_async_copy(
            plans[a].pick(ins[a], c, block), held[a].at[block], sem(LOAD, a, block)
        )

    def to_near(a, at, b3):
        return remote(
            held[a].at[slot(at, 1 - first, b3)],
            near[a].at[2 * at + b3],
            sem(NEAR, a, 2 * at + b3),
            sem(NEAR_RECV, a, 2 * at + b3),
            (d, partner1),
        )

    def to_up(a, at, b3):
        return remote(
            held[a].at[slot(at, first, b3)],
            flow_up[a].at[2 * at + b3],
            sem(UP, a, 2 * at + b3),
            sem(UP_RECV, a, 2 * at + b3),
            (d, f + 4),
        )

    def to_down(a, at, b3):
        return remote(
            held[a].at[slot(at, first, b3)],
            flow_down[a].at[2 * at + b3],
            sem(DOWN, a, 2 * at + b3),
            sem(DOWN_RECV, a, 2 * at + b3),
            (d, f - 4),
        )

    def to_cross(a):
        return remote(
            held[a].at[slot(z, first, 1 - last)],
            cross[a],
            sem(END, a, 0),
            sem(END, a, 1),
            (d, partner3),
        )

    def to_pair(a):
        return remote(outs[a].at[c], outs[a].at[c], sem(END, a, 2), sem(END, a, 3), sibling)

    def add_into(a, block, source, at):
        def rows(step, _):
            where = pl.ds(pl.multiple_of(step * 16, 16), 16)
            held[a][block, where, :] = (
                held[a][block, where, :].astype(F32) + source[at, where, :].astype(F32)
            ).astype(BF)
            return 0

        lax.fori_loop(0, plans[a].block[0] // 16, rows, 0)

    def each(body):
        for a in range(count):

            def step(t, _, a=a):
                body(a, order(t // 2), lax.rem(t, 2))
                return 0

            lax.fori_loop(0, 2 * lengthwise, step, 0)

    def begin(b1):
        def body(a, at, b3):
            block = slot(at, b1, b3)
            load(a, block).start()

        return body

    def begin_sibling(b1):
        def body(a, at, b3):
            to_sibling(a, slot(at, b1, b3)).start()

        return body

    each(begin_sibling(1 - first))
    each(begin(1 - first))
    each(begin_sibling(first))
    each(begin(first))

    def first_leg(a, at, b3):
        block = slot(at, 1 - first, b3)
        load(a, block).wait()
        to_sibling(a, block).wait_recv()
        add_into(a, block, landed[a], block)
        to_near(a, at, b3).start()

    def middle_leg(a, at, b3):
        block = slot(at, first, b3)
        load(a, block).wait()
        to_sibling(a, block).wait_recv()
        add_into(a, block, landed[a], block)
        to_near(a, at, b3).wait_recv()
        add_into(a, block, near[a], 2 * at + b3)

        @pl.when(at > z)
        def _():
            @pl.when(z > 0)
            def _():
                to_up(a, at, b3).wait_recv()
                add_into(a, block, flow_up[a], 2 * at + b3)

            to_up(a, at, b3).start()

        @pl.when(at < z)
        def _():
            @pl.when(z < lengthwise - 1)
            def _():
                to_down(a, at, b3).wait_recv()
                add_into(a, block, flow_down[a], 2 * at + b3)

            to_down(a, at, b3).start()

    def gather_own(a, b3):
        block = slot(z, first, b3)

        @pl.when(z > 0)
        def _():
            to_up(a, z, b3).wait_recv()
            add_into(a, block, flow_up[a], 2 * z + b3)

        @pl.when(z < lengthwise - 1)
        def _():
            to_down(a, z, b3).wait_recv()
            add_into(a, block, flow_down[a], 2 * z + b3)

    each(first_leg)
    each(middle_leg)
    for a in range(count):
        gather_own(a, 1 - last)
        to_cross(a).start()
    for a in range(count):
        gather_own(a, last)
        to_cross(a).wait_recv()
        block = slot(z, first, last)

        def rows(step, _, a=a, block=block):
            where = pl.ds(pl.multiple_of(step * 16, 16), 16)
            total = held[a][block, where, :].astype(F32) + cross[a][where, :].astype(F32)
            if plans[a].by_rows:
                outs[a][where, :] = total
            else:
                outs[a][c, where, :] = total
            return 0

        lax.fori_loop(0, plans[a].block[0] // 16, rows, 0)
        if not plans[a].by_rows:
            to_pair(a).start()

    def finish(a, at, b3):
        for b1 in (first, 1 - first):
            to_sibling(a, slot(at, b1, b3)).wait_send()
        to_near(a, at, b3).wait_send()

        @pl.when(at > z)
        def _():
            to_up(a, at, b3).wait_send()

        @pl.when(at < z)
        def _():
            to_down(a, at, b3).wait_send()

    each(finish)
    for a in range(count):
        to_cross(a).wait_send()
        if not plans[a].by_rows:
            to_pair(a).wait()


def reduce_scatter(plans, grads, collective_id):
    n = plans[0].fsdp
    count = len(plans)
    return pl.pallas_call(
        functools.partial(reduce_kernel, plans),
        out_shape=[
            jax.ShapeDtypeStruct(plan.block if plan.by_rows else (2,) + plan.block, F32)
            for plan in plans
        ],
        in_specs=[pl.BlockSpec(memory_space=pl.ANY)] * count,
        out_specs=[pl.BlockSpec(memory_space=pltpu.VMEM)] * count,
        scratch_shapes=[pltpu.VMEM((n,) + plan.block, BF) for plan in plans] * 2
        + [pltpu.VMEM((n // 2,) + plan.block, BF) for plan in plans] * 3
        + [pltpu.VMEM(plan.block, BF) for plan in plans]
        + [pltpu.SemaphoreType.DMA((10 * count * n,))],
        compiler_params=pltpu.CompilerParams(
            collective_id=collective_id, has_side_effects=True, vmem_limit_bytes=60 * 2**20
        ),
    )(*grads)


def hot_rows(index_ref):
    index = index_ref[...]
    lane = lax.broadcasted_iota(jnp.int32, (index.shape[0], HOT), 1)
    hit = lane == index[:, 0:1]
    for q in range(1, KMAX + 1):
        hit = jnp.logical_or(hit, lane == index[:, q : q + 1])
    return hit.astype(F32).astype(BF)


def conv_forward_kernel(filters, index_ref, length_ref, table_ref, kernel_ref, width_ref, out_ref):
    words = length_ref.shape[0]
    windows = dot(hot_rows(index_ref), table_ref[...]).astype(BF)
    chunk = 384
    for at in range(0, kernel_ref.shape[1], chunk):
        columns = slice(at, at + chunk)
        activated = jnp.tanh(dot(windows, kernel_ref[:, columns])).reshape(words, SLOTS, chunk)
        counts = jnp.maximum(length_ref[...] - width_ref[:, columns] + 1, 1)
        position = lax.broadcasted_iota(jnp.int32, (words, SLOTS, chunk), 1)
        inside = position < counts[:, None, :]
        totals = jnp.sum(jnp.where(inside, jnp.exp(activated), 0.0), axis=1)
        pooled = jnp.log(totals) - jnp.log(counts.astype(F32))
        lane = at + lax.broadcasted_iota(jnp.int32, (words, chunk), 1)
        out_ref[:, columns] = jnp.where(
            lane < filters, pooled, jnp.where(lane == filters, 1.0, 0.0)
        ).astype(BF)


def conv_backward_kernel(
    index_ref, length_ref, table_ref, kernel_ref, width_ref, grad_ref, kernel_grad_ref, hot_grad_ref
):
    words = length_ref.shape[0]

    @pl.when(pl.program_id(0) == 0)
    def _():
        kernel_grad_ref[...] = jnp.zeros_like(kernel_grad_ref)
        hot_grad_ref[...] = jnp.zeros_like(hot_grad_ref)

    hot = hot_rows(index_ref)
    windows = dot(hot, table_ref[...]).astype(BF)
    chunk = 384
    grad_windows = jnp.zeros(windows.shape, F32)
    for at in range(0, kernel_ref.shape[1], chunk):
        columns = slice(at, at + chunk)
        activated = jnp.tanh(dot(windows, kernel_ref[:, columns])).reshape(words, SLOTS, chunk)
        counts = jnp.maximum(length_ref[...] - width_ref[:, columns] + 1, 1)
        position = lax.broadcasted_iota(jnp.int32, (words, SLOTS, chunk), 1)
        inside = position < counts[:, None, :]
        weight = jnp.where(inside, jnp.exp(activated), 0.0)
        share = grad_ref[:, columns] / jnp.sum(weight, axis=1)
        grad = (share[:, None, :] * weight * (1.0 - activated * activated)).astype(BF)
        grad = grad.reshape(words * SLOTS, chunk)
        kernel_grad_ref[:, columns] += dot_rows(windows, grad)
        grad_windows += dot_cols(grad, kernel_ref[:, columns])
    hot_grad_ref[...] += dot_rows(hot, grad_windows.astype(BF))


def conv_specs(words, filters_padded):
    return [
        pl.BlockSpec((words * SLOTS, 8), lambda i: (i, 0)),
        pl.BlockSpec((words, 1), lambda i: (i, 0)),
        pl.BlockSpec((HOT, LANE), lambda i: (0, 0)),
        pl.BlockSpec((LANE, filters_padded), lambda i: (0, 0)),
        pl.BlockSpec((1, filters_padded), lambda i: (0, 0)),
    ]


def gate_parts(sums):
    parts = [sums[:, :HP]]
    for g in range(1, 4):
        begin = g * H // LANE * LANE
        moved = sums[:, begin : begin + HP + LANE]
        parts.append(pltpu.roll(moved, HP + LANE - (g * H - begin), 1)[:, :HP])
    return parts


def join_gates(parts, columns):
    rows = parts[0].shape[0]
    total = None
    for g, part in enumerate(parts):
        begin = g * H // LANE * LANE
        wide = jnp.concatenate([part, jnp.zeros((rows, LANE), F32)], axis=1)
        if g * H - begin:
            wide = pltpu.roll(wide, g * H - begin, 1)
        pieces = [wide]
        if begin:
            pieces = [jnp.zeros((rows, begin), F32)] + pieces
        if columns - begin - HP - LANE > 0:
            pieces = pieces + [jnp.zeros((rows, columns - begin - HP - LANE), F32)]
        placed = jnp.concatenate(pieces, axis=1)[:, :columns]
        total = placed if total is None else total + placed
    return total


def lstm_forward_kernel(
    batch, x_ref, w_ref, h0_ref, c0_ref, keep_ref, *outs
):
    hp_ref, cp_ref, i_ref, f_ref, u_ref, o_ref, t_ref, h_ref = outs
    per_tile = 8 // batch
    row = lax.broadcasted_iota(jnp.int32, (8, HP), 0)
    lane = lax.broadcasted_iota(jnp.int32, (8, HP), 1)

    def tile(step, carried):
        h, c = carried
        rows = pl.ds(pl.multiple_of(step * 8, 8), 8)
        x = x_ref[rows, :]
        keep = keep_ref[rows, :]
        saved = None
        for part in range(per_tile):
            hp, cp = h * keep, c * keep
            sums = x + dot(hp.astype(BF), w_ref[...])
            i, f, u, o = gate_parts(sums)
            i, f, u, o = jax.nn.sigmoid(i), jax.nn.sigmoid(f), jnp.tanh(u), jax.nn.sigmoid(o)
            c = f * cp + i * u
            t = jnp.tanh(c)
            h = (o * t).astype(BF).astype(F32)
            now = (hp, cp, i, f, u, o, t, jnp.where(lane < H, h, jnp.where(lane == H, 1.0, 0.0)))
            if saved is None:
                saved = now
            else:
                saved = tuple(jnp.where(row >= part * batch, b, a) for a, b in zip(saved, now))
            h, c = pltpu.roll(h, batch, 0), pltpu.roll(c, batch, 0)
        for ref, value in zip((hp_ref, cp_ref, i_ref, f_ref, u_ref, o_ref, t_ref, h_ref), saved):
            ref[rows, :] = value
        return h, c

    lax.fori_loop(0, x_ref.shape[0] // 8, tile, (h0_ref[...], c0_ref[...]))


def lstm_backward_kernel(
    batch, dh_ref, w_ref, keep_ref, cp_ref, i_ref, f_ref, u_ref, o_ref, t_ref, dz_ref
):
    per_tile = 8 // batch
    tiles = dh_ref.shape[0] // 8
    row = lax.broadcasted_iota(jnp.int32, (8, dz_ref.shape[1]), 0)
    real = lax.broadcasted_iota(jnp.int32, (8, HP), 1) < H

    def tile(step, carried):
        dh_carry, dc_carry = carried
        rows = pl.ds(pl.multiple_of((tiles - 1 - step) * 8, 8), 8)
        keep = keep_ref[rows, :]
        i, f, u, o, t = (r[rows, :] for r in (i_ref, f_ref, u_ref, o_ref, t_ref))
        soft = dh_ref[rows, :]
        to_c = o * (1.0 - t * t)
        to_i = jnp.where(real, u * i * (1.0 - i), 0.0)
        to_f = jnp.where(real, cp_ref[rows, :] * f * (1.0 - f), 0.0)
        to_u = jnp.where(real, i * (1.0 - u * u), 0.0)
        to_o = jnp.where(real, t * o * (1.0 - o), 0.0)
        back = f * keep
        saved = None
        for part in reversed(range(per_tile)):
            dh = jnp.where(real, soft + dh_carry, 0.0)
            dc = dc_carry + dh * to_c
            dz = join_gates([dc * to_i, dc * to_f, dc * to_u, dh * to_o], dz_ref.shape[1])
            saved = dz if saved is None else jnp.where(row >= (part + 1) * batch, saved, dz)
            dh_carry = dot(dz.astype(BF), w_ref[...]) * keep
            dc_carry = dc * back
            dh_carry, dc_carry = (
                pltpu.roll(dh_carry, 8 - batch, 0),
                pltpu.roll(dc_carry, 8 - batch, 0),
            )
        dz_ref[rows, :] = saved
        return dh_carry, dc_carry

    zero = jnp.zeros((8, HP), F32)
    lax.fori_loop(0, tiles, tile, (zero, zero))


def in_vmem(kernel, out_shapes, *operands):
    return pl.pallas_call(
        kernel,
        out_shape=out_shapes,
        in_specs=[pl.BlockSpec(memory_space=pltpu.VMEM)] * len(operands),
        out_specs=jax.tree.map(lambda _: pl.BlockSpec(memory_space=pltpu.VMEM), out_shapes),
        compiler_params=pltpu.CompilerParams(vmem_limit_bytes=48 * 2**20),
    )(*operands)


def softmax_kernel(
    vocab,
    blocks,
    h_ref,
    h_back_ref,
    w_ref,
    target_ref,
    scale_ref,
    loss_ref,
    grad_h_ref,
    grad_w_ref,
    logits,
    top,
    total,
    picked,
):
    phase, at = pl.program_id(0), pl.program_id(1)
    width = w_ref.shape[-1]
    rows = h_ref.shape[0]
    w = w_ref[...].reshape(-1, width)
    column = at * width + lax.broadcasted_iota(jnp.int32, (rows, width), 1)
    where = pl.ds(pl.multiple_of(at * width, width), width)
    hit = column == target_ref[...]

    @pl.when((phase == 0) & (at == 0))
    def _():
        top[...] = jnp.full_like(top, -1e30)
        total[...] = jnp.zeros_like(total)
        picked[...] = jnp.zeros_like(picked)

    @pl.when(phase == 0)
    def _():
        now = jnp.where(column < vocab, dot(h_ref[...], w), -1e30)
        logits[:, where] = now
        before = top[...]
        after = jnp.maximum(before, jnp.max(now, axis=1, keepdims=True))
        total[...] = total[...] * jnp.exp(before - after) + jnp.sum(
            jnp.exp(now - after), axis=1, keepdims=True
        )
        top[...] = after
        picked[...] += jnp.sum(jnp.where(hit, now, 0.0), axis=1, keepdims=True)

    @pl.when((phase == 1) & (at == 0))
    def _():
        log_total = top[...] + jnp.log(total[...])
        loss_ref[...] = log_total - picked[...]
        top[...] = log_total
        grad_h_ref[...] = jnp.zeros_like(grad_h_ref)

    @pl.when(phase == 1)
    def _():
        share = jnp.exp(logits[:, where] - top[...])
        grad = ((share - hit.astype(F32)) * scale_ref[...]).astype(BF)
        grad_w_ref[...] = dot_rows(h_back_ref[...], grad).astype(BF).reshape(grad_w_ref.shape)
        grad_h_ref[...] += dot_cols(grad, w)


def word_softmax(plan, h, h_back, weights, target, scale):
    rows, depth = h.shape
    n = plan.fsdp
    per_slot, half = plan.block
    width = 512
    while half % width:
        width -= LANE
    per_half = half // width
    whole = lambda p, j: (0, 0)
    return pl.pallas_call(
        functools.partial(softmax_kernel, plan.width, 2 * per_half),
        out_shape=[
            jax.ShapeDtypeStruct((rows, 1), F32),
            jax.ShapeDtypeStruct((rows, depth), F32),
            jax.ShapeDtypeStruct(plan.shape, BF),
        ],
        grid=(2, 2 * per_half),
        in_specs=[
            pl.BlockSpec((rows, depth), whole),
            pl.BlockSpec((rows, depth), whole),
            pl.BlockSpec(
                (n, 1, per_slot, width), lambda p, j: (0, j // per_half, 0, j % per_half)
            ),
            pl.BlockSpec((rows, 1), whole),
            pl.BlockSpec((rows, 1), whole),
        ],
        out_specs=[
            pl.BlockSpec((rows, 1), whole),
            pl.BlockSpec((rows, depth), whole),
            pl.BlockSpec(
                (1, n, per_slot, width),
                lambda p, j: (p * (j // per_half), 0, 0, p * (j % per_half)),
            ),
        ],
        scratch_shapes=[
            pltpu.VMEM((rows, 2 * half), F32),
            pltpu.VMEM((rows, 1), F32),
            pltpu.VMEM((rows, 1), F32),
            pltpu.VMEM((rows, 1), F32),
        ],
        compiler_params=pltpu.CompilerParams(vmem_limit_bytes=48 * 2**20),
    )(h, h_back, weights, target, scale)


def shards(
    fsdp_count,
    dp_count,
    chars,
    lengths,
    targets,
    resets,
    init_state,
    window_grad,
    char_table,
    conv_weight,
    conv_bias,
    highway_flat,
    lstm_flat,
    soft_flat,
):
    micro_count, streams, step_count, letters = chars.shape
    char_count, embed_dim = char_table.shape
    filters = conv_weight.shape[1]
    batch = micro_count * streams
    words = step_count * batch
    rows = up_to(words, 16)
    fp = up_to(filters + 1, LANE)
    dp_at, fsdp_at = lax.axis_index("dp"), lax.axis_index("fsdp")
    highway = Windows(
        highway_flat.shape[0] * fsdp_count, filters, 4 * (filters + 1), fsdp_count, dp_count, True
    )
    lstm_used = filters + H + 1
    lstm = Windows(
        lstm_flat.shape[0] * fsdp_count, 4 * H, lstm_used, fsdp_count, dp_count, False
    )
    soft = Windows(soft_flat.shape[0] * fsdp_count, V, H + 1, fsdp_count, dp_count, False)

    soft_own = soft.from_flat(soft_flat, fsdp_at)
    soft_all = lax.all_gather(soft_own, "fsdp", axis=0)
    highway_all, lstm_all = gather(
        [highway, lstm],
        [highway.from_flat(highway_flat, fsdp_at), lstm.from_flat(lstm_flat, fsdp_at)],
        1,
    )
    highway_all = highway_all.reshape(-1, highway.columns)
    lstm_all = lstm_all.reshape(2, -1, lstm.columns // 2)

    def by_step(array):
        return jnp.moveaxis(array.reshape((batch, step_count) + array.shape[3:]), 1, 0).reshape(
            (words,) + array.shape[3:]
        )

    def pad_rows(array, value=0):
        return jnp.pad(
            array,
            [(0, rows - words)] + [(0, 0)] * (array.ndim - 1),
            constant_values=value,
        )

    word_chars = pad_rows(by_step(chars))
    word_lengths = pad_rows(by_step(lengths))[:, None]
    position = jnp.arange(letters, dtype=jnp.int32)[None, :]
    codes = jnp.where(position < word_lengths, word_chars, -1)
    codes = jnp.pad(codes, ((0, 0), (0, SLOTS + KMAX - letters)), constant_values=-1)
    index = jnp.stack(
        [
            jnp.where(
                codes[:, q : q + SLOTS] >= 0, codes[:, q : q + SLOTS] + q * char_count, -1
            )
            for q in range(KMAX)
        ]
        + [jnp.full((rows, SLOTS), KMAX * char_count, jnp.int32)],
        axis=2,
    ).reshape(rows * SLOTS, KMAX + 1)
    column = np.arange(fp)
    widths = np.ones((fp,), np.int32)
    for cut_at in FILTER_CUTS:
        widths = widths + ((column >= filters * cut_at // 22) & (column < filters))
    widths = widths.astype(np.int32)
    kernel_mask = jnp.asarray(
        np.arange(KMAX * embed_dim)[:, None] // embed_dim < widths[None, :filters]
    )
    ones_row = KMAX * embed_dim
    kernel = jnp.concatenate(
        [jnp.where(kernel_mask, conv_weight, jnp.zeros_like(conv_weight)), conv_bias[None, :]], axis=0
    )
    kernel = jnp.pad(kernel, ((0, LANE - ones_row - 1), (0, fp - filters)))
    spread_table = jnp.concatenate(
        [
            jnp.pad(char_table, ((0, 0), (q * embed_dim, LANE - (q + 1) * embed_dim)))
            for q in range(KMAX)
        ]
        + [jnp.zeros((1, LANE), BF).at[0, ones_row].set(1.0)],
        axis=0,
    )
    spread_table = jnp.pad(spread_table, ((0, HOT - KMAX * char_count - 1), (0, 0)))
    conv_inputs = (index, word_lengths, spread_table, kernel, jnp.asarray(widths)[None, :])
    word_block = 16
    feature = pl.pallas_call(
        functools.partial(conv_forward_kernel, filters),
        out_shape=jax.ShapeDtypeStruct((rows, fp), BF),
        grid=(rows // word_block,),
        in_specs=conv_specs(word_block, fp),
        out_specs=pl.BlockSpec((word_block, fp), lambda i: (i, 0)),
        compiler_params=pltpu.CompilerParams(vmem_limit_bytes=48 * 2**20),
    )(*conv_inputs)

    filter_lane = jnp.arange(fp)[None, :]
    each_layer = 2 * (filters + 1)
    owner_rows = highway.rows

    def layer_map(row_map, layer):
        at = row_map - layer * each_layer
        inside = (row_map >= 0) & (at >= 0) & (at < each_layer)
        is_gate = inside & (at >= filters + 1)
        source = np.where(inside, np.where(is_gate, at - filters - 1, at), -1)
        return source.astype(np.int32), inside & ~is_gate, is_gate

    layers = []
    for layer in range(2):
        source, is_trans, is_gate = layer_map(highway.gathered, layer)
        live = np.nonzero(source.reshape(-1, owner_rows).max(axis=1) >= 0)[0]
        begin, end = int(live[0]) * owner_rows, (int(live[-1]) + 1) * owner_rows
        begin = begin // 16 * 16
        end = min(up_to(end, 16), source.shape[0])
        weights = highway_all[begin:end]
        mapping = one_hot_map(fp, source[begin:end])
        trans_mask = jnp.asarray(is_trans[begin:end].astype(np.float32))[None, :]
        gate_mask = jnp.asarray(is_gate[begin:end].astype(np.float32))[None, :]
        spread = dot(feature, mapping)
        both = jnp.concatenate([spread * trans_mask, spread * gate_mask], axis=0).astype(BF)
        sums = dot(both, weights)
        trans, gate = sums[:rows], jax.nn.sigmoid(sums[rows:])
        layers.append((feature, trans, gate, weights, mapping, trans_mask, gate_mask))
        value = gate * jax.nn.silu(trans) + (1.0 - gate) * feature.astype(F32)
        feature = jnp.where(
            filter_lane < filters, value, jnp.where(filter_lane == filters, 1.0, 0.0)
        ).astype(BF)

    lp = up_to(lstm_used, LANE)
    first_h = np.nonzero(lstm.gathered >= filters)[0][0] // 16 * 16
    last_x = min(up_to(int(np.nonzero((lstm.gathered >= 0) & (lstm.gathered < filters))[0][-1]) + 1, 16), lstm.gathered.shape[0])
    lstm_map = one_hot_map(lp, lstm.gathered)
    no_hidden = jnp.concatenate(
        [
            feature[:, :filters],
            jnp.zeros((rows, H), BF),
            jnp.ones((rows, 1), BF),
            jnp.zeros((rows, lp - lstm_used), BF),
        ],
        axis=1,
    )
    spread_x = dot(no_hidden, lstm_map).astype(BF)
    from_input = jnp.concatenate([dot(spread_x, lstm_all[0]), dot(spread_x, lstm_all[1])], axis=1)
    hidden_source = lstm.gathered[first_h:] - filters
    hidden_map = one_hot_map(HP, np.where((hidden_source >= 0) & (hidden_source < H), hidden_source, -1))
    recur = jnp.concatenate(
        [dot(hidden_map, lstm_all[h, first_h:]).astype(BF) for h in range(2)], axis=1
    )
    recur_t = jnp.concatenate(
        [
            lax.dot_general(
                lstm_all[h, first_h:],
                hidden_map,
                (((0,), (1,)), ((), ())),
                preferred_element_type=F32,
            ).astype(BF)
            for h in range(2)
        ],
        axis=0,
    )
    keep = pad_rows(by_step(1 - resets).astype(F32))[:, None]
    start = init_state.reshape(batch, 2, H)
    start = jnp.pad(start, ((0, 8 - batch), (0, 0), (0, HP - H)))
    states = [jax.ShapeDtypeStruct((rows, HP), F32)] * 8
    hp, cp, gate_i, gate_f, gate_u, gate_o, tanh_c, hidden = in_vmem(
        functools.partial(lstm_forward_kernel, batch),
        states,
        from_input,
        recur,
        start[:, 0].astype(BF).astype(F32),
        start[:, 1],
        keep,
    )

    hidden = hidden.astype(BF)
    soft_map = one_hot_map(HP, soft.gathered)
    spread_h = dot(hidden, soft_map).astype(BF)
    spread_h_back = dot(hidden, one_hot_map(HP, soft.reduced)).astype(BF)
    row_scale = jnp.broadcast_to(
        window_grad.reshape(1, batch) / step_count, (step_count, batch)
    ).reshape(words, 1)
    word_loss, grad_spread, soft_grad = word_softmax(
        soft,
        spread_h,
        spread_h_back,
        soft_all,
        pad_rows(by_step(targets), -1)[:, None],
        pad_rows(row_scale),
    )
    window_loss = jnp.mean(word_loss[:words, 0].reshape(step_count, batch), axis=0).reshape(
        micro_count, streams
    )
    grad_hidden = compress(grad_spread, soft_map)
    soft_part = reduce_scatter([soft], [soft_grad], 2)[0]

    dz = in_vmem(
        functools.partial(lstm_backward_kernel, batch),
        jax.ShapeDtypeStruct((rows, lstm.columns), F32),
        grad_hidden,
        recur_t,
        keep,
        cp,
        gate_i,
        gate_f,
        gate_u,
        gate_o,
        tanh_c,
    ).astype(BF)
    half = lstm.columns // 2
    lstm_in = jnp.concatenate(
        [
            feature[:, :filters],
            hp[:, :H].astype(BF),
            jnp.ones((rows, 1), BF),
            jnp.zeros((rows, lp - lstm_used), BF),
        ],
        axis=1,
    )
    lstm_in = dot(lstm_in, one_hot_map(lp, lstm.reduced)).astype(BF)
    lstm_grad = jnp.stack(
        [dot_rows(lstm_in, dz[:, h * half : (h + 1) * half]).astype(BF) for h in range(2)]
    ).reshape(lstm.shape)
    grad_spread = dot_cols(dz[:, :half], lstm_all[0, :last_x]) + dot_cols(
        dz[:, half:], lstm_all[1, :last_x]
    )
    input_source = lstm.gathered[:last_x]
    grad = compress(
        grad_spread, one_hot_map(fp, np.where(input_source < filters, input_source, -1))
    )

    grads_of, inputs_of = [], []
    for layer in (1, 0):
        layer_in, trans, gate, weights, mapping, trans_mask, gate_mask = layers[layer]
        sig = jax.nn.sigmoid(trans)
        silu = trans * sig
        grad = jnp.where(filter_lane < filters, grad, 0.0)
        grad_trans = (grad * gate * sig * (1.0 + trans * (1.0 - sig))).astype(BF)
        grad_gate = (grad * (silu - layer_in.astype(F32)) * gate * (1.0 - gate)).astype(BF)
        pair = jnp.concatenate([grad_trans, grad_gate], axis=0)
        spread = dot_cols(pair, weights)
        grad = grad * (1.0 - gate) + compress(
            spread[:rows] * trans_mask + spread[rows:] * gate_mask, mapping
        )
        source, is_trans, is_gate = layer_map(highway.reduced, layer)
        spread_in = dot(layer_in, one_hot_map(fp, source))
        inputs_of = [
            (spread_in * jnp.asarray(is_trans.astype(np.float32))[None, :]).astype(BF),
            (spread_in * jnp.asarray(is_gate.astype(np.float32))[None, :]).astype(BF),
        ] + inputs_of
        grads_of = [pair] + grads_of
    highway_grad = (
        dot_rows(jnp.concatenate(inputs_of, axis=0), jnp.concatenate(grads_of, axis=0))
        .astype(BF)
        .reshape(highway.shape)
    )

    grad = jnp.where(filter_lane < filters, grad, 0.0)
    kernel_grad, hot_grad = pl.pallas_call(
        conv_backward_kernel,
        out_shape=[
            jax.ShapeDtypeStruct((LANE, fp), F32),
            jax.ShapeDtypeStruct((HOT, LANE), F32),
        ],
        grid=(rows // word_block,),
        in_specs=conv_specs(word_block, fp) + [pl.BlockSpec((word_block, fp), lambda i: (i, 0))],
        out_specs=[
            pl.BlockSpec((LANE, fp), lambda i: (0, 0)),
            pl.BlockSpec((HOT, LANE), lambda i: (0, 0)),
        ],
        compiler_params=pltpu.CompilerParams(vmem_limit_bytes=48 * 2**20),
    )(*conv_inputs, grad)
    table_grad = sum(
        hot_grad[q * char_count : (q + 1) * char_count, q * embed_dim : (q + 1) * embed_dim]
        for q in range(KMAX)
    )
    kernel_grad, table_grad = lax.psum((kernel_grad, table_grad), ("dp", "fsdp"))
    conv_weight_grad = jnp.where(kernel_mask, kernel_grad[:ones_row, :filters], 0.0)
    conv_bias_grad = kernel_grad[ones_row, :filters]

    highway_part, lstm_part = reduce_scatter([highway, lstm], [highway_grad, lstm_grad], 3)

    def own_window(plan, part):
        if dp_count > 2:
            groups = [list(range(h, dp_count, 2)) for h in range(2)]
            part = lax.psum(part, "dp", axis_index_groups=groups)
        if plan.by_rows:
            at = dp_at // 2
        else:
            part = jnp.concatenate([part[0], part[1]], axis=1)
            at = dp_at
        window = lax.dynamic_slice_in_dim(part, at * plan.rows, plan.rows, 0)
        return plan.to_flat(window, dp_at, fsdp_at)

    return (
        window_loss,
        table_grad,
        conv_weight_grad,
        conv_bias_grad,
        own_window(highway, highway_part),
        own_window(lstm, lstm_part),
        own_window(soft, soft_part),
    )


def solution(mesh):
    in_specs = (
        P(None, ("dp", "fsdp"), None, None),
        P(None, ("dp", "fsdp"), None),
        P(None, ("dp", "fsdp"), None),
        P(None, ("dp", "fsdp"), None),
        P(None, ("dp", "fsdp"), None, None),
        P(None, ("dp", "fsdp")),
        P(),
        P(),
        P(),
        P("fsdp", None),
        P("fsdp", None),
        P("fsdp", None),
    )
    out_specs = (
        P(None, ("dp", "fsdp")),
        P(),
        P(),
        P(),
        P(("dp", "fsdp"), None),
        P(("dp", "fsdp"), None),
        P(("dp", "fsdp"), None),
    )
    return jax.shard_map(
        functools.partial(shards, mesh.shape["fsdp"], mesh.shape["dp"]),
        mesh=mesh,
        in_specs=in_specs,
        out_specs=out_specs,
        check_vma=False,
    )
```

```python
import functools

import jax
import jax.numpy as jnp
import numpy as np
from jax import lax
from jax.experimental import pallas as pl
from jax.experimental.pallas import tpu as pltpu
from jax.sharding import PartitionSpec as P

H = 650
V = 10000
KMAX = 7
LANE = 128
HP = 768
SLOTS = 24
HOT = 384
FILTER_CUTS = (1, 3, 6, 10, 14, 18)
MESH = pl.DeviceIdType.MESH
BF = jnp.bfloat16
F32 = jnp.float32


def up_to(value, unit):
    return -(-value // unit) * unit


def dot(left, right):
    return jnp.dot(left, right, preferred_element_type=F32)


def dot_rows(left, right):
    return lax.dot_general(left, right, (((0,), (0,)), ((), ())), preferred_element_type=F32)


def dot_cols(left, right):
    return lax.dot_general(left, right, (((1,), (1,)), ((), ())), preferred_element_type=F32)


class Windows:
    def __init__(self, flat_rows, width, used, fsdp, dp, by_rows):
        owners = fsdp * dp
        self.width, self.by_rows, self.fsdp, self.dp = width, by_rows, fsdp, dp
        self.entries = flat_rows * LANE // owners
        starts = [o * self.entries // width for o in range(owners)]
        spans = [
            (o * self.entries % width + self.entries - 1) // width + 1 for o in range(owners)
        ]
        rows = max(spans)
        while (dp * rows) % 16 or (by_rows and (dp // 2 * rows) % 16):
            rows += 1
        self.rows = rows
        self.columns = up_to(width, LANE) if by_rows else 2 * up_to(-(-width // 2), LANE)
        self.block = (
            (dp // 2 * rows, self.columns) if by_rows else (dp * rows, self.columns // 2)
        )
        self.shape = (fsdp, 2) + self.block if by_rows else (2, fsdp) + self.block

        def row_map(order):
            rows_of = [
                [starts[o] + i if i < spans[o] and starts[o] + i < used else -1 for i in range(rows)]
                for o in order
            ]
            return np.array(rows_of, np.int32).reshape(-1)

        self.gathered = row_map(range(owners))
        if by_rows:
            order = [
                (2 * jj + h) * fsdp + f
                for f in range(fsdp)
                for h in range(2)
                for jj in range(dp // 2)
            ]
        else:
            order = [d * fsdp + f for f in range(fsdp) for d in range(dp)]
        self.reduced = row_map(order)

    dtype = BF

    def pick(self, ref, half, slot):
        return ref.at[slot, half] if self.by_rows else ref.at[half, slot]

    def from_flat(self, shard, fsdp_at):
        parts = []
        flat = shard.reshape(-1)
        for j in range(self.dp):
            shift = lax.rem((fsdp_at * self.dp + j) * self.entries, self.width)
            piece = lax.dynamic_update_slice(
                jnp.zeros((self.rows * self.width,), BF),
                flat[j * self.entries : (j + 1) * self.entries],
                (shift,),
            ).reshape(self.rows, self.width)
            parts.append(jnp.pad(piece, ((0, 0), (0, self.columns - self.width))))
        joined = jnp.concatenate(parts, axis=0)
        if self.by_rows:
            return joined.reshape((2,) + self.block)
        half = self.columns // 2
        return jnp.stack([joined[:, :half], joined[:, half:]])

    def to_flat(self, window, dp_at, fsdp_at):
        shift = lax.rem((dp_at * self.fsdp + fsdp_at) * self.entries, self.width)
        flat = window[:, : self.width].reshape(-1)
        return lax.dynamic_slice(flat, (shift,), (self.entries,)).reshape(-1, LANE)


def one_hot_map(rows, row_map):
    return (
        lax.broadcasted_iota(jnp.int32, (rows, row_map.shape[0]), 0) == jnp.asarray(row_map)[None, :]
    ).astype(BF)


def compress(spread, mapping):
    high = lax.reduce_precision(spread, 8, 7)
    both = jnp.concatenate([high.astype(BF), (spread - high).astype(BF)], axis=0)
    product = dot_cols(both, mapping)
    count = spread.shape[0]
    return product[:count] + product[count:]


def greet(place_of, lengthwise):
    d, f, z = place_of.d, place_of.f, place_of.z
    barrier = pltpu.get_barrier_semaphore()
    for target in (place_of.partner1, place_of.partner3, place_of.sibling):
        pl.semaphore_signal(barrier, inc=1, device_id=target, device_id_type=MESH)

    @pl.when(z > 0)
    def _():
        pl.semaphore_signal(barrier, inc=1, device_id=(d, f - 4), device_id_type=MESH)

    @pl.when(z < lengthwise - 1)
    def _():
        pl.semaphore_signal(barrier, inc=1, device_id=(d, f + 4), device_id_type=MESH)

    has_down = (z > 0).astype(jnp.int32)
    has_up = (z < lengthwise - 1).astype(jnp.int32)
    pl.semaphore_wait(barrier, 3 + has_down + has_up)


class Place:
    def __init__(self):
        self.d, self.f = lax.axis_index("dp"), lax.axis_index("fsdp")
        self.c = lax.rem(self.d, 2)
        x, y, self.z = lax.rem(self.f, 2), lax.rem(self.f // 2, 2), self.f // 4
        self.first = x + self.c * (y - x)
        self.last = y + self.c * (x - y)
        self.stride1, self.stride3 = 1 + self.c, 2 - self.c
        self.flip1 = self.stride1 * (1 - 2 * self.first)
        self.flip3 = self.stride3 * (1 - 2 * self.last)
        self.partner1 = (self.d, self.f + self.flip1)
        self.partner3 = (self.d, self.f + self.flip3)
        self.sibling = (self.d + 1 - 2 * self.c, self.f)

    def last_bit(self, block):
        bit_x, bit_y = lax.rem(block, 2), lax.rem(block // 2, 2)
        return bit_y + self.c * (bit_x - bit_y)


def remote(src, dst, send, recv, target):
    return pltpu.make_async_remote_copy(
        src_ref=src,
        dst_ref=dst,
        send_sem=send,
        recv_sem=recv,
        device_id=target,
        device_id_type=MESH,
    )


class Gather:
    def __init__(self, plans, own, outs, sems, shared):
        self.plans, self.own, self.outs, self.sems, self.shared = plans, own, outs, sems, shared
        self.n = plans[0].fsdp
        self.lengthwise = self.n // 4
        self.at = Place()

    RECV, SIB_RECV, ONE, UP, DOWN, LAST, SIB, LOCAL = range(8)

    @staticmethod
    def semaphores(plans):
        return pltpu.SemaphoreType.DMA((8 * len(plans) * plans[0].fsdp,))

    def sem(self, kind, a, block):
        return self.sems.at[(kind * len(self.plans) + a) * self.n + block]

    def source(self, a, half):
        return self.own[a].at[half] if self.shared else self.own[a]

    def copy(self, kind, a, block, target, own=False):
        here = self.plans[a].pick(self.outs[a], self.at.c, block)
        return remote(
            self.source(a, self.at.c) if own else here,
            here,
            self.sem(kind, a, block),
            self.sem(self.SIB_RECV if kind == self.SIB else self.RECV, a, block),
            target,
        )

    def arrived(self, a, block, kind=RECV):
        c = self.at.c
        here = self.plans[a].pick(self.outs[a], 1 - c if kind == self.SIB_RECV else c, block)
        remote(
            here, here, self.sem(self.SIB, a, block), self.sem(kind, a, block), self.at.sibling
        ).wait_recv()

    def sent(self, kind, a, block):
        self.copy(kind, a, block, self.at.sibling).wait_send()

    def local(self, a, half):
        return pltpu.make_async_copy(
            self.source(a, half),
            self.plans[a].pick(self.outs[a], half, self.at.f),
            self.sem(self.LOCAL, a, half if self.shared else 0),
        )

    def send_up(self, a, block, own=False):
        @pl.when(self.at.z < self.lengthwise - 1)
        def _():
            self.copy(self.UP, a, block, (self.at.d, self.at.f + 4), own).start()

    def send_down(self, a, block, own=False):
        @pl.when(self.at.z > 0)
        def _():
            self.copy(self.DOWN, a, block, (self.at.d, self.at.f - 4), own).start()

    def begin(self, a):
        at = self.at
        self.copy(self.ONE, a, at.f, at.partner1, True).start()
        self.send_up(a, at.f, True)
        self.send_down(a, at.f, True)
        self.copy(self.LAST, a, at.f, at.partner3, True).start()
        if self.shared:
            for half in (0, 1):
                self.local(a, half).start()
        else:
            self.copy(self.SIB, a, at.f, at.sibling, True).start()
            self.local(a, at.c).start()

    def near(self, a):
        at = self.at
        block = at.f + at.flip1
        self.arrived(a, block)
        self.send_up(a, block)
        self.send_down(a, block)
        self.copy(self.LAST, a, block, at.partner3).start()
        self.copy(self.SIB, a, block, at.sibling).start()

    def line(self, a, distance):
        for sign in (1, -1):
            z = self.at.z - sign * distance

            def take(sign=sign):
                for flip in (0, 1):
                    block = self.at.f - 4 * sign * distance + flip * self.at.flip1
                    self.arrived(a, block)
                    (self.send_up if sign == 1 else self.send_down)(a, block)
                    self.copy(self.LAST, a, block, self.at.partner3).start()
                    self.copy(self.SIB, a, block, self.at.sibling).start()

            pl.when((z >= 0) & (z < self.lengthwise))(take)

    def across(self, a, distance):
        for sign in (1,) if distance == 0 else (1, -1):
            z = self.at.z - sign * distance

            def take(sign=sign):
                for flip in (0, 1):
                    block = (
                        self.at.f - 4 * sign * distance + flip * self.at.flip1 + self.at.flip3
                    )
                    self.arrived(a, block)
                    self.copy(self.SIB, a, block, self.at.sibling).start()

            pl.when((z >= 0) & (z < self.lengthwise))(take)

    def steps(self):
        count = len(self.plans)
        steps = [functools.partial(self.near, a) for a in range(count)]
        for distance in range(1, self.lengthwise):
            steps += [functools.partial(self.line, a, distance) for a in range(count)]
            steps += [functools.partial(self.across, a, distance - 1) for a in range(count)]
        steps += [functools.partial(self.across, a, self.lengthwise - 1) for a in range(count)]
        return steps

    def finish(self):
        at = self.at
        for a in range(len(self.plans)):

            def block_done(block, _, a=a):
                z = block // 4

                def from_sibling():
                    self.arrived(a, block, self.SIB_RECV)
                    self.sent(self.SIB, a, block)

                if self.shared:
                    pl.when(jnp.logical_not(block == at.f))(from_sibling)
                else:
                    from_sibling()

                @pl.when(at.last_bit(block) == at.last)
                def _():
                    self.sent(self.LAST, a, block)

                    @pl.when((z <= at.z) & (at.z < self.lengthwise - 1))
                    def _():
                        self.sent(self.UP, a, block)

                    @pl.when((z >= at.z) & (at.z > 0))
                    def _():
                        self.sent(self.DOWN, a, block)

                return 0

            lax.fori_loop(0, self.n, block_done, 0)
            self.sent(self.ONE, a, at.f)
            if self.shared:
                for half in (0, 1):
                    self.local(a, half).wait()
            else:
                self.local(a, at.c).wait()


def gather_kernel(plans, *refs):
    count = len(plans)
    work = Gather(plans, refs[:count], refs[count : 2 * count], refs[2 * count], True)
    greet(work.at, work.lengthwise)
    for a in range(count):
        work.begin(a)
    for step in work.steps():
        step()
    work.finish()


def gather(plans, shards, collective_id):
    count = len(plans)
    return pl.pallas_call(
        functools.partial(gather_kernel, plans),
        out_shape=[jax.ShapeDtypeStruct(plan.shape, plan.dtype) for plan in plans],
        in_specs=[pl.BlockSpec(memory_space=pl.ANY)] * count,
        out_specs=[pl.BlockSpec(memory_space=pl.ANY)] * count,
        scratch_shapes=[Gather.semaphores(plans)],
        compiler_params=pltpu.CompilerParams(collective_id=collective_id, has_side_effects=True),
    )(*shards)


class Reduce:
    SIB, SIB_RECV, LOAD, NEAR, NEAR_RECV, UP, UP_RECV, DOWN, DOWN_RECV, END = range(10)

    def __init__(self, plans, ins, totals, scratch):
        count = len(plans)
        self.plans, self.ins, self.totals = plans, ins, totals
        self.held, self.landed, self.flow_up, self.flow_down, self.close, self.cross = (
            scratch[k * count : (k + 1) * count] for k in range(6)
        )
        self.sems = scratch[6 * count]
        self.n = plans[0].fsdp
        self.lengthwise = self.n // 4
        self.at = Place()

    @staticmethod
    def scratch(plans):
        n = plans[0].fsdp
        return (
            [pltpu.VMEM((n,) + plan.block, plan.dtype) for plan in plans] * 2
            + [pltpu.VMEM((n // 2,) + plan.block, plan.dtype) for plan in plans] * 3
            + [pltpu.VMEM(plan.block, plan.dtype) for plan in plans]
            + [pltpu.SemaphoreType.DMA((10 * len(plans) * n,))]
        )

    def sem(self, kind, a, block):
        return self.sems.at[(kind * len(self.plans) + a) * self.n + block]

    def slot(self, z, b1, b3):
        return 4 * z + self.at.stride1 * b1 + self.at.stride3 * b3

    def item(self, t):
        pair, b3 = t // 2, lax.rem(t, 2)
        half = pair // 2
        z = jnp.where(lax.rem(pair, 2) == 0, half, self.lengthwise - 1 - half)
        return z, b3

    def to_sibling(self, a, block):
        return remote(
            self.plans[a].pick(self.ins[a], 1 - self.at.c, block),
            self.landed[a].at[block],
            self.sem(self.SIB, a, block),
            self.sem(self.SIB_RECV, a, block),
            self.at.sibling,
        )

    def load(self, a, block):
        return pltpu.make_async_copy(
            self.plans[a].pick(self.ins[a], self.at.c, block),
            self.held[a].at[block],
            self.sem(self.LOAD, a, block),
        )

    def to_near(self, a, z, b3):
        return remote(
            self.held[a].at[self.slot(z, 1 - self.at.first, b3)],
            self.close[a].at[2 * z + b3],
            self.sem(self.NEAR, a, 2 * z + b3),
            self.sem(self.NEAR_RECV, a, 2 * z + b3),
            self.at.partner1,
        )

    def along(self, up, a, z, b3):
        return remote(
            self.held[a].at[self.slot(z, self.at.first, b3)],
            (self.flow_up if up else self.flow_down)[a].at[2 * z + b3],
            self.sem(self.UP if up else self.DOWN, a, 2 * z + b3),
            self.sem(self.UP_RECV if up else self.DOWN_RECV, a, 2 * z + b3),
            (self.at.d, self.at.f + (4 if up else -4)),
        )

    def to_cross(self, a):
        return remote(
            self.held[a].at[self.slot(self.at.z, self.at.first, 1 - self.at.last)],
            self.cross[a],
            self.sem(self.END, a, 0),
            self.sem(self.END, a, 1),
            self.at.partner3,
        )

    def rows(self, a, body):
        unit = 16

        def step(i, _):
            body(pl.ds(pl.multiple_of(i * unit, unit), unit))
            return 0

        if self.plans[a].block[0] < unit:
            body(slice(None))
        else:
            lax.fori_loop(0, self.plans[a].block[0] // unit, step, 0)

    def add(self, a, block, sources):
        held = self.held[a]

        def body(where):
            total = held[block, where, :].astype(F32)
            for ref, at in sources:
                total += ref[at, where, :].astype(F32)
            held[block, where, :] = total.astype(held.dtype)

        self.rows(a, body)

    def begin(self, a):
        for flip in (1, 0):
            b1 = self.at.first + flip * (1 - 2 * self.at.first)

            def start(t, _, b1=b1):
                z, b3 = self.item(t)
                block = self.slot(z, b1, b3)
                self.to_sibling(a, block).start()
                self.load(a, block).start()
                return 0

            lax.fori_loop(0, 2 * self.lengthwise, start, 0)

    def first_leg(self, a, t):
        z, b3 = self.item(t)
        block = self.slot(z, 1 - self.at.first, b3)
        self.load(a, block).wait()
        self.to_sibling(a, block).wait_recv()
        self.add(a, block, [(self.landed[a], block)])
        self.to_near(a, z, b3).start()

    def middle_leg(self, a, t):
        z, b3 = self.item(t)
        block = self.slot(z, self.at.first, b3)
        flow = 2 * z + b3
        base = [(self.landed[a], block), (self.close[a], flow)]
        self.load(a, block).wait()
        self.to_sibling(a, block).wait_recv()
        self.to_near(a, z, b3).wait_recv()

        def onward(up):
            incoming = self.at.z > 0 if up else self.at.z < self.lengthwise - 1

            @pl.when(incoming)
            def _():
                self.along(up, a, z, b3).wait_recv()
                flows = self.flow_up if up else self.flow_down
                self.add(a, block, base + [(flows[a], flow)])

            @pl.when(jnp.logical_not(incoming))
            def _():
                self.add(a, block, base)

            self.along(up, a, z, b3).start()

        pl.when(z > self.at.z)(functools.partial(onward, True))
        pl.when(z < self.at.z)(functools.partial(onward, False))

        @pl.when(z == self.at.z)
        def _():
            self.add(a, block, base)

    def own(self, a, b3):
        z = self.at.z
        block = self.slot(z, self.at.first, b3)
        for up in (True, False):

            @pl.when(z > 0 if up else z < self.lengthwise - 1)
            def _(up=up):
                self.along(up, a, z, b3).wait_recv()
                flows = self.flow_up if up else self.flow_down
                self.add(a, block, [(flows[a], 2 * z + b3)])

    def cross_over(self, a):
        self.own(a, 1 - self.at.last)
        self.to_cross(a).start()

    def last_leg(self, a):
        self.own(a, self.at.last)
        self.to_cross(a).wait_recv()
        block = self.slot(self.at.z, self.at.first, self.at.last)

        def body(where):
            total = self.held[a][block, where, :].astype(F32) + self.cross[a][where, :].astype(F32)
            self.totals[a][where, :] = total

        self.rows(a, body)

    def finish(self, a):
        def done(t, _):
            z, b3 = self.item(t)
            for b1 in (self.at.first, 1 - self.at.first):
                self.to_sibling(a, self.slot(z, b1, b3)).wait_send()
            self.to_near(a, z, b3).wait_send()
            for up in (True, False):

                @pl.when(z > self.at.z if up else z < self.at.z)
                def _(up=up):
                    self.along(up, a, z, b3).wait_send()

            return 0

        lax.fori_loop(0, 2 * self.lengthwise, done, 0)
        self.to_cross(a).wait_send()


def pair_exchange(plans, totals, outs, sems, at):
    copies = []
    for a, plan in enumerate(plans):
        if not plan.by_rows:
            copies.append(
                remote(
                    totals[a], outs[a].at[at.c], sems.at[2 * a], sems.at[2 * a + 1], at.sibling
                )
            )
    return copies


def reduce_kernel(plans, *refs):
    count = len(plans)
    ins, outs, scratch = refs[:count], refs[count : 2 * count], refs[2 * count :]
    totals = [out if plan.by_rows else out.at[Place().c] for plan, out in zip(plans, outs)]
    work = Reduce(plans, ins, totals, scratch[:-1])
    at, items = work.at, 2 * work.lengthwise
    greet(at, work.lengthwise)
    for a in range(count):
        work.begin(a)

    def leg(body, a, begin, end):
        def step(t, _):
            body(a, t)
            return 0

        lax.fori_loop(begin, end, step, 0)

    for a in range(count):
        leg(work.first_leg, a, 0, items)
    for a in range(count):
        leg(work.middle_leg, a, 0, items)
    for a in range(count):
        work.cross_over(a)
    copies = pair_exchange(plans, totals, outs, scratch[-1], at)
    for a in range(count):
        work.last_leg(a)
    for copy in copies:
        copy.start()
    for a in range(count):
        work.finish(a)
    for copy in copies:
        copy.wait()


def reduce_out(plan):
    return jax.ShapeDtypeStruct(plan.block if plan.by_rows else (2,) + plan.block, F32)


def reduce_scatter(plans, grads, collective_id):
    count = len(plans)
    return pl.pallas_call(
        functools.partial(reduce_kernel, plans),
        out_shape=[reduce_out(plan) for plan in plans],
        in_specs=[pl.BlockSpec(memory_space=pl.ANY)] * count,
        out_specs=[pl.BlockSpec(memory_space=pltpu.VMEM)] * count,
        scratch_shapes=Reduce.scratch(plans) + [pltpu.SemaphoreType.DMA((2 * count,))],
        compiler_params=pltpu.CompilerParams(
            collective_id=collective_id, has_side_effects=True, vmem_limit_bytes=60 * 2**20
        ),
    )(*grads)


def hot_rows(index):
    lane = lax.broadcasted_iota(jnp.int32, (index.shape[0], HOT), 1)
    hit = lane == index[:, 0:1]
    for q in range(1, KMAX + 1):
        hit = jnp.logical_or(hit, lane == index[:, q : q + 1])
    return hit.astype(F32).astype(BF)


def conv_forward_kernel(filters, index_ref, length_ref, table_ref, kernel_ref, width_ref, out_ref):
    words = length_ref.shape[0]
    windows = dot(hot_rows(index_ref[...]), table_ref[...]).astype(BF)
    chunk = 384
    for at in range(0, kernel_ref.shape[1], chunk):
        columns = slice(at, at + chunk)
        activated = jnp.tanh(dot(windows, kernel_ref[:, columns])).reshape(words, SLOTS, chunk)
        counts = jnp.maximum(length_ref[...] - width_ref[:, columns] + 1, 1)
        position = lax.broadcasted_iota(jnp.int32, (words, SLOTS, chunk), 1)
        inside = position < counts[:, None, :]
        totals = jnp.sum(jnp.where(inside, jnp.exp(activated), 0.0), axis=1)
        pooled = jnp.log(totals) - jnp.log(counts.astype(F32))
        lane = at + lax.broadcasted_iota(jnp.int32, (words, chunk), 1)
        out_ref[:, columns] = jnp.where(
            lane < filters, pooled, jnp.where(lane == filters, 1.0, 0.0)
        ).astype(BF)


def conv_backward_block(index, lengths, refs, grad_ref, where, kernel_grad_ref, hot_grad_ref):
    table_ref, kernel_ref, width_ref = refs
    words = lengths.shape[0]
    hot = hot_rows(index)
    windows = dot(hot, table_ref[...]).astype(BF)
    chunk = 384
    grad_windows = jnp.zeros(windows.shape, F32)
    for at in range(0, kernel_ref.shape[1], chunk):
        columns = slice(at, at + chunk)
        activated = jnp.tanh(dot(windows, kernel_ref[:, columns])).reshape(words, SLOTS, chunk)
        counts = jnp.maximum(lengths - width_ref[:, columns] + 1, 1)
        position = lax.broadcasted_iota(jnp.int32, (words, SLOTS, chunk), 1)
        inside = position < counts[:, None, :]
        weight = jnp.where(inside, jnp.exp(activated), 0.0)
        share = grad_ref[where, columns] / jnp.sum(weight, axis=1)
        grad = (share[:, None, :] * weight * (1.0 - activated * activated)).astype(BF)
        grad = grad.reshape(words * SLOTS, chunk)
        kernel_grad_ref[:, columns] += dot_rows(windows, grad)
        grad_windows += dot_cols(grad, kernel_ref[:, columns])
    hot_grad_ref[...] += dot_rows(hot, grad_windows.astype(BF))


def conv_specs(words, filters_padded):
    return [
        pl.BlockSpec((words * SLOTS, 8), lambda i: (i, 0)),
        pl.BlockSpec((words, 1), lambda i: (i, 0)),
        pl.BlockSpec((HOT, LANE), lambda i: (0, 0)),
        pl.BlockSpec((LANE, filters_padded), lambda i: (0, 0)),
        pl.BlockSpec((1, filters_padded), lambda i: (0, 0)),
    ]


class Dense:
    by_rows = False
    dtype = F32

    def __init__(self, rows, columns, fsdp):
        self.fsdp = fsdp
        self.filled = rows
        self.block = (up_to(-(-rows // fsdp), 8), columns // 2)
        self.shape = (2, fsdp) + self.block

    def pick(self, ref, half, slot):
        return ref.at[half, slot]


WORD_BLOCK = 16


def tail_kernel(plans, blocks, *refs):
    conv, rest = plans[0], plans[1:]
    count = len(plans)
    ins, refs = refs[: count - 1], refs[count - 1 :]
    index_ref, length_ref, table_ref, kernel_ref, width_ref, grad_ref, mask_ref, fold_ref = refs[:8]
    outs, refs = refs[8 : 8 + count], refs[8 + count :]
    conv_out, rest_outs = outs[0], outs[1:]
    kernel_grad, hot_grad, conv_in, conv_total = refs[:4]
    pair_sems, gather_sems = refs[4:6]
    at = Place()
    totals = [conv_total] + [
        out if plan.by_rows else out.at[at.c] for plan, out in zip(rest, rest_outs)
    ]
    work = Reduce(plans, [conv_in] + list(ins), totals, refs[6:])
    items = 2 * work.lengthwise
    greet(at, work.lengthwise)
    for a in range(1, count):
        work.begin(a)
    kernel_grad[...] = jnp.zeros_like(kernel_grad)
    hot_grad[...] = jnp.zeros_like(hot_grad)
    conv_in[...] = jnp.zeros_like(conv_in)

    def compute(i):
        words = pl.ds(pl.multiple_of(i * WORD_BLOCK, WORD_BLOCK), WORD_BLOCK)
        slots = pl.ds(pl.multiple_of(i * WORD_BLOCK * SLOTS, WORD_BLOCK * SLOTS), WORD_BLOCK * SLOTS)
        conv_backward_block(
            index_ref[slots, :],
            length_ref[words, :],
            (table_ref, kernel_ref, width_ref),
            grad_ref,
            words,
            kernel_grad,
            hot_grad,
        )

    lead = 2

    def together(t, _):
        @pl.when(t < items)
        def _():
            for a in range(1, count):
                work.first_leg(a, t)

        pl.when(t < blocks)(functools.partial(compute, t))

        @pl.when((t >= lead) & (t < items + lead))
        def _():
            for a in range(1, count):
                work.middle_leg(a, t - lead)

        return 0

    lax.fori_loop(0, max(items + lead, blocks), together, 0)

    wide = kernel_ref.shape[1]
    kernel_grad[:, wide:] = jnp.dot(
        fold_ref[...],
        hot_grad[...] * mask_ref[...],
        precision=lax.Precision.HIGHEST,
        preferred_element_type=F32,
    )
    depth, half = conv.block
    for block in range(conv.filled // depth):
        for h in range(2):
            conv_in[h, block] = kernel_grad[
                block * depth : (block + 1) * depth, h * half : (h + 1) * half
            ]
    work.begin(0)

    def leg(body):
        def step(t, _):
            body(0, t)
            return 0

        lax.fori_loop(0, items, step, 0)

    leg(work.first_leg)
    leg(work.middle_leg)
    for a in range(count):
        work.cross_over(a)
    work.last_leg(0)
    spread = Gather([conv], [conv_total], [conv_out], gather_sems, False)
    spread.begin(0)
    copies = pair_exchange(rest, totals[1:], rest_outs, pair_sems, at)
    for a in range(1, count):
        work.last_leg(a)
    for copy in copies:
        copy.start()
    for step in spread.steps():
        step()
    spread.finish()
    for a in range(count):
        work.finish(a)
    for copy in copies:
        copy.wait()


def tail(plans, grads, conv_inputs, grad, mask, fold, collective_id):
    conv, rest = plans[0], plans[1:]
    words = grad.shape[0]
    return pl.pallas_call(
        functools.partial(tail_kernel, plans, words // WORD_BLOCK),
        out_shape=[jax.ShapeDtypeStruct(conv.shape, F32)] + [reduce_out(plan) for plan in rest],
        in_specs=[pl.BlockSpec(memory_space=pl.ANY)] * len(rest)
        + [pl.BlockSpec(memory_space=pltpu.VMEM)] * 8,
        out_specs=[pl.BlockSpec(memory_space=pltpu.VMEM)] * len(plans),
        scratch_shapes=[
            pltpu.VMEM((conv.filled, 2 * conv.block[1]), F32),
            pltpu.VMEM((HOT, LANE), F32),
            pltpu.VMEM(conv.shape, F32),
            pltpu.VMEM(conv.block, F32),
            pltpu.SemaphoreType.DMA((2 * len(rest),)),
            Gather.semaphores([conv]),
        ]
        + Reduce.scratch(plans),
        compiler_params=pltpu.CompilerParams(
            collective_id=collective_id, has_side_effects=True, vmem_limit_bytes=60 * 2**20
        ),
    )(*grads, *conv_inputs, grad, mask, fold)


def gate_parts(sums):
    parts = [sums[:, :HP]]
    for g in range(1, 4):
        begin = g * H // LANE * LANE
        moved = sums[:, begin : begin + HP + LANE]
        parts.append(pltpu.roll(moved, HP + LANE - (g * H - begin), 1)[:, :HP])
    return parts


def join_gates(parts, columns):
    rows = parts[0].shape[0]
    total = None
    for g, part in enumerate(parts):
        begin = g * H // LANE * LANE
        wide = jnp.concatenate([part, jnp.zeros((rows, LANE), F32)], axis=1)
        if g * H - begin:
            wide = pltpu.roll(wide, g * H - begin, 1)
        pieces = [wide]
        if begin:
            pieces = [jnp.zeros((rows, begin), F32)] + pieces
        if columns - begin - HP - LANE > 0:
            pieces = pieces + [jnp.zeros((rows, columns - begin - HP - LANE), F32)]
        placed = jnp.concatenate(pieces, axis=1)[:, :columns]
        total = placed if total is None else total + placed
    return total


def lstm_forward_kernel(
    batch, x_ref, w_ref, h0_ref, c0_ref, keep_ref, *outs
):
    hp_ref, cp_ref, i_ref, f_ref, u_ref, o_ref, t_ref, h_ref = outs
    per_tile = 8 // batch
    row = lax.broadcasted_iota(jnp.int32, (8, HP), 0)
    lane = lax.broadcasted_iota(jnp.int32, (8, HP), 1)

    def tile(step, carried):
        h, c = carried
        rows = pl.ds(pl.multiple_of(step * 8, 8), 8)
        x = x_ref[rows, :]
        keep = keep_ref[rows, :]
        saved = None
        for part in range(per_tile):
            hp, cp = h * keep, c * keep
            sums = x + dot(hp.astype(BF), w_ref[...])
            i, f, u, o = gate_parts(sums)
            i, f, u, o = jax.nn.sigmoid(i), jax.nn.sigmoid(f), jnp.tanh(u), jax.nn.sigmoid(o)
            c = f * cp + i * u
            t = jnp.tanh(c)
            h = (o * t).astype(BF).astype(F32)
            now = (hp, cp, i, f, u, o, t, jnp.where(lane < H, h, jnp.where(lane == H, 1.0, 0.0)))
            if saved is None:
                saved = now
            else:
                saved = tuple(jnp.where(row >= part * batch, b, a) for a, b in zip(saved, now))
            h, c = pltpu.roll(h, batch, 0), pltpu.roll(c, batch, 0)
        for ref, value in zip((hp_ref, cp_ref, i_ref, f_ref, u_ref, o_ref, t_ref, h_ref), saved):
            ref[rows, :] = value
        return h, c

    lax.fori_loop(0, x_ref.shape[0] // 8, tile, (h0_ref[...], c0_ref[...]))


def lstm_backward_kernel(
    batch, dh_ref, w_ref, keep_ref, cp_ref, i_ref, f_ref, u_ref, o_ref, t_ref, dz_ref
):
    per_tile = 8 // batch
    tiles = dh_ref.shape[0] // 8
    row = lax.broadcasted_iota(jnp.int32, (8, dz_ref.shape[1]), 0)
    real = lax.broadcasted_iota(jnp.int32, (8, HP), 1) < H

    def tile(step, carried):
        dh_carry, dc_carry = carried
        rows = pl.ds(pl.multiple_of((tiles - 1 - step) * 8, 8), 8)
        keep = keep_ref[rows, :]
        i, f, u, o, t = (r[rows, :] for r in (i_ref, f_ref, u_ref, o_ref, t_ref))
        soft = dh_ref[rows, :]
        to_c = o * (1.0 - t * t)
        to_i = jnp.where(real, u * i * (1.0 - i), 0.0)
        to_f = jnp.where(real, cp_ref[rows, :] * f * (1.0 - f), 0.0)
        to_u = jnp.where(real, i * (1.0 - u * u), 0.0)
        to_o = jnp.where(real, t * o * (1.0 - o), 0.0)
        back = f * keep
        saved = None
        for part in reversed(range(per_tile)):
            dh = jnp.where(real, soft + dh_carry, 0.0)
            dc = dc_carry + dh * to_c
            dz = join_gates([dc * to_i, dc * to_f, dc * to_u, dh * to_o], dz_ref.shape[1])
            saved = dz if saved is None else jnp.where(row >= (part + 1) * batch, saved, dz)
            dh_carry = dot(dz.astype(BF), w_ref[...]) * keep
            dc_carry = dc * back
            dh_carry, dc_carry = (
                pltpu.roll(dh_carry, 8 - batch, 0),
                pltpu.roll(dc_carry, 8 - batch, 0),
            )
        dz_ref[rows, :] = saved
        return dh_carry, dc_carry

    zero = jnp.zeros((8, HP), F32)
    lax.fori_loop(0, tiles, tile, (zero, zero))


def in_vmem(kernel, out_shapes, *operands):
    return pl.pallas_call(
        kernel,
        out_shape=out_shapes,
        in_specs=[pl.BlockSpec(memory_space=pltpu.VMEM)] * len(operands),
        out_specs=jax.tree.map(lambda _: pl.BlockSpec(memory_space=pltpu.VMEM), out_shapes),
        compiler_params=pltpu.CompilerParams(vmem_limit_bytes=48 * 2**20),
    )(*operands)


def softmax_kernel(
    vocab,
    blocks,
    h_ref,
    h_back_ref,
    w_ref,
    target_ref,
    scale_ref,
    loss_ref,
    grad_h_ref,
    grad_w_ref,
    logits,
    top,
    total,
    picked,
):
    phase, at = pl.program_id(0), pl.program_id(1)
    width = w_ref.shape[-1]
    rows = h_ref.shape[0]
    w = w_ref[...].reshape(-1, width)
    column = at * width + lax.broadcasted_iota(jnp.int32, (rows, width), 1)
    where = pl.ds(pl.multiple_of(at * width, width), width)
    hit = column == target_ref[...]

    @pl.when((phase == 0) & (at == 0))
    def _():
        top[...] = jnp.full_like(top, -1e30)
        total[...] = jnp.zeros_like(total)
        picked[...] = jnp.zeros_like(picked)

    @pl.when(phase == 0)
    def _():
        now = jnp.where(column < vocab, dot(h_ref[...], w), -1e30)
        logits[:, where] = now
        before = top[...]
        after = jnp.maximum(before, jnp.max(now, axis=1, keepdims=True))
        total[...] = total[...] * jnp.exp(before - after) + jnp.sum(
            jnp.exp(now - after), axis=1, keepdims=True
        )
        top[...] = after
        picked[...] += jnp.sum(jnp.where(hit, now, 0.0), axis=1, keepdims=True)

    @pl.when((phase == 1) & (at == 0))
    def _():
        log_total = top[...] + jnp.log(total[...])
        loss_ref[...] = log_total - picked[...]
        top[...] = log_total
        grad_h_ref[...] = jnp.zeros_like(grad_h_ref)

    @pl.when(phase == 1)
    def _():
        share = jnp.exp(logits[:, where] - top[...])
        grad = ((share - hit.astype(F32)) * scale_ref[...]).astype(BF)
        grad_w_ref[...] = dot_rows(h_back_ref[...], grad).astype(BF).reshape(grad_w_ref.shape)
        grad_h_ref[...] += dot_cols(grad, w)


def word_softmax(plan, h, h_back, weights, target, scale):
    rows, depth = h.shape
    n = plan.fsdp
    per_slot, half = plan.block
    width = 512
    while half % width:
        width -= LANE
    per_half = half // width
    whole = lambda p, j: (0, 0)
    return pl.pallas_call(
        functools.partial(softmax_kernel, plan.width, 2 * per_half),
        out_shape=[
            jax.ShapeDtypeStruct((rows, 1), F32),
            jax.ShapeDtypeStruct((rows, depth), F32),
            jax.ShapeDtypeStruct(plan.shape, BF),
        ],
        grid=(2, 2 * per_half),
        in_specs=[
            pl.BlockSpec((rows, depth), whole),
            pl.BlockSpec((rows, depth), whole),
            pl.BlockSpec(
                (n, 1, per_slot, width), lambda p, j: (0, j // per_half, 0, j % per_half)
            ),
            pl.BlockSpec((rows, 1), whole),
            pl.BlockSpec((rows, 1), whole),
        ],
        out_specs=[
            pl.BlockSpec((rows, 1), whole),
            pl.BlockSpec((rows, depth), whole),
            pl.BlockSpec(
                (1, n, per_slot, width),
                lambda p, j: (p * (j // per_half), 0, 0, p * (j % per_half)),
            ),
        ],
        scratch_shapes=[
            pltpu.VMEM((rows, 2 * half), F32),
            pltpu.VMEM((rows, 1), F32),
            pltpu.VMEM((rows, 1), F32),
            pltpu.VMEM((rows, 1), F32),
        ],
        compiler_params=pltpu.CompilerParams(vmem_limit_bytes=48 * 2**20),
    )(h, h_back, weights, target, scale)


def shards(
    fsdp_count,
    dp_count,
    chars,
    lengths,
    targets,
    resets,
    init_state,
    window_grad,
    char_table,
    conv_weight,
    conv_bias,
    highway_flat,
    lstm_flat,
    soft_flat,
):
    micro_count, streams, step_count, letters = chars.shape
    char_count, embed_dim = char_table.shape
    filters = conv_weight.shape[1]
    batch = micro_count * streams
    words = step_count * batch
    rows = up_to(words, 16)
    fp = up_to(filters + 1, LANE)
    dp_at, fsdp_at = lax.axis_index("dp"), lax.axis_index("fsdp")
    highway = Windows(
        highway_flat.shape[0] * fsdp_count, filters, 4 * (filters + 1), fsdp_count, dp_count, True
    )
    lstm_used = filters + H + 1
    lstm = Windows(
        lstm_flat.shape[0] * fsdp_count, 4 * H, lstm_used, fsdp_count, dp_count, False
    )
    soft = Windows(soft_flat.shape[0] * fsdp_count, V, H + 1, fsdp_count, dp_count, False)

    soft_own = soft.from_flat(soft_flat, fsdp_at)
    highway_all, lstm_all = gather(
        [highway, lstm],
        [highway.from_flat(highway_flat, fsdp_at), lstm.from_flat(lstm_flat, fsdp_at)],
        1,
    )
    highway_all, soft_own = lax.optimization_barrier((highway_all, soft_own))
    soft_all = lax.all_gather(soft_own, "fsdp", axis=0)
    highway_all = highway_all.reshape(-1, highway.columns)
    lstm_all = lstm_all.reshape(2, -1, lstm.columns // 2)

    def by_step(array):
        return jnp.moveaxis(array.reshape((batch, step_count) + array.shape[3:]), 1, 0).reshape(
            (words,) + array.shape[3:]
        )

    def pad_rows(array, value=0):
        return jnp.pad(
            array,
            [(0, rows - words)] + [(0, 0)] * (array.ndim - 1),
            constant_values=value,
        )

    word_chars = pad_rows(by_step(chars))
    word_lengths = pad_rows(by_step(lengths))[:, None]
    position = jnp.arange(letters, dtype=jnp.int32)[None, :]
    codes = jnp.where(position < word_lengths, word_chars, -1)
    codes = jnp.pad(codes, ((0, 0), (0, SLOTS + KMAX - letters)), constant_values=-1)
    index = jnp.stack(
        [
            jnp.where(
                codes[:, q : q + SLOTS] >= 0, codes[:, q : q + SLOTS] + q * char_count, -1
            )
            for q in range(KMAX)
        ]
        + [jnp.full((rows, SLOTS), KMAX * char_count, jnp.int32)],
        axis=2,
    ).reshape(rows * SLOTS, KMAX + 1)
    column = np.arange(fp)
    widths = np.ones((fp,), np.int32)
    for cut_at in FILTER_CUTS:
        widths = widths + ((column >= filters * cut_at // 22) & (column < filters))
    widths = widths.astype(np.int32)
    kernel_mask = jnp.asarray(
        np.arange(KMAX * embed_dim)[:, None] // embed_dim < widths[None, :filters]
    )
    ones_row = KMAX * embed_dim
    kernel = jnp.concatenate(
        [jnp.where(kernel_mask, conv_weight, jnp.zeros_like(conv_weight)), conv_bias[None, :]], axis=0
    )
    kernel = jnp.pad(kernel, ((0, LANE - ones_row - 1), (0, fp - filters)))
    spread_table = jnp.concatenate(
        [
            jnp.pad(char_table, ((0, 0), (q * embed_dim, LANE - (q + 1) * embed_dim)))
            for q in range(KMAX)
        ]
        + [jnp.zeros((1, LANE), BF).at[0, ones_row].set(1.0)],
        axis=0,
    )
    spread_table = jnp.pad(spread_table, ((0, HOT - KMAX * char_count - 1), (0, 0)))
    conv_inputs = (index, word_lengths, spread_table, kernel, jnp.asarray(widths)[None, :])
    word_block = WORD_BLOCK
    feature = pl.pallas_call(
        functools.partial(conv_forward_kernel, filters),
        out_shape=jax.ShapeDtypeStruct((rows, fp), BF),
        grid=(rows // word_block,),
        in_specs=conv_specs(word_block, fp),
        out_specs=pl.BlockSpec((word_block, fp), lambda i: (i, 0)),
        compiler_params=pltpu.CompilerParams(vmem_limit_bytes=48 * 2**20),
    )(*conv_inputs)

    filter_lane = jnp.arange(fp)[None, :]
    each_layer = 2 * (filters + 1)
    owner_rows = highway.rows

    def layer_map(row_map, layer):
        at = row_map - layer * each_layer
        inside = (row_map >= 0) & (at >= 0) & (at < each_layer)
        is_gate = inside & (at >= filters + 1)
        source = np.where(inside, np.where(is_gate, at - filters - 1, at), -1)
        return source.astype(np.int32), inside & ~is_gate, is_gate

    layers = []
    for layer in range(2):
        source, is_trans, is_gate = layer_map(highway.gathered, layer)
        live = np.nonzero(source.reshape(-1, owner_rows).max(axis=1) >= 0)[0]
        begin, end = int(live[0]) * owner_rows, (int(live[-1]) + 1) * owner_rows
        begin = begin // 16 * 16
        end = min(up_to(end, 16), source.shape[0])
        weights = highway_all[begin:end]
        mapping = one_hot_map(fp, source[begin:end])
        trans_mask = jnp.asarray(is_trans[begin:end].astype(np.float32))[None, :]
        gate_mask = jnp.asarray(is_gate[begin:end].astype(np.float32))[None, :]
        spread = dot(feature, mapping)
        both = jnp.concatenate([spread * trans_mask, spread * gate_mask], axis=0).astype(BF)
        sums = dot(both, weights)
        trans, gate = sums[:rows], jax.nn.sigmoid(sums[rows:])
        layers.append((feature, trans, gate, weights, mapping, trans_mask, gate_mask))
        value = gate * jax.nn.silu(trans) + (1.0 - gate) * feature.astype(F32)
        feature = jnp.where(
            filter_lane < filters, value, jnp.where(filter_lane == filters, 1.0, 0.0)
        ).astype(BF)

    lp = up_to(lstm_used, LANE)
    first_h = np.nonzero(lstm.gathered >= filters)[0][0] // 16 * 16
    last_x = min(up_to(int(np.nonzero((lstm.gathered >= 0) & (lstm.gathered < filters))[0][-1]) + 1, 16), lstm.gathered.shape[0])
    lstm_map = one_hot_map(lp, lstm.gathered)
    no_hidden = jnp.concatenate(
        [
            feature[:, :filters],
            jnp.zeros((rows, H), BF),
            jnp.ones((rows, 1), BF),
            jnp.zeros((rows, lp - lstm_used), BF),
        ],
        axis=1,
    )
    spread_x = dot(no_hidden, lstm_map).astype(BF)
    from_input = jnp.concatenate([dot(spread_x, lstm_all[0]), dot(spread_x, lstm_all[1])], axis=1)
    hidden_source = lstm.gathered[first_h:] - filters
    hidden_map = one_hot_map(HP, np.where((hidden_source >= 0) & (hidden_source < H), hidden_source, -1))
    recur = jnp.concatenate(
        [dot(hidden_map, lstm_all[h, first_h:]).astype(BF) for h in range(2)], axis=1
    )
    recur_t = jnp.concatenate(
        [
            lax.dot_general(
                lstm_all[h, first_h:],
                hidden_map,
                (((0,), (1,)), ((), ())),
                preferred_element_type=F32,
            ).astype(BF)
            for h in range(2)
        ],
        axis=0,
    )
    keep = pad_rows(by_step(1 - resets).astype(F32))[:, None]
    start = init_state.reshape(batch, 2, H)
    start = jnp.pad(start, ((0, 8 - batch), (0, 0), (0, HP - H)))
    states = [jax.ShapeDtypeStruct((rows, HP), F32)] * 8
    hp, cp, gate_i, gate_f, gate_u, gate_o, tanh_c, hidden = in_vmem(
        functools.partial(lstm_forward_kernel, batch),
        states,
        from_input,
        recur,
        start[:, 0].astype(BF).astype(F32),
        start[:, 1],
        keep,
    )

    hidden = hidden.astype(BF)
    soft_map = one_hot_map(HP, soft.gathered)
    spread_h = dot(hidden, soft_map).astype(BF)
    spread_h_back = dot(hidden, one_hot_map(HP, soft.reduced)).astype(BF)
    row_scale = jnp.broadcast_to(
        window_grad.reshape(1, batch) / step_count, (step_count, batch)
    ).reshape(words, 1)
    word_loss, grad_spread, soft_grad = word_softmax(
        soft,
        spread_h,
        spread_h_back,
        soft_all,
        pad_rows(by_step(targets), -1)[:, None],
        pad_rows(row_scale),
    )
    window_loss = jnp.mean(word_loss[:words, 0].reshape(step_count, batch), axis=0).reshape(
        micro_count, streams
    )
    grad_hidden = compress(grad_spread, soft_map)
    soft_part = reduce_scatter([soft], [soft_grad], 2)[0]

    dz = in_vmem(
        functools.partial(lstm_backward_kernel, batch),
        jax.ShapeDtypeStruct((rows, lstm.columns), F32),
        grad_hidden,
        recur_t,
        keep,
        cp,
        gate_i,
        gate_f,
        gate_u,
        gate_o,
        tanh_c,
    ).astype(BF)
    half = lstm.columns // 2
    lstm_in = jnp.concatenate(
        [
            feature[:, :filters],
            hp[:, :H].astype(BF),
            jnp.ones((rows, 1), BF),
            jnp.zeros((rows, lp - lstm_used), BF),
        ],
        axis=1,
    )
    lstm_in = dot(lstm_in, one_hot_map(lp, lstm.reduced)).astype(BF)
    lstm_grad = jnp.stack(
        [dot_rows(lstm_in, dz[:, h * half : (h + 1) * half]).astype(BF) for h in range(2)]
    ).reshape(lstm.shape)
    grad_spread = dot_cols(dz[:, :half], lstm_all[0, :last_x]) + dot_cols(
        dz[:, half:], lstm_all[1, :last_x]
    )
    input_source = lstm.gathered[:last_x]
    grad = compress(
        grad_spread, one_hot_map(fp, np.where(input_source < filters, input_source, -1))
    )

    grads_of, inputs_of = [], []
    for layer in (1, 0):
        layer_in, trans, gate, weights, mapping, trans_mask, gate_mask = layers[layer]
        sig = jax.nn.sigmoid(trans)
        silu = trans * sig
        grad = jnp.where(filter_lane < filters, grad, 0.0)
        grad_trans = (grad * gate * sig * (1.0 + trans * (1.0 - sig))).astype(BF)
        grad_gate = (grad * (silu - layer_in.astype(F32)) * gate * (1.0 - gate)).astype(BF)
        pair = jnp.concatenate([grad_trans, grad_gate], axis=0)
        spread = dot_cols(pair, weights)
        grad = grad * (1.0 - gate) + compress(
            spread[:rows] * trans_mask + spread[rows:] * gate_mask, mapping
        )
        source, is_trans, is_gate = layer_map(highway.reduced, layer)
        spread_in = dot(layer_in, one_hot_map(fp, source))
        inputs_of = [
            (spread_in * jnp.asarray(is_trans.astype(np.float32))[None, :]).astype(BF),
            (spread_in * jnp.asarray(is_gate.astype(np.float32))[None, :]).astype(BF),
        ] + inputs_of
        grads_of = [pair] + grads_of
    highway_grad = (
        dot_rows(jnp.concatenate(inputs_of, axis=0), jnp.concatenate(grads_of, axis=0))
        .astype(BF)
        .reshape(highway.shape)
    )

    grad = jnp.where(filter_lane < filters, grad, 0.0)
    hot_row, hot_lane = np.arange(HOT), np.arange(LANE)
    hot_mask = (hot_row[:, None] // char_count == hot_lane[None, :] // embed_dim) & (
        hot_row[:, None] < KMAX * char_count
    )
    hot_fold = (hot_row[None, :] % char_count == np.arange(LANE)[:, None]) & (
        hot_row[None, :] < KMAX * char_count
    )
    conv = Dense(LANE, up_to(fp + LANE, 2 * LANE), fsdp_count)
    conv_grad, highway_part, lstm_part = tail(
        [conv, highway, lstm],
        [highway_grad, lstm_grad],
        conv_inputs,
        grad,
        jnp.asarray(hot_mask.astype(np.float32)),
        jnp.asarray(hot_fold.astype(np.float32)),
        3,
    )
    conv_grad = jnp.concatenate(
        [conv_grad[h].reshape(-1, conv.block[1])[:LANE] for h in range(2)], axis=1
    )
    conv_weight_grad = jnp.where(kernel_mask, conv_grad[:ones_row, :filters], 0.0)
    conv_bias_grad = conv_grad[ones_row, :filters]
    table_grad = jnp.sum(
        conv_grad[:char_count, fp : fp + KMAX * embed_dim].reshape(char_count, KMAX, embed_dim), axis=1
    )

    def own_window(plan, part):
        if dp_count > 2:
            groups = [list(range(h, dp_count, 2)) for h in range(2)]
            part = lax.psum(part, "dp", axis_index_groups=groups)
        if plan.by_rows:
            at = dp_at // 2
        else:
            part = jnp.concatenate([part[0], part[1]], axis=1)
            at = dp_at
        window = lax.dynamic_slice_in_dim(part, at * plan.rows, plan.rows, 0)
        return plan.to_flat(window, dp_at, fsdp_at)

    return (
        window_loss,
        table_grad,
        conv_weight_grad,
        conv_bias_grad,
        own_window(highway, highway_part),
        own_window(lstm, lstm_part),
        own_window(soft, soft_part),
    )


def solution(mesh):
    in_specs = (
        P(None, ("dp", "fsdp"), None, None),
        P(None, ("dp", "fsdp"), None),
        P(None, ("dp", "fsdp"), None),
        P(None, ("dp", "fsdp"), None),
        P(None, ("dp", "fsdp"), None, None),
        P(None, ("dp", "fsdp")),
        P(),
        P(),
        P(),
        P("fsdp", None),
        P("fsdp", None),
        P("fsdp", None),
    )
    out_specs = (
        P(None, ("dp", "fsdp")),
        P(),
        P(),
        P(),
        P(("dp", "fsdp"), None),
        P(("dp", "fsdp"), None),
        P(("dp", "fsdp"), None),
    )
    return jax.shard_map(
        functools.partial(shards, mesh.shape["fsdp"], mesh.shape["dp"]),
        mesh=mesh,
        in_specs=in_specs,
        out_specs=out_specs,
        check_vma=False,
    )
```

```python
import functools

import jax
import jax.numpy as jnp
import numpy as np
from jax import lax
from jax.experimental import pallas as pl
from jax.experimental.pallas import tpu as pltpu
from jax.sharding import PartitionSpec as P

H = 650
V = 10000
KMAX = 7
LANE = 128
HP = 768
SLOTS = 24
HOT = 384
FILTER_CUTS = (1, 3, 6, 10, 14, 18)
MESH = pl.DeviceIdType.MESH
BF = jnp.bfloat16
F32 = jnp.float32


def up_to(value, unit):
    return -(-value // unit) * unit


def dot(left, right):
    return jnp.dot(left, right, preferred_element_type=F32)


def dot_rows(left, right):
    return lax.dot_general(left, right, (((0,), (0,)), ((), ())), preferred_element_type=F32)


def dot_cols(left, right):
    return lax.dot_general(left, right, (((1,), (1,)), ((), ())), preferred_element_type=F32)


class Windows:
    def __init__(self, flat_rows, width, used, fsdp, dp, by_rows, parts=2):
        owners = fsdp * dp
        self.parts = parts
        self.width, self.by_rows, self.fsdp, self.dp = width, by_rows, fsdp, dp
        self.entries = flat_rows * LANE // owners
        starts = [o * self.entries // width for o in range(owners)]
        spans = [
            (o * self.entries % width + self.entries - 1) // width + 1 for o in range(owners)
        ]
        rows = max(spans)
        while (dp * rows) % 16 or (by_rows and (dp // 2 * rows) % 16):
            rows += 1
        self.rows = rows
        self.columns = up_to(width, LANE) if by_rows else parts * up_to(-(-width // parts), LANE)
        self.block = (
            (dp // 2 * rows, self.columns) if by_rows else (dp * rows, self.columns // parts)
        )
        self.shape = (fsdp, 2) + self.block if by_rows else (parts, fsdp) + self.block

        def row_map(order):
            rows_of = [
                [starts[o] + i if i < spans[o] and starts[o] + i < used else -1 for i in range(rows)]
                for o in order
            ]
            return np.array(rows_of, np.int32).reshape(-1)

        self.gathered = row_map(range(owners))
        if by_rows:
            order = [
                (2 * jj + h) * fsdp + f
                for f in range(fsdp)
                for h in range(2)
                for jj in range(dp // 2)
            ]
        else:
            order = [d * fsdp + f for f in range(fsdp) for d in range(dp)]
        self.reduced = row_map(order)

    dtype = BF

    def pick(self, ref, half, slot):
        return ref.at[slot, half] if self.by_rows else ref.at[half, slot]

    def from_flat(self, shard, fsdp_at):
        parts = []
        flat = shard.reshape(-1)
        for j in range(self.dp):
            shift = lax.rem((fsdp_at * self.dp + j) * self.entries, self.width)
            piece = lax.dynamic_update_slice(
                jnp.zeros((self.rows * self.width,), BF),
                flat[j * self.entries : (j + 1) * self.entries],
                (shift,),
            ).reshape(self.rows, self.width)
            parts.append(jnp.pad(piece, ((0, 0), (0, self.columns - self.width))))
        joined = jnp.concatenate(parts, axis=0)
        if self.by_rows:
            return joined.reshape((2,) + self.block)
        part = self.columns // self.parts
        return jnp.stack([joined[:, p * part : (p + 1) * part] for p in range(self.parts)])

    def to_flat(self, window, dp_at, fsdp_at):
        shift = lax.rem((dp_at * self.fsdp + fsdp_at) * self.entries, self.width)
        flat = window[:, : self.width].reshape(-1)
        return lax.dynamic_slice(flat, (shift,), (self.entries,)).reshape(-1, LANE)


def one_hot_map(rows, row_map):
    return (
        lax.broadcasted_iota(jnp.int32, (rows, row_map.shape[0]), 0) == jnp.asarray(row_map)[None, :]
    ).astype(BF)


def compress(spread, mapping):
    high = lax.reduce_precision(spread, 8, 7)
    both = jnp.concatenate([high.astype(BF), (spread - high).astype(BF)], axis=0)
    product = dot_cols(both, mapping)
    count = spread.shape[0]
    return product[:count] + product[count:]


def greet(place_of, lengthwise):
    d, f, z = place_of.d, place_of.f, place_of.z
    barrier = pltpu.get_barrier_semaphore()
    for target in (place_of.partner1, place_of.partner3, place_of.sibling):
        pl.semaphore_signal(barrier, inc=1, device_id=target, device_id_type=MESH)

    @pl.when(z > 0)
    def _():
        pl.semaphore_signal(barrier, inc=1, device_id=(d, f - 4), device_id_type=MESH)

    @pl.when(z < lengthwise - 1)
    def _():
        pl.semaphore_signal(barrier, inc=1, device_id=(d, f + 4), device_id_type=MESH)

    has_down = (z > 0).astype(jnp.int32)
    has_up = (z < lengthwise - 1).astype(jnp.int32)
    pl.semaphore_wait(barrier, 3 + has_down + has_up)


class Place:
    def __init__(self):
        self.d, self.f = lax.axis_index("dp"), lax.axis_index("fsdp")
        self.c = lax.rem(self.d, 2)
        x, y, self.z = lax.rem(self.f, 2), lax.rem(self.f // 2, 2), self.f // 4
        self.first = x + self.c * (y - x)
        self.last = y + self.c * (x - y)
        self.stride1, self.stride3 = 1 + self.c, 2 - self.c
        self.flip1 = self.stride1 * (1 - 2 * self.first)
        self.flip3 = self.stride3 * (1 - 2 * self.last)
        self.partner1 = (self.d, self.f + self.flip1)
        self.partner3 = (self.d, self.f + self.flip3)
        self.sibling = (self.d + 1 - 2 * self.c, self.f)

    def last_bit(self, block):
        bit_x, bit_y = lax.rem(block, 2), lax.rem(block // 2, 2)
        return bit_y + self.c * (bit_x - bit_y)


def remote(src, dst, send, recv, target):
    return pltpu.make_async_remote_copy(
        src_ref=src,
        dst_ref=dst,
        send_sem=send,
        recv_sem=recv,
        device_id=target,
        device_id_type=MESH,
    )


class Gather:
    def __init__(self, plans, own, outs, sems, shared):
        self.plans, self.own, self.outs, self.sems, self.shared = plans, own, outs, sems, shared
        self.n = plans[0].fsdp
        self.lengthwise = self.n // 4
        self.at = Place()

    RECV, SIB_RECV, ONE, UP, DOWN, LAST, SIB, LOCAL = range(8)

    @staticmethod
    def semaphores(plans):
        return pltpu.SemaphoreType.DMA((8 * len(plans) * plans[0].fsdp,))

    def sem(self, kind, a, block):
        return self.sems.at[(kind * len(self.plans) + a) * self.n + block]

    def source(self, a, half):
        return self.own[a].at[half] if self.shared else self.own[a]

    def copy(self, kind, a, block, target, own=False):
        here = self.plans[a].pick(self.outs[a], self.at.c, block)
        return remote(
            self.source(a, self.at.c) if own else here,
            here,
            self.sem(kind, a, block),
            self.sem(self.SIB_RECV if kind == self.SIB else self.RECV, a, block),
            target,
        )

    def arrived(self, a, block, kind=RECV):
        c = self.at.c
        here = self.plans[a].pick(self.outs[a], 1 - c if kind == self.SIB_RECV else c, block)
        remote(
            here, here, self.sem(self.SIB, a, block), self.sem(kind, a, block), self.at.sibling
        ).wait_recv()

    def sent(self, kind, a, block):
        self.copy(kind, a, block, self.at.sibling).wait_send()

    def local(self, a, half):
        return pltpu.make_async_copy(
            self.source(a, half),
            self.plans[a].pick(self.outs[a], half, self.at.f),
            self.sem(self.LOCAL, a, half if self.shared else 0),
        )

    def send_up(self, a, block, own=False):
        @pl.when(self.at.z < self.lengthwise - 1)
        def _():
            self.copy(self.UP, a, block, (self.at.d, self.at.f + 4), own).start()

    def send_down(self, a, block, own=False):
        @pl.when(self.at.z > 0)
        def _():
            self.copy(self.DOWN, a, block, (self.at.d, self.at.f - 4), own).start()

    def begin(self, a):
        at = self.at
        self.copy(self.ONE, a, at.f, at.partner1, True).start()
        self.send_up(a, at.f, True)
        self.send_down(a, at.f, True)
        self.copy(self.LAST, a, at.f, at.partner3, True).start()
        if self.shared:
            for half in (0, 1):
                self.local(a, half).start()
        else:
            self.copy(self.SIB, a, at.f, at.sibling, True).start()
            self.local(a, at.c).start()

    def near(self, a):
        at = self.at
        block = at.f + at.flip1
        self.arrived(a, block)
        self.send_up(a, block)
        self.send_down(a, block)
        self.copy(self.LAST, a, block, at.partner3).start()
        self.copy(self.SIB, a, block, at.sibling).start()

    def line(self, a, distance):
        for sign in (1, -1):
            z = self.at.z - sign * distance

            def take(sign=sign):
                for flip in (0, 1):
                    block = self.at.f - 4 * sign * distance + flip * self.at.flip1
                    self.arrived(a, block)
                    (self.send_up if sign == 1 else self.send_down)(a, block)
                    self.copy(self.LAST, a, block, self.at.partner3).start()
                    self.copy(self.SIB, a, block, self.at.sibling).start()

            pl.when((z >= 0) & (z < self.lengthwise))(take)

    def across(self, a, distance):
        for sign in (1,) if distance == 0 else (1, -1):
            z = self.at.z - sign * distance

            def take(sign=sign):
                for flip in (0, 1):
                    block = (
                        self.at.f - 4 * sign * distance + flip * self.at.flip1 + self.at.flip3
                    )
                    self.arrived(a, block)
                    self.copy(self.SIB, a, block, self.at.sibling).start()

            pl.when((z >= 0) & (z < self.lengthwise))(take)

    def steps(self):
        count = len(self.plans)
        steps = [functools.partial(self.near, a) for a in range(count)]
        for distance in range(1, self.lengthwise):
            steps += [functools.partial(self.line, a, distance) for a in range(count)]
            steps += [functools.partial(self.across, a, distance - 1) for a in range(count)]
        steps += [functools.partial(self.across, a, self.lengthwise - 1) for a in range(count)]
        return steps

    def finish(self):
        at = self.at
        for a in range(len(self.plans)):

            def block_done(block, _, a=a):
                z = block // 4

                def from_sibling():
                    self.arrived(a, block, self.SIB_RECV)
                    self.sent(self.SIB, a, block)

                if self.shared:
                    pl.when(jnp.logical_not(block == at.f))(from_sibling)
                else:
                    from_sibling()

                @pl.when(at.last_bit(block) == at.last)
                def _():
                    self.sent(self.LAST, a, block)

                    @pl.when((z <= at.z) & (at.z < self.lengthwise - 1))
                    def _():
                        self.sent(self.UP, a, block)

                    @pl.when((z >= at.z) & (at.z > 0))
                    def _():
                        self.sent(self.DOWN, a, block)

                return 0

            lax.fori_loop(0, self.n, block_done, 0)
            self.sent(self.ONE, a, at.f)
            if self.shared:
                for half in (0, 1):
                    self.local(a, half).wait()
            else:
                self.local(a, at.c).wait()


def gather_kernel(plans, *refs):
    count = len(plans)
    work = Gather(plans, refs[:count], refs[count : 2 * count], refs[2 * count], True)
    greet(work.at, work.lengthwise)
    for a in range(count):
        work.begin(a)
    for step in work.steps():
        step()
    work.finish()


def gather(plans, shards, collective_id):
    count = len(plans)
    return pl.pallas_call(
        functools.partial(gather_kernel, plans),
        out_shape=[jax.ShapeDtypeStruct(plan.shape, plan.dtype) for plan in plans],
        in_specs=[pl.BlockSpec(memory_space=pl.ANY)] * count,
        out_specs=[pl.BlockSpec(memory_space=pl.ANY)] * count,
        scratch_shapes=[Gather.semaphores(plans)],
        compiler_params=pltpu.CompilerParams(collective_id=collective_id, has_side_effects=True),
    )(*shards)


class Reduce:
    SIB, SIB_RECV, LOAD, NEAR, NEAR_RECV, UP, UP_RECV, DOWN, DOWN_RECV, END = range(10)

    def __init__(self, plans, ins, totals, scratch):
        count = len(plans)
        self.plans, self.ins, self.totals = plans, ins, totals
        self.held, self.landed, self.flow_up, self.flow_down, self.close, self.cross = (
            scratch[k * count : (k + 1) * count] for k in range(6)
        )
        self.sems = scratch[6 * count]
        self.n = plans[0].fsdp
        self.lengthwise = self.n // 4
        self.at = Place()

    @staticmethod
    def scratch(plans):
        n = plans[0].fsdp
        return (
            [pltpu.VMEM((n,) + plan.block, plan.dtype) for plan in plans] * 2
            + [pltpu.VMEM((n // 2,) + plan.block, plan.dtype) for plan in plans] * 3
            + [pltpu.VMEM(plan.block, plan.dtype) for plan in plans]
            + [pltpu.SemaphoreType.DMA((10 * len(plans) * n,))]
        )

    def sem(self, kind, a, block):
        return self.sems.at[(kind * len(self.plans) + a) * self.n + block]

    def slot(self, z, b1, b3):
        return 4 * z + self.at.stride1 * b1 + self.at.stride3 * b3

    def item(self, t):
        pair, b3 = t // 2, lax.rem(t, 2)
        half = pair // 2
        z = jnp.where(lax.rem(pair, 2) == 0, half, self.lengthwise - 1 - half)
        return z, b3

    def to_sibling(self, a, block):
        return remote(
            self.plans[a].pick(self.ins[a], 1 - self.at.c, block),
            self.landed[a].at[block],
            self.sem(self.SIB, a, block),
            self.sem(self.SIB_RECV, a, block),
            self.at.sibling,
        )

    def load(self, a, block):
        return pltpu.make_async_copy(
            self.plans[a].pick(self.ins[a], self.at.c, block),
            self.held[a].at[block],
            self.sem(self.LOAD, a, block),
        )

    def to_near(self, a, z, b3):
        return remote(
            self.held[a].at[self.slot(z, 1 - self.at.first, b3)],
            self.close[a].at[2 * z + b3],
            self.sem(self.NEAR, a, 2 * z + b3),
            self.sem(self.NEAR_RECV, a, 2 * z + b3),
            self.at.partner1,
        )

    def along(self, up, a, z, b3):
        return remote(
            self.held[a].at[self.slot(z, self.at.first, b3)],
            (self.flow_up if up else self.flow_down)[a].at[2 * z + b3],
            self.sem(self.UP if up else self.DOWN, a, 2 * z + b3),
            self.sem(self.UP_RECV if up else self.DOWN_RECV, a, 2 * z + b3),
            (self.at.d, self.at.f + (4 if up else -4)),
        )

    def to_cross(self, a):
        return remote(
            self.held[a].at[self.slot(self.at.z, self.at.first, 1 - self.at.last)],
            self.cross[a],
            self.sem(self.END, a, 0),
            self.sem(self.END, a, 1),
            self.at.partner3,
        )

    def rows(self, a, body):
        unit = 16

        def step(i, _):
            body(pl.ds(pl.multiple_of(i * unit, unit), unit))
            return 0

        if self.plans[a].block[0] < unit:
            body(slice(None))
        else:
            lax.fori_loop(0, self.plans[a].block[0] // unit, step, 0)

    def add(self, a, block, sources):
        held = self.held[a]

        def body(where):
            total = held[block, where, :].astype(F32)
            for ref, at in sources:
                total += ref[at, where, :].astype(F32)
            held[block, where, :] = total.astype(held.dtype)

        self.rows(a, body)

    def begin(self, a):
        for flip in (1, 0):
            b1 = self.at.first + flip * (1 - 2 * self.at.first)

            def start(t, _, b1=b1):
                z, b3 = self.item(t)
                block = self.slot(z, b1, b3)
                self.to_sibling(a, block).start()
                self.load(a, block).start()
                return 0

            lax.fori_loop(0, 2 * self.lengthwise, start, 0)

    def first_leg(self, a, t):
        z, b3 = self.item(t)
        block = self.slot(z, 1 - self.at.first, b3)
        self.load(a, block).wait()
        self.to_sibling(a, block).wait_recv()
        self.add(a, block, [(self.landed[a], block)])
        self.to_near(a, z, b3).start()

    def middle_leg(self, a, t):
        z, b3 = self.item(t)
        block = self.slot(z, self.at.first, b3)
        flow = 2 * z + b3
        base = [(self.landed[a], block), (self.close[a], flow)]
        self.load(a, block).wait()
        self.to_sibling(a, block).wait_recv()
        self.to_near(a, z, b3).wait_recv()

        def onward(up):
            incoming = self.at.z > 0 if up else self.at.z < self.lengthwise - 1

            @pl.when(incoming)
            def _():
                self.along(up, a, z, b3).wait_recv()
                flows = self.flow_up if up else self.flow_down
                self.add(a, block, base + [(flows[a], flow)])

            @pl.when(jnp.logical_not(incoming))
            def _():
                self.add(a, block, base)

            self.along(up, a, z, b3).start()

        pl.when(z > self.at.z)(functools.partial(onward, True))
        pl.when(z < self.at.z)(functools.partial(onward, False))

        @pl.when(z == self.at.z)
        def _():
            self.add(a, block, base)

    def own(self, a, b3):
        z = self.at.z
        block = self.slot(z, self.at.first, b3)
        for up in (True, False):

            @pl.when(z > 0 if up else z < self.lengthwise - 1)
            def _(up=up):
                self.along(up, a, z, b3).wait_recv()
                flows = self.flow_up if up else self.flow_down
                self.add(a, block, [(flows[a], 2 * z + b3)])

    def cross_over(self, a):
        self.own(a, 1 - self.at.last)
        self.to_cross(a).start()

    def last_leg(self, a):
        self.own(a, self.at.last)
        self.to_cross(a).wait_recv()
        block = self.slot(self.at.z, self.at.first, self.at.last)

        def body(where):
            total = self.held[a][block, where, :].astype(F32) + self.cross[a][where, :].astype(F32)
            self.totals[a][where, :] = total

        self.rows(a, body)

    def finish(self, a):
        def done(t, _):
            z, b3 = self.item(t)
            for b1 in (self.at.first, 1 - self.at.first):
                self.to_sibling(a, self.slot(z, b1, b3)).wait_send()
            self.to_near(a, z, b3).wait_send()
            for up in (True, False):

                @pl.when(z > self.at.z if up else z < self.at.z)
                def _(up=up):
                    self.along(up, a, z, b3).wait_send()

            return 0

        lax.fori_loop(0, 2 * self.lengthwise, done, 0)
        self.to_cross(a).wait_send()


def pair_exchange(plans, totals, outs, sems, at):
    copies = []
    for a, plan in enumerate(plans):
        if not plan.by_rows:
            copies.append(
                remote(
                    totals[a], outs[a].at[at.c], sems.at[2 * a], sems.at[2 * a + 1], at.sibling
                )
            )
    return copies


def reduce_kernel(plans, *refs):
    count = len(plans)
    ins, outs, scratch = refs[:count], refs[count : 2 * count], refs[2 * count :]
    totals = [out if plan.by_rows else out.at[Place().c] for plan, out in zip(plans, outs)]
    work = Reduce(plans, ins, totals, scratch[:-1])
    at, items = work.at, 2 * work.lengthwise
    greet(at, work.lengthwise)
    for a in range(count):
        work.begin(a)

    def leg(body, a, begin, end):
        def step(t, _):
            body(a, t)
            return 0

        lax.fori_loop(begin, end, step, 0)

    for a in range(count):
        leg(work.first_leg, a, 0, items)
    for a in range(count):
        leg(work.middle_leg, a, 0, items)
    for a in range(count):
        work.cross_over(a)
    copies = pair_exchange(plans, totals, outs, scratch[-1], at)
    for a in range(count):
        work.last_leg(a)
    for copy in copies:
        copy.start()
    for a in range(count):
        work.finish(a)
    for copy in copies:
        copy.wait()


def reduce_out(plan):
    return jax.ShapeDtypeStruct(plan.block if plan.by_rows else (2,) + plan.block, F32)


def reduce_scatter(plans, grads, collective_id):
    count = len(plans)
    return pl.pallas_call(
        functools.partial(reduce_kernel, plans),
        out_shape=[reduce_out(plan) for plan in plans],
        in_specs=[pl.BlockSpec(memory_space=pl.ANY)] * count,
        out_specs=[pl.BlockSpec(memory_space=pltpu.VMEM)] * count,
        scratch_shapes=Reduce.scratch(plans) + [pltpu.SemaphoreType.DMA((2 * count,))],
        compiler_params=pltpu.CompilerParams(
            collective_id=collective_id, has_side_effects=True, vmem_limit_bytes=60 * 2**20
        ),
    )(*grads)


def hot_rows(index):
    lane = lax.broadcasted_iota(jnp.int32, (index.shape[0], HOT), 1)
    hit = lane == index[:, 0:1]
    for q in range(1, KMAX + 1):
        hit = jnp.logical_or(hit, lane == index[:, q : q + 1])
    return hit.astype(F32).astype(BF)


def conv_forward_kernel(filters, index_ref, length_ref, table_ref, kernel_ref, width_ref, out_ref):
    words = length_ref.shape[0]
    windows = dot(hot_rows(index_ref[...]), table_ref[...]).astype(BF)
    chunk = 384
    for at in range(0, kernel_ref.shape[1], chunk):
        columns = slice(at, at + chunk)
        activated = jnp.tanh(dot(windows, kernel_ref[:, columns])).reshape(words, SLOTS, chunk)
        counts = jnp.maximum(length_ref[...] - width_ref[:, columns] + 1, 1)
        position = lax.broadcasted_iota(jnp.int32, (words, SLOTS, chunk), 1)
        inside = position < counts[:, None, :]
        totals = jnp.sum(jnp.where(inside, jnp.exp(activated), 0.0), axis=1)
        pooled = jnp.log(totals) - jnp.log(counts.astype(F32))
        lane = at + lax.broadcasted_iota(jnp.int32, (words, chunk), 1)
        out_ref[:, columns] = jnp.where(
            lane < filters, pooled, jnp.where(lane == filters, 1.0, 0.0)
        ).astype(BF)


def conv_backward_block(index, lengths, refs, grad_ref, where, kernel_grad_ref, hot_grad_ref):
    table_ref, kernel_ref, width_ref = refs
    words = lengths.shape[0]
    hot = hot_rows(index)
    windows = dot(hot, table_ref[...]).astype(BF)
    chunk = 384
    grad_windows = jnp.zeros(windows.shape, F32)
    for at in range(0, kernel_ref.shape[1], chunk):
        columns = slice(at, at + chunk)
        activated = jnp.tanh(dot(windows, kernel_ref[:, columns])).reshape(words, SLOTS, chunk)
        counts = jnp.maximum(lengths - width_ref[:, columns] + 1, 1)
        position = lax.broadcasted_iota(jnp.int32, (words, SLOTS, chunk), 1)
        inside = position < counts[:, None, :]
        weight = jnp.where(inside, jnp.exp(activated), 0.0)
        share = grad_ref[where, columns] / jnp.sum(weight, axis=1)
        grad = (share[:, None, :] * weight * (1.0 - activated * activated)).astype(BF)
        grad = grad.reshape(words * SLOTS, chunk)
        kernel_grad_ref[:, columns] += dot_rows(windows, grad)
        grad_windows += dot_cols(grad, kernel_ref[:, columns])
    hot_grad_ref[...] += dot_rows(hot, grad_windows.astype(BF))


def conv_specs(words, filters_padded):
    return [
        pl.BlockSpec((words * SLOTS, 8), lambda i: (i, 0)),
        pl.BlockSpec((words, 1), lambda i: (i, 0)),
        pl.BlockSpec((HOT, LANE), lambda i: (0, 0)),
        pl.BlockSpec((LANE, filters_padded), lambda i: (0, 0)),
        pl.BlockSpec((1, filters_padded), lambda i: (0, 0)),
    ]


class Dense:
    by_rows = False
    dtype = F32

    def __init__(self, rows, columns, fsdp):
        self.fsdp = fsdp
        self.filled = rows
        self.block = (up_to(-(-rows // fsdp), 8), columns // 2)
        self.shape = (2, fsdp) + self.block

    def pick(self, ref, half, slot):
        return ref.at[half, slot]


WORD_BLOCK = 16


def tail_kernel(plans, blocks, *refs):
    conv, rest = plans[0], plans[1:]
    count = len(plans)
    ins, refs = refs[: count - 1], refs[count - 1 :]
    index_ref, length_ref, table_ref, kernel_ref, width_ref, grad_ref, mask_ref, fold_ref = refs[:8]
    outs, refs = refs[8 : 8 + count], refs[8 + count :]
    conv_out, rest_outs = outs[0], outs[1:]
    kernel_grad, hot_grad, conv_in, conv_total = refs[:4]
    pair_sems, gather_sems = refs[4:6]
    at = Place()
    totals = [conv_total] + [
        out if plan.by_rows else out.at[at.c] for plan, out in zip(rest, rest_outs)
    ]
    work = Reduce(plans, [conv_in] + list(ins), totals, refs[6:])
    items = 2 * work.lengthwise
    greet(at, work.lengthwise)
    for a in range(1, count):
        work.begin(a)
    kernel_grad[...] = jnp.zeros_like(kernel_grad)
    hot_grad[...] = jnp.zeros_like(hot_grad)
    conv_in[...] = jnp.zeros_like(conv_in)

    def compute(i):
        words = pl.ds(pl.multiple_of(i * WORD_BLOCK, WORD_BLOCK), WORD_BLOCK)
        slots = pl.ds(pl.multiple_of(i * WORD_BLOCK * SLOTS, WORD_BLOCK * SLOTS), WORD_BLOCK * SLOTS)
        conv_backward_block(
            index_ref[slots, :],
            length_ref[words, :],
            (table_ref, kernel_ref, width_ref),
            grad_ref,
            words,
            kernel_grad,
            hot_grad,
        )

    lead = 2

    def together(t, _):
        @pl.when(t < items)
        def _():
            for a in range(1, count):
                work.first_leg(a, t)

        pl.when(t < blocks)(functools.partial(compute, t))

        @pl.when((t >= lead) & (t < items + lead))
        def _():
            for a in range(1, count):
                work.middle_leg(a, t - lead)

        return 0

    lax.fori_loop(0, max(items + lead, blocks), together, 0)

    wide = kernel_ref.shape[1]
    kernel_grad[:, wide:] = jnp.dot(
        fold_ref[...],
        hot_grad[...] * mask_ref[...],
        precision=lax.Precision.HIGHEST,
        preferred_element_type=F32,
    )
    depth, half = conv.block
    for block in range(conv.filled // depth):
        for h in range(2):
            conv_in[h, block] = kernel_grad[
                block * depth : (block + 1) * depth, h * half : (h + 1) * half
            ]
    work.begin(0)

    def leg(body):
        def step(t, _):
            body(0, t)
            return 0

        lax.fori_loop(0, items, step, 0)

    leg(work.first_leg)
    leg(work.middle_leg)
    for a in range(count):
        work.cross_over(a)
    work.last_leg(0)
    spread = Gather([conv], [conv_total], [conv_out], gather_sems, False)
    spread.begin(0)
    copies = pair_exchange(rest, totals[1:], rest_outs, pair_sems, at)
    for a in range(1, count):
        work.last_leg(a)
    for copy in copies:
        copy.start()
    for step in spread.steps():
        step()
    spread.finish()
    for a in range(count):
        work.finish(a)
    for copy in copies:
        copy.wait()


def tail(plans, grads, conv_inputs, grad, mask, fold, collective_id):
    conv, rest = plans[0], plans[1:]
    words = grad.shape[0]
    return pl.pallas_call(
        functools.partial(tail_kernel, plans, words // WORD_BLOCK),
        out_shape=[jax.ShapeDtypeStruct(conv.shape, F32)] + [reduce_out(plan) for plan in rest],
        in_specs=[pl.BlockSpec(memory_space=pl.ANY)] * len(rest)
        + [pl.BlockSpec(memory_space=pltpu.VMEM)] * 8,
        out_specs=[pl.BlockSpec(memory_space=pltpu.VMEM)] * len(plans),
        scratch_shapes=[
            pltpu.VMEM((conv.filled, 2 * conv.block[1]), F32),
            pltpu.VMEM((HOT, LANE), F32),
            pltpu.VMEM(conv.shape, F32),
            pltpu.VMEM(conv.block, F32),
            pltpu.SemaphoreType.DMA((2 * len(rest),)),
            Gather.semaphores([conv]),
        ]
        + Reduce.scratch(plans),
        compiler_params=pltpu.CompilerParams(
            collective_id=collective_id, has_side_effects=True, vmem_limit_bytes=60 * 2**20
        ),
    )(*grads, *conv_inputs, grad, mask, fold)


def gate_parts(sums):
    parts = [sums[:, :HP]]
    for g in range(1, 4):
        begin = g * H // LANE * LANE
        moved = sums[:, begin : begin + HP + LANE]
        parts.append(pltpu.roll(moved, HP + LANE - (g * H - begin), 1)[:, :HP])
    return parts


def join_gates(parts, columns):
    rows = parts[0].shape[0]
    total = None
    for g, part in enumerate(parts):
        begin = g * H // LANE * LANE
        wide = jnp.concatenate([part, jnp.zeros((rows, LANE), F32)], axis=1)
        if g * H - begin:
            wide = pltpu.roll(wide, g * H - begin, 1)
        pieces = [wide]
        if begin:
            pieces = [jnp.zeros((rows, begin), F32)] + pieces
        if columns - begin - HP - LANE > 0:
            pieces = pieces + [jnp.zeros((rows, columns - begin - HP - LANE), F32)]
        placed = jnp.concatenate(pieces, axis=1)[:, :columns]
        total = placed if total is None else total + placed
    return total


class Line:
    def __init__(self, n):
        self.at = Place()
        self.length = n // 4
        self.me = 2 * self.at.z + self.at.c

    def peer(self, z, other_core=False):
        at = self.at
        return (at.d + (1 - 2 * at.c if other_core else 0), at.f + 4 * (z - at.z))

    def others(self, body):
        def step(z, _):
            pl.when(z != self.at.z)(functools.partial(body, z))
            return 0

        lax.fori_loop(0, self.length, step, 0)

    def chips(self, body):
        def step(z, _):
            body(z)
            return 0

        lax.fori_loop(0, self.length, step, 0)

    def greet(self, across, both_cores):
        barrier = pltpu.get_barrier_semaphore()

        def signal(target):
            pl.semaphore_signal(barrier, inc=1, device_id=target, device_id_type=MESH)

        signal(self.at.sibling)
        count = 1
        if across:
            signal(self.at.partner1)
            signal(self.at.partner3)
            count += 2

        def chip(z):
            signal(self.peer(z))
            if both_cores:
                signal(self.peer(z, True))

        self.others(chip)
        pl.semaphore_wait(barrier, count + (self.length - 1) * (2 if both_cores else 1))


class Semaphores:
    def __init__(self, ref, size):
        self.ref, self.size = ref, size

    def __call__(self, kind, index):
        return self.ref.at[kind * self.size + index]


HIDDEN_CHUNKS = ((0, 48), (48, 96), (96, 128), (128, 144))


def hidden_chunks(rows):
    return [(a, min(b, rows)) for a, b in HIDDEN_CHUNKS if a < rows] + (
        [(HIDDEN_CHUNKS[-1][1], rows)] if rows > HIDDEN_CHUNKS[-1][1] else []
    )


def lstm_forward_kernel(
    batch, n, x_ref, w_ref, h0_ref, c0_ref, keep_ref, extra_ref, own_ref, *refs
):
    hp_ref, cp_ref, i_ref, f_ref, u_ref, o_ref, t_ref, hall_ref, part_ref = refs[:9]
    hidden, soft_sems, hidden_sems = refs[9:]
    line = Line(n)
    at, length = line.at, line.length
    rows_all = x_ref.shape[0]
    chunks = hidden_chunks(rows_all)
    RECV, TO_LINE, TO_NEAR, TO_LAST, LOCAL = range(5)
    sem = Semaphores(soft_sems, n)
    H_RECV, H_LINE, H_SIB = range(3)
    hsem = Semaphores(hidden_sems, 2 * length * len(chunks))

    def column(z):
        return at.f + 4 * (z - at.z)

    def to_line(z):
        return remote(
            own_ref.at[2 * z + at.c],
            part_ref.at[at.f],
            sem(TO_LINE, z),
            sem(RECV, at.f),
            line.peer(z),
        )

    def pass_on(kind, index, slot, target, own=False):
        return remote(
            own_ref.at[line.me] if own else part_ref.at[slot],
            part_ref.at[slot],
            sem(kind, index),
            sem(RECV, slot),
            target,
        )

    def landed(slot):
        pass_on(TO_NEAR, 0, slot, at.partner1).wait_recv()

    local = pltpu.make_async_copy(own_ref.at[line.me], part_ref.at[at.f], sem(LOCAL, 0))

    def event_begin():
        line.others(lambda z: to_line(z).start())
        pass_on(TO_NEAR, at.z, at.f, at.partner1, True).start()
        pass_on(TO_LAST, at.z, at.f, at.partner3, True).start()
        local.start()

    def event_line():
        def chip(z):
            landed(column(z))
            pass_on(TO_NEAR, z, column(z), at.partner1).start()
            pass_on(TO_LAST, z, column(z), at.partner3).start()

        line.others(chip)

    def event_near():
        def chip(z):
            slot = column(z) + at.flip1
            landed(slot)
            pass_on(TO_LAST, length + z, slot, at.partner3).start()

        line.chips(chip)

    def event_end():
        def chip(z):
            landed(column(z) + at.flip3)
            landed(column(z) + at.flip1 + at.flip3)
            pass_on(TO_NEAR, z, column(z), at.partner1).wait_send()
            pass_on(TO_LAST, z, column(z), at.partner3).wait_send()
            pass_on(TO_LAST, length + z, column(z), at.partner3).wait_send()

        line.chips(chip)
        line.others(lambda z: to_line(z).wait_send())
        local.wait()

    def chunk_copy(k, member, kind, index, target):
        begin, end = chunks[k]
        here = hall_ref.at[member, pl.ds(begin, end - begin), :]
        return remote(
            here,
            here,
            hsem(kind, index * len(chunks) + k),
            hsem(H_RECV, member * len(chunks) + k),
            target,
        )

    def chunk_out(k):
        begin, end = chunks[k]
        hall_ref[line.me, begin:end, :] = hidden[begin:end, :].astype(BF)
        line.others(lambda z: chunk_copy(k, line.me, H_LINE, z, line.peer(z)).start())
        chunk_copy(k, line.me, H_SIB, at.z, at.sibling).start()

    def chunk_pass(k):
        def chip(z):
            member = 2 * z + at.c
            chunk_copy(k, member, H_SIB, z, at.sibling).wait_recv()
            chunk_copy(k, member, H_SIB, z, at.sibling).start()

        line.others(chip)

    def chunk_end(k):
        def chip(z):
            chunk_copy(k, 2 * z + 1 - at.c, H_SIB, z, at.sibling).wait_recv()
            chunk_copy(k, 2 * z + at.c, H_SIB, z, at.sibling).wait_send()

        line.chips(chip)
        line.others(lambda z: chunk_copy(k, line.me, H_LINE, z, line.peer(z)).wait_send())

    line.greet(True, False)
    event_begin()
    per_tile = 8 // batch
    tiles = rows_all // 8
    row = lax.broadcasted_iota(jnp.int32, (8, HP), 0)
    lane = lax.broadcasted_iota(jnp.int32, (8, LANE), 1)
    last = HP - LANE

    def tile(step, carried):
        h, c = carried
        rows = pl.ds(pl.multiple_of(step * 8, 8), 8)
        x = x_ref[rows, :]
        keep = keep_ref[rows, :]
        saved = None
        for part in range(per_tile):
            hp, cp = h * keep, c * keep
            sums = x + dot(hp.astype(BF), w_ref[...])
            i, f, u, o = gate_parts(sums)
            i, f, u, o = jax.nn.sigmoid(i), jax.nn.sigmoid(f), jnp.tanh(u), jax.nn.sigmoid(o)
            c = f * cp + i * u
            t = jnp.tanh(c)
            h = (o * t).astype(BF).astype(F32)
            now = (hp, cp, i, f, u, o, t, h)
            if saved is None:
                saved = now
            else:
                saved = tuple(jnp.where(row >= part * batch, b, a) for a, b in zip(saved, now))
            h, c = pltpu.roll(h, batch, 0), pltpu.roll(c, batch, 0)
        for ref, value in zip((hp_ref, cp_ref, i_ref, f_ref, u_ref, o_ref, t_ref), saved):
            ref[rows, :] = value
        hidden[rows, :last] = saved[-1][:, :last]
        hidden[rows, last:] = jnp.where(lane < H - last, saved[-1][:, last:], extra_ref[rows, :])

        pl.when(step == tiles // 3)(event_line)
        pl.when(step == tiles * 2 // 3)(event_near)
        for k, (_, end) in enumerate(chunks):
            pl.when(step == end // 8 - 1)(functools.partial(chunk_out, k))
        return h, c

    lax.fori_loop(0, tiles, tile, (h0_ref[...], c0_ref[...]))
    for k in range(len(chunks)):
        chunk_pass(k)
    event_end()
    for k in range(len(chunks)):
        chunk_end(k)


def lstm_forward(batch, plan, x, recur, h0, c0, keep, extra, own, collective_id):
    rows, n = x.shape[0], plan.fsdp
    members = plan.parts
    chunks = len(hidden_chunks(rows))
    vmem = pl.BlockSpec(memory_space=pltpu.VMEM)
    anywhere = pl.BlockSpec(memory_space=pl.ANY)
    return pl.pallas_call(
        functools.partial(lstm_forward_kernel, batch, n),
        out_shape=[jax.ShapeDtypeStruct((rows, HP), F32)] * 7
        + [
            jax.ShapeDtypeStruct((members, rows, HP), BF),
            jax.ShapeDtypeStruct((n,) + plan.block, BF),
        ],
        in_specs=[vmem] * 6 + [anywhere],
        out_specs=[vmem] * 8 + [anywhere],
        scratch_shapes=[
            pltpu.VMEM((rows, HP), F32),
            pltpu.SemaphoreType.DMA((5 * n,)),
            pltpu.SemaphoreType.DMA((3 * members * chunks,)),
        ],
        compiler_params=pltpu.CompilerParams(
            collective_id=collective_id, has_side_effects=True, vmem_limit_bytes=48 * 2**20
        ),
    )(x, recur, h0, c0, keep, extra, own)


def lstm_backward_kernel(
    batch,
    n,
    dh_ref,
    w_ref,
    keep_ref,
    cp_ref,
    i_ref,
    f_ref,
    u_ref,
    o_ref,
    t_ref,
    grad_ref,
    dz_ref,
    out_ref,
    held_near,
    held_line,
    from_last,
    from_near,
    sems,
):
    line = Line(n)
    at, length = line.at, line.length
    LAST, LAST_RECV, NEAR, NEAR_RECV, TO_LINE, LINE_RECV, SIB, SIB_RECV = range(8)
    sem = Semaphores(sems, 2 * length)

    def slot(z, b1, b3):
        return 4 * z + at.stride1 * b1 + at.stride3 * b3

    def to_last(z, b1):
        return remote(
            grad_ref.at[slot(z, b1, 1 - at.last)],
            from_last.at[2 * z + b1],
            sem(LAST, 2 * z + b1),
            sem(LAST_RECV, 2 * z + b1),
            at.partner3,
        )

    def to_near(z):
        return remote(
            held_near.at[z], from_near.at[z], sem(NEAR, z), sem(NEAR_RECV, z), at.partner1
        )

    def to_line(z):
        return remote(
            held_line.at[z], out_ref.at[line.me], sem(TO_LINE, z), sem(LINE_RECV, at.z), line.peer(z)
        )

    def line_arrived(z):
        here = out_ref.at[2 * z + at.c]
        remote(here, here, sem(TO_LINE, z), sem(LINE_RECV, z), line.peer(z)).wait_recv()

    def to_sibling(z, other=False):
        here = out_ref.at[2 * z + (1 - at.c if other else at.c)]
        return remote(here, here, sem(SIB, z), sem(SIB_RECV, z), at.sibling)

    def event_begin():
        def chip(z):
            to_last(z, 1 - at.first).start()

        line.chips(chip)

        def chip_own(z):
            to_last(z, at.first).start()

        line.chips(chip_own)

    def event_last():
        def chip(z):
            b1 = 1 - at.first
            to_last(z, b1).wait_recv()
            held_near[z] = (
                grad_ref[slot(z, b1, at.last)].astype(F32) + from_last[2 * z + b1].astype(F32)
            ).astype(BF)
            to_near(z).start()

        line.chips(chip)

    def event_near():
        def chip(z):
            to_last(z, at.first).wait_recv()
            to_near(z).wait_recv()
            total = (
                grad_ref[slot(z, at.first, at.last)].astype(F32)
                + from_last[2 * z + at.first].astype(F32)
                + from_near[z].astype(F32)
            ).astype(BF)
            held_line[z] = total

            @pl.when(z == at.z)
            def _():
                out_ref[line.me] = total

            @pl.when(z != at.z)
            def _():
                to_line(z).start()

        line.chips(chip)
        to_sibling(at.z).start()

    def event_line():
        def chip(z):
            line_arrived(z)
            to_sibling(z).start()

        line.others(chip)

    def event_end():
        def chip(z):
            to_sibling(z, True).wait_recv()
            to_sibling(z).wait_send()
            to_near(z).wait_send()
            to_last(z, 0).wait_send()
            to_last(z, 1).wait_send()

        line.chips(chip)
        line.others(lambda z: to_line(z).wait_send())

    line.greet(True, False)
    event_begin()
    per_tile = 8 // batch
    tiles = dh_ref.shape[0] // 8
    row = lax.broadcasted_iota(jnp.int32, (8, dz_ref.shape[1]), 0)
    real = lax.broadcasted_iota(jnp.int32, (8, HP), 1) < H

    def tile(step, carried):
        dh_carry, dc_carry = carried
        rows = pl.ds(pl.multiple_of((tiles - 1 - step) * 8, 8), 8)
        keep = keep_ref[rows, :]
        i, f, u, o, t = (r[rows, :] for r in (i_ref, f_ref, u_ref, o_ref, t_ref))
        soft = dh_ref[rows, :]
        to_c = o * (1.0 - t * t)
        to_i = jnp.where(real, u * i * (1.0 - i), 0.0)
        to_f = jnp.where(real, cp_ref[rows, :] * f * (1.0 - f), 0.0)
        to_u = jnp.where(real, i * (1.0 - u * u), 0.0)
        to_o = jnp.where(real, t * o * (1.0 - o), 0.0)
        back = f * keep
        saved = None
        for part in reversed(range(per_tile)):
            dh = jnp.where(real, soft + dh_carry, 0.0)
            dc = dc_carry + dh * to_c
            dz = join_gates([dc * to_i, dc * to_f, dc * to_u, dh * to_o], dz_ref.shape[1])
            saved = dz if saved is None else jnp.where(row >= (part + 1) * batch, saved, dz)
            dh_carry = dot(dz.astype(BF), w_ref[...]) * keep
            dc_carry = dc * back
            dh_carry, dc_carry = (
                pltpu.roll(dh_carry, 8 - batch, 0),
                pltpu.roll(dc_carry, 8 - batch, 0),
            )
        dz_ref[rows, :] = saved
        pl.when(step == tiles // 3)(event_last)
        pl.when(step == tiles * 2 // 3)(event_near)
        pl.when(step == tiles - 2)(event_line)
        return dh_carry, dc_carry

    zero = jnp.zeros((8, HP), F32)
    lax.fori_loop(0, tiles, tile, (zero, zero))
    event_end()


def lstm_backward(batch, plan, columns, dh, recur_t, keep, states, grad, collective_id):
    rows, n = dh.shape[0], plan.fsdp
    length = n // 4
    vmem = pl.BlockSpec(memory_space=pltpu.VMEM)
    return pl.pallas_call(
        functools.partial(lstm_backward_kernel, batch, n),
        out_shape=[
            jax.ShapeDtypeStruct((rows, columns), F32),
            jax.ShapeDtypeStruct((plan.parts,) + plan.block, BF),
        ],
        in_specs=[vmem] * 10,
        out_specs=[vmem] * 2,
        scratch_shapes=[
            pltpu.VMEM((length,) + plan.block, BF),
            pltpu.VMEM((length,) + plan.block, BF),
            pltpu.VMEM((2 * length,) + plan.block, BF),
            pltpu.VMEM((length,) + plan.block, BF),
            pltpu.SemaphoreType.DMA((8 * 2 * length,)),
        ],
        compiler_params=pltpu.CompilerParams(
            collective_id=collective_id, has_side_effects=True, vmem_limit_bytes=48 * 2**20
        ),
    )(dh, recur_t, keep, *states, grad)


def softmax_kernel(
    vocab,
    n,
    h_ref,
    w_ref,
    map_ref,
    map_back_ref,
    loss_ref,
    grad_h_ref,
    grad_w_ref,
    spread_back,
    logits,
    grads,
    stats,
    for_sibling,
    from_sibling,
    for_line,
    from_line,
    own_total,
    sems,
):
    line = Line(n)
    at, length, me = line.at, line.length, line.me
    members, rows, _ = h_ref.shape
    width = w_ref.shape[-1]
    w = w_ref[...].reshape(-1, width)
    STAT, STAT_RECV, SIB, SIB_RECV, TO_LINE, LINE_RECV = range(6)
    sem = Semaphores(sems, members)
    column = me * width + lax.broadcasted_iota(jnp.int32, (rows, width), 1)
    real_column = column.astype(F32)
    words = up_to(rows, LANE)
    lane = lax.broadcasted_iota(jnp.int32, (rows, LANE), 1)
    aside = HP - LANE

    def pieces(b):
        tail = h_ref[b, :, aside:].astype(F32)
        first = H + 1 - aside
        target = tail[:, first : first + 1] * 256.0 + tail[:, first + 1 : first + 2]
        scale = (
            tail[:, first + 2 : first + 3]
            + tail[:, first + 3 : first + 4]
            + tail[:, first + 4 : first + 5]
        )
        return target, scale

    line.greet(False, True)

    def forward(b, _):
        h = h_ref[b]
        wide = dot(h, map_ref[...]).astype(BF)
        spread_back[b] = dot(h, map_back_ref[...]).astype(BF)
        now = jnp.where(column < vocab, dot(wide, w), -1e30)
        logits[b] = now
        target, _ = pieces(b)
        top = jnp.max(now, axis=1, keepdims=True)
        log_sum = top + jnp.log(jnp.sum(jnp.exp(now - top), axis=1, keepdims=True))
        picked = jnp.sum(jnp.where(real_column == target, now, 0.0), axis=1, keepdims=True)
        both = jnp.where(lane == 0, log_sum, jnp.where(lane == 1, picked, 0.0))
        both = jnp.concatenate([both, jnp.zeros((words - rows, LANE), F32)], axis=0).T
        stats[me, 0, pl.ds(b, 1), :] = both[0:1, :]
        stats[me, 1, pl.ds(b, 1), :] = both[1:2, :]
        return 0

    lax.fori_loop(0, members, forward, 0)

    def stat(member, target):
        here = stats.at[member]
        return remote(here, here, sem(STAT, member), sem(STAT_RECV, member), target)

    def stat_out(z):
        return [
            remote(
                stats.at[me], stats.at[me], sem(STAT, 2 * z + core), sem(STAT_RECV, me), target
            )
            for core, target in ((at.c, line.peer(z)), (1 - at.c, line.peer(z, True)))
        ]

    def send_stats(z):
        for copy in stat_out(z):
            copy.start()

    line.others(send_stats)
    to_pair = remote(
        stats.at[me], stats.at[me], sem(STAT, 2 * at.z + 1 - at.c), sem(STAT_RECV, me), at.sibling
    )
    to_pair.start()

    def stats_in(z):
        for core in (at.c, 1 - at.c):
            stat(2 * z + core, at.sibling).wait_recv()

    line.others(stats_in)
    stat(2 * at.z + 1 - at.c, at.sibling).wait_recv()
    top = stats[0, 0]
    for q in range(1, members):
        top = jnp.maximum(top, stats[q, 0])
    total = jnp.zeros_like(top)
    picked = jnp.zeros_like(top)
    for q in range(members):
        total += jnp.exp(stats[q, 0] - top)
        picked += stats[q, 1]
    log_total = top + jnp.log(total)
    loss_ref[...] = log_total - picked
    log_columns = jnp.concatenate(
        [log_total, jnp.zeros((LANE - members, words), F32)], axis=0
    ).T[:rows]

    def to_sibling(z):
        return remote(
            for_sibling.at[z], from_sibling.at[z], sem(SIB, z), sem(SIB_RECV, z), at.sibling
        )

    def to_line(z):
        return remote(
            for_line.at[z], from_line.at[at.z], sem(TO_LINE, z), sem(LINE_RECV, at.z), line.peer(z)
        )

    def backward(k, _):
        z = lax.rem(k, length)
        mine = k >= length
        b = 2 * z + jnp.where(mine, at.c, 1 - at.c)
        target, scale = pieces(b)
        log_sum = jnp.sum(jnp.where(lane == b, log_columns, 0.0), axis=1, keepdims=True)
        share = jnp.exp(logits[b] - log_sum)
        grad = ((share - (real_column == target).astype(F32)) * scale).astype(BF)
        grads[b] = grad
        back = dot_cols(grad, w)

        @pl.when(jnp.logical_not(mine))
        def _():
            for_sibling[z] = back.astype(BF)
            to_sibling(z).start()

        @pl.when(mine)
        def _():
            to_sibling(z).wait_recv()
            total = back + from_sibling[z].astype(F32)

            @pl.when(z == at.z)
            def _():
                own_total[...] = total

            @pl.when(z != at.z)
            def _():
                for_line[z] = total.astype(BF)
                to_line(z).start()

        return 0

    lax.fori_loop(0, 2 * length, backward, 0)

    depth = map_ref.shape[1]
    unit = 256
    everything = grads[...].reshape(members * rows, width)

    def weight_grad(m, _):
        left = spread_back[:, :, pl.ds(pl.multiple_of(m * unit, unit), unit)]
        result = dot_rows(left.reshape(members * rows, unit), everything).astype(BF)
        grad_w_ref[pl.ds(m * unit, unit), :] = result
        return 0

    lax.fori_loop(0, depth // unit, weight_grad, 0)

    def arrived(z):
        remote(
            from_line.at[z], from_line.at[z], sem(TO_LINE, z), sem(LINE_RECV, z), line.peer(z)
        ).wait_recv()
        own_total[...] += from_line[z].astype(F32)

    line.others(arrived)
    spread_grad = own_total[...]
    high = spread_grad.astype(BF)
    low = (spread_grad - high.astype(F32)).astype(BF)
    grad_h_ref[...] = dot_cols(high, map_ref[...]) + dot_cols(low, map_ref[...])

    def finish(z):
        for copy in stat_out(z):
            copy.wait_send()
        to_line(z).wait_send()

    line.others(finish)
    line.chips(lambda z: to_sibling(z).wait_send())
    to_pair.wait_send()


def word_softmax(plan, h, weights, mapping, mapping_back, collective_id):
    members, rows, depth = h.shape
    n = plan.fsdp
    spread = mapping.shape[1]
    per_slot, width = plan.block
    words = up_to(rows, LANE)
    length = members // 2
    vmem = pl.BlockSpec(memory_space=pltpu.VMEM)
    loss, grad_h, grad_w = pl.pallas_call(
        functools.partial(softmax_kernel, plan.width, n),
        out_shape=[
            jax.ShapeDtypeStruct((members, words), F32),
            jax.ShapeDtypeStruct((rows, depth), F32),
            jax.ShapeDtypeStruct((spread, width), BF),
        ],
        in_specs=[vmem] * 4,
        out_specs=[vmem] * 3,
        scratch_shapes=[
            pltpu.VMEM((members, rows, spread), BF),
            pltpu.VMEM((members, rows, width), F32),
            pltpu.VMEM((members, rows, width), BF),
            pltpu.VMEM((members, 2, members, words), F32),
            pltpu.VMEM((length, rows, spread), BF),
            pltpu.VMEM((length, rows, spread), BF),
            pltpu.VMEM((length, rows, spread), BF),
            pltpu.VMEM((length, rows, spread), BF),
            pltpu.VMEM((rows, spread), F32),
            pltpu.SemaphoreType.DMA((6 * members,)),
        ],
        compiler_params=pltpu.CompilerParams(
            collective_id=collective_id, has_side_effects=True, vmem_limit_bytes=56 * 2**20
        ),
    )(h, weights, mapping, mapping_back)
    return loss, grad_h, grad_w.reshape((n,) + plan.block)


def shards(
    fsdp_count,
    dp_count,
    chars,
    lengths,
    targets,
    resets,
    init_state,
    window_grad,
    char_table,
    conv_weight,
    conv_bias,
    highway_flat,
    lstm_flat,
    soft_flat,
):
    micro_count, streams, step_count, letters = chars.shape
    char_count, embed_dim = char_table.shape
    filters = conv_weight.shape[1]
    batch = micro_count * streams
    words = step_count * batch
    rows = up_to(words, 16)
    fp = up_to(filters + 1, LANE)
    dp_at, fsdp_at = lax.axis_index("dp"), lax.axis_index("fsdp")
    highway = Windows(
        highway_flat.shape[0] * fsdp_count, filters, 4 * (filters + 1), fsdp_count, dp_count, True
    )
    lstm_used = filters + H + 1
    lstm = Windows(
        lstm_flat.shape[0] * fsdp_count, 4 * H, lstm_used, fsdp_count, dp_count, False
    )
    soft = Windows(
        soft_flat.shape[0] * fsdp_count, V, H + 1, fsdp_count, dp_count, False, fsdp_count // 2
    )
    member = 2 * (fsdp_at // 4) + lax.rem(dp_at, 2)

    soft_own = soft.from_flat(soft_flat, fsdp_at)
    highway_all, lstm_all = gather(
        [highway, lstm],
        [highway.from_flat(highway_flat, fsdp_at), lstm.from_flat(lstm_flat, fsdp_at)],
        1,
    )
    highway_all = highway_all.reshape(-1, highway.columns)
    lstm_all = lstm_all.reshape(2, -1, lstm.columns // 2)

    def by_step(array):
        return jnp.moveaxis(array.reshape((batch, step_count) + array.shape[3:]), 1, 0).reshape(
            (words,) + array.shape[3:]
        )

    def pad_rows(array, value=0):
        return jnp.pad(
            array,
            [(0, rows - words)] + [(0, 0)] * (array.ndim - 1),
            constant_values=value,
        )

    word_chars = pad_rows(by_step(chars))
    word_lengths = pad_rows(by_step(lengths))[:, None]
    position = jnp.arange(letters, dtype=jnp.int32)[None, :]
    codes = jnp.where(position < word_lengths, word_chars, -1)
    codes = jnp.pad(codes, ((0, 0), (0, SLOTS + KMAX - letters)), constant_values=-1)
    index = jnp.stack(
        [
            jnp.where(
                codes[:, q : q + SLOTS] >= 0, codes[:, q : q + SLOTS] + q * char_count, -1
            )
            for q in range(KMAX)
        ]
        + [jnp.full((rows, SLOTS), KMAX * char_count, jnp.int32)],
        axis=2,
    ).reshape(rows * SLOTS, KMAX + 1)
    column = np.arange(fp)
    widths = np.ones((fp,), np.int32)
    for cut_at in FILTER_CUTS:
        widths = widths + ((column >= filters * cut_at // 22) & (column < filters))
    widths = widths.astype(np.int32)
    kernel_mask = jnp.asarray(
        np.arange(KMAX * embed_dim)[:, None] // embed_dim < widths[None, :filters]
    )
    ones_row = KMAX * embed_dim
    kernel = jnp.concatenate(
        [jnp.where(kernel_mask, conv_weight, jnp.zeros_like(conv_weight)), conv_bias[None, :]], axis=0
    )
    kernel = jnp.pad(kernel, ((0, LANE - ones_row - 1), (0, fp - filters)))
    spread_table = jnp.concatenate(
        [
            jnp.pad(char_table, ((0, 0), (q * embed_dim, LANE - (q + 1) * embed_dim)))
            for q in range(KMAX)
        ]
        + [jnp.zeros((1, LANE), BF).at[0, ones_row].set(1.0)],
        axis=0,
    )
    spread_table = jnp.pad(spread_table, ((0, HOT - KMAX * char_count - 1), (0, 0)))
    conv_inputs = (index, word_lengths, spread_table, kernel, jnp.asarray(widths)[None, :])
    word_block = WORD_BLOCK
    feature = pl.pallas_call(
        functools.partial(conv_forward_kernel, filters),
        out_shape=jax.ShapeDtypeStruct((rows, fp), BF),
        grid=(rows // word_block,),
        in_specs=conv_specs(word_block, fp),
        out_specs=pl.BlockSpec((word_block, fp), lambda i: (i, 0)),
        compiler_params=pltpu.CompilerParams(vmem_limit_bytes=48 * 2**20),
    )(*conv_inputs)

    filter_lane = jnp.arange(fp)[None, :]
    each_layer = 2 * (filters + 1)
    owner_rows = highway.rows

    def layer_map(row_map, layer):
        at = row_map - layer * each_layer
        inside = (row_map >= 0) & (at >= 0) & (at < each_layer)
        is_gate = inside & (at >= filters + 1)
        source = np.where(inside, np.where(is_gate, at - filters - 1, at), -1)
        return source.astype(np.int32), inside & ~is_gate, is_gate

    layers = []
    for layer in range(2):
        source, is_trans, is_gate = layer_map(highway.gathered, layer)
        live = np.nonzero(source.reshape(-1, owner_rows).max(axis=1) >= 0)[0]
        begin, end = int(live[0]) * owner_rows, (int(live[-1]) + 1) * owner_rows
        begin = begin // 16 * 16
        end = min(up_to(end, 16), source.shape[0])
        weights = highway_all[begin:end]
        mapping = one_hot_map(fp, source[begin:end])
        trans_mask = jnp.asarray(is_trans[begin:end].astype(np.float32))[None, :]
        gate_mask = jnp.asarray(is_gate[begin:end].astype(np.float32))[None, :]
        spread = dot(feature, mapping)
        both = jnp.concatenate([spread * trans_mask, spread * gate_mask], axis=0).astype(BF)
        sums = dot(both, weights)
        trans, gate = sums[:rows], jax.nn.sigmoid(sums[rows:])
        layers.append((feature, trans, gate, weights, mapping, trans_mask, gate_mask))
        value = gate * jax.nn.silu(trans) + (1.0 - gate) * feature.astype(F32)
        feature = jnp.where(
            filter_lane < filters, value, jnp.where(filter_lane == filters, 1.0, 0.0)
        ).astype(BF)

    lp = up_to(lstm_used, LANE)
    first_h = np.nonzero(lstm.gathered >= filters)[0][0] // 16 * 16
    last_x = min(up_to(int(np.nonzero((lstm.gathered >= 0) & (lstm.gathered < filters))[0][-1]) + 1, 16), lstm.gathered.shape[0])
    lstm_map = one_hot_map(lp, lstm.gathered)
    no_hidden = jnp.concatenate(
        [
            feature[:, :filters],
            jnp.zeros((rows, H), BF),
            jnp.ones((rows, 1), BF),
            jnp.zeros((rows, lp - lstm_used), BF),
        ],
        axis=1,
    )
    spread_x = dot(no_hidden, lstm_map).astype(BF)
    from_input = jnp.concatenate([dot(spread_x, lstm_all[0]), dot(spread_x, lstm_all[1])], axis=1)
    hidden_source = lstm.gathered[first_h:] - filters
    hidden_map = one_hot_map(HP, np.where((hidden_source >= 0) & (hidden_source < H), hidden_source, -1))
    recur = jnp.concatenate(
        [dot(hidden_map, lstm_all[h, first_h:]).astype(BF) for h in range(2)], axis=1
    )
    recur_t = jnp.concatenate(
        [
            lax.dot_general(
                lstm_all[h, first_h:],
                hidden_map,
                (((0,), (1,)), ((), ())),
                preferred_element_type=F32,
            ).astype(BF)
            for h in range(2)
        ],
        axis=0,
    )
    keep = pad_rows(by_step(1 - resets).astype(F32))[:, None]
    start = init_state.reshape(batch, 2, H)
    start = jnp.pad(start, ((0, 8 - batch), (0, 0), (0, HP - H)))
    row_scale = jnp.broadcast_to(
        window_grad.reshape(1, batch) / step_count, (step_count, batch)
    ).reshape(words)
    goal = by_step(targets)
    scale_high = lax.reduce_precision(row_scale, 8, 7)
    scale_mid = lax.reduce_precision(row_scale - scale_high, 8, 7)
    extra = jnp.stack(
        [
            jnp.ones((words,), F32),
            (goal // 256).astype(F32),
            (goal % 256).astype(F32),
            scale_high,
            scale_mid,
            row_scale - scale_high - scale_mid,
        ],
        axis=1,
    )
    aside = H - (HP - LANE)
    extra = jnp.pad(extra, ((0, rows - words), (aside, LANE - aside - extra.shape[1])))
    *states, hidden_all, soft_part = lstm_forward(
        batch,
        soft,
        from_input,
        recur,
        start[:, 0].astype(BF).astype(F32),
        start[:, 1],
        keep,
        extra,
        soft_own,
        4,
    )
    hp = states[0]

    word_loss, grad_hidden, soft_grad = word_softmax(
        soft,
        hidden_all,
        soft_part,
        one_hot_map(HP, soft.gathered),
        one_hot_map(HP, soft.reduced),
        5,
    )
    word_loss = lax.dynamic_index_in_dim(word_loss, member, 0, keepdims=False)
    window_loss = jnp.mean(word_loss[:words].reshape(step_count, batch), axis=0).reshape(
        micro_count, streams
    )

    dz, soft_part = lstm_backward(
        batch, soft, lstm.columns, grad_hidden, recur_t, keep, states[1:], soft_grad, 6
    )
    dz = dz.astype(BF)
    half = lstm.columns // 2
    lstm_in = jnp.concatenate(
        [
            feature[:, :filters],
            hp[:, :H].astype(BF),
            jnp.ones((rows, 1), BF),
            jnp.zeros((rows, lp - lstm_used), BF),
        ],
        axis=1,
    )
    lstm_in = dot(lstm_in, one_hot_map(lp, lstm.reduced)).astype(BF)
    lstm_grad = jnp.stack(
        [dot_rows(lstm_in, dz[:, h * half : (h + 1) * half]).astype(BF) for h in range(2)]
    ).reshape(lstm.shape)
    grad_spread = dot_cols(dz[:, :half], lstm_all[0, :last_x]) + dot_cols(
        dz[:, half:], lstm_all[1, :last_x]
    )
    input_source = lstm.gathered[:last_x]
    grad = compress(
        grad_spread, one_hot_map(fp, np.where(input_source < filters, input_source, -1))
    )

    grads_of, inputs_of = [], []
    for layer in (1, 0):
        layer_in, trans, gate, weights, mapping, trans_mask, gate_mask = layers[layer]
        sig = jax.nn.sigmoid(trans)
        silu = trans * sig
        grad = jnp.where(filter_lane < filters, grad, 0.0)
        grad_trans = (grad * gate * sig * (1.0 + trans * (1.0 - sig))).astype(BF)
        grad_gate = (grad * (silu - layer_in.astype(F32)) * gate * (1.0 - gate)).astype(BF)
        pair = jnp.concatenate([grad_trans, grad_gate], axis=0)
        spread = dot_cols(pair, weights)
        grad = grad * (1.0 - gate) + compress(
            spread[:rows] * trans_mask + spread[rows:] * gate_mask, mapping
        )
        source, is_trans, is_gate = layer_map(highway.reduced, layer)
        spread_in = dot(layer_in, one_hot_map(fp, source))
        inputs_of = [
            (spread_in * jnp.asarray(is_trans.astype(np.float32))[None, :]).astype(BF),
            (spread_in * jnp.asarray(is_gate.astype(np.float32))[None, :]).astype(BF),
        ] + inputs_of
        grads_of = [pair] + grads_of
    highway_grad = (
        dot_rows(jnp.concatenate(inputs_of, axis=0), jnp.concatenate(grads_of, axis=0))
        .astype(BF)
        .reshape(highway.shape)
    )

    grad = jnp.where(filter_lane < filters, grad, 0.0)
    hot_row, hot_lane = np.arange(HOT), np.arange(LANE)
    hot_mask = (hot_row[:, None] // char_count == hot_lane[None, :] // embed_dim) & (
        hot_row[:, None] < KMAX * char_count
    )
    hot_fold = (hot_row[None, :] % char_count == np.arange(LANE)[:, None]) & (
        hot_row[None, :] < KMAX * char_count
    )
    conv = Dense(LANE, up_to(fp + LANE, 2 * LANE), fsdp_count)
    conv_grad, highway_part, lstm_part = tail(
        [conv, highway, lstm],
        [highway_grad, lstm_grad],
        conv_inputs,
        grad,
        jnp.asarray(hot_mask.astype(np.float32)),
        jnp.asarray(hot_fold.astype(np.float32)),
        3,
    )
    conv_grad = jnp.concatenate(
        [conv_grad[h].reshape(-1, conv.block[1])[:LANE] for h in range(2)], axis=1
    )
    conv_weight_grad = jnp.where(kernel_mask, conv_grad[:ones_row, :filters], 0.0)
    conv_bias_grad = conv_grad[ones_row, :filters]
    table_grad = jnp.sum(
        conv_grad[:char_count, fp : fp + KMAX * embed_dim].reshape(char_count, KMAX, embed_dim), axis=1
    )

    def own_window(plan, part):
        if dp_count > 2:
            groups = [list(range(h, dp_count, 2)) for h in range(2)]
            part = lax.psum(part.astype(F32), "dp", axis_index_groups=groups)
        if plan.by_rows:
            at = dp_at // 2
        else:
            at = dp_at
            part = jnp.concatenate(
                [
                    lax.dynamic_slice_in_dim(part[p], at * plan.rows, plan.rows, 0)
                    for p in range(plan.parts)
                ],
                axis=1,
            ).astype(F32)
            return plan.to_flat(part, dp_at, fsdp_at)
        window = lax.dynamic_slice_in_dim(part, at * plan.rows, plan.rows, 0)
        return plan.to_flat(window, dp_at, fsdp_at)

    return (
        window_loss,
        table_grad,
        conv_weight_grad,
        conv_bias_grad,
        own_window(highway, highway_part),
        own_window(lstm, lstm_part),
        own_window(soft, soft_part),
    )


def solution(mesh):
    in_specs = (
        P(None, ("dp", "fsdp"), None, None),
        P(None, ("dp", "fsdp"), None),
        P(None, ("dp", "fsdp"), None),
        P(None, ("dp", "fsdp"), None),
        P(None, ("dp", "fsdp"), None, None),
        P(None, ("dp", "fsdp")),
        P(),
        P(),
        P(),
        P("fsdp", None),
        P("fsdp", None),
        P("fsdp", None),
    )
    out_specs = (
        P(None, ("dp", "fsdp")),
        P(),
        P(),
        P(),
        P(("dp", "fsdp"), None),
        P(("dp", "fsdp"), None),
        P(("dp", "fsdp"), None),
    )
    return jax.shard_map(
        functools.partial(shards, mesh.shape["fsdp"], mesh.shape["dp"]),
        mesh=mesh,
        in_specs=in_specs,
        out_specs=out_specs,
        check_vma=False,
    )
```

```python
import functools

import jax
import jax.numpy as jnp
import numpy as np
from jax import lax
from jax.experimental import pallas as pl
from jax.experimental.pallas import tpu as pltpu
from jax.sharding import PartitionSpec as P

H = 650
V = 10000
KMAX = 7
LANE = 128
HP = 768
SLOTS = 24
CHARS = 51
HOT = 384
FILTER_CUTS = (1, 3, 6, 10, 14, 18)
MESH = pl.DeviceIdType.MESH
BF = jnp.bfloat16
F32 = jnp.float32


def up_to(value, unit):
    return -(-value // unit) * unit


def dot(left, right):
    return jnp.dot(left, right, preferred_element_type=F32)


def dot_rows(left, right):
    return lax.dot_general(left, right, (((0,), (0,)), ((), ())), preferred_element_type=F32)


def dot_cols(left, right):
    return lax.dot_general(left, right, (((1,), (1,)), ((), ())), preferred_element_type=F32)


class Windows:
    dtype = BF

    def __init__(self, flat_rows, width, used, fsdp, dp, by_rows, parts=2):
        owners = fsdp * dp
        self.parts = parts
        self.width, self.by_rows, self.fsdp, self.dp, self.used = width, by_rows, fsdp, dp, used
        self.entries = flat_rows * LANE // owners
        self.starts = [o * self.entries // width for o in range(owners)]
        self.spans = [
            (o * self.entries % width + self.entries - 1) // width + 1 for o in range(owners)
        ]
        unit = 16 if by_rows else 8
        rows = up_to(max(self.spans), unit)
        while (dp * rows) % 16:
            rows += unit
        self.rows = rows
        self.total = owners * rows
        self.columns = up_to(width, LANE) if by_rows else parts * up_to(-(-width // parts), LANE)
        self.block = (
            (dp // 2 * rows, self.columns) if by_rows else (dp * rows, self.columns // parts)
        )
        self.shape = (
            (self.total, self.columns)
            if by_rows
            else (parts, self.total, self.columns // parts)
        )
        if by_rows:
            order = [
                (2 * jj + h) * fsdp + f
                for f in range(fsdp)
                for h in range(2)
                for jj in range(dp // 2)
            ]
        else:
            order = [d * fsdp + f for f in range(fsdp) for d in range(dp)]
        self.position = [order.index(o) for o in range(owners)]
        self.gathered = self.row_map(range(owners))
        self.reduced = self.row_map(order)

    def row_map(self, order):
        rows_of = [
            [
                self.starts[o] + i if i < self.spans[o] and self.starts[o] + i < self.used else -1
                for i in range(self.rows)
            ]
            for o in order
        ]
        return np.array(rows_of, np.int32).reshape(-1)

    def pick(self, ref, half, slot):
        depth = self.block[0]
        if self.by_rows:
            return ref.at[pl.ds(pl.multiple_of((2 * slot + half) * depth, 16), depth)]
        return ref.at[half, pl.ds(pl.multiple_of(slot * depth, 16), depth)]

    def meeting(self, begin, end):
        found = []
        for o, (start, span) in enumerate(zip(self.starts, self.spans)):
            first, last = max(0, begin - start), min(span, end - start)
            if first < last:
                found.append((o, first, last))
        return found

    def from_flat(self, shard, fsdp_at):
        parts = []
        flat = shard.reshape(-1)
        for j in range(self.dp):
            shift = lax.rem((fsdp_at * self.dp + j) * self.entries, self.width)
            piece = lax.dynamic_update_slice(
                jnp.zeros((self.rows * self.width,), BF),
                flat[j * self.entries : (j + 1) * self.entries],
                (shift,),
            ).reshape(self.rows, self.width)
            parts.append(jnp.pad(piece, ((0, 0), (0, self.columns - self.width))))
        joined = jnp.concatenate(parts, axis=0)
        if self.by_rows:
            return joined.reshape((2,) + self.block)
        part = self.columns // self.parts
        return jnp.stack([joined[:, p * part : (p + 1) * part] for p in range(self.parts)])

    def to_flat(self, window, dp_at, fsdp_at):
        shift = lax.rem((dp_at * self.fsdp + fsdp_at) * self.entries, self.width)
        flat = window[:, : self.width].reshape(-1)
        return lax.dynamic_slice(flat, (shift,), (self.entries,)).reshape(-1, LANE)


def one_hot_map(rows, row_map):
    return (
        lax.broadcasted_iota(jnp.int32, (rows, row_map.shape[0]), 0) == jnp.asarray(row_map)[None, :]
    ).astype(BF)


def greet(place_of, lengthwise):
    d, f, z = place_of.d, place_of.f, place_of.z
    barrier = pltpu.get_barrier_semaphore()
    for target in (place_of.partner1, place_of.partner3, place_of.sibling):
        pl.semaphore_signal(barrier, inc=1, device_id=target, device_id_type=MESH)

    @pl.when(z > 0)
    def _():
        pl.semaphore_signal(barrier, inc=1, device_id=(d, f - 4), device_id_type=MESH)

    @pl.when(z < lengthwise - 1)
    def _():
        pl.semaphore_signal(barrier, inc=1, device_id=(d, f + 4), device_id_type=MESH)

    has_down = (z > 0).astype(jnp.int32)
    has_up = (z < lengthwise - 1).astype(jnp.int32)
    pl.semaphore_wait(barrier, 3 + has_down + has_up)


class Place:
    def __init__(self):
        self.d, self.f = lax.axis_index("dp"), lax.axis_index("fsdp")
        self.c = lax.rem(self.d, 2)
        x, y, self.z = lax.rem(self.f, 2), lax.rem(self.f // 2, 2), self.f // 4
        self.first = x + self.c * (y - x)
        self.last = y + self.c * (x - y)
        self.stride1, self.stride3 = 1 + self.c, 2 - self.c
        self.flip1 = self.stride1 * (1 - 2 * self.first)
        self.flip3 = self.stride3 * (1 - 2 * self.last)
        self.partner1 = (self.d, self.f + self.flip1)
        self.partner3 = (self.d, self.f + self.flip3)
        self.sibling = (self.d + 1 - 2 * self.c, self.f)

    def last_bit(self, block):
        bit_x, bit_y = lax.rem(block, 2), lax.rem(block // 2, 2)
        return bit_y + self.c * (bit_x - bit_y)


def remote(src, dst, send, recv, target):
    return pltpu.make_async_remote_copy(
        src_ref=src,
        dst_ref=dst,
        send_sem=send,
        recv_sem=recv,
        device_id=target,
        device_id_type=MESH,
    )


class Gather:
    def __init__(self, plans, own, outs, sems, shared):
        self.plans, self.own, self.outs, self.sems, self.shared = plans, own, outs, sems, shared
        self.n = plans[0].fsdp
        self.lengthwise = self.n // 4
        self.at = Place()

    RECV, SIB_RECV, ONE, UP, DOWN, LAST, SIB, LOCAL = range(8)

    @staticmethod
    def semaphores(plans):
        return pltpu.SemaphoreType.DMA((8 * len(plans) * plans[0].fsdp,))

    def sem(self, kind, a, block):
        return self.sems.at[(kind * len(self.plans) + a) * self.n + block]

    def source(self, a, half):
        return self.own[a].at[half] if self.shared else self.own[a]

    def copy(self, kind, a, block, target, own=False):
        here = self.plans[a].pick(self.outs[a], self.at.c, block)
        return remote(
            self.source(a, self.at.c) if own else here,
            here,
            self.sem(kind, a, block),
            self.sem(self.SIB_RECV if kind == self.SIB else self.RECV, a, block),
            target,
        )

    def arrived(self, a, block, kind=RECV):
        c = self.at.c
        here = self.plans[a].pick(self.outs[a], 1 - c if kind == self.SIB_RECV else c, block)
        remote(
            here, here, self.sem(self.SIB, a, block), self.sem(kind, a, block), self.at.sibling
        ).wait_recv()

    def sent(self, kind, a, block):
        self.copy(kind, a, block, self.at.sibling).wait_send()

    def local(self, a, half):
        return pltpu.make_async_copy(
            self.source(a, half),
            self.plans[a].pick(self.outs[a], half, self.at.f),
            self.sem(self.LOCAL, a, half if self.shared else 0),
        )

    def send_up(self, a, block, own=False):
        @pl.when(self.at.z < self.lengthwise - 1)
        def _():
            self.copy(self.UP, a, block, (self.at.d, self.at.f + 4), own).start()

    def send_down(self, a, block, own=False):
        @pl.when(self.at.z > 0)
        def _():
            self.copy(self.DOWN, a, block, (self.at.d, self.at.f - 4), own).start()

    def begin(self, a):
        at = self.at
        self.copy(self.ONE, a, at.f, at.partner1, True).start()
        self.send_up(a, at.f, True)
        self.send_down(a, at.f, True)
        self.copy(self.LAST, a, at.f, at.partner3, True).start()
        if self.shared:
            for half in (0, 1):
                self.local(a, half).start()
        else:
            self.copy(self.SIB, a, at.f, at.sibling, True).start()
            self.local(a, at.c).start()

    def near(self, a):
        at = self.at
        block = at.f + at.flip1
        self.arrived(a, block)
        self.send_up(a, block)
        self.send_down(a, block)
        self.copy(self.LAST, a, block, at.partner3).start()
        self.copy(self.SIB, a, block, at.sibling).start()

    def line(self, a, distance):
        for sign in (1, -1):
            z = self.at.z - sign * distance

            def take(sign=sign):
                for flip in (0, 1):
                    block = self.at.f - 4 * sign * distance + flip * self.at.flip1
                    self.arrived(a, block)
                    (self.send_up if sign == 1 else self.send_down)(a, block)
                    self.copy(self.LAST, a, block, self.at.partner3).start()
                    self.copy(self.SIB, a, block, self.at.sibling).start()

            pl.when((z >= 0) & (z < self.lengthwise))(take)

    def across(self, a, distance):
        for sign in (1,) if distance == 0 else (1, -1):
            z = self.at.z - sign * distance

            def take(sign=sign):
                for flip in (0, 1):
                    block = (
                        self.at.f - 4 * sign * distance + flip * self.at.flip1 + self.at.flip3
                    )
                    self.arrived(a, block)
                    self.copy(self.SIB, a, block, self.at.sibling).start()

            pl.when((z >= 0) & (z < self.lengthwise))(take)

    def steps(self, a):
        steps = [functools.partial(self.near, a)]
        for distance in range(1, self.lengthwise):
            steps += [functools.partial(self.line, a, distance)]
            steps += [functools.partial(self.across, a, distance - 1)]
        return steps + [functools.partial(self.across, a, self.lengthwise - 1)]

    def from_sibling(self, a):
        def block_in(block, _):
            if self.shared:

                @pl.when(jnp.logical_not(block == self.at.f))
                def _():
                    self.arrived(a, block, self.SIB_RECV)

            else:
                self.arrived(a, block, self.SIB_RECV)
            return 0

        lax.fori_loop(0, self.n, block_in, 0)
        if self.shared:
            for half in (0, 1):
                self.local(a, half).wait()
        else:
            self.local(a, self.at.c).wait()

    def finish(self, a):
        at = self.at

        def block_done(block, _):
            z = block // 4
            if self.shared:
                pl.when(jnp.logical_not(block == at.f))(lambda: self.sent(self.SIB, a, block))
            else:
                self.sent(self.SIB, a, block)

            @pl.when(at.last_bit(block) == at.last)
            def _():
                self.sent(self.LAST, a, block)

                @pl.when((z <= at.z) & (at.z < self.lengthwise - 1))
                def _():
                    self.sent(self.UP, a, block)

                @pl.when((z >= at.z) & (at.z > 0))
                def _():
                    self.sent(self.DOWN, a, block)

            return 0

        lax.fori_loop(0, self.n, block_done, 0)
        self.sent(self.ONE, a, at.f)


class Reduce:
    SIB, SIB_RECV, LOAD, NEAR, NEAR_RECV, UP, UP_RECV, DOWN, DOWN_RECV, END = range(10)

    def __init__(self, plans, ins, totals, scratch, in_place=False):
        count = len(plans)
        self.plans, self.ins, self.totals, self.in_place = plans, ins, totals, in_place
        self.held = [None] * count if in_place else scratch[:count]
        scratch = scratch if in_place else scratch[count:]
        self.landed, self.flow_up, self.flow_down, self.close, self.cross = (
            scratch[k * count : (k + 1) * count] for k in range(5)
        )
        self.sems = scratch[5 * count]
        self.n = plans[0].fsdp
        self.lengthwise = self.n // 4
        self.at = Place()

    @staticmethod
    def scratch(plans, in_place=False):
        n = plans[0].fsdp
        return (
            [pltpu.VMEM((n,) + plan.block, plan.dtype) for plan in plans] * (1 if in_place else 2)
            + [pltpu.VMEM((n // 2,) + plan.block, plan.dtype) for plan in plans] * 3
            + [pltpu.VMEM(plan.block, plan.dtype) for plan in plans]
            + [pltpu.SemaphoreType.DMA((10 * len(plans) * n,))]
        )

    def sem(self, kind, a, block):
        return self.sems.at[(kind * len(self.plans) + a) * self.n + block]

    def slot(self, z, b1, b3):
        return 4 * z + self.at.stride1 * b1 + self.at.stride3 * b3

    def item(self, t):
        length = self.lengthwise
        pair, b3 = t // 2, t % 2
        z = jnp.int32(0)
        for here in range(length):
            order = sorted(range(length), key=lambda there: (-abs(there - here), there))
            for k, there in enumerate(order):
                z = jnp.where((self.at.z == here) & (pair == k), there, z)
        return z, b3

    def hold(self, a, block):
        if self.in_place:
            return self.plans[a].pick(self.ins[a], self.at.c, block)
        return self.held[a].at[block]

    def to_sibling(self, a, block):
        return remote(
            self.plans[a].pick(self.ins[a], 1 - self.at.c, block),
            self.landed[a].at[block],
            self.sem(self.SIB, a, block),
            self.sem(self.SIB_RECV, a, block),
            self.at.sibling,
        )

    def load(self, a, block):
        return pltpu.make_async_copy(
            self.plans[a].pick(self.ins[a], self.at.c, block),
            self.held[a].at[block],
            self.sem(self.LOAD, a, block),
        )

    def to_near(self, a, z, b3):
        return remote(
            self.hold(a, self.slot(z, 1 - self.at.first, b3)),
            self.close[a].at[2 * z + b3],
            self.sem(self.NEAR, a, 2 * z + b3),
            self.sem(self.NEAR_RECV, a, 2 * z + b3),
            self.at.partner1,
        )

    def along(self, up, a, z, b3):
        return remote(
            self.hold(a, self.slot(z, self.at.first, b3)),
            (self.flow_up if up else self.flow_down)[a].at[2 * z + b3],
            self.sem(self.UP if up else self.DOWN, a, 2 * z + b3),
            self.sem(self.UP_RECV if up else self.DOWN_RECV, a, 2 * z + b3),
            (self.at.d, self.at.f + (4 if up else -4)),
        )

    def to_cross(self, a):
        return remote(
            self.hold(a, self.slot(self.at.z, self.at.first, 1 - self.at.last)),
            self.cross[a],
            self.sem(self.END, a, 0),
            self.sem(self.END, a, 1),
            self.at.partner3,
        )

    def rows(self, a, body):
        unit = 16

        def step(i, _):
            body(pl.ds(pl.multiple_of(i * unit, unit), unit))
            return 0

        if self.plans[a].block[0] < unit:
            body(slice(None))
        else:
            lax.fori_loop(0, self.plans[a].block[0] // unit, step, 0)

    def add(self, a, block, sources):
        held = self.hold(a, block)

        def body(where):
            total = held[where, :].astype(F32)
            for ref, at in sources:
                total += ref[at, where, :].astype(F32)
            held[where, :] = total.astype(held.dtype)

        self.rows(a, body)

    def begin(self, a):
        for flip in (1, 0):
            b1 = self.at.first + flip * (1 - 2 * self.at.first)

            def start(t, _, b1=b1):
                z, b3 = self.item(t)
                block = self.slot(z, b1, b3)
                self.to_sibling(a, block).start()
                if not self.in_place:
                    self.load(a, block).start()
                return 0

            lax.fori_loop(0, 2 * self.lengthwise, start, 0)

    def first_leg(self, a, t):
        z, b3 = self.item(t)
        block = self.slot(z, 1 - self.at.first, b3)
        if not self.in_place:
            self.load(a, block).wait()
        self.to_sibling(a, block).wait_recv()
        self.add(a, block, [(self.landed[a], block)])
        self.to_near(a, z, b3).start()

    def middle_leg(self, a, t):
        z, b3 = self.item(t)
        block = self.slot(z, self.at.first, b3)
        flow = 2 * z + b3
        base = [(self.landed[a], block), (self.close[a], flow)]
        if not self.in_place:
            self.load(a, block).wait()
        self.to_sibling(a, block).wait_recv()
        self.to_near(a, z, b3).wait_recv()

        def onward(up):
            incoming = self.at.z > 0 if up else self.at.z < self.lengthwise - 1

            @pl.when(incoming)
            def _():
                self.along(up, a, z, b3).wait_recv()
                flows = self.flow_up if up else self.flow_down
                self.add(a, block, base + [(flows[a], flow)])

            @pl.when(jnp.logical_not(incoming))
            def _():
                self.add(a, block, base)

            self.along(up, a, z, b3).start()

        pl.when(z > self.at.z)(functools.partial(onward, True))
        pl.when(z < self.at.z)(functools.partial(onward, False))

        @pl.when(z == self.at.z)
        def _():
            self.add(a, block, base)

    def own(self, a, b3):
        z = self.at.z
        block = self.slot(z, self.at.first, b3)
        for up in (True, False):

            @pl.when(z > 0 if up else z < self.lengthwise - 1)
            def _(up=up):
                self.along(up, a, z, b3).wait_recv()
                flows = self.flow_up if up else self.flow_down
                self.add(a, block, [(flows[a], 2 * z + b3)])

    def cross_over(self, a):
        self.own(a, 1 - self.at.last)
        self.to_cross(a).start()

    def last_leg(self, a):
        self.own(a, self.at.last)
        self.to_cross(a).wait_recv()
        block = self.slot(self.at.z, self.at.first, self.at.last)

        def body(where):
            total = self.hold(a, block)[where, :].astype(F32) + self.cross[a][where, :].astype(F32)
            self.totals[a][where, :] = total

        self.rows(a, body)

    def finish(self, a):
        def done(t, _):
            z, b3 = self.item(t)
            for b1 in (self.at.first, 1 - self.at.first):
                self.to_sibling(a, self.slot(z, b1, b3)).wait_send()
            self.to_near(a, z, b3).wait_send()
            for up in (True, False):

                @pl.when(z > self.at.z if up else z < self.at.z)
                def _(up=up):
                    self.along(up, a, z, b3).wait_send()

            return 0

        lax.fori_loop(0, 2 * self.lengthwise, done, 0)
        self.to_cross(a).wait_send()


def pair_exchange(plans, totals, outs, sems, at):
    copies = []
    for a, plan in enumerate(plans):
        if not plan.by_rows:
            copies.append(
                remote(
                    totals[a], outs[a].at[at.c], sems.at[2 * a], sems.at[2 * a + 1], at.sibling
                )
            )
    return copies


def reduce_out(plan):
    return jax.ShapeDtypeStruct(plan.block if plan.by_rows else (2,) + plan.block, F32)


def hot_rows(codes):
    count = codes.shape[0]
    slot = lax.rem(lax.broadcasted_iota(jnp.int32, (count, 1), 0), SLOTS)
    lane = lax.broadcasted_iota(jnp.int32, (count, HOT), 1)
    hit = lane == KMAX * CHARS
    for q in range(KMAX):
        moved = codes if q == 0 else pltpu.roll(codes, count - q, 0)
        moved = jnp.where((moved >= 0) & (slot + q < SLOTS), moved + q * CHARS, -1)
        hit = jnp.logical_or(hit, lane == moved)
    return hit.astype(F32).astype(BF)


def conv_forward_block(filters, codes, lengths, refs, out_ref, where):
    table_ref, kernel_ref, width_ref = refs
    words = lengths.shape[0]
    windows = dot(hot_rows(codes), table_ref[...]).astype(BF)
    chunk = 384
    for at in range(0, kernel_ref.shape[1], chunk):
        columns = slice(at, at + chunk)
        activated = jnp.tanh(dot(windows, kernel_ref[:, columns])).reshape(words, SLOTS, chunk)
        counts = jnp.maximum(lengths - width_ref[:, columns] + 1, 1)
        position = lax.broadcasted_iota(jnp.int32, (words, SLOTS, chunk), 1)
        inside = position < counts[:, None, :]
        totals = jnp.sum(jnp.where(inside, jnp.exp(activated), 0.0), axis=1)
        pooled = jnp.log(totals) - jnp.log(counts.astype(F32))
        lane = at + lax.broadcasted_iota(jnp.int32, (words, chunk), 1)
        out_ref[where, columns] = keep_feature(pooled, lane, filters)


def keep_feature(value, lane, filters):
    value = value.astype(BF).astype(F32)
    return jnp.where(lane < filters, value, jnp.where(lane == filters, 1.0, 0.0))


def conv_backward_block(codes, lengths, refs, grad_ref, where, kernel_grad_ref, hot_grad_ref):
    table_ref, kernel_ref, width_ref = refs
    words = lengths.shape[0]
    hot = hot_rows(codes)
    windows = dot(hot, table_ref[...]).astype(BF)
    chunk = 384
    grad_windows = jnp.zeros(windows.shape, F32)
    for at in range(0, kernel_ref.shape[1], chunk):
        columns = slice(at, at + chunk)
        activated = jnp.tanh(dot(windows, kernel_ref[:, columns])).reshape(words, SLOTS, chunk)
        counts = jnp.maximum(lengths - width_ref[:, columns] + 1, 1)
        position = lax.broadcasted_iota(jnp.int32, (words, SLOTS, chunk), 1)
        inside = position < counts[:, None, :]
        weight = jnp.where(inside, jnp.exp(activated), 0.0)
        share = grad_ref[where, columns] / jnp.sum(weight, axis=1)
        grad = (share[:, None, :] * weight * (1.0 - activated * activated)).astype(BF)
        grad = grad.reshape(words * SLOTS, chunk)
        kernel_grad_ref[:, columns] += dot_rows(windows, grad)
        grad_windows += dot_cols(grad, kernel_ref[:, columns])
    hot_grad_ref[...] += dot_rows(hot, grad_windows.astype(BF))


class Dense:
    by_rows = False
    dtype = F32

    def __init__(self, rows, columns, fsdp):
        self.fsdp = fsdp
        self.filled = rows
        self.block = (up_to(-(-rows // fsdp), 8), columns // 2)
        self.shape = (2, fsdp) + self.block

    def pick(self, ref, half, slot):
        return ref.at[half, slot]


WORD_BLOCK = 16


def tail_kernel(plans, blocks, *refs):
    conv, rest = plans[0], plans[1:]
    count = len(plans)
    ins, refs = refs[: count - 1], refs[count - 1 :]
    codes_ref, length_ref, table_ref, kernel_ref, width_ref, grad_ref, mask_ref, fold_ref = refs[:8]
    outs, refs = refs[8 : 8 + count], refs[8 + count :]
    conv_out, rest_outs = outs[0], outs[1:]
    kernel_grad, hot_grad, conv_in, conv_total = refs[:4]
    pair_sems, gather_sems = refs[4:6]
    at = Place()
    totals = [conv_total] + [
        out if plan.by_rows else out.at[at.c] for plan, out in zip(rest, rest_outs)
    ]
    work = Reduce(plans, [conv_in] + list(ins), totals, refs[6:])
    items = 2 * work.lengthwise
    greet(at, work.lengthwise)
    for a in range(1, count):
        work.begin(a)
    kernel_grad[...] = jnp.zeros_like(kernel_grad)
    hot_grad[...] = jnp.zeros_like(hot_grad)
    conv_in[...] = jnp.zeros_like(conv_in)

    def compute(i):
        words = pl.ds(pl.multiple_of(i * WORD_BLOCK, WORD_BLOCK), WORD_BLOCK)
        slots = pl.ds(pl.multiple_of(i * WORD_BLOCK * SLOTS, WORD_BLOCK * SLOTS), WORD_BLOCK * SLOTS)
        conv_backward_block(
            codes_ref[slots, :],
            length_ref[words, :],
            (table_ref, kernel_ref, width_ref),
            grad_ref,
            words,
            kernel_grad,
            hot_grad,
        )

    def leg(body, a):
        def step(t, _):
            body(a, t)
            return 0

        lax.fori_loop(0, items, step, 0)

    for a in range(1, count):
        leg(work.first_leg, a)

    def together(t, _):
        pl.when(t < blocks)(functools.partial(compute, t))

        @pl.when(t < items)
        def _():
            for a in range(1, count):
                work.middle_leg(a, t)

        return 0

    lax.fori_loop(0, max(items, blocks), together, 0)

    wide = kernel_ref.shape[1]
    kernel_grad[:, wide:] = jnp.dot(
        fold_ref[...],
        hot_grad[...] * mask_ref[...],
        precision=lax.Precision.HIGHEST,
        preferred_element_type=F32,
    )
    depth, half = conv.block
    for block in range(conv.filled // depth):
        for h in range(2):
            conv_in[h, block] = kernel_grad[
                block * depth : (block + 1) * depth, h * half : (h + 1) * half
            ]
    work.begin(0)

    leg(work.first_leg, 0)
    leg(work.middle_leg, 0)
    for a in range(count):
        work.cross_over(a)
    work.last_leg(0)
    spread = Gather([conv], [conv_total], [conv_out], gather_sems, False)
    spread.begin(0)
    copies = pair_exchange(rest, totals[1:], rest_outs, pair_sems, at)
    for a in range(1, count):
        work.last_leg(a)
    for copy in copies:
        copy.start()
    for step in spread.steps(0):
        step()
    spread.from_sibling(0)
    spread.finish(0)
    for a in range(count):
        work.finish(a)
    for copy in copies:
        copy.wait()


def tail(plans, grads, conv_inputs, grad, mask, fold, collective_id):
    conv, rest = plans[0], plans[1:]
    words = grad.shape[0]
    return pl.pallas_call(
        functools.partial(tail_kernel, plans, words // WORD_BLOCK),
        out_shape=[jax.ShapeDtypeStruct(conv.shape, F32)] + [reduce_out(plan) for plan in rest],
        in_specs=[pl.BlockSpec(memory_space=pl.ANY)] * len(rest)
        + [pl.BlockSpec(memory_space=pltpu.VMEM)] * 8,
        out_specs=[pl.BlockSpec(memory_space=pltpu.VMEM)] * len(plans),
        scratch_shapes=[
            pltpu.VMEM((conv.filled, 2 * conv.block[1]), F32),
            pltpu.VMEM((HOT, LANE), F32),
            pltpu.VMEM(conv.shape, F32),
            pltpu.VMEM(conv.block, F32),
            pltpu.SemaphoreType.DMA((2 * len(rest),)),
            Gather.semaphores([conv]),
        ]
        + Reduce.scratch(plans),
        compiler_params=pltpu.CompilerParams(
            collective_id=collective_id, has_side_effects=True, vmem_limit_bytes=60 * 2**20
        ),
    )(*grads, *conv_inputs, grad, mask, fold)


def gate_parts(sums):
    parts = [sums[:, :HP]]
    for g in range(1, 4):
        begin = g * H // LANE * LANE
        moved = sums[:, begin : begin + HP + LANE]
        parts.append(pltpu.roll(moved, HP + LANE - (g * H - begin), 1)[:, :HP])
    return parts


def join_gates(parts, columns):
    rows = parts[0].shape[0]
    total = None
    for g, part in enumerate(parts):
        begin = g * H // LANE * LANE
        wide = jnp.concatenate([part, jnp.zeros((rows, LANE), F32)], axis=1)
        if g * H - begin:
            wide = pltpu.roll(wide, g * H - begin, 1)
        pieces = [wide]
        if begin:
            pieces = [jnp.zeros((rows, begin), F32)] + pieces
        if columns - begin - HP - LANE > 0:
            pieces = pieces + [jnp.zeros((rows, columns - begin - HP - LANE), F32)]
        placed = jnp.concatenate(pieces, axis=1)[:, :columns]
        total = placed if total is None else total + placed
    return total


class Line:
    def __init__(self, n):
        self.at = Place()
        self.length = n // 4
        self.me = 2 * self.at.z + self.at.c

    def peer(self, z, other_core=False):
        at = self.at
        return (at.d + (1 - 2 * at.c if other_core else 0), at.f + 4 * (z - at.z))

    def others(self, body):
        def step(z, _):
            pl.when(z != self.at.z)(functools.partial(body, z))
            return 0

        lax.fori_loop(0, self.length, step, 0)

    def chips(self, body):
        def step(z, _):
            body(z)
            return 0

        lax.fori_loop(0, self.length, step, 0)

    def greet(self, across, both_cores):
        barrier = pltpu.get_barrier_semaphore()

        def signal(target):
            pl.semaphore_signal(barrier, inc=1, device_id=target, device_id_type=MESH)

        signal(self.at.sibling)
        count = 1
        if across:
            signal(self.at.partner1)
            signal(self.at.partner3)
            count += 2

        def chip(z):
            signal(self.peer(z))
            if both_cores:
                signal(self.peer(z, True))

        self.others(chip)
        pl.semaphore_wait(barrier, count + (self.length - 1) * (2 if both_cores else 1))


class Semaphores:
    def __init__(self, ref, size):
        self.ref, self.size = ref, size

    def __call__(self, kind, index):
        return self.ref.at[kind * self.size + index]


HIDDEN_CHUNKS = ((0, 48), (48, 96), (96, 128), (128, 144))


def hidden_chunks(rows):
    return [(a, min(b, rows)) for a, b in HIDDEN_CHUNKS if a < rows] + (
        [(HIDDEN_CHUNKS[-1][1], rows)] if rows > HIDDEN_CHUNKS[-1][1] else []
    )


def lstm_forward_kernel(
    batch, n, x_ref, w_ref, h0_ref, c0_ref, keep_ref, extra_ref, own_ref, *refs
):
    hp_ref, cp_ref, i_ref, f_ref, u_ref, o_ref, t_ref, hall_ref, part_ref = refs[:9]
    hidden, soft_sems, hidden_sems = refs[9:]
    line = Line(n)
    at, length = line.at, line.length
    rows_all = x_ref.shape[0]
    chunks = hidden_chunks(rows_all)
    RECV, TO_LINE, TO_NEAR, TO_LAST, LOCAL = range(5)
    sem = Semaphores(soft_sems, n)
    H_RECV, H_LINE, H_SIB = range(3)
    hsem = Semaphores(hidden_sems, 2 * length * len(chunks))

    def column(z):
        return at.f + 4 * (z - at.z)

    def to_line(z):
        return remote(
            own_ref.at[2 * z + at.c],
            part_ref.at[at.f],
            sem(TO_LINE, z),
            sem(RECV, at.f),
            line.peer(z),
        )

    def pass_on(kind, index, slot, target, own=False):
        return remote(
            own_ref.at[line.me] if own else part_ref.at[slot],
            part_ref.at[slot],
            sem(kind, index),
            sem(RECV, slot),
            target,
        )

    def landed(slot):
        pass_on(TO_NEAR, 0, slot, at.partner1).wait_recv()

    local = pltpu.make_async_copy(own_ref.at[line.me], part_ref.at[at.f], sem(LOCAL, 0))

    def event_begin():
        line.others(lambda z: to_line(z).start())
        pass_on(TO_NEAR, at.z, at.f, at.partner1, True).start()
        pass_on(TO_LAST, at.z, at.f, at.partner3, True).start()
        local.start()

    def event_line():
        def chip(z):
            landed(column(z))
            pass_on(TO_NEAR, z, column(z), at.partner1).start()
            pass_on(TO_LAST, z, column(z), at.partner3).start()

        line.others(chip)

    def event_near():
        def chip(z):
            slot = column(z) + at.flip1
            landed(slot)
            pass_on(TO_LAST, length + z, slot, at.partner3).start()

        line.chips(chip)

    def event_end():
        def chip(z):
            landed(column(z) + at.flip3)
            landed(column(z) + at.flip1 + at.flip3)
            pass_on(TO_NEAR, z, column(z), at.partner1).wait_send()
            pass_on(TO_LAST, z, column(z), at.partner3).wait_send()
            pass_on(TO_LAST, length + z, column(z), at.partner3).wait_send()

        line.chips(chip)
        line.others(lambda z: to_line(z).wait_send())
        local.wait()

    def chunk_copy(k, member, kind, index, target):
        begin, end = chunks[k]
        here = hall_ref.at[member, pl.ds(begin, end - begin), :]
        return remote(
            here,
            here,
            hsem(kind, index * len(chunks) + k),
            hsem(H_RECV, member * len(chunks) + k),
            target,
        )

    def chunk_out(k):
        begin, end = chunks[k]
        hall_ref[line.me, begin:end, :] = hidden[begin:end, :].astype(BF)
        line.others(lambda z: chunk_copy(k, line.me, H_LINE, z, line.peer(z)).start())
        chunk_copy(k, line.me, H_SIB, at.z, at.sibling).start()

    def chunk_pass(k):
        def chip(z):
            member = 2 * z + at.c
            chunk_copy(k, member, H_SIB, z, at.sibling).wait_recv()
            chunk_copy(k, member, H_SIB, z, at.sibling).start()

        line.others(chip)

    def chunk_end(k):
        def chip(z):
            chunk_copy(k, 2 * z + 1 - at.c, H_SIB, z, at.sibling).wait_recv()
            chunk_copy(k, 2 * z + at.c, H_SIB, z, at.sibling).wait_send()

        line.chips(chip)
        line.others(lambda z: chunk_copy(k, line.me, H_LINE, z, line.peer(z)).wait_send())

    line.greet(True, False)
    event_begin()
    per_tile = 8 // batch
    tiles = rows_all // 8
    row = lax.broadcasted_iota(jnp.int32, (8, HP), 0)
    lane = lax.broadcasted_iota(jnp.int32, (8, LANE), 1)
    last = HP - LANE

    def tile(step, carried):
        h, c = carried
        rows = pl.ds(pl.multiple_of(step * 8, 8), 8)
        x = x_ref[rows, :]
        keep = keep_ref[rows, :]
        saved = None
        for part in range(per_tile):
            hp, cp = h * keep, c * keep
            sums = x + dot(hp.astype(BF), w_ref[...])
            i, f, u, o = gate_parts(sums)
            i, f, u, o = jax.nn.sigmoid(i), jax.nn.sigmoid(f), jnp.tanh(u), jax.nn.sigmoid(o)
            c = f * cp + i * u
            t = jnp.tanh(c)
            h = (o * t).astype(BF).astype(F32)
            now = (hp, cp, i, f, u, o, t, h)
            if saved is None:
                saved = now
            else:
                saved = tuple(jnp.where(row >= part * batch, b, a) for a, b in zip(saved, now))
            h, c = pltpu.roll(h, batch, 0), pltpu.roll(c, batch, 0)
        for ref, value in zip((hp_ref, cp_ref, i_ref, f_ref, u_ref, o_ref, t_ref), saved):
            ref[rows, :] = value
        hidden[rows, :last] = saved[-1][:, :last]
        hidden[rows, last:] = jnp.where(lane < H - last, saved[-1][:, last:], extra_ref[rows, :])

        pl.when(step == tiles // 3)(event_line)
        pl.when(step == tiles * 2 // 3)(event_near)
        for k, (_, end) in enumerate(chunks):
            pl.when(step == end // 8 - 1)(functools.partial(chunk_out, k))
        return h, c

    lax.fori_loop(0, tiles, tile, (h0_ref[...], c0_ref[...]))
    for k in range(len(chunks)):
        chunk_pass(k)
    event_end()
    for k in range(len(chunks)):
        chunk_end(k)


def lstm_forward(batch, plan, x, recur, h0, c0, keep, extra, own, collective_id):
    rows, n = x.shape[0], plan.fsdp
    members = plan.parts
    chunks = len(hidden_chunks(rows))
    vmem = pl.BlockSpec(memory_space=pltpu.VMEM)
    anywhere = pl.BlockSpec(memory_space=pl.ANY)
    return pl.pallas_call(
        functools.partial(lstm_forward_kernel, batch, n),
        out_shape=[jax.ShapeDtypeStruct((rows, HP), F32)] * 7
        + [
            jax.ShapeDtypeStruct((members, rows, HP), BF),
            jax.ShapeDtypeStruct((n,) + plan.block, BF),
        ],
        in_specs=[vmem] * 6 + [anywhere],
        out_specs=[vmem] * 8 + [anywhere],
        scratch_shapes=[
            pltpu.VMEM((rows, HP), F32),
            pltpu.SemaphoreType.DMA((5 * n,)),
            pltpu.SemaphoreType.DMA((3 * members * chunks,)),
        ],
        compiler_params=pltpu.CompilerParams(
            collective_id=collective_id, has_side_effects=True, vmem_limit_bytes=48 * 2**20
        ),
    )(x, recur, h0, c0, keep, extra, own)


def lstm_backward_kernel(
    batch,
    n,
    dh_ref,
    w_ref,
    keep_ref,
    cp_ref,
    i_ref,
    f_ref,
    u_ref,
    o_ref,
    t_ref,
    grad_ref,
    dz_ref,
    out_ref,
    held_near,
    held_line,
    from_last,
    from_near,
    sems,
):
    line = Line(n)
    at, length = line.at, line.length
    LAST, LAST_RECV, NEAR, NEAR_RECV, TO_LINE, LINE_RECV, SIB, SIB_RECV = range(8)
    sem = Semaphores(sems, 2 * length)

    def slot(z, b1, b3):
        return 4 * z + at.stride1 * b1 + at.stride3 * b3

    def to_last(z, b1):
        return remote(
            grad_ref.at[slot(z, b1, 1 - at.last)],
            from_last.at[2 * z + b1],
            sem(LAST, 2 * z + b1),
            sem(LAST_RECV, 2 * z + b1),
            at.partner3,
        )

    def to_near(z):
        return remote(
            held_near.at[z], from_near.at[z], sem(NEAR, z), sem(NEAR_RECV, z), at.partner1
        )

    def to_line(z):
        return remote(
            held_line.at[z], out_ref.at[line.me], sem(TO_LINE, z), sem(LINE_RECV, at.z), line.peer(z)
        )

    def line_arrived(z):
        here = out_ref.at[2 * z + at.c]
        remote(here, here, sem(TO_LINE, z), sem(LINE_RECV, z), line.peer(z)).wait_recv()

    def to_sibling(z, other=False):
        here = out_ref.at[2 * z + (1 - at.c if other else at.c)]
        return remote(here, here, sem(SIB, z), sem(SIB_RECV, z), at.sibling)

    def event_begin():
        def chip(z):
            to_last(z, 1 - at.first).start()

        line.chips(chip)

        def chip_own(z):
            to_last(z, at.first).start()

        line.chips(chip_own)

    def event_last():
        def chip(z):
            b1 = 1 - at.first
            to_last(z, b1).wait_recv()
            held_near[z] = (
                grad_ref[slot(z, b1, at.last)].astype(F32) + from_last[2 * z + b1].astype(F32)
            ).astype(BF)
            to_near(z).start()

        line.chips(chip)

    def event_near():
        def chip(z):
            to_last(z, at.first).wait_recv()
            to_near(z).wait_recv()
            total = (
                grad_ref[slot(z, at.first, at.last)].astype(F32)
                + from_last[2 * z + at.first].astype(F32)
                + from_near[z].astype(F32)
            ).astype(BF)
            held_line[z] = total

            @pl.when(z == at.z)
            def _():
                out_ref[line.me] = total

            @pl.when(z != at.z)
            def _():
                to_line(z).start()

        line.chips(chip)
        to_sibling(at.z).start()

    def event_line():
        def chip(z):
            line_arrived(z)
            to_sibling(z).start()

        line.others(chip)

    def event_end():
        def chip(z):
            to_sibling(z, True).wait_recv()
            to_sibling(z).wait_send()
            to_near(z).wait_send()
            to_last(z, 0).wait_send()
            to_last(z, 1).wait_send()

        line.chips(chip)
        line.others(lambda z: to_line(z).wait_send())

    line.greet(True, False)
    event_begin()
    per_tile = 8 // batch
    tiles = dh_ref.shape[0] // 8
    row = lax.broadcasted_iota(jnp.int32, (8, dz_ref.shape[1]), 0)
    real = lax.broadcasted_iota(jnp.int32, (8, HP), 1) < H

    def tile(step, carried):
        dh_carry, dc_carry = carried
        rows = pl.ds(pl.multiple_of((tiles - 1 - step) * 8, 8), 8)
        keep = keep_ref[rows, :]
        i, f, u, o, t = (r[rows, :] for r in (i_ref, f_ref, u_ref, o_ref, t_ref))
        soft = dh_ref[rows, :]
        to_c = o * (1.0 - t * t)
        to_i = jnp.where(real, u * i * (1.0 - i), 0.0)
        to_f = jnp.where(real, cp_ref[rows, :] * f * (1.0 - f), 0.0)
        to_u = jnp.where(real, i * (1.0 - u * u), 0.0)
        to_o = jnp.where(real, t * o * (1.0 - o), 0.0)
        back = f * keep
        saved = None
        for part in reversed(range(per_tile)):
            dh = jnp.where(real, soft + dh_carry, 0.0)
            dc = dc_carry + dh * to_c
            dz = join_gates([dc * to_i, dc * to_f, dc * to_u, dh * to_o], dz_ref.shape[1])
            saved = dz if saved is None else jnp.where(row >= (part + 1) * batch, saved, dz)
            dh_carry = dot(dz.astype(BF), w_ref[...]) * keep
            dc_carry = dc * back
            dh_carry, dc_carry = (
                pltpu.roll(dh_carry, 8 - batch, 0),
                pltpu.roll(dc_carry, 8 - batch, 0),
            )
        dz_ref[rows, :] = saved
        pl.when(step == tiles // 3)(event_last)
        pl.when(step == tiles * 2 // 3)(event_near)
        pl.when(step == tiles - 2)(event_line)
        return dh_carry, dc_carry

    zero = jnp.zeros((8, HP), F32)
    lax.fori_loop(0, tiles, tile, (zero, zero))
    event_end()


def lstm_backward(batch, plan, columns, dh, recur_t, keep, states, grad, collective_id):
    rows, n = dh.shape[0], plan.fsdp
    length = n // 4
    vmem = pl.BlockSpec(memory_space=pltpu.VMEM)
    return pl.pallas_call(
        functools.partial(lstm_backward_kernel, batch, n),
        out_shape=[
            jax.ShapeDtypeStruct((rows, columns), F32),
            jax.ShapeDtypeStruct((plan.parts,) + plan.block, BF),
        ],
        in_specs=[vmem] * 10,
        out_specs=[vmem] * 2,
        scratch_shapes=[
            pltpu.VMEM((length,) + plan.block, BF),
            pltpu.VMEM((length,) + plan.block, BF),
            pltpu.VMEM((2 * length,) + plan.block, BF),
            pltpu.VMEM((length,) + plan.block, BF),
            pltpu.SemaphoreType.DMA((8 * 2 * length,)),
        ],
        compiler_params=pltpu.CompilerParams(
            collective_id=collective_id, has_side_effects=True, vmem_limit_bytes=48 * 2**20
        ),
    )(dh, recur_t, keep, *states, grad)


def turned(value, lanes):
    rows = value.shape[0]
    if rows < lanes:
        value = jnp.concatenate([value, jnp.zeros((lanes - rows, value.shape[1]), F32)], axis=0)
    return value.T


def copy_windows(plan, source, target, base, found, place):
    target[...] = jnp.zeros_like(target)
    for o, first, last in found:
        start, to = plan.starts[o] - base, place(o) * plan.rows
        target[to + first : to + last, :] = source[start + first : start + last, :]


def add_windows(plan, source, target, base, found, begin):
    for o, first, last in found:
        start, at = plan.starts[o] - base, o * plan.rows - begin
        target[start + first : start + last, :] += source[at + first : at + last, :]


def matrices_of(plan, filters):
    result = []
    for m in range(4):
        base = m * (filters + 1)
        found = plan.meeting(base, base + filters + 1)
        result.append((base, found, found[0][0] * plan.rows, (found[-1][0] + 1) * plan.rows))
    return result


def head_kernel(plans, filters, blocks, *refs):
    highway, lstm = plans
    owns = refs[:2]
    codes_ref, length_ref, table_ref, kernel_ref, width_ref = refs[2:7]
    highway_out, lstm_out, x_ref, recur_ref = refs[7:11]
    features, trans_refs, gate_refs = refs[11:14], refs[14:16], refs[16:18]
    highway_w, lstm_w, turned_ref, wide, recur_sum, gather_sems, out_sems = refs[18:]
    rows, fp = features[0].shape
    words = turned_ref.shape[1]
    work = Gather(plans, owns, (highway_w, lstm_w), gather_sems, True)
    length = work.lengthwise
    greet(work.at, length)

    def conv(begin, end):
        def block(i, _):
            at = pl.ds(pl.multiple_of(i * WORD_BLOCK, WORD_BLOCK), WORD_BLOCK)
            slots = pl.ds(
                pl.multiple_of(i * WORD_BLOCK * SLOTS, WORD_BLOCK * SLOTS), WORD_BLOCK * SLOTS
            )
            conv_forward_block(
                filters,
                codes_ref[slots, :],
                length_ref[at, :],
                (table_ref, kernel_ref, width_ref),
                features[0],
                at,
            )
            return 0

        lax.fori_loop(begin, end, block, 0)

    chunk = 384

    def layer_sum(m, wide=wide):
        base, found, begin, end = matrices[m]
        copy_windows(
            highway, turned_ref, wide.at[: end - begin], base, found, lambda o: o - found[0][0]
        )
        target = (trans_refs if m % 2 == 0 else gate_refs)[m // 2]

        def columns(j, _):
            where = pl.ds(pl.multiple_of(j * chunk, chunk), chunk)
            left = wide[: end - begin, :].astype(BF)
            target[:, where] = dot_rows(left, highway_w[begin:end, where])[:rows]
            return 0

        lax.fori_loop(0, fp // chunk, columns, 0)

    def layer(l):
        turned_ref[:fp, :] = turned(features[l][...], words)
        layer_sum(2 * l)

    def layer_end(l):
        layer_sum(2 * l + 1)
        trans, gate = trans_refs[l][...], jax.nn.sigmoid(gate_refs[l][...])
        gate_refs[l][...] = gate
        value = gate * trans * jax.nn.sigmoid(trans) + (1.0 - gate) * features[l][...]
        lane = lax.broadcasted_iota(jnp.int32, (rows, fp), 1)
        features[l + 1][...] = keep_feature(value, lane, filters)

    matrices = matrices_of(highway, filters)
    of_highway, of_lstm = work.steps(0), work.steps(1)
    count = len(of_highway)
    work.begin(0)
    third = -(-blocks // 3)
    for k in range(3):
        conv(k * third, min((k + 1) * third, blocks))
        if k < count:
            of_highway[k]()
    late = count - 4
    for k in range(3, count):
        if k == max(late, 3):
            work.begin(1)
        of_highway[k]()
    work.from_sibling(0)
    out_copies = [
        pltpu.make_async_copy(highway_w, highway_out, out_sems.at[0]),
        pltpu.make_async_copy(lstm_w, lstm_out, out_sems.at[1]),
    ]
    out_copies[0].start()
    of_lstm[0]()
    compute = [
        functools.partial(layer, 0),
        functools.partial(layer_end, 0),
        functools.partial(layer, 1),
        functools.partial(layer_end, 1),
    ]
    for k in range(1, max(count, 5)):
        if k <= 4:
            compute[k - 1]()
        if k < count:
            of_lstm[k]()

    turned_ref[...] = jnp.zeros_like(turned_ref)
    sub = lax.broadcasted_iota(jnp.int32, (fp, words), 0)
    turned_ref[:fp, :] = jnp.where(sub < filters, turned(features[2][...], words), 0.0)
    turned_ref[lstm.used - 1 : lstm.used, :] = jnp.ones((1, words), F32)
    wide = wide.at[: lstm.total]
    copy_windows(lstm, turned_ref, wide, 0, lstm.meeting(0, lstm.used), lambda o: o)
    work.from_sibling(1)
    out_copies[1].start()
    left = wide[...].astype(BF)
    half = lstm.block[1]
    for h in range(2):
        x_ref[:, h * half : (h + 1) * half] = dot_rows(left, lstm_w[h])[:rows]

    recur_sum[...] = jnp.zeros_like(recur_sum)
    depth = lstm.block[0]
    for h in range(2):
        for slot in sorted({o // lstm.dp for o, _, _ in lstm.meeting(filters, filters + H)}):
            piece = lstm_w[h, slot * depth : (slot + 1) * depth, :].astype(F32)
            for o, first, last in lstm.meeting(filters, filters + H):
                if o // lstm.dp == slot:
                    start, at = lstm.starts[o] - filters, (o % lstm.dp) * lstm.rows
                    recur_sum[start + first : start + last, h * half : (h + 1) * half] += piece[
                        at + first : at + last
                    ]
    recur_ref[...] = recur_sum[...].astype(BF)
    for a in range(2):
        work.finish(a)
    for copy in out_copies:
        copy.wait()


def head(plans, filters, own, conv_inputs, rows, fp, collective_id):
    highway, lstm = plans
    words = up_to(rows, 2 * LANE)
    vmem = pl.BlockSpec(memory_space=pltpu.VMEM)
    anywhere = pl.BlockSpec(memory_space=pl.ANY)
    feature = jax.ShapeDtypeStruct((rows, fp), F32)
    matrices = matrices_of(highway, filters)
    longest = max([lstm.total] + [end - begin for _, _, begin, end in matrices])
    return pl.pallas_call(
        functools.partial(head_kernel, plans, filters, rows // WORD_BLOCK),
        out_shape=[
            jax.ShapeDtypeStruct(highway.shape, BF),
            jax.ShapeDtypeStruct(lstm.shape, BF),
            jax.ShapeDtypeStruct((rows, lstm.columns), F32),
            jax.ShapeDtypeStruct((HP, lstm.columns), BF),
        ]
        + [feature] * 7,
        in_specs=[anywhere] * 2 + [vmem] * 5,
        out_specs=[anywhere] * 2 + [vmem] * 9,
        scratch_shapes=[
            pltpu.VMEM(highway.shape, BF),
            pltpu.VMEM(lstm.shape, BF),
            pltpu.VMEM((up_to(max(lstm.used, fp), LANE), words), F32),
            pltpu.VMEM((longest, words), F32),
            pltpu.VMEM((HP, lstm.columns), F32),
            Gather.semaphores(plans),
            pltpu.SemaphoreType.DMA((2,)),
        ],
        compiler_params=pltpu.CompilerParams(
            collective_id=collective_id, has_side_effects=True, vmem_limit_bytes=60 * 2**20
        ),
    )(*own, *conv_inputs)


def highway_backward_kernel(plans, filters, *refs):
    highway, lstm = plans
    dz_ref, hp_ref = refs[:2]
    features, trans_refs, gate_refs = refs[2:5], refs[5:7], refs[7:9]
    highway_all, lstm_all = refs[9:11]
    grad_out, feature_grad, total_out = refs[11:14]
    lstm_grad, highway_w, lstm_w, turned_ref, wide, back, dz, pairs = refs[14:22]
    staged, carry, load_sems, pair_sems, out_sems = refs[22:27]
    rows, fp = features[0].shape
    words = turned_ref.shape[1]
    at = Place()
    work = Reduce([lstm], [lstm_grad], [total_out.at[at.c]], refs[27:], True)
    length, items = work.lengthwise, 2 * work.lengthwise
    matrices = matrices_of(highway, filters)
    half = lstm.block[1]
    of_input = lstm.meeting(0, filters)
    input_rows = lstm_w.shape[0]

    def layer_rows(l):
        begin, end = matrices[2 * l][2], matrices[2 * l + 1][3]
        return begin, end

    def load_layer(l):
        begin, end = layer_rows(l)
        return pltpu.make_async_copy(
            highway_all.at[pl.ds(begin, end - begin)],
            highway_w.at[pl.ds(0, end - begin)],
            load_sems.at[l],
        )

    def load_lstm(h):
        return pltpu.make_async_copy(
            lstm_all.at[h, pl.ds(0, input_rows)], lstm_w, load_sems.at[2 + h]
        )

    load_layer(1).start()
    load_lstm(0).start()
    greet(at, length)

    dz[...] = jnp.zeros_like(dz)
    dz[:rows, :] = dz_ref[...].astype(BF)
    lane = lax.broadcasted_iota(jnp.int32, (rows, HP), 1)
    hidden = jnp.where(lane < H, hp_ref[...], jnp.where(lane == H, 1.0, 0.0))
    sub = lax.broadcasted_iota(jnp.int32, (fp, words), 0)
    turned_ref[:fp, :] = jnp.where(sub < filters, turned(features[2][...], words), 0.0)
    kept = up_to(H + 1, 8)
    turned_ref[filters : filters + kept, :] = turned(hidden, words)[:kept]
    copy_windows(
        lstm,
        turned_ref,
        wide.at[: lstm.total],
        0,
        lstm.meeting(0, lstm.used),
        lambda o: lstm.position[o],
    )
    unit = lstm.total // (2 * length)

    def lstm_weights(i, _):
        where = pl.ds(pl.multiple_of(i * unit, unit), unit)
        left = wide[where, :].astype(BF)
        for h in range(2):
            lstm_grad[h, where, :] = dot(left, dz[:, h * half : (h + 1) * half]).astype(BF)
        return 0

    lax.fori_loop(0, 2 * length, lstm_weights, 0)
    work.begin(0)

    lane = lax.broadcasted_iota(jnp.int32, (rows, fp), 1)
    back[...] = jnp.zeros_like(back)
    for h in range(2):
        load_lstm(h).wait()
        wide[:input_rows, :] = dot_cols(lstm_w[...], dz[:, h * half : (h + 1) * half])
        if h == 0:
            load_lstm(1).start()
        add_windows(lstm, wide, back, 0, of_input, 0)
    grad = jnp.where(lane < filters, back[...].T[:rows], 0.0)

    def legs(body, begin, end):
        def step(t, _):
            body(0, t)
            return 0

        lax.fori_loop(begin, end, step, 0)

    legs(work.first_leg, 0, items)
    spots = 8

    def middle(k):
        legs(work.middle_leg, k * items // spots, (k + 1) * items // spots)

    pairs[...] = jnp.zeros_like(pairs)
    for l in (1, 0):
        trans, gate = trans_refs[l][...], gate_refs[l][...]
        sig = jax.nn.sigmoid(trans)
        pairs[2 * l, :rows, :] = (grad * gate * sig * (1.0 + trans * (1.0 - sig))).astype(BF)
        pairs[2 * l + 1, :rows, :] = (
            grad * (trans * sig - features[l][...]) * gate * (1.0 - gate)
        ).astype(BF)
        load_layer(l).wait()
        back[...] = jnp.zeros_like(back)
        begin = layer_rows(l)[0]
        for m in (2 * l, 2 * l + 1):
            base, found, low, high = matrices[m]
            result = dot_cols(highway_w[low - begin : high - begin, :], pairs[m])
            add_windows(highway, result, back, base, found, low)
            if m % 2 and l:
                load_layer(0).start()
            middle(2 * (1 - l) + m % 2)
        grad = grad * (1.0 - gate) + back[...].T[:rows]
        grad = jnp.where(lane < filters, grad, 0.0)
    feature_grad[...] = grad

    chunk = 384
    size = highway.rows
    pending, shared = [], None
    empty = [o for o in range(len(highway.starts)) if all(o != f[0] for m in matrices for f in m[1])]
    for m in range(4):
        base, found, low, high = matrices[m]
        if m % 2 == 0:
            turned_ref[:fp, :] = turned(features[m // 2][...], words)
        copy_windows(
            highway, turned_ref, wide.at[: high - low], base, found, lambda o: o - found[0][0]
        )
        for copy in pending:
            copy.wait()
        adds = shared == found[0][0]
        shares = m < 3 and matrices[m + 1][1][0][0] == found[-1][0]
        count = len(found)

        def columns(j, _):
            where = pl.ds(pl.multiple_of(j * chunk, chunk), chunk)
            result = dot(wide[: high - low, :].astype(BF), pairs[m, :, where])
            if adds:
                first = result[:size] + carry[:, where]
                staged[:size, where] = first.astype(BF)
                staged[size : high - low, where] = result[size:].astype(BF)
            else:
                staged[: high - low, where] = result.astype(BF)
            if shares:
                carry[:, where] = result[(count - 1) * size :]
            return 0

        lax.fori_loop(0, fp // chunk, columns, 0)
        shared = found[-1][0] if shares else None
        sent = found[:-1] if shares else found
        pending = [
            pltpu.make_async_copy(
                staged.at[pl.ds(k * size, size)],
                grad_out.at[pl.ds(highway.position[o] * size, size)],
                out_sems.at[k],
            )
            for k, (o, _, _) in enumerate(sent)
        ]
        for copy in pending:
            copy.start()
        middle(4 + m)
    for copy in pending:
        copy.wait()
    if empty:
        staged[:size, :] = jnp.zeros((size, fp), BF)
        for o in empty:
            copy = pltpu.make_async_copy(
                staged.at[pl.ds(0, size)],
                grad_out.at[pl.ds(highway.position[o] * size, size)],
                out_sems.at[0],
            )
            copy.start()
            copy.wait()
    work.cross_over(0)
    work.last_leg(0)
    copy = remote(
        total_out.at[at.c], total_out.at[at.c], pair_sems.at[0], pair_sems.at[1], at.sibling
    )
    copy.start()
    work.finish(0)
    copy.wait()


def highway_backward(plans, filters, dz, hp, features, trans, gates, everywhere, collective_id):
    highway, lstm = plans
    rows, fp = features[0].shape
    words = up_to(rows, 2 * LANE)
    vmem = pl.BlockSpec(memory_space=pltpu.VMEM)
    anywhere = pl.BlockSpec(memory_space=pl.ANY)
    matrices = matrices_of(highway, filters)
    longest = max([lstm.total] + [end - begin for _, _, begin, end in matrices])
    layer = max(matrices[2 * l + 1][3] - matrices[2 * l][2] for l in range(2))
    input_rows = up_to((lstm.meeting(0, filters)[-1][0] + 1) * lstm.rows, 16)
    return pl.pallas_call(
        functools.partial(highway_backward_kernel, plans, filters),
        out_shape=[
            jax.ShapeDtypeStruct(highway.shape, BF),
            jax.ShapeDtypeStruct((rows, fp), F32),
            jax.ShapeDtypeStruct((2,) + lstm.block, F32),
        ],
        in_specs=[vmem] * 9 + [anywhere] * 2,
        out_specs=[anywhere] + [vmem] * 2,
        scratch_shapes=[
            pltpu.VMEM(lstm.shape, BF),
            pltpu.VMEM((layer, highway.columns), BF),
            pltpu.VMEM((input_rows, lstm.block[1]), BF),
            pltpu.VMEM((up_to(max(lstm.used + 8, fp), LANE), words), F32),
            pltpu.VMEM((longest, words), F32),
            pltpu.VMEM((fp, words), F32),
            pltpu.VMEM((words, lstm.columns), BF),
            pltpu.VMEM((4, words, fp), BF),
            pltpu.VMEM((max(end - begin for _, _, begin, end in matrices), fp), BF),
            pltpu.VMEM((highway.rows, fp), F32),
            pltpu.SemaphoreType.DMA((4,)),
            pltpu.SemaphoreType.DMA((2,)),
            pltpu.SemaphoreType.DMA((max(len(found) for _, found, _, _ in matrices),)),
        ]
        + Reduce.scratch([lstm], True),
        compiler_params=pltpu.CompilerParams(
            collective_id=collective_id, has_side_effects=True, vmem_limit_bytes=62 * 2**20
        ),
    )(dz, hp, *features, *trans, *gates, *everywhere)


def softmax_kernel(
    vocab,
    n,
    h_ref,
    w_ref,
    map_ref,
    map_back_ref,
    loss_ref,
    grad_h_ref,
    grad_w_ref,
    spread_back,
    logits,
    grads,
    stats,
    for_sibling,
    from_sibling,
    for_line,
    from_line,
    own_total,
    sems,
):
    line = Line(n)
    at, length, me = line.at, line.length, line.me
    members, rows, _ = h_ref.shape
    width = w_ref.shape[-1]
    w = w_ref[...].reshape(-1, width)
    STAT, STAT_RECV, SIB, SIB_RECV, TO_LINE, LINE_RECV = range(6)
    sem = Semaphores(sems, members)
    column = me * width + lax.broadcasted_iota(jnp.int32, (rows, width), 1)
    real_column = column.astype(F32)
    words = up_to(rows, LANE)
    lane = lax.broadcasted_iota(jnp.int32, (rows, LANE), 1)
    aside = HP - LANE

    def pieces(b):
        tail = h_ref[b, :, aside:].astype(F32)
        first = H + 1 - aside
        target = tail[:, first : first + 1] * 256.0 + tail[:, first + 1 : first + 2]
        scale = (
            tail[:, first + 2 : first + 3]
            + tail[:, first + 3 : first + 4]
            + tail[:, first + 4 : first + 5]
        )
        return target, scale

    line.greet(False, True)

    def forward(b, _):
        h = h_ref[b]
        wide = dot(h, map_ref[...]).astype(BF)
        spread_back[b] = dot(h, map_back_ref[...]).astype(BF)
        now = jnp.where(column < vocab, dot(wide, w), -1e30)
        logits[b] = now
        target, _ = pieces(b)
        top = jnp.max(now, axis=1, keepdims=True)
        log_sum = top + jnp.log(jnp.sum(jnp.exp(now - top), axis=1, keepdims=True))
        picked = jnp.sum(jnp.where(real_column == target, now, 0.0), axis=1, keepdims=True)
        both = jnp.where(lane == 0, log_sum, jnp.where(lane == 1, picked, 0.0))
        both = jnp.concatenate([both, jnp.zeros((words - rows, LANE), F32)], axis=0).T
        stats[me, 0, pl.ds(b, 1), :] = both[0:1, :]
        stats[me, 1, pl.ds(b, 1), :] = both[1:2, :]
        return 0

    lax.fori_loop(0, members, forward, 0)

    def stat(member, target):
        here = stats.at[member]
        return remote(here, here, sem(STAT, member), sem(STAT_RECV, member), target)

    def stat_out(z):
        return [
            remote(
                stats.at[me], stats.at[me], sem(STAT, 2 * z + core), sem(STAT_RECV, me), target
            )
            for core, target in ((at.c, line.peer(z)), (1 - at.c, line.peer(z, True)))
        ]

    def send_stats(z):
        for copy in stat_out(z):
            copy.start()

    line.others(send_stats)
    to_pair = remote(
        stats.at[me], stats.at[me], sem(STAT, 2 * at.z + 1 - at.c), sem(STAT_RECV, me), at.sibling
    )
    to_pair.start()

    def stats_in(z):
        for core in (at.c, 1 - at.c):
            stat(2 * z + core, at.sibling).wait_recv()

    line.others(stats_in)
    stat(2 * at.z + 1 - at.c, at.sibling).wait_recv()
    top = stats[0, 0]
    for q in range(1, members):
        top = jnp.maximum(top, stats[q, 0])
    total = jnp.zeros_like(top)
    picked = jnp.zeros_like(top)
    for q in range(members):
        total += jnp.exp(stats[q, 0] - top)
        picked += stats[q, 1]
    log_total = top + jnp.log(total)
    loss_ref[...] = log_total - picked
    log_columns = jnp.concatenate(
        [log_total, jnp.zeros((LANE - members, words), F32)], axis=0
    ).T[:rows]

    def to_sibling(z):
        return remote(
            for_sibling.at[z], from_sibling.at[z], sem(SIB, z), sem(SIB_RECV, z), at.sibling
        )

    def to_line(z):
        return remote(
            for_line.at[z], from_line.at[at.z], sem(TO_LINE, z), sem(LINE_RECV, at.z), line.peer(z)
        )

    def backward(k, _):
        z = lax.rem(k, length)
        mine = k >= length
        b = 2 * z + jnp.where(mine, at.c, 1 - at.c)
        target, scale = pieces(b)
        log_sum = jnp.sum(jnp.where(lane == b, log_columns, 0.0), axis=1, keepdims=True)
        share = jnp.exp(logits[b] - log_sum)
        grad = ((share - (real_column == target).astype(F32)) * scale).astype(BF)
        grads[b] = grad
        back = dot_cols(grad, w)

        @pl.when(jnp.logical_not(mine))
        def _():
            for_sibling[z] = back.astype(BF)
            to_sibling(z).start()

        @pl.when(mine)
        def _():
            to_sibling(z).wait_recv()
            total = back + from_sibling[z].astype(F32)

            @pl.when(z == at.z)
            def _():
                own_total[...] = total

            @pl.when(z != at.z)
            def _():
                for_line[z] = total.astype(BF)
                to_line(z).start()

        return 0

    lax.fori_loop(0, 2 * length, backward, 0)

    depth = map_ref.shape[1]
    unit = 256
    everything = grads[...].reshape(members * rows, width)

    def weight_grad(m, _):
        left = spread_back[:, :, pl.ds(pl.multiple_of(m * unit, unit), unit)]
        result = dot_rows(left.reshape(members * rows, unit), everything).astype(BF)
        grad_w_ref[pl.ds(m * unit, unit), :] = result
        return 0

    lax.fori_loop(0, depth // unit, weight_grad, 0)

    def arrived(z):
        remote(
            from_line.at[z], from_line.at[z], sem(TO_LINE, z), sem(LINE_RECV, z), line.peer(z)
        ).wait_recv()
        own_total[...] += from_line[z].astype(F32)

    line.others(arrived)
    spread_grad = own_total[...]
    high = spread_grad.astype(BF)
    low = (spread_grad - high.astype(F32)).astype(BF)
    grad_h_ref[...] = dot_cols(high, map_ref[...]) + dot_cols(low, map_ref[...])

    def finish(z):
        for copy in stat_out(z):
            copy.wait_send()
        to_line(z).wait_send()

    line.others(finish)
    line.chips(lambda z: to_sibling(z).wait_send())
    to_pair.wait_send()


def word_softmax(plan, h, weights, mapping, mapping_back, collective_id):
    members, rows, depth = h.shape
    n = plan.fsdp
    spread = mapping.shape[1]
    per_slot, width = plan.block
    words = up_to(rows, LANE)
    length = members // 2
    vmem = pl.BlockSpec(memory_space=pltpu.VMEM)
    loss, grad_h, grad_w = pl.pallas_call(
        functools.partial(softmax_kernel, plan.width, n),
        out_shape=[
            jax.ShapeDtypeStruct((members, words), F32),
            jax.ShapeDtypeStruct((rows, depth), F32),
            jax.ShapeDtypeStruct((spread, width), BF),
        ],
        in_specs=[vmem] * 4,
        out_specs=[vmem] * 3,
        scratch_shapes=[
            pltpu.VMEM((members, rows, spread), BF),
            pltpu.VMEM((members, rows, width), F32),
            pltpu.VMEM((members, rows, width), BF),
            pltpu.VMEM((members, 2, members, words), F32),
            pltpu.VMEM((length, rows, spread), BF),
            pltpu.VMEM((length, rows, spread), BF),
            pltpu.VMEM((length, rows, spread), BF),
            pltpu.VMEM((length, rows, spread), BF),
            pltpu.VMEM((rows, spread), F32),
            pltpu.SemaphoreType.DMA((6 * members,)),
        ],
        compiler_params=pltpu.CompilerParams(
            collective_id=collective_id, has_side_effects=True, vmem_limit_bytes=62 * 2**20
        ),
    )(h, weights, mapping, mapping_back)
    return loss, grad_h, grad_w.reshape((n,) + plan.block)


def shards(
    fsdp_count,
    dp_count,
    chars,
    lengths,
    targets,
    resets,
    init_state,
    window_grad,
    char_table,
    conv_weight,
    conv_bias,
    highway_flat,
    lstm_flat,
    soft_flat,
):
    micro_count, streams, step_count, letters = chars.shape
    char_count, embed_dim = char_table.shape
    filters = conv_weight.shape[1]
    batch = micro_count * streams
    words = step_count * batch
    rows = up_to(words, 16)
    fp = up_to(filters + 1, LANE)
    dp_at, fsdp_at = lax.axis_index("dp"), lax.axis_index("fsdp")
    highway = Windows(
        highway_flat.shape[0] * fsdp_count, filters, 4 * (filters + 1), fsdp_count, dp_count, True
    )
    lstm = Windows(
        lstm_flat.shape[0] * fsdp_count, 4 * H, filters + H + 1, fsdp_count, dp_count, False
    )
    soft = Windows(
        soft_flat.shape[0] * fsdp_count, V, H + 1, fsdp_count, dp_count, False, fsdp_count // 2
    )
    member = 2 * (fsdp_at // 4) + lax.rem(dp_at, 2)

    def by_step(array):
        return jnp.moveaxis(array.reshape((batch, step_count) + array.shape[3:]), 1, 0).reshape(
            (words,) + array.shape[3:]
        )

    def pad_rows(array, value=0):
        return jnp.pad(
            array,
            [(0, rows - words)] + [(0, 0)] * (array.ndim - 1),
            constant_values=value,
        )

    word_chars = pad_rows(by_step(chars))
    word_lengths = pad_rows(by_step(lengths))[:, None]
    position = jnp.arange(letters, dtype=jnp.int32)[None, :]
    codes = jnp.where(position < word_lengths, word_chars, -1)
    codes = jnp.pad(codes, ((0, 0), (0, SLOTS - letters)), constant_values=-1)
    codes = codes.reshape(rows * SLOTS, 1)
    column = np.arange(fp)
    widths = np.ones((fp,), np.int32)
    for cut_at in FILTER_CUTS:
        widths = widths + ((column >= filters * cut_at // 22) & (column < filters))
    widths = widths.astype(np.int32)
    kernel_mask = jnp.asarray(
        np.arange(KMAX * embed_dim)[:, None] // embed_dim < widths[None, :filters]
    )
    ones_row = KMAX * embed_dim
    kernel = jnp.concatenate(
        [jnp.where(kernel_mask, conv_weight, jnp.zeros_like(conv_weight)), conv_bias[None, :]], axis=0
    )
    kernel = jnp.pad(kernel, ((0, LANE - ones_row - 1), (0, fp - filters)))
    spread_table = jnp.concatenate(
        [
            jnp.pad(char_table, ((0, 0), (q * embed_dim, LANE - (q + 1) * embed_dim)))
            for q in range(KMAX)
        ]
        + [jnp.zeros((1, LANE), BF).at[0, ones_row].set(1.0)],
        axis=0,
    )
    spread_table = jnp.pad(spread_table, ((0, HOT - KMAX * char_count - 1), (0, 0)))
    conv_inputs = (codes, word_lengths, spread_table, kernel, jnp.asarray(widths)[None, :])

    highway_all, lstm_all, from_input, recur, *kept = head(
        [highway, lstm],
        filters,
        [highway.from_flat(highway_flat, fsdp_at), lstm.from_flat(lstm_flat, fsdp_at)],
        conv_inputs,
        rows,
        fp,
        1,
    )
    features, trans, gates = kept[:3], kept[3:5], kept[5:7]

    soft_own = soft.from_flat(soft_flat, fsdp_at)
    recur_t = recur.T
    keep = pad_rows(by_step(1 - resets).astype(F32))[:, None]
    start = init_state.reshape(batch, 2, H)
    start = jnp.pad(start, ((0, 8 - batch), (0, 0), (0, HP - H)))
    row_scale = jnp.broadcast_to(
        window_grad.reshape(1, batch) / step_count, (step_count, batch)
    ).reshape(words)
    goal = by_step(targets)
    scale_high = lax.reduce_precision(row_scale, 8, 7)
    scale_mid = lax.reduce_precision(row_scale - scale_high, 8, 7)
    extra = jnp.stack(
        [
            jnp.ones((words,), F32),
            (goal // 256).astype(F32),
            (goal % 256).astype(F32),
            scale_high,
            scale_mid,
            row_scale - scale_high - scale_mid,
        ],
        axis=1,
    )
    aside = H - (HP - LANE)
    extra = jnp.pad(extra, ((0, rows - words), (aside, LANE - aside - extra.shape[1])))
    *states, hidden_all, soft_part = lstm_forward(
        batch,
        soft,
        from_input,
        recur,
        start[:, 0].astype(BF).astype(F32),
        start[:, 1],
        keep,
        extra,
        soft_own,
        4,
    )
    hp = states[0]

    word_loss, grad_hidden, soft_grad = word_softmax(
        soft,
        hidden_all,
        soft_part,
        one_hot_map(HP, soft.gathered),
        one_hot_map(HP, soft.reduced),
        5,
    )
    word_loss = lax.dynamic_index_in_dim(word_loss, member, 0, keepdims=False)
    window_loss = jnp.mean(word_loss[:words].reshape(step_count, batch), axis=0).reshape(
        micro_count, streams
    )

    dz, soft_part = lstm_backward(
        batch, soft, lstm.columns, grad_hidden, recur_t, keep, states[1:], soft_grad, 6
    )
    highway_grad, grad, lstm_part = highway_backward(
        [highway, lstm], filters, dz, hp, features, trans, gates, (highway_all, lstm_all), 7
    )

    hot_row, hot_lane = np.arange(HOT), np.arange(LANE)
    hot_mask = (hot_row[:, None] // char_count == hot_lane[None, :] // embed_dim) & (
        hot_row[:, None] < KMAX * char_count
    )
    hot_fold = (hot_row[None, :] % char_count == np.arange(LANE)[:, None]) & (
        hot_row[None, :] < KMAX * char_count
    )
    conv = Dense(LANE, up_to(fp + LANE, 2 * LANE), fsdp_count)
    conv_grad, highway_part = tail(
        [conv, highway],
        [highway_grad],
        conv_inputs,
        grad,
        jnp.asarray(hot_mask.astype(np.float32)),
        jnp.asarray(hot_fold.astype(np.float32)),
        3,
    )
    conv_grad = jnp.concatenate(
        [conv_grad[h].reshape(-1, conv.block[1])[:LANE] for h in range(2)], axis=1
    )
    conv_weight_grad = jnp.where(kernel_mask, conv_grad[:ones_row, :filters], 0.0)
    conv_bias_grad = conv_grad[ones_row, :filters]
    table_grad = jnp.sum(
        conv_grad[:char_count, fp : fp + KMAX * embed_dim].reshape(char_count, KMAX, embed_dim), axis=1
    )

    def own_window(plan, part):
        if dp_count > 2:
            groups = [list(range(h, dp_count, 2)) for h in range(2)]
            part = lax.psum(part.astype(F32), "dp", axis_index_groups=groups)
        if plan.by_rows:
            at = dp_at // 2
        else:
            at = dp_at
            part = jnp.concatenate(
                [
                    lax.dynamic_slice_in_dim(part[p], at * plan.rows, plan.rows, 0)
                    for p in range(plan.parts)
                ],
                axis=1,
            ).astype(F32)
            return plan.to_flat(part, dp_at, fsdp_at)
        window = lax.dynamic_slice_in_dim(part, at * plan.rows, plan.rows, 0)
        return plan.to_flat(window, dp_at, fsdp_at)

    return (
        window_loss,
        table_grad,
        conv_weight_grad,
        conv_bias_grad,
        own_window(highway, highway_part),
        own_window(lstm, lstm_part),
        own_window(soft, soft_part),
    )


def solution(mesh):
    in_specs = (
        P(None, ("dp", "fsdp"), None, None),
        P(None, ("dp", "fsdp"), None),
        P(None, ("dp", "fsdp"), None),
        P(None, ("dp", "fsdp"), None),
        P(None, ("dp", "fsdp"), None, None),
        P(None, ("dp", "fsdp")),
        P(),
        P(),
        P(),
        P("fsdp", None),
        P("fsdp", None),
        P("fsdp", None),
    )
    out_specs = (
        P(None, ("dp", "fsdp")),
        P(),
        P(),
        P(),
        P(("dp", "fsdp"), None),
        P(("dp", "fsdp"), None),
        P(("dp", "fsdp"), None),
    )
    return jax.shard_map(
        functools.partial(shards, mesh.shape["fsdp"], mesh.shape["dp"]),
        mesh=mesh,
        in_specs=in_specs,
        out_specs=out_specs,
        check_vma=False,
    )
```

```python
import functools

import jax
import jax.numpy as jnp
import numpy as np
from jax import lax
from jax.experimental import pallas as pl
from jax.experimental.pallas import tpu as pltpu
from jax.sharding import PartitionSpec as P

H = 650
V = 10000
KMAX = 7
LANE = 128
HP = 768
SLOTS = 24
CHARS = 51
HOT = 384
FILTER_CUTS = (1, 3, 6, 10, 14, 18)
MESH = pl.DeviceIdType.MESH
BF = jnp.bfloat16
F32 = jnp.float32


def up_to(value, unit):
    return -(-value // unit) * unit


def dot(left, right):
    return jnp.dot(left, right, preferred_element_type=F32)


def dot_rows(left, right):
    return lax.dot_general(left, right, (((0,), (0,)), ((), ())), preferred_element_type=F32)


def dot_cols(left, right):
    return lax.dot_general(left, right, (((1,), (1,)), ((), ())), preferred_element_type=F32)


class Windows:
    dtype = BF

    def __init__(self, flat_rows, width, used, fsdp, dp, by_rows, parts=2):
        owners = fsdp * dp
        self.parts = parts
        self.width, self.by_rows, self.fsdp, self.dp, self.used = width, by_rows, fsdp, dp, used
        self.entries = flat_rows * LANE // owners
        self.starts = [o * self.entries // width for o in range(owners)]
        self.spans = [
            (o * self.entries % width + self.entries - 1) // width + 1 for o in range(owners)
        ]
        unit = 16 if by_rows else 8
        rows = up_to(max(self.spans), unit)
        while (dp * rows) % 16:
            rows += unit
        self.rows = rows
        self.total = owners * rows
        self.columns = up_to(width, LANE) if by_rows else parts * up_to(-(-width // parts), LANE)
        self.block = (
            (dp // 2 * rows, self.columns) if by_rows else (dp * rows, self.columns // parts)
        )
        self.shape = (
            (self.total, self.columns)
            if by_rows
            else (parts, self.total, self.columns // parts)
        )
        if by_rows:
            order = [
                (2 * jj + h) * fsdp + f
                for f in range(fsdp)
                for h in range(2)
                for jj in range(dp // 2)
            ]
        else:
            order = [d * fsdp + f for f in range(fsdp) for d in range(dp)]
        self.position = [order.index(o) for o in range(owners)]
        self.gathered = self.row_map(range(owners))
        self.reduced = self.row_map(order)

    def row_map(self, order):
        rows_of = [
            [
                self.starts[o] + i if i < self.spans[o] and self.starts[o] + i < self.used else -1
                for i in range(self.rows)
            ]
            for o in order
        ]
        return np.array(rows_of, np.int32).reshape(-1)

    def pick(self, ref, half, slot):
        depth = self.block[0]
        if self.by_rows:
            return ref.at[pl.ds(pl.multiple_of((2 * slot + half) * depth, 16), depth)]
        return ref.at[half, pl.ds(pl.multiple_of(slot * depth, 16), depth)]

    def meeting(self, begin, end):
        found = []
        for o, (start, span) in enumerate(zip(self.starts, self.spans)):
            first, last = max(0, begin - start), min(span, end - start)
            if first < last:
                found.append((o, first, last))
        return found

    @property
    def lines(self):
        return up_to(-(-self.rows * self.width // LANE), 16) + 32

    def place_blocks(self, shard_ref, out_ref):
        fsdp_at = lax.axis_index("fsdp")
        count = self.entries // LANE
        out_ref[...] = jnp.zeros_like(out_ref)
        for j in range(self.dp):
            shift = lax.rem((fsdp_at * self.dp + j) * self.entries, self.width)
            lanes, lines = lax.rem(shift, LANE), lax.rem(shift // LANE, 16)
            block = shard_ref[j].astype(F32)
            extra = up_to(count, 16) + 16 - count
            block = jnp.concatenate([block, jnp.zeros((extra, LANE), F32)], axis=0)
            block = pltpu.roll(block, lanes, 1)
            lane = lax.broadcasted_iota(jnp.int32, block.shape, 1)
            block = jnp.where(lane < lanes, pltpu.roll(block, 1, 0), block)
            for step in (1, 2, 4, 8):
                moved = lax.rem(lines // step, 2) == 1
                block = jnp.where(moved, pltpu.roll(block, step, 0), block)
            begin = pl.multiple_of(shift // (16 * LANE) * 16, 16)
            out_ref[j, pl.ds(begin, count + extra), :] = block.astype(BF)

    def placed_shape(self):
        return jax.ShapeDtypeStruct((self.dp, self.lines, LANE), BF)

    def blocks_of(self, shard):
        return shard.reshape(self.dp, self.entries // LANE, LANE)

    def from_placed(self, placed):
        size = self.rows * self.width
        joined = jnp.concatenate(
            [
                jnp.pad(
                    placed[j].reshape(-1)[:size].reshape(self.rows, self.width),
                    ((0, 0), (0, self.columns - self.width)),
                )
                for j in range(self.dp)
            ],
            axis=0,
        )
        if self.by_rows:
            return joined.reshape((2,) + self.block)
        part = self.columns // self.parts
        return jnp.stack([joined[:, p * part : (p + 1) * part] for p in range(self.parts)])

    def to_flat(self, window, dp_at, fsdp_at):
        shift = lax.rem((dp_at * self.fsdp + fsdp_at) * self.entries, self.width)
        flat = window[:, : self.width].reshape(-1)
        return lax.dynamic_slice(flat, (shift,), (self.entries,)).reshape(-1, LANE)


def one_hot_map(rows, row_map):
    return (
        lax.broadcasted_iota(jnp.int32, (rows, row_map.shape[0]), 0) == jnp.asarray(row_map)[None, :]
    ).astype(BF)


def greet(place_of, lengthwise):
    d, f, z = place_of.d, place_of.f, place_of.z
    barrier = pltpu.get_barrier_semaphore()
    for target in (place_of.partner1, place_of.partner3, place_of.sibling):
        pl.semaphore_signal(barrier, inc=1, device_id=target, device_id_type=MESH)

    @pl.when(z > 0)
    def _():
        pl.semaphore_signal(barrier, inc=1, device_id=(d, f - 4), device_id_type=MESH)

    @pl.when(z < lengthwise - 1)
    def _():
        pl.semaphore_signal(barrier, inc=1, device_id=(d, f + 4), device_id_type=MESH)

    has_down = (z > 0).astype(jnp.int32)
    has_up = (z < lengthwise - 1).astype(jnp.int32)
    pl.semaphore_wait(barrier, 3 + has_down + has_up)


class Place:
    def __init__(self):
        self.d, self.f = lax.axis_index("dp"), lax.axis_index("fsdp")
        self.c = lax.rem(self.d, 2)
        x, y, self.z = lax.rem(self.f, 2), lax.rem(self.f // 2, 2), self.f // 4
        self.first = x + self.c * (y - x)
        self.last = y + self.c * (x - y)
        self.stride1, self.stride3 = 1 + self.c, 2 - self.c
        self.flip1 = self.stride1 * (1 - 2 * self.first)
        self.flip3 = self.stride3 * (1 - 2 * self.last)
        self.partner1 = (self.d, self.f + self.flip1)
        self.partner3 = (self.d, self.f + self.flip3)
        self.sibling = (self.d + 1 - 2 * self.c, self.f)

    def last_bit(self, block):
        bit_x, bit_y = lax.rem(block, 2), lax.rem(block // 2, 2)
        return bit_y + self.c * (bit_x - bit_y)


def remote(src, dst, send, recv, target):
    return pltpu.make_async_remote_copy(
        src_ref=src,
        dst_ref=dst,
        send_sem=send,
        recv_sem=recv,
        device_id=target,
        device_id_type=MESH,
    )


class Gather:
    def __init__(self, plans, own, outs, sems, shared):
        self.plans, self.own, self.outs, self.sems, self.shared = plans, own, outs, sems, shared
        self.n = plans[0].fsdp
        self.lengthwise = self.n // 4
        self.at = Place()

    RECV, SIB_RECV, ONE, UP, DOWN, LAST, SIB, LOCAL = range(8)

    @staticmethod
    def semaphores(plans):
        return pltpu.SemaphoreType.DMA((8 * len(plans) * plans[0].fsdp,))

    def sem(self, kind, a, block):
        return self.sems.at[(kind * len(self.plans) + a) * self.n + block]

    def source(self, a, half):
        return self.own[a].at[half] if self.shared else self.own[a]

    def copy(self, kind, a, block, target, own=False):
        here = self.plans[a].pick(self.outs[a], self.at.c, block)
        return remote(
            self.source(a, self.at.c) if own else here,
            here,
            self.sem(kind, a, block),
            self.sem(self.SIB_RECV if kind == self.SIB else self.RECV, a, block),
            target,
        )

    def arrived(self, a, block, kind=RECV):
        c = self.at.c
        here = self.plans[a].pick(self.outs[a], 1 - c if kind == self.SIB_RECV else c, block)
        remote(
            here, here, self.sem(self.SIB, a, block), self.sem(kind, a, block), self.at.sibling
        ).wait_recv()

    def sent(self, kind, a, block):
        self.copy(kind, a, block, self.at.sibling).wait_send()

    def local(self, a, half):
        return pltpu.make_async_copy(
            self.source(a, half),
            self.plans[a].pick(self.outs[a], half, self.at.f),
            self.sem(self.LOCAL, a, half if self.shared else 0),
        )

    def send_up(self, a, block, own=False):
        @pl.when(self.at.z < self.lengthwise - 1)
        def _():
            self.copy(self.UP, a, block, (self.at.d, self.at.f + 4), own).start()

    def send_down(self, a, block, own=False):
        @pl.when(self.at.z > 0)
        def _():
            self.copy(self.DOWN, a, block, (self.at.d, self.at.f - 4), own).start()

    def begin(self, a):
        at = self.at
        self.copy(self.ONE, a, at.f, at.partner1, True).start()
        self.send_up(a, at.f, True)
        self.send_down(a, at.f, True)
        self.copy(self.LAST, a, at.f, at.partner3, True).start()
        if self.shared:
            for half in (0, 1):
                self.local(a, half).start()
        else:
            self.copy(self.SIB, a, at.f, at.sibling, True).start()
            self.local(a, at.c).start()

    def near(self, a):
        at = self.at
        block = at.f + at.flip1
        self.arrived(a, block)
        self.send_up(a, block)
        self.send_down(a, block)
        self.copy(self.LAST, a, block, at.partner3).start()
        self.copy(self.SIB, a, block, at.sibling).start()

    def line(self, a, distance):
        for sign in (1, -1):
            z = self.at.z - sign * distance

            def take(sign=sign):
                for flip in (0, 1):
                    block = self.at.f - 4 * sign * distance + flip * self.at.flip1
                    self.arrived(a, block)
                    (self.send_up if sign == 1 else self.send_down)(a, block)
                    self.copy(self.LAST, a, block, self.at.partner3).start()
                    self.copy(self.SIB, a, block, self.at.sibling).start()

            pl.when((z >= 0) & (z < self.lengthwise))(take)

    def across(self, a, distance):
        for sign in (1,) if distance == 0 else (1, -1):
            z = self.at.z - sign * distance

            def take(sign=sign):
                for flip in (0, 1):
                    block = (
                        self.at.f - 4 * sign * distance + flip * self.at.flip1 + self.at.flip3
                    )
                    self.arrived(a, block)
                    self.copy(self.SIB, a, block, self.at.sibling).start()

            pl.when((z >= 0) & (z < self.lengthwise))(take)

    def steps(self, a):
        steps = [functools.partial(self.near, a)]
        for distance in range(1, self.lengthwise):
            steps += [functools.partial(self.line, a, distance)]
            steps += [functools.partial(self.across, a, distance - 1)]
        return steps + [functools.partial(self.across, a, self.lengthwise - 1)]

    def from_sibling(self, a):
        def block_in(block, _):
            if self.shared:

                @pl.when(jnp.logical_not(block == self.at.f))
                def _():
                    self.arrived(a, block, self.SIB_RECV)

            else:
                self.arrived(a, block, self.SIB_RECV)
            return 0

        lax.fori_loop(0, self.n, block_in, 0)
        if self.shared:
            for half in (0, 1):
                self.local(a, half).wait()
        else:
            self.local(a, self.at.c).wait()

    def finish(self, a):
        at = self.at

        def block_done(block, _):
            z = block // 4
            if self.shared:
                pl.when(jnp.logical_not(block == at.f))(lambda: self.sent(self.SIB, a, block))
            else:
                self.sent(self.SIB, a, block)

            @pl.when(at.last_bit(block) == at.last)
            def _():
                self.sent(self.LAST, a, block)

                @pl.when((z <= at.z) & (at.z < self.lengthwise - 1))
                def _():
                    self.sent(self.UP, a, block)

                @pl.when((z >= at.z) & (at.z > 0))
                def _():
                    self.sent(self.DOWN, a, block)

            return 0

        lax.fori_loop(0, self.n, block_done, 0)
        self.sent(self.ONE, a, at.f)


class Reduce:
    SIB, SIB_RECV, LOAD, NEAR, NEAR_RECV, UP, UP_RECV, DOWN, DOWN_RECV, END = range(10)

    def __init__(self, plans, ins, totals, scratch, in_place=False):
        count = len(plans)
        self.plans, self.ins, self.totals, self.in_place = plans, ins, totals, in_place
        self.held = [None] * count if in_place else scratch[:count]
        scratch = scratch if in_place else scratch[count:]
        self.landed, self.flow, self.close, self.cross = (
            scratch[k * count : (k + 1) * count] for k in range(4)
        )
        self.sems = scratch[4 * count]
        self.n = plans[0].fsdp
        self.lengthwise = self.n // 4
        self.at = Place()

    @staticmethod
    def scratch(plans, in_place=False):
        n = plans[0].fsdp
        return (
            [pltpu.VMEM((n,) + plan.block, plan.dtype) for plan in plans] * (1 if in_place else 2)
            + [pltpu.VMEM((n // 2 + 2,) + plan.block, plan.dtype) for plan in plans]
            + [pltpu.VMEM((n // 2,) + plan.block, plan.dtype) for plan in plans]
            + [pltpu.VMEM(plan.block, plan.dtype) for plan in plans]
            + [pltpu.SemaphoreType.DMA((10 * len(plans) * n,))]
        )

    def sem(self, kind, a, block):
        return self.sems.at[(kind * len(self.plans) + a) * self.n + block]

    def slot(self, z, b1, b3):
        return 4 * z + self.at.stride1 * b1 + self.at.stride3 * b3

    def item(self, t):
        length = self.lengthwise
        pair, b3 = t // 2, t % 2
        z = jnp.int32(0)
        for here in range(length):
            order = sorted(range(length), key=lambda there: (-abs(there - here), there))
            for k, there in enumerate(order):
                z = jnp.where((self.at.z == here) & (pair == k), there, z)
        return z, b3

    def hold(self, a, block):
        if self.in_place:
            return self.plans[a].pick(self.ins[a], self.at.c, block)
        return self.held[a].at[block]

    def to_sibling(self, a, block):
        return remote(
            self.plans[a].pick(self.ins[a], 1 - self.at.c, block),
            self.landed[a].at[block],
            self.sem(self.SIB, a, block),
            self.sem(self.SIB_RECV, a, block),
            self.at.sibling,
        )

    def load(self, a, block):
        return pltpu.make_async_copy(
            self.plans[a].pick(self.ins[a], self.at.c, block),
            self.held[a].at[block],
            self.sem(self.LOAD, a, block),
        )

    def to_near(self, a, z, b3):
        return remote(
            self.hold(a, self.slot(z, 1 - self.at.first, b3)),
            self.close[a].at[2 * z + b3],
            self.sem(self.NEAR, a, 2 * z + b3),
            self.sem(self.NEAR_RECV, a, 2 * z + b3),
            self.at.partner1,
        )

    def flow_at(self, up, here, z, b3):
        if up:
            return 2 * z + b3
        return jnp.where(z == here, self.n // 2 + b3, 2 * z + b3)

    def along(self, up, a, z, b3):
        return remote(
            self.hold(a, self.slot(z, self.at.first, b3)),
            self.flow[a].at[self.flow_at(up, self.at.z + (1 if up else -1), z, b3)],
            self.sem(self.UP if up else self.DOWN, a, 2 * z + b3),
            self.sem(self.UP_RECV if up else self.DOWN_RECV, a, 2 * z + b3),
            (self.at.d, self.at.f + (4 if up else -4)),
        )

    def to_cross(self, a):
        return remote(
            self.hold(a, self.slot(self.at.z, self.at.first, 1 - self.at.last)),
            self.cross[a],
            self.sem(self.END, a, 0),
            self.sem(self.END, a, 1),
            self.at.partner3,
        )

    def rows(self, a, body):
        unit = 16

        def step(i, _):
            body(pl.ds(pl.multiple_of(i * unit, unit), unit))
            return 0

        if self.plans[a].block[0] < unit:
            body(slice(None))
        else:
            lax.fori_loop(0, self.plans[a].block[0] // unit, step, 0)

    def add(self, a, block, sources):
        held = self.hold(a, block)

        def body(where):
            total = held[where, :].astype(F32)
            for ref, at in sources:
                total += ref[at, where, :].astype(F32)
            held[where, :] = total.astype(held.dtype)

        self.rows(a, body)

    def begin(self, a):
        for flip in (1, 0):
            b1 = self.at.first + flip * (1 - 2 * self.at.first)

            def start(t, _, b1=b1):
                z, b3 = self.item(t)
                block = self.slot(z, b1, b3)
                self.to_sibling(a, block).start()
                if not self.in_place:
                    self.load(a, block).start()
                return 0

            lax.fori_loop(0, 2 * self.lengthwise, start, 0)

    def first_leg(self, a, t):
        z, b3 = self.item(t)
        block = self.slot(z, 1 - self.at.first, b3)
        if not self.in_place:
            self.load(a, block).wait()
        self.to_sibling(a, block).wait_recv()
        self.add(a, block, [(self.landed[a], block)])
        self.to_near(a, z, b3).start()

    def middle_leg(self, a, t):
        z, b3 = self.item(t)
        block = self.slot(z, self.at.first, b3)
        flow = 2 * z + b3
        base = [(self.landed[a], block), (self.close[a], flow)]
        if not self.in_place:
            self.load(a, block).wait()
        self.to_sibling(a, block).wait_recv()
        self.to_near(a, z, b3).wait_recv()

        def onward(up):
            incoming = self.at.z > 0 if up else self.at.z < self.lengthwise - 1

            @pl.when(incoming)
            def _():
                self.along(up, a, z, b3).wait_recv()
                self.add(a, block, base + [(self.flow[a], self.flow_at(up, self.at.z, z, b3))])

            @pl.when(jnp.logical_not(incoming))
            def _():
                self.add(a, block, base)

            self.along(up, a, z, b3).start()

        pl.when(z > self.at.z)(functools.partial(onward, True))
        pl.when(z < self.at.z)(functools.partial(onward, False))

        @pl.when(z == self.at.z)
        def _():
            self.add(a, block, base)

    def own(self, a, b3):
        z = self.at.z
        block = self.slot(z, self.at.first, b3)
        for up in (True, False):

            @pl.when(z > 0 if up else z < self.lengthwise - 1)
            def _(up=up):
                self.along(up, a, z, b3).wait_recv()
                self.add(a, block, [(self.flow[a], self.flow_at(up, z, z, b3))])

    def cross_over(self, a):
        self.own(a, 1 - self.at.last)
        self.to_cross(a).start()

    def last_leg(self, a):
        self.own(a, self.at.last)
        self.to_cross(a).wait_recv()
        block = self.slot(self.at.z, self.at.first, self.at.last)

        def body(where):
            total = self.hold(a, block)[where, :].astype(F32) + self.cross[a][where, :].astype(F32)
            self.totals[a][where, :] = total

        self.rows(a, body)

    def finish(self, a):
        def done(t, _):
            z, b3 = self.item(t)
            for b1 in (self.at.first, 1 - self.at.first):
                self.to_sibling(a, self.slot(z, b1, b3)).wait_send()
            self.to_near(a, z, b3).wait_send()
            for up in (True, False):

                @pl.when(z > self.at.z if up else z < self.at.z)
                def _(up=up):
                    self.along(up, a, z, b3).wait_send()

            return 0

        lax.fori_loop(0, 2 * self.lengthwise, done, 0)
        self.to_cross(a).wait_send()


def pair_exchange(plans, totals, outs, sems, at):
    copies = []
    for a, plan in enumerate(plans):
        if not plan.by_rows:
            copies.append(
                remote(
                    totals[a], outs[a].at[at.c], sems.at[2 * a], sems.at[2 * a + 1], at.sibling
                )
            )
    return copies


def reduce_out(plan):
    return jax.ShapeDtypeStruct(plan.block if plan.by_rows else (2,) + plan.block, F32)


def hot_rows(codes):
    count = codes.shape[0]
    slot = lax.rem(lax.broadcasted_iota(jnp.int32, (count, 1), 0), SLOTS)
    lane = lax.broadcasted_iota(jnp.int32, (count, HOT), 1)
    hit = lane == KMAX * CHARS
    for q in range(KMAX):
        moved = codes if q == 0 else pltpu.roll(codes, count - q, 0)
        moved = jnp.where((moved >= 0) & (slot + q < SLOTS), moved + q * CHARS, -1)
        hit = jnp.logical_or(hit, lane == moved)
    return hit.astype(F32).astype(BF)


def conv_forward_block(filters, codes, lengths, refs, out_ref, where):
    table_ref, kernel_ref, width_ref = refs
    words = lengths.shape[0]
    windows = dot(hot_rows(codes), table_ref[...]).astype(BF)
    chunk = 384
    for at in range(0, kernel_ref.shape[1], chunk):
        columns = slice(at, at + chunk)
        activated = jnp.tanh(dot(windows, kernel_ref[:, columns])).reshape(words, SLOTS, chunk)
        counts = jnp.maximum(lengths - width_ref[:, columns] + 1, 1)
        position = lax.broadcasted_iota(jnp.int32, (words, SLOTS, chunk), 1)
        inside = position < counts[:, None, :]
        totals = jnp.sum(jnp.where(inside, jnp.exp(activated), 0.0), axis=1)
        pooled = jnp.log(totals) - jnp.log(counts.astype(F32))
        lane = at + lax.broadcasted_iota(jnp.int32, (words, chunk), 1)
        out_ref[where, columns] = keep_feature(pooled, lane, filters)


def keep_feature(value, lane, filters):
    value = value.astype(BF).astype(F32)
    return jnp.where(lane < filters, value, jnp.where(lane == filters, 1.0, 0.0))


def conv_backward_block(codes, lengths, refs, grad_ref, where, kernel_grad_ref, hot_grad_ref):
    table_ref, kernel_ref, width_ref = refs
    words = lengths.shape[0]
    hot = hot_rows(codes)
    windows = dot(hot, table_ref[...]).astype(BF)
    chunk = 384
    grad_windows = jnp.zeros(windows.shape, F32)
    for at in range(0, kernel_ref.shape[1], chunk):
        columns = slice(at, at + chunk)
        activated = jnp.tanh(dot(windows, kernel_ref[:, columns])).reshape(words, SLOTS, chunk)
        counts = jnp.maximum(lengths - width_ref[:, columns] + 1, 1)
        position = lax.broadcasted_iota(jnp.int32, (words, SLOTS, chunk), 1)
        inside = position < counts[:, None, :]
        weight = jnp.where(inside, jnp.exp(activated), 0.0)
        share = grad_ref[where, columns] / jnp.sum(weight, axis=1)
        grad = (share[:, None, :] * weight * (1.0 - activated * activated)).astype(BF)
        grad = grad.reshape(words * SLOTS, chunk)
        kernel_grad_ref[:, columns] += dot_rows(windows, grad)
        grad_windows += dot_cols(grad, kernel_ref[:, columns])
    hot_grad_ref[...] += dot_rows(hot, grad_windows.astype(BF))


def place_kernel(plans, *refs):
    for plan, shard, out in zip(plans, refs[: len(plans)], refs[len(plans) :]):
        plan.place_blocks(shard, out)


def place_all(plans, shards):
    vmem = pl.BlockSpec(memory_space=pltpu.VMEM)
    placed = pl.pallas_call(
        functools.partial(place_kernel, plans),
        out_shape=[plan.placed_shape() for plan in plans],
        in_specs=[vmem] * len(plans),
        out_specs=[vmem] * len(plans),
        compiler_params=pltpu.CompilerParams(vmem_limit_bytes=48 * 2**20),
    )(*[plan.blocks_of(shard) for plan, shard in zip(plans, shards)])
    return [plan.from_placed(each) for plan, each in zip(plans, placed)]


class Dense:
    by_rows = False
    dtype = F32

    def __init__(self, rows, columns, fsdp):
        self.fsdp = fsdp
        self.filled = rows
        self.block = (up_to(-(-rows // fsdp), 8), columns // 2)
        self.shape = (2, fsdp) + self.block

    def pick(self, ref, half, slot):
        return ref.at[half, slot]


WORD_BLOCK = 16


def tail_kernel(plans, conv_ref, grad_ref, conv_out, total_out, conv_in, conv_total, gather_sems, *scratch):
    conv, highway = plans
    work = Reduce(plans, [conv_in, grad_ref], [conv_total, total_out], scratch)
    items = 2 * work.lengthwise
    greet(work.at, work.lengthwise)
    conv_in[...] = jnp.zeros_like(conv_in)
    depth, half = conv.block
    for block in range(conv.filled // depth):
        for h in range(2):
            conv_in[h, block] = conv_ref[
                block * depth : (block + 1) * depth, h * half : (h + 1) * half
            ]
    work.begin(0)
    work.begin(1)

    def legs(body, a, begin, end):
        def step(t, _):
            body(a, t)
            return 0

        lax.fori_loop(begin, end, step, 0)

    legs(work.first_leg, 0, 0, items)
    legs(work.first_leg, 1, 0, items // 2)
    legs(work.middle_leg, 0, 0, items)
    legs(work.first_leg, 1, items // 2, items)
    work.cross_over(0)
    legs(work.middle_leg, 1, 0, 1)
    work.last_leg(0)
    spread = Gather([conv], [conv_total], [conv_out], gather_sems, False)
    spread.begin(0)
    steps = spread.steps(0)
    for k in range(1, max(items, len(steps))):
        if k < items:
            legs(work.middle_leg, 1, k, k + 1)
        if k - 1 < len(steps):
            steps[k - 1]()
    work.cross_over(1)
    for step in steps[max(items, len(steps)) - 1 :]:
        step()
    work.last_leg(1)
    spread.from_sibling(0)
    spread.finish(0)
    for a in range(2):
        work.finish(a)


def tail(plans, conv_grad, highway_grad, collective_id):
    conv, highway = plans
    vmem = pl.BlockSpec(memory_space=pltpu.VMEM)
    return pl.pallas_call(
        functools.partial(tail_kernel, plans),
        out_shape=[
            jax.ShapeDtypeStruct(conv.shape, F32),
            jax.ShapeDtypeStruct(highway.block, F32),
        ],
        in_specs=[vmem, pl.BlockSpec(memory_space=pl.ANY)],
        out_specs=[vmem] * 2,
        scratch_shapes=[
            pltpu.VMEM(conv.shape, F32),
            pltpu.VMEM(conv.block, F32),
            Gather.semaphores([conv]),
        ]
        + Reduce.scratch(plans),
        compiler_params=pltpu.CompilerParams(
            collective_id=collective_id, has_side_effects=True, vmem_limit_bytes=48 * 2**20
        ),
    )(conv_grad, highway_grad)


def gate_parts(sums):
    parts = [sums[:, :HP]]
    for g in range(1, 4):
        begin = g * H // LANE * LANE
        moved = sums[:, begin : begin + HP + LANE]
        parts.append(pltpu.roll(moved, HP + LANE - (g * H - begin), 1)[:, :HP])
    return parts


def join_gates(parts, columns):
    rows = parts[0].shape[0]
    total = None
    for g, part in enumerate(parts):
        begin = g * H // LANE * LANE
        wide = jnp.concatenate([part, jnp.zeros((rows, LANE), F32)], axis=1)
        if g * H - begin:
            wide = pltpu.roll(wide, g * H - begin, 1)
        pieces = [wide]
        if begin:
            pieces = [jnp.zeros((rows, begin), F32)] + pieces
        if columns - begin - HP - LANE > 0:
            pieces = pieces + [jnp.zeros((rows, columns - begin - HP - LANE), F32)]
        placed = jnp.concatenate(pieces, axis=1)[:, :columns]
        total = placed if total is None else total + placed
    return total


class Line:
    def __init__(self, n):
        self.at = Place()
        self.length = n // 4
        self.me = 2 * self.at.z + self.at.c

    def peer(self, z, other_core=False):
        at = self.at
        return (at.d + (1 - 2 * at.c if other_core else 0), at.f + 4 * (z - at.z))

    def others(self, body):
        def step(z, _):
            pl.when(z != self.at.z)(functools.partial(body, z))
            return 0

        lax.fori_loop(0, self.length, step, 0)

    def chips(self, body):
        def step(z, _):
            body(z)
            return 0

        lax.fori_loop(0, self.length, step, 0)

    def greet(self, across, both_cores):
        barrier = pltpu.get_barrier_semaphore()

        def signal(target):
            pl.semaphore_signal(barrier, inc=1, device_id=target, device_id_type=MESH)

        signal(self.at.sibling)
        count = 1
        if across:
            signal(self.at.partner1)
            signal(self.at.partner3)
            count += 2

        def chip(z):
            signal(self.peer(z))
            if both_cores:
                signal(self.peer(z, True))

        self.others(chip)
        pl.semaphore_wait(barrier, count + (self.length - 1) * (2 if both_cores else 1))


class Semaphores:
    def __init__(self, ref, size):
        self.ref, self.size = ref, size

    def __call__(self, kind, index):
        return self.ref.at[kind * self.size + index]


HIDDEN_CHUNKS = ((0, 48), (48, 96), (96, 128), (128, 144))


def hidden_chunks(rows):
    return [(a, min(b, rows)) for a, b in HIDDEN_CHUNKS if a < rows] + (
        [(HIDDEN_CHUNKS[-1][1], rows)] if rows > HIDDEN_CHUNKS[-1][1] else []
    )


def lstm_forward_kernel(
    batch, n, x_ref, w_ref, h0_ref, c0_ref, keep_ref, extra_ref, own_ref, *refs
):
    hp_ref, cp_ref, i_ref, f_ref, u_ref, o_ref, t_ref, hall_ref, part_ref = refs[:9]
    hidden, soft_sems, hidden_sems = refs[9:]
    line = Line(n)
    at, length = line.at, line.length
    rows_all = x_ref.shape[0]
    chunks = hidden_chunks(rows_all)
    RECV, TO_LINE, TO_NEAR, TO_LAST, LOCAL = range(5)
    sem = Semaphores(soft_sems, n)
    H_RECV, H_LINE, H_SIB = range(3)
    hsem = Semaphores(hidden_sems, 2 * length * len(chunks))

    def column(z):
        return at.f + 4 * (z - at.z)

    def to_line(z):
        return remote(
            own_ref.at[2 * z + at.c],
            part_ref.at[at.f],
            sem(TO_LINE, z),
            sem(RECV, at.f),
            line.peer(z),
        )

    def pass_on(kind, index, slot, target, own=False):
        return remote(
            own_ref.at[line.me] if own else part_ref.at[slot],
            part_ref.at[slot],
            sem(kind, index),
            sem(RECV, slot),
            target,
        )

    def landed(slot):
        pass_on(TO_NEAR, 0, slot, at.partner1).wait_recv()

    local = pltpu.make_async_copy(own_ref.at[line.me], part_ref.at[at.f], sem(LOCAL, 0))

    def event_begin():
        line.others(lambda z: to_line(z).start())
        pass_on(TO_NEAR, at.z, at.f, at.partner1, True).start()
        pass_on(TO_LAST, at.z, at.f, at.partner3, True).start()
        local.start()

    def event_line():
        def chip(z):
            landed(column(z))
            pass_on(TO_NEAR, z, column(z), at.partner1).start()
            pass_on(TO_LAST, z, column(z), at.partner3).start()

        line.others(chip)

    def event_near():
        def chip(z):
            slot = column(z) + at.flip1
            landed(slot)
            pass_on(TO_LAST, length + z, slot, at.partner3).start()

        line.chips(chip)

    def event_end():
        def chip(z):
            landed(column(z) + at.flip3)
            landed(column(z) + at.flip1 + at.flip3)
            pass_on(TO_NEAR, z, column(z), at.partner1).wait_send()
            pass_on(TO_LAST, z, column(z), at.partner3).wait_send()
            pass_on(TO_LAST, length + z, column(z), at.partner3).wait_send()

        line.chips(chip)
        line.others(lambda z: to_line(z).wait_send())
        local.wait()

    def chunk_copy(k, member, kind, index, target):
        begin, end = chunks[k]
        here = hall_ref.at[member, pl.ds(begin, end - begin), :]
        return remote(
            here,
            here,
            hsem(kind, index * len(chunks) + k),
            hsem(H_RECV, member * len(chunks) + k),
            target,
        )

    def chunk_out(k):
        begin, end = chunks[k]
        hall_ref[line.me, begin:end, :] = hidden[begin:end, :].astype(BF)
        line.others(lambda z: chunk_copy(k, line.me, H_LINE, z, line.peer(z)).start())
        chunk_copy(k, line.me, H_SIB, at.z, at.sibling).start()

    def chunk_pass(k):
        def chip(z):
            member = 2 * z + at.c
            chunk_copy(k, member, H_SIB, z, at.sibling).wait_recv()
            chunk_copy(k, member, H_SIB, z, at.sibling).start()

        line.others(chip)

    def chunk_end(k):
        def chip(z):
            chunk_copy(k, 2 * z + 1 - at.c, H_SIB, z, at.sibling).wait_recv()
            chunk_copy(k, 2 * z + at.c, H_SIB, z, at.sibling).wait_send()

        line.chips(chip)
        line.others(lambda z: chunk_copy(k, line.me, H_LINE, z, line.peer(z)).wait_send())

    line.greet(True, False)
    event_begin()
    per_tile = 8 // batch
    tiles = rows_all // 8
    row = lax.broadcasted_iota(jnp.int32, (8, HP), 0)
    lane = lax.broadcasted_iota(jnp.int32, (8, LANE), 1)
    last = HP - LANE

    def tile(step, carried):
        h, c = carried
        rows = pl.ds(pl.multiple_of(step * 8, 8), 8)
        x = x_ref[rows, :]
        keep = keep_ref[rows, :]
        saved = None
        for part in range(per_tile):
            hp, cp = h * keep, c * keep
            sums = x + dot(hp.astype(BF), w_ref[...])
            i, f, u, o = gate_parts(sums)
            i, f, u, o = jax.nn.sigmoid(i), jax.nn.sigmoid(f), jnp.tanh(u), jax.nn.sigmoid(o)
            c = f * cp + i * u
            t = jnp.tanh(c)
            h = (o * t).astype(BF).astype(F32)
            now = (hp, cp, i, f, u, o, t, h)
            if saved is None:
                saved = now
            else:
                saved = tuple(jnp.where(row >= part * batch, b, a) for a, b in zip(saved, now))
            h, c = pltpu.roll(h, batch, 0), pltpu.roll(c, batch, 0)
        for ref, value in zip((hp_ref, cp_ref, i_ref, f_ref, u_ref, o_ref, t_ref), saved):
            ref[rows, :] = value
        hidden[rows, :last] = saved[-1][:, :last]
        hidden[rows, last:] = jnp.where(lane < H - last, saved[-1][:, last:], extra_ref[rows, :])

        pl.when(step == tiles // 3)(event_line)
        pl.when(step == tiles * 2 // 3)(event_near)
        for k, (_, end) in enumerate(chunks):
            pl.when(step == end // 8 - 1)(functools.partial(chunk_out, k))
        return h, c

    lax.fori_loop(0, tiles, tile, (h0_ref[...], c0_ref[...]))
    for k in range(len(chunks)):
        chunk_pass(k)
    event_end()
    for k in range(len(chunks)):
        chunk_end(k)


def lstm_forward(batch, plan, x, recur, h0, c0, keep, extra, own, collective_id):
    rows, n = x.shape[0], plan.fsdp
    members = plan.parts
    chunks = len(hidden_chunks(rows))
    vmem = pl.BlockSpec(memory_space=pltpu.VMEM)
    anywhere = pl.BlockSpec(memory_space=pl.ANY)
    return pl.pallas_call(
        functools.partial(lstm_forward_kernel, batch, n),
        out_shape=[jax.ShapeDtypeStruct((rows, HP), F32)] * 7
        + [
            jax.ShapeDtypeStruct((members, rows, HP), BF),
            jax.ShapeDtypeStruct((n,) + plan.block, BF),
        ],
        in_specs=[vmem] * 6 + [anywhere],
        out_specs=[vmem] * 8 + [anywhere],
        scratch_shapes=[
            pltpu.VMEM((rows, HP), F32),
            pltpu.SemaphoreType.DMA((5 * n,)),
            pltpu.SemaphoreType.DMA((3 * members * chunks,)),
        ],
        compiler_params=pltpu.CompilerParams(
            collective_id=collective_id, has_side_effects=True, vmem_limit_bytes=48 * 2**20
        ),
    )(x, recur, h0, c0, keep, extra, own)


def lstm_backward_kernel(
    batch,
    n,
    dh_ref,
    w_ref,
    keep_ref,
    cp_ref,
    i_ref,
    f_ref,
    u_ref,
    o_ref,
    t_ref,
    grad_ref,
    dz_ref,
    out_ref,
    held_near,
    held_line,
    from_last,
    from_near,
    sems,
):
    line = Line(n)
    at, length = line.at, line.length
    LAST, LAST_RECV, NEAR, NEAR_RECV, TO_LINE, LINE_RECV, SIB, SIB_RECV = range(8)
    sem = Semaphores(sems, 2 * length)

    def slot(z, b1, b3):
        return 4 * z + at.stride1 * b1 + at.stride3 * b3

    def to_last(z, b1):
        return remote(
            grad_ref.at[slot(z, b1, 1 - at.last)],
            from_last.at[2 * z + b1],
            sem(LAST, 2 * z + b1),
            sem(LAST_RECV, 2 * z + b1),
            at.partner3,
        )

    def to_near(z):
        return remote(
            held_near.at[z], from_near.at[z], sem(NEAR, z), sem(NEAR_RECV, z), at.partner1
        )

    def to_line(z):
        return remote(
            held_line.at[z], out_ref.at[line.me], sem(TO_LINE, z), sem(LINE_RECV, at.z), line.peer(z)
        )

    def line_arrived(z):
        here = out_ref.at[2 * z + at.c]
        remote(here, here, sem(TO_LINE, z), sem(LINE_RECV, z), line.peer(z)).wait_recv()

    def to_sibling(z, other=False):
        here = out_ref.at[2 * z + (1 - at.c if other else at.c)]
        return remote(here, here, sem(SIB, z), sem(SIB_RECV, z), at.sibling)

    def event_begin():
        def chip(z):
            to_last(z, 1 - at.first).start()

        line.chips(chip)

        def chip_own(z):
            to_last(z, at.first).start()

        line.chips(chip_own)

    def event_last():
        def chip(z):
            b1 = 1 - at.first
            to_last(z, b1).wait_recv()
            held_near[z] = (
                grad_ref[slot(z, b1, at.last)].astype(F32) + from_last[2 * z + b1].astype(F32)
            ).astype(BF)
            to_near(z).start()

        line.chips(chip)

    def event_near():
        def chip(z):
            to_last(z, at.first).wait_recv()
            to_near(z).wait_recv()
            total = (
                grad_ref[slot(z, at.first, at.last)].astype(F32)
                + from_last[2 * z + at.first].astype(F32)
                + from_near[z].astype(F32)
            ).astype(BF)
            held_line[z] = total

            @pl.when(z == at.z)
            def _():
                out_ref[line.me] = total

            @pl.when(z != at.z)
            def _():
                to_line(z).start()

        line.chips(chip)
        to_sibling(at.z).start()

    def event_line():
        def chip(z):
            line_arrived(z)
            to_sibling(z).start()

        line.others(chip)

    def event_end():
        def chip(z):
            to_sibling(z, True).wait_recv()
            to_sibling(z).wait_send()
            to_near(z).wait_send()
            to_last(z, 0).wait_send()
            to_last(z, 1).wait_send()

        line.chips(chip)
        line.others(lambda z: to_line(z).wait_send())

    line.greet(True, False)
    event_begin()
    per_tile = 8 // batch
    tiles = dh_ref.shape[0] // 8
    row = lax.broadcasted_iota(jnp.int32, (8, dz_ref.shape[1]), 0)
    real = lax.broadcasted_iota(jnp.int32, (8, HP), 1) < H

    def tile(step, carried):
        dh_carry, dc_carry = carried
        rows = pl.ds(pl.multiple_of((tiles - 1 - step) * 8, 8), 8)
        keep = keep_ref[rows, :]
        i, f, u, o, t = (r[rows, :] for r in (i_ref, f_ref, u_ref, o_ref, t_ref))
        soft = dh_ref[rows, :]
        to_c = o * (1.0 - t * t)
        to_i = jnp.where(real, u * i * (1.0 - i), 0.0)
        to_f = jnp.where(real, cp_ref[rows, :] * f * (1.0 - f), 0.0)
        to_u = jnp.where(real, i * (1.0 - u * u), 0.0)
        to_o = jnp.where(real, t * o * (1.0 - o), 0.0)
        back = f * keep
        saved = None
        for part in reversed(range(per_tile)):
            dh = jnp.where(real, soft + dh_carry, 0.0)
            dc = dc_carry + dh * to_c
            dz = join_gates([dc * to_i, dc * to_f, dc * to_u, dh * to_o], dz_ref.shape[1])
            saved = dz if saved is None else jnp.where(row >= (part + 1) * batch, saved, dz)
            dh_carry = dot(dz.astype(BF), w_ref[...]) * keep
            dc_carry = dc * back
            dh_carry, dc_carry = (
                pltpu.roll(dh_carry, 8 - batch, 0),
                pltpu.roll(dc_carry, 8 - batch, 0),
            )
        dz_ref[rows, :] = saved
        pl.when(step == tiles // 3)(event_last)
        pl.when(step == tiles * 2 // 3)(event_near)
        pl.when(step == tiles - 2)(event_line)
        return dh_carry, dc_carry

    zero = jnp.zeros((8, HP), F32)
    lax.fori_loop(0, tiles, tile, (zero, zero))
    event_end()


def lstm_backward(batch, plan, columns, dh, recur_t, keep, states, grad, collective_id):
    rows, n = dh.shape[0], plan.fsdp
    length = n // 4
    vmem = pl.BlockSpec(memory_space=pltpu.VMEM)
    return pl.pallas_call(
        functools.partial(lstm_backward_kernel, batch, n),
        out_shape=[
            jax.ShapeDtypeStruct((rows, columns), F32),
            jax.ShapeDtypeStruct((plan.parts,) + plan.block, BF),
        ],
        in_specs=[vmem] * 10,
        out_specs=[vmem] * 2,
        scratch_shapes=[
            pltpu.VMEM((length,) + plan.block, BF),
            pltpu.VMEM((length,) + plan.block, BF),
            pltpu.VMEM((2 * length,) + plan.block, BF),
            pltpu.VMEM((length,) + plan.block, BF),
            pltpu.SemaphoreType.DMA((8 * 2 * length,)),
        ],
        compiler_params=pltpu.CompilerParams(
            collective_id=collective_id, has_side_effects=True, vmem_limit_bytes=48 * 2**20
        ),
    )(dh, recur_t, keep, *states, grad)


def turned(value, lanes):
    rows = value.shape[0]
    if rows < lanes:
        value = jnp.concatenate([value, jnp.zeros((lanes - rows, value.shape[1]), F32)], axis=0)
    return value.T


def copy_windows(plan, source, target, base, found, place):
    target[...] = jnp.zeros_like(target)
    for o, first, last in found:
        start, to = plan.starts[o] - base, place(o) * plan.rows
        target[to + first : to + last, :] = source[start + first : start + last, :]


def add_windows(plan, source, target, base, found, begin):
    for o, first, last in found:
        start, at = plan.starts[o] - base, o * plan.rows - begin
        target[start + first : start + last, :] += source[at + first : at + last, :]


def matrices_of(plan, filters):
    result = []
    for m in range(4):
        base = m * (filters + 1)
        found = plan.meeting(base, base + filters + 1)
        result.append((base, found, found[0][0] * plan.rows, (found[-1][0] + 1) * plan.rows))
    return result


def head_kernel(plans, soft, filters, blocks, *refs):
    highway, lstm = plans
    owns = refs[:2]
    codes_ref, length_ref, table_ref, kernel_ref, width_ref, soft_ref = refs[2:8]
    highway_out, lstm_out, x_ref, recur_ref, soft_out = refs[8:13]
    features, trans_refs, gate_refs = refs[13:16], refs[16:18], refs[18:20]
    highway_w, lstm_w, turned_ref, wide, recur_sum, gather_sems, out_sems = refs[20:]
    rows, fp = features[0].shape
    words = turned_ref.shape[1]
    work = Gather(plans, owns, (highway_w, lstm_w), gather_sems, True)
    length = work.lengthwise
    greet(work.at, length)

    def conv(begin, end):
        def block(i, _):
            at = pl.ds(pl.multiple_of(i * WORD_BLOCK, WORD_BLOCK), WORD_BLOCK)
            slots = pl.ds(
                pl.multiple_of(i * WORD_BLOCK * SLOTS, WORD_BLOCK * SLOTS), WORD_BLOCK * SLOTS
            )
            conv_forward_block(
                filters,
                codes_ref[slots, :],
                length_ref[at, :],
                (table_ref, kernel_ref, width_ref),
                features[0],
                at,
            )
            return 0

        lax.fori_loop(begin, end, block, 0)

    chunk = 384

    def layer_sum(m, wide=wide):
        base, found, begin, end = matrices[m]
        copy_windows(
            highway, turned_ref, wide.at[: end - begin], base, found, lambda o: o - found[0][0]
        )
        target = (trans_refs if m % 2 == 0 else gate_refs)[m // 2]

        def columns(j, _):
            where = pl.ds(pl.multiple_of(j * chunk, chunk), chunk)
            left = wide[: end - begin, :].astype(BF)
            target[:, where] = dot_rows(left, highway_w[begin:end, where])[:rows]
            return 0

        lax.fori_loop(0, fp // chunk, columns, 0)

    def layer(l):
        turned_ref[:fp, :] = turned(features[l][...], words)
        layer_sum(2 * l)

    def layer_end(l):
        layer_sum(2 * l + 1)
        trans, gate = trans_refs[l][...], jax.nn.sigmoid(gate_refs[l][...])
        gate_refs[l][...] = gate
        value = gate * trans * jax.nn.sigmoid(trans) + (1.0 - gate) * features[l][...]
        lane = lax.broadcasted_iota(jnp.int32, (rows, fp), 1)
        features[l + 1][...] = keep_feature(value, lane, filters)

    matrices = matrices_of(highway, filters)
    of_highway, of_lstm = work.steps(0), work.steps(1)
    count = len(of_highway)
    work.begin(0)
    third = -(-blocks // 3)
    for k in range(3):
        conv(k * third, min((k + 1) * third, blocks))
        if k < count:
            of_highway[k]()
    soft.place_blocks(soft_ref, soft_out)
    late = count - 4
    for k in range(3, count):
        if k == max(late, 3):
            work.begin(1)
        of_highway[k]()
    work.from_sibling(0)
    out_copies = [
        pltpu.make_async_copy(highway_w, highway_out, out_sems.at[0]),
        pltpu.make_async_copy(lstm_w, lstm_out, out_sems.at[1]),
    ]
    out_copies[0].start()
    of_lstm[0]()
    compute = [
        functools.partial(layer, 0),
        functools.partial(layer_end, 0),
        functools.partial(layer, 1),
        functools.partial(layer_end, 1),
    ]
    for k in range(1, max(count, 5)):
        if k <= 4:
            compute[k - 1]()
        if k < count:
            of_lstm[k]()

    turned_ref[...] = jnp.zeros_like(turned_ref)
    sub = lax.broadcasted_iota(jnp.int32, (fp, words), 0)
    turned_ref[:fp, :] = jnp.where(sub < filters, turned(features[2][...], words), 0.0)
    turned_ref[lstm.used - 1 : lstm.used, :] = jnp.ones((1, words), F32)
    wide = wide.at[: lstm.total]
    copy_windows(lstm, turned_ref, wide, 0, lstm.meeting(0, lstm.used), lambda o: o)
    work.from_sibling(1)
    out_copies[1].start()
    left = wide[...].astype(BF)
    half = lstm.block[1]
    for h in range(2):
        x_ref[:, h * half : (h + 1) * half] = dot_rows(left, lstm_w[h])[:rows]

    recur_sum[...] = jnp.zeros_like(recur_sum)
    depth = lstm.block[0]
    for h in range(2):
        for slot in sorted({o // lstm.dp for o, _, _ in lstm.meeting(filters, filters + H)}):
            piece = lstm_w[h, slot * depth : (slot + 1) * depth, :].astype(F32)
            for o, first, last in lstm.meeting(filters, filters + H):
                if o // lstm.dp == slot:
                    start, at = lstm.starts[o] - filters, (o % lstm.dp) * lstm.rows
                    recur_sum[start + first : start + last, h * half : (h + 1) * half] += piece[
                        at + first : at + last
                    ]
    recur_ref[...] = recur_sum[...].astype(BF)
    for a in range(2):
        work.finish(a)
    for copy in out_copies:
        copy.wait()


def head(plans, soft, filters, own, conv_inputs, soft_flat, rows, fp, collective_id):
    highway, lstm = plans
    words = up_to(rows, 2 * LANE)
    vmem = pl.BlockSpec(memory_space=pltpu.VMEM)
    anywhere = pl.BlockSpec(memory_space=pl.ANY)
    feature = jax.ShapeDtypeStruct((rows, fp), F32)
    matrices = matrices_of(highway, filters)
    longest = max([lstm.total] + [end - begin for _, _, begin, end in matrices])
    return pl.pallas_call(
        functools.partial(head_kernel, plans, soft, filters, rows // WORD_BLOCK),
        out_shape=[
            jax.ShapeDtypeStruct(highway.shape, BF),
            jax.ShapeDtypeStruct(lstm.shape, BF),
            jax.ShapeDtypeStruct((rows, lstm.columns), F32),
            jax.ShapeDtypeStruct((HP, lstm.columns), BF),
            soft.placed_shape(),
        ]
        + [feature] * 7,
        in_specs=[anywhere] * 2 + [vmem] * 6,
        out_specs=[anywhere] * 2 + [vmem] * 10,
        scratch_shapes=[
            pltpu.VMEM(highway.shape, BF),
            pltpu.VMEM(lstm.shape, BF),
            pltpu.VMEM((up_to(max(lstm.used, fp), LANE), words), F32),
            pltpu.VMEM((longest, words), F32),
            pltpu.VMEM((HP, lstm.columns), F32),
            Gather.semaphores(plans),
            pltpu.SemaphoreType.DMA((2,)),
        ],
        compiler_params=pltpu.CompilerParams(
            collective_id=collective_id, has_side_effects=True, vmem_limit_bytes=60 * 2**20
        ),
    )(*own, *conv_inputs, soft.blocks_of(soft_flat))


def highway_backward_kernel(plans, filters, blocks, *refs):
    highway, lstm = plans
    dz_ref, hp_ref = refs[:2]
    features, trans_refs, gate_refs = refs[2:5], refs[5:7], refs[7:9]
    codes_ref, length_ref, table_ref, kernel_ref, width_ref, mask_ref, fold_ref = refs[9:16]
    highway_all, lstm_all = refs[16:18]
    grad_out, kernel_grad, total_out = refs[18:21]
    refs = refs[21:]
    lstm_grad, highway_w, lstm_w, turned_ref, wide, back, dz, pairs = refs[:8]
    staged, carry, feature_grad, hot_grad, load_sems, pair_sems, out_sems = refs[8:15]
    rows, fp = features[0].shape
    words = turned_ref.shape[1]
    at = Place()
    work = Reduce([lstm], [lstm_grad], [total_out.at[at.c]], refs[15:], True)
    length, items = work.lengthwise, 2 * work.lengthwise
    matrices = matrices_of(highway, filters)
    half = lstm.block[1]
    of_input = lstm.meeting(0, filters)
    input_rows = lstm_w.shape[0]

    def layer_rows(l):
        begin, end = matrices[2 * l][2], matrices[2 * l + 1][3]
        return begin, end

    def load_layer(l):
        begin, end = layer_rows(l)
        return pltpu.make_async_copy(
            highway_all.at[pl.ds(begin, end - begin)],
            highway_w.at[pl.ds(0, end - begin)],
            load_sems.at[l],
        )

    def load_lstm(h):
        return pltpu.make_async_copy(
            lstm_all.at[h, pl.ds(0, input_rows)], lstm_w, load_sems.at[2 + h]
        )

    load_layer(1).start()
    load_lstm(0).start()
    greet(at, length)

    dz[...] = jnp.zeros_like(dz)
    dz[:rows, :] = dz_ref[...].astype(BF)
    lane = lax.broadcasted_iota(jnp.int32, (rows, HP), 1)
    hidden = jnp.where(lane < H, hp_ref[...], jnp.where(lane == H, 1.0, 0.0))
    sub = lax.broadcasted_iota(jnp.int32, (fp, words), 0)
    turned_ref[:fp, :] = jnp.where(sub < filters, turned(features[2][...], words), 0.0)
    kept = up_to(H + 1, 8)
    turned_ref[filters : filters + kept, :] = turned(hidden, words)[:kept]
    copy_windows(
        lstm,
        turned_ref,
        wide.at[: lstm.total],
        0,
        lstm.meeting(0, lstm.used),
        lambda o: lstm.position[o],
    )
    unit = lstm.total // (2 * length)

    def lstm_weights(i, _):
        where = pl.ds(pl.multiple_of(i * unit, unit), unit)
        left = wide[where, :].astype(BF)
        for h in range(2):
            lstm_grad[h, where, :] = dot(left, dz[:, h * half : (h + 1) * half]).astype(BF)
        return 0

    lax.fori_loop(0, 2 * length, lstm_weights, 0)
    work.begin(0)

    lane = lax.broadcasted_iota(jnp.int32, (rows, fp), 1)
    back[...] = jnp.zeros_like(back)
    for h in range(2):
        load_lstm(h).wait()
        wide[:input_rows, :] = dot_cols(lstm_w[...], dz[:, h * half : (h + 1) * half])
        if h == 0:
            load_lstm(1).start()
        add_windows(lstm, wide, back, 0, of_input, 0)
    grad = jnp.where(lane < filters, back[...].T[:rows], 0.0)

    def legs(body, begin, end):
        def step(t, _):
            body(0, t)
            return 0

        lax.fori_loop(begin, end, step, 0)

    legs(work.first_leg, 0, items)
    spots = 4 + blocks

    def middle(k):
        legs(work.middle_leg, k * items // spots, (k + 1) * items // spots)

    pairs[...] = jnp.zeros_like(pairs)
    for l in (1, 0):
        trans, gate = trans_refs[l][...], gate_refs[l][...]
        sig = jax.nn.sigmoid(trans)
        pairs[2 * l, :rows, :] = (grad * gate * sig * (1.0 + trans * (1.0 - sig))).astype(BF)
        pairs[2 * l + 1, :rows, :] = (
            grad * (trans * sig - features[l][...]) * gate * (1.0 - gate)
        ).astype(BF)
        load_layer(l).wait()
        back[...] = jnp.zeros_like(back)
        begin = layer_rows(l)[0]
        for m in (2 * l, 2 * l + 1):
            base, found, low, high = matrices[m]
            result = dot_cols(highway_w[low - begin : high - begin, :], pairs[m])
            add_windows(highway, result, back, base, found, low)
            if m % 2 and l:
                load_layer(0).start()
            middle(2 * (1 - l) + m % 2)
        grad = grad * (1.0 - gate) + back[...].T[:rows]
        grad = jnp.where(lane < filters, grad, 0.0)
    feature_grad[...] = grad

    kernel_grad[...] = jnp.zeros_like(kernel_grad)
    hot_grad[...] = jnp.zeros_like(hot_grad)

    def conv_block(i, _):
        where = pl.ds(pl.multiple_of(i * WORD_BLOCK, WORD_BLOCK), WORD_BLOCK)
        slots = pl.ds(pl.multiple_of(i * WORD_BLOCK * SLOTS, WORD_BLOCK * SLOTS), WORD_BLOCK * SLOTS)
        conv_backward_block(
            codes_ref[slots, :],
            length_ref[where, :],
            (table_ref, kernel_ref, width_ref),
            feature_grad,
            where,
            kernel_grad,
            hot_grad,
        )
        middle(4 + i)
        return 0

    lax.fori_loop(0, blocks, conv_block, 0)
    kernel_grad[:, fp:] = jnp.dot(
        fold_ref[...],
        hot_grad[...] * mask_ref[...],
        precision=lax.Precision.HIGHEST,
        preferred_element_type=F32,
    )
    work.cross_over(0)

    chunk = 384
    size = highway.rows
    pending, shared = [], None
    empty = [o for o in range(len(highway.starts)) if all(o != f[0] for m in matrices for f in m[1])]
    for m in range(4):
        base, found, low, high = matrices[m]
        if m % 2 == 0:
            turned_ref[:fp, :] = turned(features[m // 2][...], words)
        copy_windows(
            highway, turned_ref, wide.at[: high - low], base, found, lambda o: o - found[0][0]
        )
        for copy in pending:
            copy.wait()
        adds = shared == found[0][0]
        shares = m < 3 and matrices[m + 1][1][0][0] == found[-1][0]
        count = len(found)

        def columns(j, _):
            where = pl.ds(pl.multiple_of(j * chunk, chunk), chunk)
            result = dot(wide[: high - low, :].astype(BF), pairs[m, :, where])
            if adds:
                first = result[:size] + carry[:, where]
                staged[:size, where] = first.astype(BF)
                staged[size : high - low, where] = result[size:].astype(BF)
            else:
                staged[: high - low, where] = result.astype(BF)
            if shares:
                carry[:, where] = result[(count - 1) * size :]
            return 0

        lax.fori_loop(0, fp // chunk, columns, 0)
        shared = found[-1][0] if shares else None
        sent = found[:-1] if shares else found
        pending = [
            pltpu.make_async_copy(
                staged.at[pl.ds(k * size, size)],
                grad_out.at[pl.ds(highway.position[o] * size, size)],
                out_sems.at[k],
            )
            for k, (o, _, _) in enumerate(sent)
        ]
        for copy in pending:
            copy.start()
    for copy in pending:
        copy.wait()
    if empty:
        staged[:size, :] = jnp.zeros((size, fp), BF)
        for o in empty:
            copy = pltpu.make_async_copy(
                staged.at[pl.ds(0, size)],
                grad_out.at[pl.ds(highway.position[o] * size, size)],
                out_sems.at[0],
            )
            copy.start()
            copy.wait()
    work.last_leg(0)
    copy = remote(
        total_out.at[at.c], total_out.at[at.c], pair_sems.at[0], pair_sems.at[1], at.sibling
    )
    copy.start()
    work.finish(0)
    copy.wait()


def highway_backward(
    plans, filters, dz, hp, features, trans, gates, conv_inputs, everywhere, collective_id
):
    highway, lstm = plans
    rows, fp = features[0].shape
    words = up_to(rows, 2 * LANE)
    vmem = pl.BlockSpec(memory_space=pltpu.VMEM)
    anywhere = pl.BlockSpec(memory_space=pl.ANY)
    matrices = matrices_of(highway, filters)
    longest = max([lstm.total] + [end - begin for _, _, begin, end in matrices])
    layer = max(matrices[2 * l + 1][3] - matrices[2 * l][2] for l in range(2))
    input_rows = up_to((lstm.meeting(0, filters)[-1][0] + 1) * lstm.rows, 16)
    return pl.pallas_call(
        functools.partial(highway_backward_kernel, plans, filters, rows // WORD_BLOCK),
        out_shape=[
            jax.ShapeDtypeStruct(highway.shape, BF),
            jax.ShapeDtypeStruct((LANE, up_to(fp + LANE, 2 * LANE)), F32),
            jax.ShapeDtypeStruct((2,) + lstm.block, F32),
        ],
        in_specs=[vmem] * 16 + [anywhere] * 2,
        out_specs=[anywhere] + [vmem] * 2,
        scratch_shapes=[
            pltpu.VMEM(lstm.shape, BF),
            pltpu.VMEM((layer, highway.columns), BF),
            pltpu.VMEM((input_rows, lstm.block[1]), BF),
            pltpu.VMEM((up_to(max(lstm.used + 8, fp), LANE), words), F32),
            pltpu.VMEM((longest, words), F32),
            pltpu.VMEM((fp, words), F32),
            pltpu.VMEM((words, lstm.columns), BF),
            pltpu.VMEM((4, words, fp), BF),
            pltpu.VMEM((max(end - begin for _, _, begin, end in matrices), fp), BF),
            pltpu.VMEM((highway.rows, fp), F32),
            pltpu.VMEM((rows, fp), F32),
            pltpu.VMEM((HOT, LANE), F32),
            pltpu.SemaphoreType.DMA((4,)),
            pltpu.SemaphoreType.DMA((2,)),
            pltpu.SemaphoreType.DMA((max(len(found) for _, found, _, _ in matrices),)),
        ]
        + Reduce.scratch([lstm], True),
        compiler_params=pltpu.CompilerParams(
            collective_id=collective_id, has_side_effects=True, vmem_limit_bytes=255 * 2**18
        ),
    )(dz, hp, *features, *trans, *gates, *conv_inputs, *everywhere)


def softmax_kernel(
    vocab,
    n,
    h_ref,
    w_ref,
    map_ref,
    map_back_ref,
    loss_ref,
    grad_h_ref,
    grad_w_ref,
    spread_back,
    logits,
    grads,
    stats,
    for_sibling,
    from_sibling,
    for_line,
    from_line,
    own_total,
    sems,
):
    line = Line(n)
    at, length, me = line.at, line.length, line.me
    members, rows, _ = h_ref.shape
    width = w_ref.shape[-1]
    w = w_ref[...].reshape(-1, width)
    STAT, STAT_RECV, SIB, SIB_RECV, TO_LINE, LINE_RECV = range(6)
    sem = Semaphores(sems, members)
    column = me * width + lax.broadcasted_iota(jnp.int32, (rows, width), 1)
    real_column = column.astype(F32)
    words = up_to(rows, LANE)
    lane = lax.broadcasted_iota(jnp.int32, (rows, LANE), 1)
    aside = HP - LANE

    def pieces(b):
        tail = h_ref[b, :, aside:].astype(F32)
        first = H + 1 - aside
        target = tail[:, first : first + 1] * 256.0 + tail[:, first + 1 : first + 2]
        scale = (
            tail[:, first + 2 : first + 3]
            + tail[:, first + 3 : first + 4]
            + tail[:, first + 4 : first + 5]
        )
        return target, scale

    line.greet(False, True)

    def forward(b, _):
        h = h_ref[b]
        wide = dot(h, map_ref[...]).astype(BF)
        spread_back[b] = dot(h, map_back_ref[...]).astype(BF)
        now = jnp.where(column < vocab, dot(wide, w), -1e30)
        logits[b] = now
        target, _ = pieces(b)
        top = jnp.max(now, axis=1, keepdims=True)
        log_sum = top + jnp.log(jnp.sum(jnp.exp(now - top), axis=1, keepdims=True))
        picked = jnp.sum(jnp.where(real_column == target, now, 0.0), axis=1, keepdims=True)
        both = jnp.where(lane == 0, log_sum, jnp.where(lane == 1, picked, 0.0))
        both = jnp.concatenate([both, jnp.zeros((words - rows, LANE), F32)], axis=0).T
        stats[me, 0, pl.ds(b, 1), :] = both[0:1, :]
        stats[me, 1, pl.ds(b, 1), :] = both[1:2, :]
        return 0

    lax.fori_loop(0, members, forward, 0)

    def stat(member, target):
        here = stats.at[member]
        return remote(here, here, sem(STAT, member), sem(STAT_RECV, member), target)

    def stat_out(z):
        return [
            remote(
                stats.at[me], stats.at[me], sem(STAT, 2 * z + core), sem(STAT_RECV, me), target
            )
            for core, target in ((at.c, line.peer(z)), (1 - at.c, line.peer(z, True)))
        ]

    def send_stats(z):
        for copy in stat_out(z):
            copy.start()

    line.others(send_stats)
    to_pair = remote(
        stats.at[me], stats.at[me], sem(STAT, 2 * at.z + 1 - at.c), sem(STAT_RECV, me), at.sibling
    )
    to_pair.start()

    def stats_in(z):
        for core in (at.c, 1 - at.c):
            stat(2 * z + core, at.sibling).wait_recv()

    line.others(stats_in)
    stat(2 * at.z + 1 - at.c, at.sibling).wait_recv()
    top = stats[0, 0]
    for q in range(1, members):
        top = jnp.maximum(top, stats[q, 0])
    total = jnp.zeros_like(top)
    picked = jnp.zeros_like(top)
    for q in range(members):
        total += jnp.exp(stats[q, 0] - top)
        picked += stats[q, 1]
    log_total = top + jnp.log(total)
    loss_ref[...] = log_total - picked
    log_columns = jnp.concatenate(
        [log_total, jnp.zeros((LANE - members, words), F32)], axis=0
    ).T[:rows]

    def to_sibling(z):
        return remote(
            for_sibling.at[z], from_sibling.at[z], sem(SIB, z), sem(SIB_RECV, z), at.sibling
        )

    def to_line(z):
        return remote(
            for_line.at[z], from_line.at[at.z], sem(TO_LINE, z), sem(LINE_RECV, at.z), line.peer(z)
        )

    def backward(k, _):
        z = lax.rem(k, length)
        mine = k >= length
        b = 2 * z + jnp.where(mine, at.c, 1 - at.c)
        target, scale = pieces(b)
        log_sum = jnp.sum(jnp.where(lane == b, log_columns, 0.0), axis=1, keepdims=True)
        share = jnp.exp(logits[b] - log_sum)
        grad = ((share - (real_column == target).astype(F32)) * scale).astype(BF)
        grads[b] = grad
        back = dot_cols(grad, w)

        @pl.when(jnp.logical_not(mine))
        def _():
            for_sibling[z] = back.astype(BF)
            to_sibling(z).start()

        @pl.when(mine)
        def _():
            to_sibling(z).wait_recv()
            total = back + from_sibling[z].astype(F32)

            @pl.when(z == at.z)
            def _():
                own_total[...] = total

            @pl.when(z != at.z)
            def _():
                for_line[z] = total.astype(BF)
                to_line(z).start()

        return 0

    lax.fori_loop(0, 2 * length, backward, 0)

    depth = map_ref.shape[1]
    unit = 256
    everything = grads[...].reshape(members * rows, width)

    def weight_grad(m, _):
        left = spread_back[:, :, pl.ds(pl.multiple_of(m * unit, unit), unit)]
        result = dot_rows(left.reshape(members * rows, unit), everything).astype(BF)
        grad_w_ref[pl.ds(m * unit, unit), :] = result
        return 0

    lax.fori_loop(0, depth // unit, weight_grad, 0)

    def arrived(z):
        remote(
            from_line.at[z], from_line.at[z], sem(TO_LINE, z), sem(LINE_RECV, z), line.peer(z)
        ).wait_recv()
        own_total[...] += from_line[z].astype(F32)

    line.others(arrived)
    spread_grad = own_total[...]
    high = spread_grad.astype(BF)
    low = (spread_grad - high.astype(F32)).astype(BF)
    grad_h_ref[...] = dot_cols(high, map_ref[...]) + dot_cols(low, map_ref[...])

    def finish(z):
        for copy in stat_out(z):
            copy.wait_send()
        to_line(z).wait_send()

    line.others(finish)
    line.chips(lambda z: to_sibling(z).wait_send())
    to_pair.wait_send()


def word_softmax(plan, h, weights, mapping, mapping_back, collective_id):
    members, rows, depth = h.shape
    n = plan.fsdp
    spread = mapping.shape[1]
    per_slot, width = plan.block
    words = up_to(rows, LANE)
    length = members // 2
    vmem = pl.BlockSpec(memory_space=pltpu.VMEM)
    loss, grad_h, grad_w = pl.pallas_call(
        functools.partial(softmax_kernel, plan.width, n),
        out_shape=[
            jax.ShapeDtypeStruct((members, words), F32),
            jax.ShapeDtypeStruct((rows, depth), F32),
            jax.ShapeDtypeStruct((spread, width), BF),
        ],
        in_specs=[vmem] * 4,
        out_specs=[vmem] * 3,
        scratch_shapes=[
            pltpu.VMEM((members, rows, spread), BF),
            pltpu.VMEM((members, rows, width), F32),
            pltpu.VMEM((members, rows, width), BF),
            pltpu.VMEM((members, 2, members, words), F32),
            pltpu.VMEM((length, rows, spread), BF),
            pltpu.VMEM((length, rows, spread), BF),
            pltpu.VMEM((length, rows, spread), BF),
            pltpu.VMEM((length, rows, spread), BF),
            pltpu.VMEM((rows, spread), F32),
            pltpu.SemaphoreType.DMA((6 * members,)),
        ],
        compiler_params=pltpu.CompilerParams(
            collective_id=collective_id, has_side_effects=True, vmem_limit_bytes=62 * 2**20
        ),
    )(h, weights, mapping, mapping_back)
    return loss, grad_h, grad_w.reshape((n,) + plan.block)


def shards(
    fsdp_count,
    dp_count,
    chars,
    lengths,
    targets,
    resets,
    init_state,
    window_grad,
    char_table,
    conv_weight,
    conv_bias,
    highway_flat,
    lstm_flat,
    soft_flat,
):
    micro_count, streams, step_count, letters = chars.shape
    char_count, embed_dim = char_table.shape
    filters = conv_weight.shape[1]
    batch = micro_count * streams
    words = step_count * batch
    rows = up_to(words, 16)
    fp = up_to(filters + 1, LANE)
    dp_at, fsdp_at = lax.axis_index("dp"), lax.axis_index("fsdp")
    highway = Windows(
        highway_flat.shape[0] * fsdp_count, filters, 4 * (filters + 1), fsdp_count, dp_count, True
    )
    lstm = Windows(
        lstm_flat.shape[0] * fsdp_count, 4 * H, filters + H + 1, fsdp_count, dp_count, False
    )
    soft = Windows(
        soft_flat.shape[0] * fsdp_count, V, H + 1, fsdp_count, dp_count, False, fsdp_count // 2
    )
    member = 2 * (fsdp_at // 4) + lax.rem(dp_at, 2)

    def by_step(array):
        return jnp.moveaxis(array.reshape((batch, step_count) + array.shape[3:]), 1, 0).reshape(
            (words,) + array.shape[3:]
        )

    def pad_rows(array, value=0):
        return jnp.pad(
            array,
            [(0, rows - words)] + [(0, 0)] * (array.ndim - 1),
            constant_values=value,
        )

    word_chars = pad_rows(by_step(chars))
    word_lengths = pad_rows(by_step(lengths))[:, None]
    position = jnp.arange(letters, dtype=jnp.int32)[None, :]
    codes = jnp.where(position < word_lengths, word_chars, -1)
    codes = jnp.pad(codes, ((0, 0), (0, SLOTS - letters)), constant_values=-1)
    codes = codes.reshape(rows * SLOTS, 1)
    column = np.arange(fp)
    widths = np.ones((fp,), np.int32)
    for cut_at in FILTER_CUTS:
        widths = widths + ((column >= filters * cut_at // 22) & (column < filters))
    widths = widths.astype(np.int32)
    kernel_mask = jnp.asarray(
        np.arange(KMAX * embed_dim)[:, None] // embed_dim < widths[None, :filters]
    )
    ones_row = KMAX * embed_dim
    kernel = jnp.concatenate(
        [jnp.where(kernel_mask, conv_weight, jnp.zeros_like(conv_weight)), conv_bias[None, :]], axis=0
    )
    kernel = jnp.pad(kernel, ((0, LANE - ones_row - 1), (0, fp - filters)))
    spread_table = jnp.concatenate(
        [
            jnp.pad(char_table, ((0, 0), (q * embed_dim, LANE - (q + 1) * embed_dim)))
            for q in range(KMAX)
        ]
        + [jnp.asarray((np.arange(LANE) == ones_row)[None, :].astype(np.float32)).astype(BF)],
        axis=0,
    )
    spread_table = jnp.pad(spread_table, ((0, HOT - KMAX * char_count - 1), (0, 0)))
    conv_inputs = (codes, word_lengths, spread_table, kernel, jnp.asarray(widths)[None, :])

    highway_all, lstm_all, from_input, recur, soft_placed, *kept = head(
        [highway, lstm],
        soft,
        filters,
        place_all([highway, lstm], [highway_flat, lstm_flat]),
        conv_inputs,
        soft_flat,
        rows,
        fp,
        1,
    )
    features, trans, gates = kept[:3], kept[3:5], kept[5:7]

    soft_own = soft.from_placed(soft_placed)
    recur_t = recur.T
    keep = pad_rows(by_step(1 - resets).astype(F32))[:, None]
    start = init_state.reshape(batch, 2, H)
    start = jnp.pad(start, ((0, 8 - batch), (0, 0), (0, HP - H)))
    row_scale = jnp.broadcast_to(
        window_grad.reshape(1, batch) / step_count, (step_count, batch)
    ).reshape(words)
    goal = by_step(targets)
    scale_high = lax.reduce_precision(row_scale, 8, 7)
    scale_mid = lax.reduce_precision(row_scale - scale_high, 8, 7)
    extra = jnp.stack(
        [
            jnp.ones((words,), F32),
            (goal // 256).astype(F32),
            (goal % 256).astype(F32),
            scale_high,
            scale_mid,
            row_scale - scale_high - scale_mid,
        ],
        axis=1,
    )
    aside = H - (HP - LANE)
    extra = jnp.pad(extra, ((0, rows - words), (aside, LANE - aside - extra.shape[1])))
    *states, hidden_all, soft_part = lstm_forward(
        batch,
        soft,
        from_input,
        recur,
        start[:, 0].astype(BF).astype(F32),
        start[:, 1],
        keep,
        extra,
        soft_own,
        4,
    )
    hp = states[0]

    word_loss, grad_hidden, soft_grad = word_softmax(
        soft,
        hidden_all,
        soft_part,
        one_hot_map(HP, soft.gathered),
        one_hot_map(HP, soft.reduced),
        5,
    )
    word_loss = lax.dynamic_index_in_dim(word_loss, member, 0, keepdims=False)
    window_loss = jnp.mean(word_loss[:words].reshape(step_count, batch), axis=0).reshape(
        micro_count, streams
    )

    dz, soft_part = lstm_backward(
        batch, soft, lstm.columns, grad_hidden, recur_t, keep, states[1:], soft_grad, 6
    )
    hot_row, hot_lane = np.arange(HOT), np.arange(LANE)
    hot_mask = (hot_row[:, None] // char_count == hot_lane[None, :] // embed_dim) & (
        hot_row[:, None] < KMAX * char_count
    )
    hot_fold = (hot_row[None, :] % char_count == np.arange(LANE)[:, None]) & (
        hot_row[None, :] < KMAX * char_count
    )
    highway_grad, conv_grad, lstm_part = highway_backward(
        [highway, lstm],
        filters,
        dz,
        hp,
        features,
        trans,
        gates,
        (
            *conv_inputs,
            jnp.asarray(hot_mask.astype(np.float32)),
            jnp.asarray(hot_fold.astype(np.float32)),
        ),
        (highway_all, lstm_all),
        7,
    )
    conv = Dense(LANE, conv_grad.shape[1], fsdp_count)
    conv_grad, highway_part = tail([conv, highway], conv_grad, highway_grad, 3)
    conv_grad = jnp.concatenate(
        [conv_grad[h].reshape(-1, conv.block[1])[:LANE] for h in range(2)], axis=1
    )
    conv_weight_grad = jnp.where(kernel_mask, conv_grad[:ones_row, :filters], 0.0)
    conv_bias_grad = conv_grad[ones_row, :filters]
    table_grad = jnp.sum(
        conv_grad[:char_count, fp : fp + KMAX * embed_dim].reshape(char_count, KMAX, embed_dim), axis=1
    )

    def own_window(plan, part):
        if dp_count > 2:
            groups = [list(range(h, dp_count, 2)) for h in range(2)]
            part = lax.psum(part.astype(F32), "dp", axis_index_groups=groups)
        if plan.by_rows:
            at = dp_at // 2
        else:
            at = dp_at
            part = jnp.concatenate(
                [
                    lax.dynamic_slice_in_dim(part[p], at * plan.rows, plan.rows, 0)
                    for p in range(plan.parts)
                ],
                axis=1,
            ).astype(F32)
            return plan.to_flat(part, dp_at, fsdp_at)
        window = lax.dynamic_slice_in_dim(part, at * plan.rows, plan.rows, 0)
        return plan.to_flat(window, dp_at, fsdp_at)

    return (
        window_loss,
        table_grad,
        conv_weight_grad,
        conv_bias_grad,
        own_window(highway, highway_part),
        own_window(lstm, lstm_part),
        own_window(soft, soft_part),
    )


def solution(mesh):
    in_specs = (
        P(None, ("dp", "fsdp"), None, None),
        P(None, ("dp", "fsdp"), None),
        P(None, ("dp", "fsdp"), None),
        P(None, ("dp", "fsdp"), None),
        P(None, ("dp", "fsdp"), None, None),
        P(None, ("dp", "fsdp")),
        P(),
        P(),
        P(),
        P("fsdp", None),
        P("fsdp", None),
        P("fsdp", None),
    )
    out_specs = (
        P(None, ("dp", "fsdp")),
        P(),
        P(),
        P(),
        P(("dp", "fsdp"), None),
        P(("dp", "fsdp"), None),
        P(("dp", "fsdp"), None),
    )
    return jax.shard_map(
        functools.partial(shards, mesh.shape["fsdp"], mesh.shape["dp"]),
        mesh=mesh,
        in_specs=in_specs,
        out_specs=out_specs,
        check_vma=False,
    )
```

```python
import functools

import jax
import jax.numpy as jnp
import numpy as np
from jax import lax
from jax.experimental import pallas as pl
from jax.experimental.pallas import tpu as pltpu
from jax.sharding import PartitionSpec as P

H = 650
V = 10000
KMAX = 7
LANE = 128
HP = 768
SLOTS = 24
CHARS = 51
HOT = 384
FILTER_CUTS = (1, 3, 6, 10, 14, 18)
MESH = pl.DeviceIdType.MESH
BF = jnp.bfloat16
F32 = jnp.float32


def up_to(value, unit):
    return -(-value // unit) * unit


def dot(left, right):
    return jnp.dot(left, right, preferred_element_type=F32)


def dot_rows(left, right):
    return lax.dot_general(left, right, (((0,), (0,)), ((), ())), preferred_element_type=F32)


def dot_cols(left, right):
    return lax.dot_general(left, right, (((1,), (1,)), ((), ())), preferred_element_type=F32)


class Windows:
    dtype = BF

    def __init__(self, flat_rows, width, used, fsdp, dp, by_rows, parts=2):
        owners = fsdp * dp
        self.parts = parts
        self.width, self.by_rows, self.fsdp, self.dp, self.used = width, by_rows, fsdp, dp, used
        self.entries = flat_rows * LANE // owners
        self.starts = [o * self.entries // width for o in range(owners)]
        self.spans = [
            (o * self.entries % width + self.entries - 1) // width + 1 for o in range(owners)
        ]
        unit = 16 if by_rows else 8
        rows = up_to(max(self.spans), unit)
        while (dp * rows) % 16:
            rows += unit
        self.rows = rows
        self.total = owners * rows
        self.columns = up_to(width, LANE) if by_rows else parts * up_to(-(-width // parts), LANE)
        self.block = (
            (dp // 2 * rows, self.columns) if by_rows else (dp * rows, self.columns // parts)
        )
        self.shape = (
            (self.total, self.columns)
            if by_rows
            else (parts, self.total, self.columns // parts)
        )
        if by_rows:
            order = [
                (2 * jj + h) * fsdp + f
                for f in range(fsdp)
                for h in range(2)
                for jj in range(dp // 2)
            ]
        else:
            order = [d * fsdp + f for f in range(fsdp) for d in range(dp)]
        self.position = [order.index(o) for o in range(owners)]
        self.gathered = self.row_map(range(owners))
        self.reduced = self.row_map(order)

    def row_map(self, order):
        rows_of = [
            [
                self.starts[o] + i if i < self.spans[o] and self.starts[o] + i < self.used else -1
                for i in range(self.rows)
            ]
            for o in order
        ]
        return np.array(rows_of, np.int32).reshape(-1)

    def pick(self, ref, half, slot):
        depth = self.block[0]
        if self.by_rows:
            return ref.at[pl.ds(pl.multiple_of((2 * slot + half) * depth, 16), depth)]
        return ref.at[half, pl.ds(pl.multiple_of(slot * depth, 16), depth)]

    def meeting(self, begin, end):
        found = []
        for o, (start, span) in enumerate(zip(self.starts, self.spans)):
            first, last = max(0, begin - start), min(span, end - start)
            if first < last:
                found.append((o, first, last))
        return found

    @property
    def lines(self):
        return up_to(-(-self.rows * self.width // LANE), 16) + 32

    def place_blocks(self, shard_ref, out_ref):
        fsdp_at = lax.axis_index("fsdp")
        count = self.entries // LANE
        out_ref[...] = jnp.zeros_like(out_ref)
        for j in range(self.dp):
            shift = lax.rem((fsdp_at * self.dp + j) * self.entries, self.width)
            lanes, lines = lax.rem(shift, LANE), lax.rem(shift // LANE, 16)
            block = shard_ref[j].astype(F32)
            extra = up_to(count, 16) + 16 - count
            block = jnp.concatenate([block, jnp.zeros((extra, LANE), F32)], axis=0)
            block = pltpu.roll(block, lanes, 1)
            lane = lax.broadcasted_iota(jnp.int32, block.shape, 1)
            block = jnp.where(lane < lanes, pltpu.roll(block, 1, 0), block)
            for step in (1, 2, 4, 8):
                moved = lax.rem(lines // step, 2) == 1
                block = jnp.where(moved, pltpu.roll(block, step, 0), block)
            begin = pl.multiple_of(shift // (16 * LANE) * 16, 16)
            out_ref[j, pl.ds(begin, count + extra), :] = block.astype(BF)

    def placed_shape(self):
        return jax.ShapeDtypeStruct((self.dp, self.lines, LANE), BF)

    def blocks_of(self, shard):
        return shard.reshape(self.dp, self.entries // LANE, LANE)

    def from_placed(self, placed):
        size = self.rows * self.width
        joined = jnp.concatenate(
            [
                jnp.pad(
                    placed[j].reshape(-1)[:size].reshape(self.rows, self.width),
                    ((0, 0), (0, self.columns - self.width)),
                )
                for j in range(self.dp)
            ],
            axis=0,
        )
        if self.by_rows:
            return joined.reshape((2,) + self.block)
        part = self.columns // self.parts
        return jnp.stack([joined[:, p * part : (p + 1) * part] for p in range(self.parts)])

    def to_flat(self, window, dp_at, fsdp_at):
        shift = lax.rem((dp_at * self.fsdp + fsdp_at) * self.entries, self.width)
        flat = window[:, : self.width].reshape(-1)
        return lax.dynamic_slice(flat, (shift,), (self.entries,)).reshape(-1, LANE)


def one_hot_map(rows, row_map):
    return (
        lax.broadcasted_iota(jnp.int32, (rows, row_map.shape[0]), 0) == jnp.asarray(row_map)[None, :]
    ).astype(BF)


class Place:
    def __init__(self):
        self.d, self.f = lax.axis_index("dp"), lax.axis_index("fsdp")
        self.c = lax.rem(self.d, 2)
        x, y, self.z = lax.rem(self.f, 2), lax.rem(self.f // 2, 2), self.f // 4
        self.first = x + self.c * (y - x)
        self.last = y + self.c * (x - y)
        self.stride1, self.stride3 = 1 + self.c, 2 - self.c
        self.flip1 = self.stride1 * (1 - 2 * self.first)
        self.flip3 = self.stride3 * (1 - 2 * self.last)
        self.partner1 = (self.d, self.f + self.flip1)
        self.partner3 = (self.d, self.f + self.flip3)
        self.sibling = (self.d + 1 - 2 * self.c, self.f)

    def last_bit(self, block):
        bit_x, bit_y = lax.rem(block, 2), lax.rem(block // 2, 2)
        return bit_y + self.c * (bit_x - bit_y)


def remote(src, dst, send, recv, target):
    return pltpu.make_async_remote_copy(
        src_ref=src,
        dst_ref=dst,
        send_sem=send,
        recv_sem=recv,
        device_id=target,
        device_id_type=MESH,
    )


class Line:
    def __init__(self, n):
        self.at = Place()
        self.length = n // 4
        self.me = 2 * self.at.z + self.at.c

    def peer(self, z, other_core=False):
        at = self.at
        return (at.d + (1 - 2 * at.c if other_core else 0), at.f + 4 * (z - at.z))

    def column(self, z):
        return self.at.f + 4 * (z - self.at.z)

    def others(self, body):
        def step(z, _):
            pl.when(z != self.at.z)(functools.partial(body, z))
            return 0

        lax.fori_loop(0, self.length, step, 0)

    def chips(self, body):
        def step(z, _):
            body(z)
            return 0

        lax.fori_loop(0, self.length, step, 0)

    def far(self, k):
        z = jnp.int32(0)
        for here in range(self.length):
            order = sorted(range(self.length), key=lambda there: (-abs(there - here), there))
            for i, there in enumerate(order):
                z = jnp.where((self.at.z == here) & (k == i), there, z)
        return z

    def greet(self, across=True, both_cores=False):
        barrier = pltpu.get_barrier_semaphore()

        def signal(target):
            pl.semaphore_signal(barrier, inc=1, device_id=target, device_id_type=MESH)

        signal(self.at.sibling)
        count = 1
        if across:
            signal(self.at.partner1)
            signal(self.at.partner3)
            count += 2

        def chip(z):
            signal(self.peer(z))
            if both_cores:
                signal(self.peer(z, True))

        self.others(chip)
        pl.semaphore_wait(barrier, count + (self.length - 1) * (2 if both_cores else 1))


class Semaphores:
    def __init__(self, ref, size):
        self.ref, self.size = ref, size

    def __call__(self, kind, index):
        return self.ref.at[kind * self.size + index]


class Gather:
    RECV, SIB_RECV, LINE, NEAR, LAST, SIB, LOCAL = range(7)

    def __init__(self, plans, own, outs, sems, shared):
        self.plans, self.own, self.outs, self.sems, self.shared = plans, own, outs, sems, shared
        self.n = plans[0].fsdp
        self.line = Line(self.n)
        self.at = self.line.at

    @staticmethod
    def semaphores(plans):
        return pltpu.SemaphoreType.DMA((7 * len(plans) * plans[0].fsdp,))

    def sem(self, kind, a, index):
        return self.sems.at[(kind * len(self.plans) + a) * self.n + index]

    def source(self, a, half):
        return self.own[a].at[half] if self.shared else self.own[a]

    def copy(self, kind, a, index, block, target, own=False):
        here = self.plans[a].pick(self.outs[a], self.at.c, block)
        return remote(
            self.source(a, self.at.c) if own else here,
            here,
            self.sem(kind, a, index),
            self.sem(self.SIB_RECV if kind == self.SIB else self.RECV, a, block),
            target,
        )

    def arrived(self, a, block, kind=RECV):
        c = self.at.c
        here = self.plans[a].pick(self.outs[a], 1 - c if kind == self.SIB_RECV else c, block)
        remote(
            here, here, self.sem(self.SIB, a, block), self.sem(kind, a, block), self.at.sibling
        ).wait_recv()

    def local(self, a, half):
        return pltpu.make_async_copy(
            self.source(a, half),
            self.plans[a].pick(self.outs[a], half, self.at.f),
            self.sem(self.LOCAL, a, half if self.shared else 0),
        )

    def to_sibling(self, a, block, own=False):
        return self.copy(self.SIB, a, block, block, self.at.sibling, own)

    def begin(self, a):
        at, line = self.at, self.line
        line.others(lambda z: self.copy(self.LINE, a, z, at.f, line.peer(z), True).start())
        self.copy(self.NEAR, a, at.z, at.f, at.partner1, True).start()
        self.copy(self.LAST, a, at.z, at.f, at.partner3, True).start()
        if self.shared:
            for half in (0, 1):
                self.local(a, half).start()
        else:
            self.to_sibling(a, at.f, True).start()
            self.local(a, at.c).start()

    def from_line(self, a):
        at, line = self.at, self.line

        def chip(z):
            block = line.column(z)
            self.arrived(a, block)
            self.copy(self.NEAR, a, z, block, at.partner1).start()
            self.copy(self.LAST, a, z, block, at.partner3).start()
            self.to_sibling(a, block).start()

        line.others(chip)

    def from_near(self, a):
        line = self.line

        def chip(k):
            z = lax.rem(self.at.z + k, line.length)
            block = line.column(z) + self.at.flip1
            self.arrived(a, block)
            self.copy(self.LAST, a, line.length + z, block, self.at.partner3).start()
            self.to_sibling(a, block).start()

        line.chips(chip)

    def from_last(self, a):
        line = self.line

        def chip(k):
            z = lax.rem(self.at.z + k, line.length)
            block = line.column(z) + self.at.flip3
            self.arrived(a, block)
            self.to_sibling(a, block).start()

        def chip_near(k):
            z = lax.rem(self.at.z + k, line.length)
            block = line.column(z) + self.at.flip1 + self.at.flip3
            self.arrived(a, block)
            self.to_sibling(a, block).start()

        line.chips(chip)
        line.chips(chip_near)

    def from_sibling(self, a):
        def block_in(block, _):
            if self.shared:

                @pl.when(jnp.logical_not(block == self.at.f))
                def _():
                    self.arrived(a, block, self.SIB_RECV)

            else:
                self.arrived(a, block, self.SIB_RECV)
            return 0

        lax.fori_loop(0, self.n, block_in, 0)
        if self.shared:
            for half in (0, 1):
                self.local(a, half).wait()
        else:
            self.local(a, self.at.c).wait()

    def finish(self, a):
        at, line = self.at, self.line

        def sent(kind, index):
            self.copy(kind, a, index, at.f, at.sibling).wait_send()

        def chip(z):
            sent(self.NEAR, z)
            sent(self.LAST, z)
            sent(self.LAST, line.length + z)

        line.chips(chip)
        line.others(lambda z: sent(self.LINE, z))

        def block_done(block, _):
            if self.shared:
                pl.when(jnp.logical_not(block == at.f))(lambda: sent(self.SIB, block))
            else:
                sent(self.SIB, block)
            return 0

        lax.fori_loop(0, self.n, block_done, 0)


class Reduce:
    SIB, SIB_RECV, LOAD, NEAR, NEAR_RECV, CROSS, CROSS_RECV, LINE, LINE_RECV, STAGE = range(10)

    def __init__(self, plans, ins, totals, landed, scratch, in_place):
        count = len(plans)
        self.plans, self.ins, self.totals, self.in_place = plans, ins, totals, in_place
        scratch = list(scratch)
        self.held = [None if here else scratch.pop(0) for here in in_place]
        self.staged = [ref is not None for ref in landed]
        self.stage = [scratch.pop(0) if far else None for far in self.staged]
        self.landed = [scratch.pop(0) if ref is None else ref for ref in landed]
        self.close, self.cross, self.lined = (
            scratch[k * count : (k + 1) * count] for k in range(3)
        )
        self.sems = scratch[3 * count]
        self.n = plans[0].fsdp
        self.line = Line(self.n)
        self.at = self.line.at
        self.items = 2 * self.line.length

    @staticmethod
    def scratch(plans, in_place, staged):
        def buffers(size, kept=None):
            return [
                pltpu.VMEM((size,) + plan.block, plan.dtype)
                for a, plan in enumerate(plans)
                if kept is None or kept[a]
            ]

        n = plans[0].fsdp
        return (
            buffers(n, [not here for here in in_place])
            + buffers(2, staged)
            + buffers(n, [not far for far in staged])
            + buffers(n // 2)
            + buffers(n // 4) * 2
            + [pltpu.SemaphoreType.DMA((10 * len(plans) * n,))]
        )

    def sem(self, kind, a, index):
        return self.sems.at[(kind * len(self.plans) + a) * self.n + index]

    def slot(self, z, b1, b3):
        return 4 * z + self.at.stride1 * b1 + self.at.stride3 * b3

    def item(self, t):
        length = self.line.length
        ours = t >= length
        z = self.line.far(t - length * jnp.int32(ours))
        return z, jnp.where(ours, self.at.last, 1 - self.at.last)

    def hold(self, a, block):
        if self.in_place[a]:
            return self.plans[a].pick(self.ins[a], self.at.c, block)
        return self.held[a].at[block]

    def to_sibling(self, a, block):
        return remote(
            self.plans[a].pick(self.ins[a], 1 - self.at.c, block),
            self.landed[a].at[block],
            self.sem(self.SIB, a, block),
            self.sem(self.SIB_RECV, a, block),
            self.at.sibling,
        )

    def load(self, a, block):
        return pltpu.make_async_copy(
            self.plans[a].pick(self.ins[a], self.at.c, block),
            self.held[a].at[block],
            self.sem(self.LOAD, a, block),
        )

    def to_near(self, a, z, b3):
        return remote(
            self.hold(a, self.slot(z, 1 - self.at.first, b3)),
            self.close[a].at[2 * z + b3],
            self.sem(self.NEAR, a, 2 * z + b3),
            self.sem(self.NEAR_RECV, a, 2 * z + b3),
            self.at.partner1,
        )

    def to_cross(self, a, z):
        return remote(
            self.hold(a, self.slot(z, self.at.first, 1 - self.at.last)),
            self.cross[a].at[z],
            self.sem(self.CROSS, a, z),
            self.sem(self.CROSS_RECV, a, z),
            self.at.partner3,
        )

    def to_line(self, a, z):
        return remote(
            self.hold(a, self.slot(z, self.at.first, self.at.last)),
            self.lined[a].at[self.at.z],
            self.sem(self.LINE, a, z),
            self.sem(self.LINE_RECV, a, self.at.z),
            self.line.peer(z),
        )

    def line_arrived(self, a, z):
        here = self.lined[a].at[z]
        remote(
            here, here, self.sem(self.LINE, a, z), self.sem(self.LINE_RECV, a, z), self.line.peer(z)
        ).wait_recv()

    def rows(self, a, body):
        unit = 16

        def step(i, _):
            body(pl.ds(pl.multiple_of(i * unit, unit), unit))
            return 0

        if self.plans[a].block[0] < unit:
            body(slice(None))
        else:
            lax.fori_loop(0, self.plans[a].block[0] // unit, step, 0)

    def add(self, a, block, sources):
        held = self.hold(a, block)

        def body(where):
            total = held[where, :].astype(F32)
            for ref, at in sources:
                total += ref[at, where, :].astype(F32)
            held[where, :] = total.astype(held.dtype)

        self.rows(a, body)

    def begin(self, a):
        for flip in (1, 0):
            b1 = self.at.first + flip * (1 - 2 * self.at.first)

            def start(t, _, b1=b1):
                z, b3 = self.item(t)
                block = self.slot(z, b1, b3)
                self.to_sibling(a, block).start()
                if not self.in_place[a]:
                    self.load(a, block).start()
                return 0

            lax.fori_loop(0, self.items, start, 0)

    def in_order(self, q):
        late = jnp.int32(q >= self.items)
        z, b3 = self.item(q - self.items * late)
        return self.slot(z, (1 - self.at.first) + late * (2 * self.at.first - 1), b3)

    def to_stage(self, a, q):
        k = lax.rem(q, 2)
        return pltpu.make_async_copy(
            self.landed[a].at[self.in_order(q)], self.stage[a].at[k], self.sem(self.STAGE, a, k)
        )

    def ready(self, a, block, q):
        if not self.in_place[a]:
            self.load(a, block).wait()
        if not self.staged[a]:
            self.to_sibling(a, block).wait_recv()
            return self.landed[a], block

        @pl.when(q == 0)
        def _():
            self.to_sibling(a, block).wait_recv()
            self.to_stage(a, q).start()

        self.to_stage(a, q).wait()

        @pl.when(q + 1 < 2 * self.items)
        def _():
            self.to_sibling(a, self.in_order(q + 1)).wait_recv()
            self.to_stage(a, q + 1).start()

        return self.stage[a], lax.rem(q, 2)

    def first_leg(self, a, t):
        z, b3 = self.item(t)
        block = self.slot(z, 1 - self.at.first, b3)
        self.add(a, block, [self.ready(a, block, t)])
        self.to_near(a, z, b3).start()

    def middle_leg(self, a, t):
        z, b3 = self.item(t)
        block = self.slot(z, self.at.first, b3)
        sources = [self.ready(a, block, self.items + t), (self.close[a], 2 * z + b3)]
        self.to_near(a, z, b3).wait_recv()

        @pl.when(t < self.line.length)
        def _():
            self.add(a, block, sources)
            self.to_cross(a, z).start()

        @pl.when(t >= self.line.length)
        def _():
            self.to_cross(a, z).wait_recv()
            self.add(a, block, sources + [(self.cross[a], z)])

            @pl.when(z != self.at.z)
            def _():
                self.to_line(a, z).start()

    def legs(self, body, a, begin, end):
        def step(t, _):
            body(a, t)
            return 0

        lax.fori_loop(begin, end, step, 0)

    def last_leg(self, a):
        block = self.slot(self.at.z, self.at.first, self.at.last)

        def body(where):
            self.totals[a][where, :] = self.hold(a, block)[where, :].astype(F32)

        self.rows(a, body)

        def chip(z):
            self.line_arrived(a, z)

            def body(where):
                self.totals[a][where, :] += self.lined[a][z, where, :].astype(F32)

            self.rows(a, body)

        self.line.others(chip)

    def finish(self, a):
        def done(t, _):
            z, b3 = self.item(t)
            for b1 in (self.at.first, 1 - self.at.first):
                self.to_sibling(a, self.slot(z, b1, b3)).wait_send()
            self.to_near(a, z, b3).wait_send()
            return 0

        lax.fori_loop(0, self.items, done, 0)
        self.line.chips(lambda z: self.to_cross(a, z).wait_send())
        self.line.others(lambda z: self.to_line(a, z).wait_send())


def reduce_out(plan):
    return jax.ShapeDtypeStruct(plan.block if plan.by_rows else (2,) + plan.block, F32)


def hot_rows(codes):
    count = codes.shape[0]
    slot = lax.rem(lax.broadcasted_iota(jnp.int32, (count, 1), 0), SLOTS)
    lane = lax.broadcasted_iota(jnp.int32, (count, HOT), 1)
    hit = lane == KMAX * CHARS
    for q in range(KMAX):
        moved = codes if q == 0 else pltpu.roll(codes, count - q, 0)
        moved = jnp.where((moved >= 0) & (slot + q < SLOTS), moved + q * CHARS, -1)
        hit = jnp.logical_or(hit, lane == moved)
    return hit.astype(F32).astype(BF)


def conv_forward_block(filters, codes, lengths, refs, out_ref, where):
    table_ref, kernel_ref, width_ref = refs
    words = lengths.shape[0]
    windows = dot(hot_rows(codes), table_ref[...]).astype(BF)
    chunk = 384
    for at in range(0, kernel_ref.shape[1], chunk):
        columns = slice(at, at + chunk)
        activated = jnp.tanh(dot(windows, kernel_ref[:, columns])).reshape(words, SLOTS, chunk)
        counts = jnp.maximum(lengths - width_ref[:, columns] + 1, 1)
        position = lax.broadcasted_iota(jnp.int32, (words, SLOTS, chunk), 1)
        inside = position < counts[:, None, :]
        totals = jnp.sum(jnp.where(inside, jnp.exp(activated), 0.0), axis=1)
        pooled = jnp.log(totals) - jnp.log(counts.astype(F32))
        lane = at + lax.broadcasted_iota(jnp.int32, (words, chunk), 1)
        out_ref[where, columns] = keep_feature(pooled, lane, filters)


def keep_feature(value, lane, filters):
    value = value.astype(BF).astype(F32)
    return jnp.where(lane < filters, value, jnp.where(lane == filters, 1.0, 0.0))


def conv_backward_block(codes, lengths, refs, grad_ref, where, kernel_grad_ref, hot_grad_ref):
    table_ref, kernel_ref, width_ref = refs
    words = lengths.shape[0]
    hot = hot_rows(codes)
    windows = dot(hot, table_ref[...]).astype(BF)
    chunk = 384
    grad_windows = jnp.zeros(windows.shape, F32)
    for at in range(0, kernel_ref.shape[1], chunk):
        columns = slice(at, at + chunk)
        activated = jnp.tanh(dot(windows, kernel_ref[:, columns])).reshape(words, SLOTS, chunk)
        counts = jnp.maximum(lengths - width_ref[:, columns] + 1, 1)
        position = lax.broadcasted_iota(jnp.int32, (words, SLOTS, chunk), 1)
        inside = position < counts[:, None, :]
        weight = jnp.where(inside, jnp.exp(activated), 0.0)
        share = grad_ref[where, columns] / jnp.sum(weight, axis=1)
        grad = (share[:, None, :] * weight * (1.0 - activated * activated)).astype(BF)
        grad = grad.reshape(words * SLOTS, chunk)
        kernel_grad_ref[:, columns] += dot_rows(windows, grad)
        grad_windows += dot_cols(grad, kernel_ref[:, columns])
    hot_grad_ref[...] += dot_rows(hot, grad_windows.astype(BF))


def place_kernel(plans, *refs):
    for plan, shard, out in zip(plans, refs[: len(plans)], refs[len(plans) :]):
        plan.place_blocks(shard, out)


def place_all(plans, shards):
    vmem = pl.BlockSpec(memory_space=pltpu.VMEM)
    placed = pl.pallas_call(
        functools.partial(place_kernel, plans),
        out_shape=[plan.placed_shape() for plan in plans],
        in_specs=[vmem] * len(plans),
        out_specs=[vmem] * len(plans),
        compiler_params=pltpu.CompilerParams(vmem_limit_bytes=48 * 2**20),
    )(*[plan.blocks_of(shard) for plan, shard in zip(plans, shards)])
    return [plan.from_placed(each) for plan, each in zip(plans, placed)]


class Dense:
    by_rows = False
    dtype = F32

    def __init__(self, rows, columns, fsdp):
        self.fsdp = fsdp
        self.filled = rows
        self.block = (up_to(-(-rows // fsdp), 8), columns // 2)
        self.shape = (2, fsdp) + self.block

    def pick(self, ref, half, slot):
        return ref.at[half, slot]

    def fill(self, slots, source):
        slots[...] = jnp.zeros_like(slots)
        depth, half = self.block
        for block in range(self.filled // depth):
            for h in range(2):
                slots[h, block] = source[
                    block * depth : (block + 1) * depth, h * half : (h + 1) * half
                ]


WORD_BLOCK = 16


def tail_kernel(plans, conv_ref, grad_ref, conv_out, total_out, conv_in, conv_total, gather_sems, *scratch):
    conv, highway = plans
    work = Reduce(
        plans,
        [conv_in, grad_ref],
        [conv_total, total_out],
        [None, None],
        scratch,
        [True, False],
    )
    items, half_way = work.items, work.line.length
    work.line.greet()
    conv.fill(conv_in, conv_ref)
    work.begin(0)
    work.begin(1)

    work.legs(work.first_leg, 0, 0, items)
    work.legs(work.first_leg, 1, 0, half_way)
    work.legs(work.middle_leg, 0, 0, half_way)
    work.legs(work.first_leg, 1, half_way, items)
    work.legs(work.middle_leg, 0, half_way, items)
    work.legs(work.middle_leg, 1, 0, 1)
    work.last_leg(0)
    spread = Gather([conv], [conv_total], [conv_out], gather_sems, False)
    spread.begin(0)
    work.legs(work.middle_leg, 1, 1, half_way)
    spread.from_line(0)
    spread.from_near(0)
    work.legs(work.middle_leg, 1, half_way, items)
    spread.from_last(0)
    work.last_leg(1)
    spread.from_sibling(0)
    spread.finish(0)
    for a in range(2):
        work.finish(a)


def tail(plans, conv_grad, highway_grad, collective_id):
    conv, highway = plans
    vmem = pl.BlockSpec(memory_space=pltpu.VMEM)
    return pl.pallas_call(
        functools.partial(tail_kernel, plans),
        out_shape=[
            jax.ShapeDtypeStruct(conv.shape, F32),
            jax.ShapeDtypeStruct(highway.block, F32),
        ],
        in_specs=[vmem, pl.BlockSpec(memory_space=pl.ANY)],
        out_specs=[vmem] * 2,
        scratch_shapes=[
            pltpu.VMEM(conv.shape, F32),
            pltpu.VMEM(conv.block, F32),
            Gather.semaphores([conv]),
        ]
        + Reduce.scratch(plans, [True, False], [False, False]),
        compiler_params=pltpu.CompilerParams(
            collective_id=collective_id, has_side_effects=True, vmem_limit_bytes=48 * 2**20
        ),
    )(conv_grad, highway_grad)


def gate_parts(sums):
    parts = [sums[:, :HP]]
    for g in range(1, 4):
        begin = g * H // LANE * LANE
        moved = sums[:, begin : begin + HP + LANE]
        parts.append(pltpu.roll(moved, HP + LANE - (g * H - begin), 1)[:, :HP])
    return parts


def join_gates(parts, columns):
    rows = parts[0].shape[0]
    total = None
    for g, part in enumerate(parts):
        begin = g * H // LANE * LANE
        wide = jnp.concatenate([part, jnp.zeros((rows, LANE), F32)], axis=1)
        if g * H - begin:
            wide = pltpu.roll(wide, g * H - begin, 1)
        pieces = [wide]
        if begin:
            pieces = [jnp.zeros((rows, begin), F32)] + pieces
        if columns - begin - HP - LANE > 0:
            pieces = pieces + [jnp.zeros((rows, columns - begin - HP - LANE), F32)]
        placed = jnp.concatenate(pieces, axis=1)[:, :columns]
        total = placed if total is None else total + placed
    return total


HIDDEN_CHUNKS = ((0, 48), (48, 96), (96, 128), (128, 144))


def hidden_chunks(rows):
    return [(a, min(b, rows)) for a, b in HIDDEN_CHUNKS if a < rows] + (
        [(HIDDEN_CHUNKS[-1][1], rows)] if rows > HIDDEN_CHUNKS[-1][1] else []
    )


def lstm_forward_kernel(
    batch, n, x_ref, w_ref, h0_ref, c0_ref, keep_ref, extra_ref, own_ref, *refs
):
    hp_ref, cp_ref, i_ref, f_ref, u_ref, o_ref, t_ref, hall_ref, part_ref = refs[:9]
    hidden, soft_sems, hidden_sems = refs[9:]
    line = Line(n)
    at, length = line.at, line.length
    rows_all = x_ref.shape[0]
    chunks = hidden_chunks(rows_all)
    RECV, TO_LINE, TO_NEAR, TO_LAST, LOCAL = range(5)
    sem = Semaphores(soft_sems, n)
    H_RECV, H_LINE, H_SIB = range(3)
    hsem = Semaphores(hidden_sems, 2 * length * len(chunks))

    def column(z):
        return at.f + 4 * (z - at.z)

    def to_line(z):
        return remote(
            own_ref.at[2 * z + at.c],
            part_ref.at[at.f],
            sem(TO_LINE, z),
            sem(RECV, at.f),
            line.peer(z),
        )

    def pass_on(kind, index, slot, target, own=False):
        return remote(
            own_ref.at[line.me] if own else part_ref.at[slot],
            part_ref.at[slot],
            sem(kind, index),
            sem(RECV, slot),
            target,
        )

    def landed(slot):
        pass_on(TO_NEAR, 0, slot, at.partner1).wait_recv()

    local = pltpu.make_async_copy(own_ref.at[line.me], part_ref.at[at.f], sem(LOCAL, 0))

    def event_begin():
        line.others(lambda z: to_line(z).start())
        pass_on(TO_NEAR, at.z, at.f, at.partner1, True).start()
        pass_on(TO_LAST, at.z, at.f, at.partner3, True).start()
        local.start()

    def event_line():
        def chip(z):
            landed(column(z))
            pass_on(TO_NEAR, z, column(z), at.partner1).start()
            pass_on(TO_LAST, z, column(z), at.partner3).start()

        line.others(chip)

    def event_near():
        def chip(z):
            slot = column(z) + at.flip1
            landed(slot)
            pass_on(TO_LAST, length + z, slot, at.partner3).start()

        line.chips(chip)

    def event_end():
        def chip(z):
            landed(column(z) + at.flip3)
            landed(column(z) + at.flip1 + at.flip3)
            pass_on(TO_NEAR, z, column(z), at.partner1).wait_send()
            pass_on(TO_LAST, z, column(z), at.partner3).wait_send()
            pass_on(TO_LAST, length + z, column(z), at.partner3).wait_send()

        line.chips(chip)
        line.others(lambda z: to_line(z).wait_send())
        local.wait()

    def chunk_copy(k, member, kind, index, target):
        begin, end = chunks[k]
        here = hall_ref.at[member, pl.ds(begin, end - begin), :]
        return remote(
            here,
            here,
            hsem(kind, index * len(chunks) + k),
            hsem(H_RECV, member * len(chunks) + k),
            target,
        )

    def chunk_out(k):
        begin, end = chunks[k]
        hall_ref[line.me, begin:end, :] = hidden[begin:end, :].astype(BF)
        line.others(lambda z: chunk_copy(k, line.me, H_LINE, z, line.peer(z)).start())
        chunk_copy(k, line.me, H_SIB, at.z, at.sibling).start()

    def chunk_pass(k):
        def chip(z):
            member = 2 * z + at.c
            chunk_copy(k, member, H_SIB, z, at.sibling).wait_recv()
            chunk_copy(k, member, H_SIB, z, at.sibling).start()

        line.others(chip)

    def chunk_end(k):
        def chip(z):
            chunk_copy(k, 2 * z + 1 - at.c, H_SIB, z, at.sibling).wait_recv()
            chunk_copy(k, 2 * z + at.c, H_SIB, z, at.sibling).wait_send()

        line.chips(chip)
        line.others(lambda z: chunk_copy(k, line.me, H_LINE, z, line.peer(z)).wait_send())

    line.greet(True, False)
    event_begin()
    per_tile = 8 // batch
    tiles = rows_all // 8
    row = lax.broadcasted_iota(jnp.int32, (8, HP), 0)
    lane = lax.broadcasted_iota(jnp.int32, (8, LANE), 1)
    last = HP - LANE

    def tile(step, carried):
        h, c = carried
        rows = pl.ds(pl.multiple_of(step * 8, 8), 8)
        x = x_ref[rows, :]
        keep = keep_ref[rows, :]
        saved = None
        for part in range(per_tile):
            hp, cp = h * keep, c * keep
            sums = x + dot(hp.astype(BF), w_ref[...])
            i, f, u, o = gate_parts(sums)
            i, f, u, o = jax.nn.sigmoid(i), jax.nn.sigmoid(f), jnp.tanh(u), jax.nn.sigmoid(o)
            c = f * cp + i * u
            t = jnp.tanh(c)
            h = (o * t).astype(BF).astype(F32)
            now = (hp, cp, i, f, u, o, t, h)
            if saved is None:
                saved = now
            else:
                saved = tuple(jnp.where(row >= part * batch, b, a) for a, b in zip(saved, now))
            h, c = pltpu.roll(h, batch, 0), pltpu.roll(c, batch, 0)
        for ref, value in zip((hp_ref, cp_ref, i_ref, f_ref, u_ref, o_ref, t_ref), saved):
            ref[rows, :] = value
        hidden[rows, :last] = saved[-1][:, :last]
        hidden[rows, last:] = jnp.where(lane < H - last, saved[-1][:, last:], extra_ref[rows, :])

        pl.when(step == tiles // 3)(event_line)
        pl.when(step == tiles * 2 // 3)(event_near)
        for k, (_, end) in enumerate(chunks):
            pl.when(step == end // 8 - 1)(functools.partial(chunk_out, k))
        return h, c

    lax.fori_loop(0, tiles, tile, (h0_ref[...], c0_ref[...]))
    for k in range(len(chunks)):
        chunk_pass(k)
    event_end()
    for k in range(len(chunks)):
        chunk_end(k)


def lstm_forward(batch, plan, x, recur, h0, c0, keep, extra, own, collective_id):
    rows, n = x.shape[0], plan.fsdp
    members = plan.parts
    chunks = len(hidden_chunks(rows))
    vmem = pl.BlockSpec(memory_space=pltpu.VMEM)
    anywhere = pl.BlockSpec(memory_space=pl.ANY)
    return pl.pallas_call(
        functools.partial(lstm_forward_kernel, batch, n),
        out_shape=[jax.ShapeDtypeStruct((rows, HP), F32)] * 7
        + [
            jax.ShapeDtypeStruct((members, rows, HP), BF),
            jax.ShapeDtypeStruct((n,) + plan.block, BF),
        ],
        in_specs=[vmem] * 6 + [anywhere],
        out_specs=[vmem] * 8 + [anywhere],
        scratch_shapes=[
            pltpu.VMEM((rows, HP), F32),
            pltpu.SemaphoreType.DMA((5 * n,)),
            pltpu.SemaphoreType.DMA((3 * members * chunks,)),
        ],
        compiler_params=pltpu.CompilerParams(
            collective_id=collective_id, has_side_effects=True, vmem_limit_bytes=48 * 2**20
        ),
    )(x, recur, h0, c0, keep, extra, own)


def lstm_backward_kernel(
    batch,
    n,
    dh_ref,
    w_ref,
    keep_ref,
    cp_ref,
    i_ref,
    f_ref,
    u_ref,
    o_ref,
    t_ref,
    grad_ref,
    dz_ref,
    out_ref,
    held_near,
    held_line,
    from_last,
    from_near,
    sems,
):
    line = Line(n)
    at, length = line.at, line.length
    LAST, LAST_RECV, NEAR, NEAR_RECV, TO_LINE, LINE_RECV, SIB, SIB_RECV = range(8)
    sem = Semaphores(sems, 2 * length)

    def slot(z, b1, b3):
        return 4 * z + at.stride1 * b1 + at.stride3 * b3

    def to_last(z, b1):
        return remote(
            grad_ref.at[slot(z, b1, 1 - at.last)],
            from_last.at[2 * z + b1],
            sem(LAST, 2 * z + b1),
            sem(LAST_RECV, 2 * z + b1),
            at.partner3,
        )

    def to_near(z):
        return remote(
            held_near.at[z], from_near.at[z], sem(NEAR, z), sem(NEAR_RECV, z), at.partner1
        )

    def to_line(z):
        return remote(
            held_line.at[z], out_ref.at[line.me], sem(TO_LINE, z), sem(LINE_RECV, at.z), line.peer(z)
        )

    def line_arrived(z):
        here = out_ref.at[2 * z + at.c]
        remote(here, here, sem(TO_LINE, z), sem(LINE_RECV, z), line.peer(z)).wait_recv()

    def to_sibling(z, other=False):
        here = out_ref.at[2 * z + (1 - at.c if other else at.c)]
        return remote(here, here, sem(SIB, z), sem(SIB_RECV, z), at.sibling)

    def event_begin():
        def chip(z):
            to_last(z, 1 - at.first).start()

        line.chips(chip)

        def chip_own(z):
            to_last(z, at.first).start()

        line.chips(chip_own)

    def event_last():
        def chip(z):
            b1 = 1 - at.first
            to_last(z, b1).wait_recv()
            held_near[z] = (
                grad_ref[slot(z, b1, at.last)].astype(F32) + from_last[2 * z + b1].astype(F32)
            ).astype(BF)
            to_near(z).start()

        line.chips(chip)

    def event_near():
        def chip(z):
            to_last(z, at.first).wait_recv()
            to_near(z).wait_recv()
            total = (
                grad_ref[slot(z, at.first, at.last)].astype(F32)
                + from_last[2 * z + at.first].astype(F32)
                + from_near[z].astype(F32)
            ).astype(BF)
            held_line[z] = total

            @pl.when(z == at.z)
            def _():
                out_ref[line.me] = total

            @pl.when(z != at.z)
            def _():
                to_line(z).start()

        line.chips(chip)
        to_sibling(at.z).start()

    def event_line():
        def chip(z):
            line_arrived(z)
            to_sibling(z).start()

        line.others(chip)

    def event_end():
        def chip(z):
            to_sibling(z, True).wait_recv()
            to_sibling(z).wait_send()
            to_near(z).wait_send()
            to_last(z, 0).wait_send()
            to_last(z, 1).wait_send()

        line.chips(chip)
        line.others(lambda z: to_line(z).wait_send())

    line.greet(True, False)
    event_begin()
    per_tile = 8 // batch
    tiles = dh_ref.shape[0] // 8
    row = lax.broadcasted_iota(jnp.int32, (8, dz_ref.shape[1]), 0)
    real = lax.broadcasted_iota(jnp.int32, (8, HP), 1) < H

    def tile(step, carried):
        dh_carry, dc_carry = carried
        rows = pl.ds(pl.multiple_of((tiles - 1 - step) * 8, 8), 8)
        keep = keep_ref[rows, :]
        i, f, u, o, t = (r[rows, :] for r in (i_ref, f_ref, u_ref, o_ref, t_ref))
        soft = dh_ref[rows, :]
        to_c = o * (1.0 - t * t)
        to_i = jnp.where(real, u * i * (1.0 - i), 0.0)
        to_f = jnp.where(real, cp_ref[rows, :] * f * (1.0 - f), 0.0)
        to_u = jnp.where(real, i * (1.0 - u * u), 0.0)
        to_o = jnp.where(real, t * o * (1.0 - o), 0.0)
        back = f * keep
        saved = None
        for part in reversed(range(per_tile)):
            dh = jnp.where(real, soft + dh_carry, 0.0)
            dc = dc_carry + dh * to_c
            dz = join_gates([dc * to_i, dc * to_f, dc * to_u, dh * to_o], dz_ref.shape[1])
            saved = dz if saved is None else jnp.where(row >= (part + 1) * batch, saved, dz)
            dh_carry = dot(dz.astype(BF), w_ref[...]) * keep
            dc_carry = dc * back
            dh_carry, dc_carry = (
                pltpu.roll(dh_carry, 8 - batch, 0),
                pltpu.roll(dc_carry, 8 - batch, 0),
            )
        dz_ref[rows, :] = saved
        pl.when(step == tiles // 3)(event_last)
        pl.when(step == tiles * 2 // 3)(event_near)
        pl.when(step == tiles - 2)(event_line)
        return dh_carry, dc_carry

    zero = jnp.zeros((8, HP), F32)
    lax.fori_loop(0, tiles, tile, (zero, zero))
    event_end()


def lstm_backward(batch, plan, columns, dh, recur_t, keep, states, grad, collective_id):
    rows, n = dh.shape[0], plan.fsdp
    length = n // 4
    vmem = pl.BlockSpec(memory_space=pltpu.VMEM)
    return pl.pallas_call(
        functools.partial(lstm_backward_kernel, batch, n),
        out_shape=[
            jax.ShapeDtypeStruct((rows, columns), F32),
            jax.ShapeDtypeStruct((plan.parts,) + plan.block, BF),
        ],
        in_specs=[vmem] * 10,
        out_specs=[vmem] * 2,
        scratch_shapes=[
            pltpu.VMEM((length,) + plan.block, BF),
            pltpu.VMEM((length,) + plan.block, BF),
            pltpu.VMEM((2 * length,) + plan.block, BF),
            pltpu.VMEM((length,) + plan.block, BF),
            pltpu.SemaphoreType.DMA((8 * 2 * length,)),
        ],
        compiler_params=pltpu.CompilerParams(
            collective_id=collective_id, has_side_effects=True, vmem_limit_bytes=48 * 2**20
        ),
    )(dh, recur_t, keep, *states, grad)


def turned(value, lanes):
    rows = value.shape[0]
    if rows < lanes:
        value = jnp.concatenate([value, jnp.zeros((lanes - rows, value.shape[1]), F32)], axis=0)
    return value.T


def copy_windows(plan, source, target, base, found, place):
    target[...] = jnp.zeros_like(target)
    for o, first, last in found:
        start, to = plan.starts[o] - base, place(o) * plan.rows
        target[to + first : to + last, :] = source[start + first : start + last, :]


def add_windows(plan, source, target, base, found, begin):
    for o, first, last in found:
        start, at = plan.starts[o] - base, o * plan.rows - begin
        target[start + first : start + last, :] += source[at + first : at + last, :]


def matrices_of(plan, filters):
    result = []
    for m in range(4):
        base = m * (filters + 1)
        found = plan.meeting(base, base + filters + 1)
        result.append((base, found, found[0][0] * plan.rows, (found[-1][0] + 1) * plan.rows))
    return result


def head_kernel(plans, soft, filters, blocks, *refs):
    highway, lstm = plans
    owns = refs[:2]
    codes_ref, length_ref, table_ref, kernel_ref, width_ref, soft_ref = refs[2:8]
    highway_out, lstm_out, x_ref, recur_ref, soft_out = refs[8:13]
    features, trans_refs, gate_refs = refs[13:16], refs[16:18], refs[18:20]
    highway_w, lstm_w, turned_ref, wide, recur_sum, gather_sems, out_sems = refs[20:]
    rows, fp = features[0].shape
    words = turned_ref.shape[1]
    work = Gather(plans, owns, (highway_w, lstm_w), gather_sems, True)
    work.line.greet()

    def conv(begin, end):
        def block(i, _):
            at = pl.ds(pl.multiple_of(i * WORD_BLOCK, WORD_BLOCK), WORD_BLOCK)
            slots = pl.ds(
                pl.multiple_of(i * WORD_BLOCK * SLOTS, WORD_BLOCK * SLOTS), WORD_BLOCK * SLOTS
            )
            conv_forward_block(
                filters,
                codes_ref[slots, :],
                length_ref[at, :],
                (table_ref, kernel_ref, width_ref),
                features[0],
                at,
            )
            return 0

        lax.fori_loop(begin, end, block, 0)

    chunk = 384

    def layer_sum(m, wide=wide):
        base, found, begin, end = matrices[m]
        copy_windows(
            highway, turned_ref, wide.at[: end - begin], base, found, lambda o: o - found[0][0]
        )
        target = (trans_refs if m % 2 == 0 else gate_refs)[m // 2]

        def columns(j, _):
            where = pl.ds(pl.multiple_of(j * chunk, chunk), chunk)
            left = wide[: end - begin, :].astype(BF)
            target[:, where] = dot_rows(left, highway_w[begin:end, where])[:rows]
            return 0

        lax.fori_loop(0, fp // chunk, columns, 0)

    def layer(l):
        turned_ref[:fp, :] = turned(features[l][...], words)
        layer_sum(2 * l)

    def layer_end(l):
        layer_sum(2 * l + 1)
        trans, gate = trans_refs[l][...], jax.nn.sigmoid(gate_refs[l][...])
        gate_refs[l][...] = gate
        value = gate * trans * jax.nn.sigmoid(trans) + (1.0 - gate) * features[l][...]
        lane = lax.broadcasted_iota(jnp.int32, (rows, fp), 1)
        features[l + 1][...] = keep_feature(value, lane, filters)

    matrices = matrices_of(highway, filters)
    work.begin(0)
    third = -(-blocks // 3)
    conv(0, third)
    work.from_line(0)
    conv(third, 2 * third)
    work.from_near(0)
    work.begin(1)
    conv(2 * third, blocks)
    soft.place_blocks(soft_ref, soft_out)
    work.from_line(1)
    work.from_last(0)
    work.from_sibling(0)
    out_copies = [
        pltpu.make_async_copy(highway_w, highway_out, out_sems.at[0]),
        pltpu.make_async_copy(lstm_w, lstm_out, out_sems.at[1]),
    ]
    out_copies[0].start()
    layer(0)
    layer_end(0)
    work.from_near(1)
    layer(1)
    layer_end(1)

    turned_ref[...] = jnp.zeros_like(turned_ref)
    sub = lax.broadcasted_iota(jnp.int32, (fp, words), 0)
    turned_ref[:fp, :] = jnp.where(sub < filters, turned(features[2][...], words), 0.0)
    turned_ref[lstm.used - 1 : lstm.used, :] = jnp.ones((1, words), F32)
    wide = wide.at[: lstm.total]
    copy_windows(lstm, turned_ref, wide, 0, lstm.meeting(0, lstm.used), lambda o: o)
    work.from_last(1)
    work.from_sibling(1)
    out_copies[1].start()
    left = wide[...].astype(BF)
    half = lstm.block[1]
    for h in range(2):
        x_ref[:, h * half : (h + 1) * half] = dot_rows(left, lstm_w[h])[:rows]

    recur_sum[...] = jnp.zeros_like(recur_sum)
    depth = lstm.block[0]
    for h in range(2):
        for slot in sorted({o // lstm.dp for o, _, _ in lstm.meeting(filters, filters + H)}):
            piece = lstm_w[h, slot * depth : (slot + 1) * depth, :].astype(F32)
            for o, first, last in lstm.meeting(filters, filters + H):
                if o // lstm.dp == slot:
                    start, at = lstm.starts[o] - filters, (o % lstm.dp) * lstm.rows
                    recur_sum[start + first : start + last, h * half : (h + 1) * half] += piece[
                        at + first : at + last
                    ]
    recur_ref[...] = recur_sum[...].astype(BF)
    for a in range(2):
        work.finish(a)
    for copy in out_copies:
        copy.wait()


def head(plans, soft, filters, own, conv_inputs, soft_flat, rows, fp, collective_id):
    highway, lstm = plans
    words = up_to(rows, 2 * LANE)
    vmem = pl.BlockSpec(memory_space=pltpu.VMEM)
    anywhere = pl.BlockSpec(memory_space=pl.ANY)
    feature = jax.ShapeDtypeStruct((rows, fp), F32)
    matrices = matrices_of(highway, filters)
    longest = max([lstm.total] + [end - begin for _, _, begin, end in matrices])
    return pl.pallas_call(
        functools.partial(head_kernel, plans, soft, filters, rows // WORD_BLOCK),
        out_shape=[
            jax.ShapeDtypeStruct(highway.shape, BF),
            jax.ShapeDtypeStruct(lstm.shape, BF),
            jax.ShapeDtypeStruct((rows, lstm.columns), F32),
            jax.ShapeDtypeStruct((HP, lstm.columns), BF),
            soft.placed_shape(),
        ]
        + [feature] * 7,
        in_specs=[anywhere] * 2 + [vmem] * 6,
        out_specs=[anywhere] * 2 + [vmem] * 10,
        scratch_shapes=[
            pltpu.VMEM(highway.shape, BF),
            pltpu.VMEM(lstm.shape, BF),
            pltpu.VMEM((up_to(max(lstm.used, fp), LANE), words), F32),
            pltpu.VMEM((longest, words), F32),
            pltpu.VMEM((HP, lstm.columns), F32),
            Gather.semaphores(plans),
            pltpu.SemaphoreType.DMA((2,)),
        ],
        compiler_params=pltpu.CompilerParams(
            collective_id=collective_id, has_side_effects=True, vmem_limit_bytes=60 * 2**20
        ),
    )(*own, *conv_inputs, soft.blocks_of(soft_flat))


def highway_backward_kernel(plans, conv, filters, blocks, *refs):
    highway, lstm = plans
    dz_ref, hp_ref = refs[:2]
    features, trans_refs, gate_refs = refs[2:5], refs[5:7], refs[7:9]
    codes_ref, length_ref, table_ref, kernel_ref, width_ref, mask_ref, fold_ref = refs[9:16]
    highway_all, lstm_all = refs[16:18]
    lstm_landed, grad_out, kernel_grad, total_out = refs[18:22]
    refs = refs[22:]
    if conv:
        highway_landed, highway_total, conv_out = refs[:3]
        conv_in, conv_total, gather_sems = refs[3:6]
        refs = refs[6:]
    lstm_grad, highway_w, lstm_w, turned_ref, wide, back, dz, pairs = refs[:8]
    staged, carry, feature_grad, hot_grad, load_sems, pair_sems, out_sems = refs[8:15]
    rows, fp = features[0].shape
    words = turned_ref.shape[1]
    at = Place()
    total = total_out.at[at.c]
    if conv:
        work = Reduce(
            [lstm, highway, conv],
            [lstm_grad, grad_out, conv_in],
            [total, highway_total, conv_total],
            [lstm_landed, highway_landed, None],
            refs[15:],
            [True, False, True],
        )
    else:
        work = Reduce([lstm], [lstm_grad], [total], [lstm_landed], refs[15:], [True])
    length, items = work.line.length, work.items
    matrices = matrices_of(highway, filters)
    half = lstm.block[1]
    of_input = lstm.meeting(0, filters)
    input_rows = lstm_w.shape[0]

    def layer_rows(l):
        begin, end = matrices[2 * l][2], matrices[2 * l + 1][3]
        return begin, end

    def load_layer(l):
        begin, end = layer_rows(l)
        return pltpu.make_async_copy(
            highway_all.at[pl.ds(begin, end - begin)],
            highway_w.at[pl.ds(0, end - begin)],
            load_sems.at[l],
        )

    def load_lstm(h):
        return pltpu.make_async_copy(
            lstm_all.at[h, pl.ds(0, input_rows)], lstm_w, load_sems.at[2 + h]
        )

    load_layer(1).start()
    load_lstm(0).start()
    work.line.greet()

    dz[...] = jnp.zeros_like(dz)
    dz[:rows, :] = dz_ref[...].astype(BF)
    lane = lax.broadcasted_iota(jnp.int32, (rows, HP), 1)
    hidden = jnp.where(lane < H, hp_ref[...], jnp.where(lane == H, 1.0, 0.0))
    sub = lax.broadcasted_iota(jnp.int32, (fp, words), 0)
    turned_ref[:fp, :] = jnp.where(sub < filters, turned(features[2][...], words), 0.0)
    kept = up_to(H + 1, 8)
    turned_ref[filters : filters + kept, :] = turned(hidden, words)[:kept]
    copy_windows(
        lstm,
        turned_ref,
        wide.at[: lstm.total],
        0,
        lstm.meeting(0, lstm.used),
        lambda o: lstm.position[o],
    )
    unit = lstm.total // (2 * length)

    def lstm_weights(i, _):
        where = pl.ds(pl.multiple_of(i * unit, unit), unit)
        left = wide[where, :].astype(BF)
        for h in range(2):
            lstm_grad[h, where, :] = dot(left, dz[:, h * half : (h + 1) * half]).astype(BF)
        return 0

    lax.fori_loop(0, 2 * length, lstm_weights, 0)
    work.begin(0)

    lane = lax.broadcasted_iota(jnp.int32, (rows, fp), 1)
    back[...] = jnp.zeros_like(back)
    for h in range(2):
        load_lstm(h).wait()
        wide[:input_rows, :] = dot_cols(lstm_w[...], dz[:, h * half : (h + 1) * half])
        if h == 0:
            load_lstm(1).start()
        add_windows(lstm, wide, back, 0, of_input, 0)
    grad = jnp.where(lane < filters, back[...].T[:rows], 0.0)

    work.legs(work.first_leg, 0, 0, items)
    def middle(k):
        work.legs(work.middle_leg, 0, k, k + 1)

    pairs[...] = jnp.zeros_like(pairs)
    for l in (1, 0):
        trans, gate = trans_refs[l][...], gate_refs[l][...]
        sig = jax.nn.sigmoid(trans)
        pairs[2 * l, :rows, :] = (grad * gate * sig * (1.0 + trans * (1.0 - sig))).astype(BF)
        pairs[2 * l + 1, :rows, :] = (
            grad * (trans * sig - features[l][...]) * gate * (1.0 - gate)
        ).astype(BF)
        load_layer(l).wait()
        back[...] = jnp.zeros_like(back)
        begin = layer_rows(l)[0]
        for m in (2 * l, 2 * l + 1):
            base, found, low, high = matrices[m]
            result = dot_cols(highway_w[low - begin : high - begin, :], pairs[m])
            add_windows(highway, result, back, base, found, low)
            if m % 2 and l:
                load_layer(0).start()
            middle(2 * (1 - l) + m % 2)
        grad = grad * (1.0 - gate) + back[...].T[:rows]
        grad = jnp.where(lane < filters, grad, 0.0)
    feature_grad[...] = grad

    chunk = 384
    size = highway.rows
    pending, shared = [], None
    empty = [o for o in range(len(highway.starts)) if all(o != f[0] for m in matrices for f in m[1])]
    for m in range(4):
        base, found, low, high = matrices[m]
        if m % 2 == 0:
            turned_ref[:fp, :] = turned(features[m // 2][...], words)
        copy_windows(
            highway, turned_ref, wide.at[: high - low], base, found, lambda o: o - found[0][0]
        )
        for copy in pending:
            copy.wait()
        adds = shared == found[0][0]
        shares = m < 3 and matrices[m + 1][1][0][0] == found[-1][0]
        count = len(found)

        def columns(j, _):
            where = pl.ds(pl.multiple_of(j * chunk, chunk), chunk)
            result = dot(wide[: high - low, :].astype(BF), pairs[m, :, where])
            if adds:
                first = result[:size] + carry[:, where]
                staged[:size, where] = first.astype(BF)
                staged[size : high - low, where] = result[size:].astype(BF)
            else:
                staged[: high - low, where] = result.astype(BF)
            if shares:
                carry[:, where] = result[(count - 1) * size :]
            return 0

        lax.fori_loop(0, fp // chunk, columns, 0)
        shared = found[-1][0] if shares else None
        sent = found[:-1] if shares else found
        pending = [
            pltpu.make_async_copy(
                staged.at[pl.ds(k * size, size)],
                grad_out.at[pl.ds(highway.position[o] * size, size)],
                out_sems.at[k],
            )
            for k, (o, _, _) in enumerate(sent)
        ]
        for copy in pending:
            copy.start()
    for copy in pending:
        copy.wait()
    if empty:
        staged[:size, :] = jnp.zeros((size, fp), BF)
        for o in empty:
            copy = pltpu.make_async_copy(
                staged.at[pl.ds(0, size)],
                grad_out.at[pl.ds(highway.position[o] * size, size)],
                out_sems.at[0],
            )
            copy.start()
            copy.wait()
    if conv:
        work.begin(1)

    kernel_grad[...] = jnp.zeros_like(kernel_grad)
    hot_grad[...] = jnp.zeros_like(hot_grad)

    def conv_block(i, _):
        where = pl.ds(pl.multiple_of(i * WORD_BLOCK, WORD_BLOCK), WORD_BLOCK)
        slots = pl.ds(pl.multiple_of(i * WORD_BLOCK * SLOTS, WORD_BLOCK * SLOTS), WORD_BLOCK * SLOTS)
        conv_backward_block(
            codes_ref[slots, :],
            length_ref[where, :],
            (table_ref, kernel_ref, width_ref),
            feature_grad,
            where,
            kernel_grad,
            hot_grad,
        )
        if conv:
            work.legs(work.first_leg, 1, i * items // blocks, (i + 1) * items // blocks)

        left = items - 4
        work.legs(work.middle_leg, 0, 4 + i * left // blocks, 4 + (i + 1) * left // blocks)
        return 0

    lax.fori_loop(0, blocks, conv_block, 0)
    kernel_grad[:, fp:] = jnp.dot(
        fold_ref[...],
        hot_grad[...] * mask_ref[...],
        precision=lax.Precision.HIGHEST,
        preferred_element_type=F32,
    )
    copy = remote(total, total, pair_sems.at[0], pair_sems.at[1], at.sibling)
    if not conv:
        work.last_leg(0)
        copy.start()
    else:
        conv.fill(conv_in, kernel_grad)
        work.begin(2)
        work.legs(work.first_leg, 2, 0, items)
        work.legs(work.middle_leg, 1, 0, 1)
        work.legs(work.middle_leg, 2, 0, length)
        work.legs(work.middle_leg, 1, 1, length // 2)
        work.legs(work.middle_leg, 2, length, items)
        work.legs(work.middle_leg, 1, length // 2, length)
        work.last_leg(0)
        copy.start()
        work.last_leg(2)
        spread = Gather([conv], [conv_total], [conv_out], gather_sems, False)
        spread.begin(0)
        work.legs(work.middle_leg, 1, length, length + 1)
        spread.from_line(0)
        work.legs(work.middle_leg, 1, length + 1, length + 2)
        spread.from_near(0)
        work.legs(work.middle_leg, 1, length + 2, items)
        spread.from_last(0)
        work.last_leg(1)
        spread.from_sibling(0)
        spread.finish(0)
    for a in range(3 if conv else 1):
        work.finish(a)
    copy.wait()


def conv_columns(fp):
    return up_to(fp + LANE, 2 * LANE)


def highway_backward(
    plans, conv, filters, dz, hp, features, trans, gates, conv_inputs, everywhere, collective_id
):
    highway, lstm = plans
    rows, fp = features[0].shape
    words = up_to(rows, 2 * LANE)
    vmem = pl.BlockSpec(memory_space=pltpu.VMEM)
    anywhere = pl.BlockSpec(memory_space=pl.ANY)
    matrices = matrices_of(highway, filters)
    longest = max([lstm.total] + [end - begin for _, _, begin, end in matrices])
    layer = max(matrices[2 * l + 1][3] - matrices[2 * l][2] for l in range(2))
    input_rows = up_to((lstm.meeting(0, filters)[-1][0] + 1) * lstm.rows, 16)
    return pl.pallas_call(
        functools.partial(highway_backward_kernel, plans, conv, filters, rows // WORD_BLOCK),
        out_shape=[
            jax.ShapeDtypeStruct((lstm.fsdp,) + lstm.block, BF),
            jax.ShapeDtypeStruct(highway.shape, BF),
            jax.ShapeDtypeStruct((LANE, conv_columns(fp)), F32),
            jax.ShapeDtypeStruct((2,) + lstm.block, F32),
        ]
        + (
            [
                jax.ShapeDtypeStruct((highway.fsdp,) + highway.block, BF),
                jax.ShapeDtypeStruct(highway.block, F32),
                jax.ShapeDtypeStruct(conv.shape, F32),
            ]
            if conv
            else []
        ),
        in_specs=[vmem] * 16 + [anywhere] * 2,
        out_specs=[anywhere] * 2 + [vmem] * 2 + ([anywhere, vmem, vmem] if conv else []),
        scratch_shapes=(
            [
                pltpu.VMEM(conv.shape, F32),
                pltpu.VMEM(conv.block, F32),
                Gather.semaphores([conv]),
            ]
            if conv
            else []
        )
        + [
            pltpu.VMEM(lstm.shape, BF),
            pltpu.VMEM((layer, highway.columns), BF),
            pltpu.VMEM((input_rows, lstm.block[1]), BF),
            pltpu.VMEM((up_to(max(lstm.used + 8, fp), LANE), words), F32),
            pltpu.VMEM((longest, words), F32),
            pltpu.VMEM((fp, words), F32),
            pltpu.VMEM((words, lstm.columns), BF),
            pltpu.VMEM((4, words, fp), BF),
            pltpu.VMEM((max(end - begin for _, _, begin, end in matrices), fp), BF),
            pltpu.VMEM((highway.rows, fp), F32),
            pltpu.VMEM((rows, fp), F32),
            pltpu.VMEM((HOT, LANE), F32),
            pltpu.SemaphoreType.DMA((4,)),
            pltpu.SemaphoreType.DMA((2,)),
            pltpu.SemaphoreType.DMA((max(len(found) for _, found, _, _ in matrices),)),
        ]
        + (
            Reduce.scratch([lstm, highway, conv], [True, False, True], [True, True, False])
            if conv
            else Reduce.scratch([lstm], [True], [True])
        ),
        compiler_params=pltpu.CompilerParams(
            collective_id=collective_id, has_side_effects=True, vmem_limit_bytes=255 * 2**18
        ),
    )(dz, hp, *features, *trans, *gates, *conv_inputs, *everywhere)


def softmax_kernel(
    vocab,
    n,
    h_ref,
    w_ref,
    map_ref,
    map_back_ref,
    loss_ref,
    grad_h_ref,
    grad_w_ref,
    spread_back,
    logits,
    grads,
    stats,
    for_sibling,
    from_sibling,
    for_line,
    from_line,
    own_total,
    sems,
):
    line = Line(n)
    at, length, me = line.at, line.length, line.me
    members, rows, _ = h_ref.shape
    width = w_ref.shape[-1]
    w = w_ref[...].reshape(-1, width)
    STAT, STAT_RECV, SIB, SIB_RECV, TO_LINE, LINE_RECV = range(6)
    sem = Semaphores(sems, members)
    column = me * width + lax.broadcasted_iota(jnp.int32, (rows, width), 1)
    real_column = column.astype(F32)
    words = up_to(rows, LANE)
    lane = lax.broadcasted_iota(jnp.int32, (rows, LANE), 1)
    aside = HP - LANE

    def pieces(b):
        tail = h_ref[b, :, aside:].astype(F32)
        first = H + 1 - aside
        target = tail[:, first : first + 1] * 256.0 + tail[:, first + 1 : first + 2]
        scale = (
            tail[:, first + 2 : first + 3]
            + tail[:, first + 3 : first + 4]
            + tail[:, first + 4 : first + 5]
        )
        return target, scale

    line.greet(False, True)

    def forward(b, _):
        h = h_ref[b]
        wide = dot(h, map_ref[...]).astype(BF)
        spread_back[b] = dot(h, map_back_ref[...]).astype(BF)
        now = jnp.where(column < vocab, dot(wide, w), -1e30)
        logits[b] = now
        target, _ = pieces(b)
        top = jnp.max(now, axis=1, keepdims=True)
        log_sum = top + jnp.log(jnp.sum(jnp.exp(now - top), axis=1, keepdims=True))
        picked = jnp.sum(jnp.where(real_column == target, now, 0.0), axis=1, keepdims=True)
        both = jnp.where(lane == 0, log_sum, jnp.where(lane == 1, picked, 0.0))
        both = jnp.concatenate([both, jnp.zeros((words - rows, LANE), F32)], axis=0).T
        stats[me, 0, pl.ds(b, 1), :] = both[0:1, :]
        stats[me, 1, pl.ds(b, 1), :] = both[1:2, :]
        return 0

    lax.fori_loop(0, members, forward, 0)

    def stat(member, target):
        here = stats.at[member]
        return remote(here, here, sem(STAT, member), sem(STAT_RECV, member), target)

    def stat_out(z):
        return [
            remote(
                stats.at[me], stats.at[me], sem(STAT, 2 * z + core), sem(STAT_RECV, me), target
            )
            for core, target in ((at.c, line.peer(z)), (1 - at.c, line.peer(z, True)))
        ]

    def send_stats(z):
        for copy in stat_out(z):
            copy.start()

    line.others(send_stats)
    to_pair = remote(
        stats.at[me], stats.at[me], sem(STAT, 2 * at.z + 1 - at.c), sem(STAT_RECV, me), at.sibling
    )
    to_pair.start()

    def stats_in(z):
        for core in (at.c, 1 - at.c):
            stat(2 * z + core, at.sibling).wait_recv()

    line.others(stats_in)
    stat(2 * at.z + 1 - at.c, at.sibling).wait_recv()
    top = stats[0, 0]
    for q in range(1, members):
        top = jnp.maximum(top, stats[q, 0])
    total = jnp.zeros_like(top)
    picked = jnp.zeros_like(top)
    for q in range(members):
        total += jnp.exp(stats[q, 0] - top)
        picked += stats[q, 1]
    log_total = top + jnp.log(total)
    loss_ref[...] = log_total - picked
    log_columns = jnp.concatenate(
        [log_total, jnp.zeros((LANE - members, words), F32)], axis=0
    ).T[:rows]

    def to_sibling(z):
        return remote(
            for_sibling.at[z], from_sibling.at[z], sem(SIB, z), sem(SIB_RECV, z), at.sibling
        )

    def to_line(z):
        return remote(
            for_line.at[z], from_line.at[at.z], sem(TO_LINE, z), sem(LINE_RECV, at.z), line.peer(z)
        )

    def backward(k, _):
        z = lax.rem(k, length)
        mine = k >= length
        b = 2 * z + jnp.where(mine, at.c, 1 - at.c)
        target, scale = pieces(b)
        log_sum = jnp.sum(jnp.where(lane == b, log_columns, 0.0), axis=1, keepdims=True)
        share = jnp.exp(logits[b] - log_sum)
        grad = ((share - (real_column == target).astype(F32)) * scale).astype(BF)
        grads[b] = grad
        back = dot_cols(grad, w)

        @pl.when(jnp.logical_not(mine))
        def _():
            for_sibling[z] = back.astype(BF)
            to_sibling(z).start()

        @pl.when(mine)
        def _():
            to_sibling(z).wait_recv()
            total = back + from_sibling[z].astype(F32)

            @pl.when(z == at.z)
            def _():
                own_total[...] = total

            @pl.when(z != at.z)
            def _():
                for_line[z] = total.astype(BF)
                to_line(z).start()

        return 0

    lax.fori_loop(0, 2 * length, backward, 0)

    depth = map_ref.shape[1]
    unit = 256
    everything = grads[...].reshape(members * rows, width)

    def weight_grad(m, _):
        left = spread_back[:, :, pl.ds(pl.multiple_of(m * unit, unit), unit)]
        result = dot_rows(left.reshape(members * rows, unit), everything).astype(BF)
        grad_w_ref[pl.ds(m * unit, unit), :] = result
        return 0

    lax.fori_loop(0, depth // unit, weight_grad, 0)

    def arrived(z):
        remote(
            from_line.at[z], from_line.at[z], sem(TO_LINE, z), sem(LINE_RECV, z), line.peer(z)
        ).wait_recv()
        own_total[...] += from_line[z].astype(F32)

    line.others(arrived)
    spread_grad = own_total[...]
    high = spread_grad.astype(BF)
    low = (spread_grad - high.astype(F32)).astype(BF)
    grad_h_ref[...] = dot_cols(high, map_ref[...]) + dot_cols(low, map_ref[...])

    def finish(z):
        for copy in stat_out(z):
            copy.wait_send()
        to_line(z).wait_send()

    line.others(finish)
    line.chips(lambda z: to_sibling(z).wait_send())
    to_pair.wait_send()


def word_softmax(plan, h, weights, mapping, mapping_back, collective_id):
    members, rows, depth = h.shape
    n = plan.fsdp
    spread = mapping.shape[1]
    per_slot, width = plan.block
    words = up_to(rows, LANE)
    length = members // 2
    vmem = pl.BlockSpec(memory_space=pltpu.VMEM)
    loss, grad_h, grad_w = pl.pallas_call(
        functools.partial(softmax_kernel, plan.width, n),
        out_shape=[
            jax.ShapeDtypeStruct((members, words), F32),
            jax.ShapeDtypeStruct((rows, depth), F32),
            jax.ShapeDtypeStruct((spread, width), BF),
        ],
        in_specs=[vmem] * 4,
        out_specs=[vmem] * 3,
        scratch_shapes=[
            pltpu.VMEM((members, rows, spread), BF),
            pltpu.VMEM((members, rows, width), F32),
            pltpu.VMEM((members, rows, width), BF),
            pltpu.VMEM((members, 2, members, words), F32),
            pltpu.VMEM((length, rows, spread), BF),
            pltpu.VMEM((length, rows, spread), BF),
            pltpu.VMEM((length, rows, spread), BF),
            pltpu.VMEM((length, rows, spread), BF),
            pltpu.VMEM((rows, spread), F32),
            pltpu.SemaphoreType.DMA((6 * members,)),
        ],
        compiler_params=pltpu.CompilerParams(
            collective_id=collective_id, has_side_effects=True, vmem_limit_bytes=62 * 2**20
        ),
    )(h, weights, mapping, mapping_back)
    return loss, grad_h, grad_w.reshape((n,) + plan.block)


def shards(
    fsdp_count,
    dp_count,
    chars,
    lengths,
    targets,
    resets,
    init_state,
    window_grad,
    char_table,
    conv_weight,
    conv_bias,
    highway_flat,
    lstm_flat,
    soft_flat,
):
    micro_count, streams, step_count, letters = chars.shape
    char_count, embed_dim = char_table.shape
    filters = conv_weight.shape[1]
    batch = micro_count * streams
    words = step_count * batch
    rows = up_to(words, 16)
    fp = up_to(filters + 1, LANE)
    dp_at, fsdp_at = lax.axis_index("dp"), lax.axis_index("fsdp")
    highway = Windows(
        highway_flat.shape[0] * fsdp_count, filters, 4 * (filters + 1), fsdp_count, dp_count, True
    )
    lstm = Windows(
        lstm_flat.shape[0] * fsdp_count, 4 * H, filters + H + 1, fsdp_count, dp_count, False
    )
    soft = Windows(
        soft_flat.shape[0] * fsdp_count, V, H + 1, fsdp_count, dp_count, False, fsdp_count // 2
    )
    member = 2 * (fsdp_at // 4) + lax.rem(dp_at, 2)

    def by_step(array):
        return jnp.moveaxis(array.reshape((batch, step_count) + array.shape[3:]), 1, 0).reshape(
            (words,) + array.shape[3:]
        )

    def pad_rows(array, value=0):
        return jnp.pad(
            array,
            [(0, rows - words)] + [(0, 0)] * (array.ndim - 1),
            constant_values=value,
        )

    word_chars = pad_rows(by_step(chars))
    word_lengths = pad_rows(by_step(lengths))[:, None]
    position = jnp.arange(letters, dtype=jnp.int32)[None, :]
    codes = jnp.where(position < word_lengths, word_chars, -1)
    codes = jnp.pad(codes, ((0, 0), (0, SLOTS - letters)), constant_values=-1)
    codes = codes.reshape(rows * SLOTS, 1)
    column = np.arange(fp)
    widths = np.ones((fp,), np.int32)
    for cut_at in FILTER_CUTS:
        widths = widths + ((column >= filters * cut_at // 22) & (column < filters))
    widths = widths.astype(np.int32)
    kernel_mask = jnp.asarray(
        np.arange(KMAX * embed_dim)[:, None] // embed_dim < widths[None, :filters]
    )
    ones_row = KMAX * embed_dim
    kernel = jnp.concatenate(
        [jnp.where(kernel_mask, conv_weight, jnp.zeros_like(conv_weight)), conv_bias[None, :]], axis=0
    )
    kernel = jnp.pad(kernel, ((0, LANE - ones_row - 1), (0, fp - filters)))
    spread_table = jnp.concatenate(
        [
            jnp.pad(char_table, ((0, 0), (q * embed_dim, LANE - (q + 1) * embed_dim)))
            for q in range(KMAX)
        ]
        + [jnp.asarray((np.arange(LANE) == ones_row)[None, :].astype(np.float32)).astype(BF)],
        axis=0,
    )
    spread_table = jnp.pad(spread_table, ((0, HOT - KMAX * char_count - 1), (0, 0)))
    conv_inputs = (codes, word_lengths, spread_table, kernel, jnp.asarray(widths)[None, :])

    highway_all, lstm_all, from_input, recur, soft_placed, *kept = head(
        [highway, lstm],
        soft,
        filters,
        place_all([highway, lstm], [highway_flat, lstm_flat]),
        conv_inputs,
        soft_flat,
        rows,
        fp,
        1,
    )
    features, trans, gates = kept[:3], kept[3:5], kept[5:7]

    soft_own = soft.from_placed(soft_placed)
    recur_t = recur.T
    keep = pad_rows(by_step(1 - resets).astype(F32))[:, None]
    start = init_state.reshape(batch, 2, H)
    start = jnp.pad(start, ((0, 8 - batch), (0, 0), (0, HP - H)))
    row_scale = jnp.broadcast_to(
        window_grad.reshape(1, batch) / step_count, (step_count, batch)
    ).reshape(words)
    goal = by_step(targets)
    scale_high = lax.reduce_precision(row_scale, 8, 7)
    scale_mid = lax.reduce_precision(row_scale - scale_high, 8, 7)
    extra = jnp.stack(
        [
            jnp.ones((words,), F32),
            (goal // 256).astype(F32),
            (goal % 256).astype(F32),
            scale_high,
            scale_mid,
            row_scale - scale_high - scale_mid,
        ],
        axis=1,
    )
    aside = H - (HP - LANE)
    extra = jnp.pad(extra, ((0, rows - words), (aside, LANE - aside - extra.shape[1])))
    *states, hidden_all, soft_part = lstm_forward(
        batch,
        soft,
        from_input,
        recur,
        start[:, 0].astype(BF).astype(F32),
        start[:, 1],
        keep,
        extra,
        soft_own,
        4,
    )
    hp = states[0]

    word_loss, grad_hidden, soft_grad = word_softmax(
        soft,
        hidden_all,
        soft_part,
        one_hot_map(HP, soft.gathered),
        one_hot_map(HP, soft.reduced),
        5,
    )
    word_loss = lax.dynamic_index_in_dim(word_loss, member, 0, keepdims=False)
    window_loss = jnp.mean(word_loss[:words].reshape(step_count, batch), axis=0).reshape(
        micro_count, streams
    )

    dz, soft_part = lstm_backward(
        batch, soft, lstm.columns, grad_hidden, recur_t, keep, states[1:], soft_grad, 6
    )
    hot_row, hot_lane = np.arange(HOT), np.arange(LANE)
    hot_mask = (hot_row[:, None] // char_count == hot_lane[None, :] // embed_dim) & (
        hot_row[:, None] < KMAX * char_count
    )
    hot_fold = (hot_row[None, :] % char_count == np.arange(LANE)[:, None]) & (
        hot_row[None, :] < KMAX * char_count
    )
    conv = Dense(LANE, conv_columns(fp), fsdp_count)
    at_once = 2 * fsdp_count * highway.block[0] * highway.block[1] * 2 <= 12 * 2**20
    _, highway_grad, conv_grad, lstm_part, *rest = highway_backward(
        [highway, lstm],
        conv if at_once else None,
        filters,
        dz,
        hp,
        features,
        trans,
        gates,
        (
            *conv_inputs,
            jnp.asarray(hot_mask.astype(np.float32)),
            jnp.asarray(hot_fold.astype(np.float32)),
        ),
        (highway_all, lstm_all),
        7,
    )
    if at_once:
        _, highway_part, conv_grad = rest
    else:
        conv_grad, highway_part = tail([conv, highway], conv_grad, highway_grad, 3)
    conv_grad = jnp.concatenate(
        [conv_grad[h].reshape(-1, conv.block[1])[:LANE] for h in range(2)], axis=1
    )
    conv_weight_grad = jnp.where(kernel_mask, conv_grad[:ones_row, :filters], 0.0)
    conv_bias_grad = conv_grad[ones_row, :filters]
    table_grad = jnp.sum(
        conv_grad[:char_count, fp : fp + KMAX * embed_dim].reshape(char_count, KMAX, embed_dim), axis=1
    )

    def own_window(plan, part):
        if dp_count > 2:
            groups = [list(range(h, dp_count, 2)) for h in range(2)]
            part = lax.psum(part.astype(F32), "dp", axis_index_groups=groups)
        if plan.by_rows:
            at = dp_at // 2
        else:
            at = dp_at
            part = jnp.concatenate(
                [
                    lax.dynamic_slice_in_dim(part[p], at * plan.rows, plan.rows, 0)
                    for p in range(plan.parts)
                ],
                axis=1,
            ).astype(F32)
            return plan.to_flat(part, dp_at, fsdp_at)
        window = lax.dynamic_slice_in_dim(part, at * plan.rows, plan.rows, 0)
        return plan.to_flat(window, dp_at, fsdp_at)

    return (
        window_loss,
        table_grad,
        conv_weight_grad,
        conv_bias_grad,
        own_window(highway, highway_part),
        own_window(lstm, lstm_part),
        own_window(soft, soft_part),
    )


def solution(mesh):
    in_specs = (
        P(None, ("dp", "fsdp"), None, None),
        P(None, ("dp", "fsdp"), None),
        P(None, ("dp", "fsdp"), None),
        P(None, ("dp", "fsdp"), None),
        P(None, ("dp", "fsdp"), None, None),
        P(None, ("dp", "fsdp")),
        P(),
        P(),
        P(),
        P("fsdp", None),
        P("fsdp", None),
        P("fsdp", None),
    )
    out_specs = (
        P(None, ("dp", "fsdp")),
        P(),
        P(),
        P(),
        P(("dp", "fsdp"), None),
        P(("dp", "fsdp"), None),
        P(("dp", "fsdp"), None),
    )
    return jax.shard_map(
        functools.partial(shards, mesh.shape["fsdp"], mesh.shape["dp"]),
        mesh=mesh,
        in_specs=in_specs,
        out_specs=out_specs,
        check_vma=False,
    )
```

```python
import functools

import jax
import jax.numpy as jnp
import numpy as np
from jax import lax
from jax.experimental import pallas as pl
from jax.experimental.pallas import tpu as pltpu
from jax.sharding import PartitionSpec as P

H = 650
V = 10000
KMAX = 7
LANE = 128
HP = 768
SLOTS = 24
CHARS = 51
HOT = 384
FILTER_CUTS = (1, 3, 6, 10, 14, 18)
MESH = pl.DeviceIdType.MESH
BF = jnp.bfloat16
F32 = jnp.float32


def up_to(value, unit):
    return -(-value // unit) * unit


def dot(left, right):
    return jnp.dot(left, right, preferred_element_type=F32)


def dot_rows(left, right):
    return lax.dot_general(left, right, (((0,), (0,)), ((), ())), preferred_element_type=F32)


def dot_cols(left, right):
    return lax.dot_general(left, right, (((1,), (1,)), ((), ())), preferred_element_type=F32)


class Windows:
    dtype = BF

    def __init__(self, flat_rows, width, used, fsdp, dp, by_rows, parts=2):
        owners = fsdp * dp
        self.parts = parts
        self.width, self.by_rows, self.fsdp, self.dp, self.used = width, by_rows, fsdp, dp, used
        self.entries = flat_rows * LANE // owners
        self.starts = [o * self.entries // width for o in range(owners)]
        self.spans = [
            (o * self.entries % width + self.entries - 1) // width + 1 for o in range(owners)
        ]
        unit = 16 if by_rows else 8
        rows = up_to(max(self.spans), unit)
        while (dp * rows) % 16:
            rows += unit
        self.rows = rows
        self.total = owners * rows
        self.columns = up_to(width, LANE) if by_rows else parts * up_to(-(-width // parts), LANE)
        self.block = (
            (dp // 2 * rows, self.columns) if by_rows else (dp * rows, self.columns // parts)
        )
        self.shape = (
            (self.total, self.columns)
            if by_rows
            else (parts, self.total, self.columns // parts)
        )
        if by_rows:
            order = [
                (2 * jj + h) * fsdp + f
                for f in range(fsdp)
                for h in range(2)
                for jj in range(dp // 2)
            ]
        else:
            order = [d * fsdp + f for f in range(fsdp) for d in range(dp)]
        self.position = [order.index(o) for o in range(owners)]
        self.gathered = self.row_map(range(owners))
        self.reduced = self.row_map(order)

    def row_map(self, order):
        rows_of = [
            [
                self.starts[o] + i if i < self.spans[o] and self.starts[o] + i < self.used else -1
                for i in range(self.rows)
            ]
            for o in order
        ]
        return np.array(rows_of, np.int32).reshape(-1)

    def pick(self, ref, half, slot):
        depth = self.block[0]
        if self.by_rows:
            return ref.at[pl.ds(pl.multiple_of((2 * slot + half) * depth, 16), depth)]
        return ref.at[half, pl.ds(pl.multiple_of(slot * depth, 16), depth)]

    def meeting(self, begin, end):
        found = []
        for o, (start, span) in enumerate(zip(self.starts, self.spans)):
            first, last = max(0, begin - start), min(span, end - start)
            if first < last:
                found.append((o, first, last))
        return found

    @property
    def lines(self):
        return up_to(-(-self.rows * self.width // LANE), 16) + 32

    def place_blocks(self, shard_ref, out_ref):
        fsdp_at = lax.axis_index("fsdp")
        count = self.entries // LANE
        out_ref[...] = jnp.zeros_like(out_ref)
        for j in range(self.dp):
            shift = lax.rem((fsdp_at * self.dp + j) * self.entries, self.width)
            lanes, lines = lax.rem(shift, LANE), lax.rem(shift // LANE, 16)
            block = shard_ref[j].astype(F32)
            extra = up_to(count, 16) + 16 - count
            block = jnp.concatenate([block, jnp.zeros((extra, LANE), F32)], axis=0)
            block = pltpu.roll(block, lanes, 1)
            lane = lax.broadcasted_iota(jnp.int32, block.shape, 1)
            block = jnp.where(lane < lanes, pltpu.roll(block, 1, 0), block)
            for step in (1, 2, 4, 8):
                moved = lax.rem(lines // step, 2) == 1
                block = jnp.where(moved, pltpu.roll(block, step, 0), block)
            begin = pl.multiple_of(shift // (16 * LANE) * 16, 16)
            out_ref[j, pl.ds(begin, count + extra), :] = block.astype(BF)

    def placed_shape(self):
        return jax.ShapeDtypeStruct((self.dp, self.lines, LANE), BF)

    def blocks_of(self, shard):
        return shard.reshape(self.dp, self.entries // LANE, LANE)

    def from_placed(self, placed):
        size = self.rows * self.width
        joined = jnp.concatenate(
            [
                jnp.pad(
                    placed[j].reshape(-1)[:size].reshape(self.rows, self.width),
                    ((0, 0), (0, self.columns - self.width)),
                )
                for j in range(self.dp)
            ],
            axis=0,
        )
        if self.by_rows:
            return joined.reshape((2,) + self.block)
        part = self.columns // self.parts
        return jnp.stack([joined[:, p * part : (p + 1) * part] for p in range(self.parts)])

    def to_flat(self, window, dp_at, fsdp_at):
        shift = lax.rem((dp_at * self.fsdp + fsdp_at) * self.entries, self.width)
        flat = window[:, : self.width].reshape(-1)
        return lax.dynamic_slice(flat, (shift,), (self.entries,)).reshape(-1, LANE)


def one_hot_map(rows, row_map):
    return (
        lax.broadcasted_iota(jnp.int32, (rows, row_map.shape[0]), 0) == jnp.asarray(row_map)[None, :]
    ).astype(BF)


class Place:
    def __init__(self):
        self.d, self.f = lax.axis_index("dp"), lax.axis_index("fsdp")
        self.c = lax.rem(self.d, 2)
        x, y, self.z = lax.rem(self.f, 2), lax.rem(self.f // 2, 2), self.f // 4
        self.first = x + self.c * (y - x)
        self.last = y + self.c * (x - y)
        self.stride1, self.stride3 = 1 + self.c, 2 - self.c
        self.flip1 = self.stride1 * (1 - 2 * self.first)
        self.flip3 = self.stride3 * (1 - 2 * self.last)
        self.partner1 = (self.d, self.f + self.flip1)
        self.partner3 = (self.d, self.f + self.flip3)
        self.sibling = (self.d + 1 - 2 * self.c, self.f)

    def last_bit(self, block):
        bit_x, bit_y = lax.rem(block, 2), lax.rem(block // 2, 2)
        return bit_y + self.c * (bit_x - bit_y)


def remote(src, dst, send, recv, target):
    return pltpu.make_async_remote_copy(
        src_ref=src,
        dst_ref=dst,
        send_sem=send,
        recv_sem=recv,
        device_id=target,
        device_id_type=MESH,
    )


class Line:
    def __init__(self, n):
        self.at = Place()
        self.length = n // 4
        self.me = 2 * self.at.z + self.at.c

    def peer(self, z, other_core=False):
        at = self.at
        return (at.d + (1 - 2 * at.c if other_core else 0), at.f + 4 * (z - at.z))

    def column(self, z):
        return self.at.f + 4 * (z - self.at.z)

    def others(self, body):
        def step(z, _):
            pl.when(z != self.at.z)(functools.partial(body, z))
            return 0

        lax.fori_loop(0, self.length, step, 0)

    def chips(self, body):
        def step(z, _):
            body(z)
            return 0

        lax.fori_loop(0, self.length, step, 0)

    def far(self, k):
        z = jnp.int32(0)
        for here in range(self.length):
            order = sorted(range(self.length), key=lambda there: (-abs(there - here), there))
            for i, there in enumerate(order):
                z = jnp.where((self.at.z == here) & (k == i), there, z)
        return z

    def greet(self, across=True, both_cores=False):
        barrier = pltpu.get_barrier_semaphore()

        def signal(target):
            pl.semaphore_signal(barrier, inc=1, device_id=target, device_id_type=MESH)

        signal(self.at.sibling)
        count = 1
        if across:
            signal(self.at.partner1)
            signal(self.at.partner3)
            count += 2

        def chip(z):
            signal(self.peer(z))
            if both_cores:
                signal(self.peer(z, True))

        self.others(chip)
        pl.semaphore_wait(barrier, count + (self.length - 1) * (2 if both_cores else 1))


class Semaphores:
    def __init__(self, ref, size):
        self.ref, self.size = ref, size

    def __call__(self, kind, index):
        return self.ref.at[kind * self.size + index]


class Gather:
    RECV, SIB_RECV, LINE, NEAR, LAST, SIB, LOCAL = range(7)

    def __init__(self, plans, own, outs, sems, shared):
        self.plans, self.own, self.outs, self.sems, self.shared = plans, own, outs, sems, shared
        self.n = plans[0].fsdp
        self.line = Line(self.n)
        self.at = self.line.at

    @staticmethod
    def semaphores(plans):
        return pltpu.SemaphoreType.DMA((7 * len(plans) * plans[0].fsdp,))

    def sem(self, kind, a, index):
        return self.sems.at[(kind * len(self.plans) + a) * self.n + index]

    def source(self, a, half):
        return self.own[a].at[half] if self.shared else self.own[a]

    def copy(self, kind, a, index, block, target, own=False):
        here = self.plans[a].pick(self.outs[a], self.at.c, block)
        return remote(
            self.source(a, self.at.c) if own else here,
            here,
            self.sem(kind, a, index),
            self.sem(self.SIB_RECV if kind == self.SIB else self.RECV, a, block),
            target,
        )

    def arrived(self, a, block, kind=RECV):
        c = self.at.c
        here = self.plans[a].pick(self.outs[a], 1 - c if kind == self.SIB_RECV else c, block)
        remote(
            here, here, self.sem(self.SIB, a, block), self.sem(kind, a, block), self.at.sibling
        ).wait_recv()

    def local(self, a, half):
        return pltpu.make_async_copy(
            self.source(a, half),
            self.plans[a].pick(self.outs[a], half, self.at.f),
            self.sem(self.LOCAL, a, half if self.shared else 0),
        )

    def to_sibling(self, a, block, own=False):
        return self.copy(self.SIB, a, block, block, self.at.sibling, own)

    def close_by(self, k):
        return self.line.far(self.line.length - 1 - k)

    def begin(self, a):
        at, line = self.at, self.line
        self.copy(self.NEAR, a, at.z, at.f, at.partner1, True).start()
        self.copy(self.LAST, a, at.z, at.f, at.partner3, True).start()

        def chip(k, _):
            z = self.close_by(k)
            self.copy(self.LINE, a, z, at.f, line.peer(z), True).start()
            return 0

        lax.fori_loop(1, line.length, chip, 0)
        if self.shared:
            for half in (0, 1):
                self.local(a, half).start()
        else:
            self.to_sibling(a, at.f, True).start()
            self.local(a, at.c).start()

    def from_line(self, a, k):
        z = self.close_by(k)
        block = self.line.column(z)
        self.arrived(a, block)
        self.copy(self.NEAR, a, z, block, self.at.partner1).start()
        self.copy(self.LAST, a, z, block, self.at.partner3).start()
        self.to_sibling(a, block).start()

    def from_near(self, a, k):
        z = self.close_by(k)
        block = self.line.column(z) + self.at.flip1
        self.arrived(a, block)
        self.copy(self.LAST, a, self.line.length + z, block, self.at.partner3).start()
        self.to_sibling(a, block).start()

    def from_last(self, a, k):
        length = self.line.length
        block = (
            self.line.column(self.close_by(lax.rem(k, length)))
            + self.at.flip3
            + self.at.flip1 * (k // length)
        )
        self.arrived(a, block)
        self.to_sibling(a, block).start()

    def steps(self, a):
        length = self.line.length
        order = [(self.from_near, 0), (self.from_line, 1)]
        for k in range(2, length):
            order += [(self.from_line, k), (self.from_near, k - 1)]
        order += [(self.from_near, length - 1)] if length > 1 else []
        order += [(self.from_last, k) for k in range(2 * length)]
        return [functools.partial(step, a, k) for step, k in order]

    def run(self, steps):
        for step in steps:
            step()

    def from_sibling(self, a):
        def block_in(block, _):
            if self.shared:

                @pl.when(jnp.logical_not(block == self.at.f))
                def _():
                    self.arrived(a, block, self.SIB_RECV)

            else:
                self.arrived(a, block, self.SIB_RECV)
            return 0

        lax.fori_loop(0, self.n, block_in, 0)
        if self.shared:
            for half in (0, 1):
                self.local(a, half).wait()
        else:
            self.local(a, self.at.c).wait()

    def finish(self, a):
        at, line = self.at, self.line

        def sent(kind, index):
            self.copy(kind, a, index, at.f, at.sibling).wait_send()

        def chip(z):
            sent(self.NEAR, z)
            sent(self.LAST, z)
            sent(self.LAST, line.length + z)

        line.chips(chip)
        line.others(lambda z: sent(self.LINE, z))

        def block_done(block, _):
            if self.shared:
                pl.when(jnp.logical_not(block == at.f))(lambda: sent(self.SIB, block))
            else:
                sent(self.SIB, block)
            return 0

        lax.fori_loop(0, self.n, block_done, 0)


STAGES = 4


class Reduce:
    SIB, SIB_RECV, LOAD, NEAR, NEAR_RECV, CROSS, CROSS_RECV, LINE, LINE_RECV, STAGE = range(10)

    def __init__(self, plans, ins, totals, landed, scratch, in_place):
        count = len(plans)
        self.plans, self.ins, self.totals, self.in_place = plans, ins, totals, in_place
        scratch = list(scratch)
        self.held = [None if here else scratch.pop(0) for here in in_place]
        self.staged = [ref is not None for ref in landed]
        self.stage = [scratch.pop(0) if far else None for far in self.staged]
        self.landed = [scratch.pop(0) if ref is None else ref for ref in landed]
        self.close, self.cross, self.lined = (
            scratch[k * count : (k + 1) * count] for k in range(3)
        )
        self.sems = scratch[3 * count]
        self.n = plans[0].fsdp
        self.line = Line(self.n)
        self.at = self.line.at
        self.items = 2 * self.line.length

    @staticmethod
    def scratch(plans, in_place, staged):
        def buffers(size, kept=None):
            return [
                pltpu.VMEM((size,) + plan.block, plan.dtype)
                for a, plan in enumerate(plans)
                if kept is None or kept[a]
            ]

        n = plans[0].fsdp
        return (
            buffers(n, [not here for here in in_place])
            + buffers(STAGES, staged)
            + buffers(n, [not far for far in staged])
            + buffers(n // 2)
            + buffers(n // 4) * 2
            + [pltpu.SemaphoreType.DMA((10 * len(plans) * n,))]
        )

    def sem(self, kind, a, index):
        return self.sems.at[(kind * len(self.plans) + a) * self.n + index]

    def slot(self, z, b1, b3):
        return 4 * z + self.at.stride1 * b1 + self.at.stride3 * b3

    def item(self, t):
        ours = lax.rem(t, 2)
        return self.line.far(t // 2), (1 - self.at.last) + ours * (2 * self.at.last - 1)

    def turn(self, m):
        swapped = jnp.where(lax.rem(m, 2) == 0, m - 1, m + 1)
        return jnp.where((m == 0) | (m == self.items - 1), m, swapped)

    def hold(self, a, block):
        if self.in_place[a]:
            return self.plans[a].pick(self.ins[a], self.at.c, block)
        return self.held[a].at[block]

    def to_sibling(self, a, block):
        return remote(
            self.plans[a].pick(self.ins[a], 1 - self.at.c, block),
            self.landed[a].at[block],
            self.sem(self.SIB, a, block),
            self.sem(self.SIB_RECV, a, block),
            self.at.sibling,
        )

    def load(self, a, block):
        return pltpu.make_async_copy(
            self.plans[a].pick(self.ins[a], self.at.c, block),
            self.held[a].at[block],
            self.sem(self.LOAD, a, block),
        )

    def to_near(self, a, z, b3):
        return remote(
            self.hold(a, self.slot(z, 1 - self.at.first, b3)),
            self.close[a].at[2 * z + b3],
            self.sem(self.NEAR, a, 2 * z + b3),
            self.sem(self.NEAR_RECV, a, 2 * z + b3),
            self.at.partner1,
        )

    def to_cross(self, a, z):
        return remote(
            self.hold(a, self.slot(z, self.at.first, 1 - self.at.last)),
            self.cross[a].at[z],
            self.sem(self.CROSS, a, z),
            self.sem(self.CROSS_RECV, a, z),
            self.at.partner3,
        )

    def to_line(self, a, z):
        return remote(
            self.hold(a, self.slot(z, self.at.first, self.at.last)),
            self.lined[a].at[self.at.z],
            self.sem(self.LINE, a, z),
            self.sem(self.LINE_RECV, a, self.at.z),
            self.line.peer(z),
        )

    def line_arrived(self, a, z):
        here = self.lined[a].at[z]
        remote(
            here, here, self.sem(self.LINE, a, z), self.sem(self.LINE_RECV, a, z), self.line.peer(z)
        ).wait_recv()

    def rows(self, a, body):
        unit = 16

        def step(i, _):
            body(pl.ds(pl.multiple_of(i * unit, unit), unit))
            return 0

        if self.plans[a].block[0] < unit:
            body(slice(None))
        else:
            lax.fori_loop(0, self.plans[a].block[0] // unit, step, 0)

    def add(self, a, block, sources):
        held = self.hold(a, block)

        def body(where):
            total = held[where, :].astype(F32)
            for ref, at in sources:
                total += ref[at, where, :].astype(F32)
            held[where, :] = total.astype(held.dtype)

        self.rows(a, body)

    def begin(self, a):
        for flip in (1, 0):
            b1 = self.at.first + flip * (1 - 2 * self.at.first)

            def start(t, _, b1=b1):
                z, b3 = self.item(t)
                block = self.slot(z, b1, b3)
                self.to_sibling(a, block).start()
                if not self.in_place[a]:
                    self.load(a, block).start()
                return 0

            lax.fori_loop(0, self.items, start, 0)

    def in_order(self, q):
        late = jnp.int32(q >= self.items)
        z, b3 = self.item(jnp.where(q >= self.items, self.turn(q - self.items), q))
        return self.slot(z, (1 - self.at.first) + late * (2 * self.at.first - 1), b3)

    def to_stage(self, a, q):
        k = lax.rem(q, STAGES)
        return pltpu.make_async_copy(
            self.landed[a].at[self.in_order(q)], self.stage[a].at[k], self.sem(self.STAGE, a, k)
        )

    def fetch(self, a, q):
        self.to_sibling(a, self.in_order(q)).wait_recv()
        self.to_stage(a, q).start()

    def ready(self, a, block, q):
        if not self.in_place[a]:
            self.load(a, block).wait()
        if not self.staged[a]:
            self.to_sibling(a, block).wait_recv()
            return self.landed[a], block

        @pl.when(q == 0)
        def _():
            for k in range(STAGES):
                self.fetch(a, jnp.int32(k))

        self.to_stage(a, q).wait()
        return self.stage[a], lax.rem(q, STAGES)

    def used(self, a, q):
        if self.staged[a]:
            pl.when(q + STAGES < 2 * self.items)(lambda: self.fetch(a, q + STAGES))

    def first_leg(self, a, t):
        z, b3 = self.item(t)
        block = self.slot(z, 1 - self.at.first, b3)
        self.add(a, block, [self.ready(a, block, t)])
        self.to_near(a, z, b3).start()
        self.used(a, t)

    def middle_leg(self, a, m):
        t = self.turn(m)
        z, b3 = self.item(t)
        block = self.slot(z, self.at.first, b3)
        sources = [self.ready(a, block, self.items + m), (self.close[a], 2 * z + b3)]
        self.to_near(a, z, b3).wait_recv()

        @pl.when(lax.rem(t, 2) == 0)
        def _():
            self.add(a, block, sources)
            self.to_cross(a, z).start()

        @pl.when(lax.rem(t, 2) == 1)
        def _():
            self.to_cross(a, z).wait_recv()
            self.add(a, block, sources + [(self.cross[a], z)])

            @pl.when(z != self.at.z)
            def _():
                self.to_line(a, z).start()

        self.used(a, self.items + m)

    def legs(self, body, a, begin, end):
        def step(t, _):
            body(a, t)
            return 0

        lax.fori_loop(begin, end, step, 0)

    def last_leg(self, a):
        block = self.slot(self.at.z, self.at.first, self.at.last)

        def body(where):
            self.totals[a][where, :] = self.hold(a, block)[where, :].astype(F32)

        self.rows(a, body)

        def chip(z):
            self.line_arrived(a, z)

            def body(where):
                self.totals[a][where, :] += self.lined[a][z, where, :].astype(F32)

            self.rows(a, body)

        self.line.others(chip)

    def finish(self, a):
        def done(t, _):
            z, b3 = self.item(t)
            for b1 in (self.at.first, 1 - self.at.first):
                self.to_sibling(a, self.slot(z, b1, b3)).wait_send()
            self.to_near(a, z, b3).wait_send()
            return 0

        lax.fori_loop(0, self.items, done, 0)
        self.line.chips(lambda z: self.to_cross(a, z).wait_send())
        self.line.others(lambda z: self.to_line(a, z).wait_send())


def reduce_out(plan):
    return jax.ShapeDtypeStruct(plan.block if plan.by_rows else (2,) + plan.block, F32)


def hot_rows(codes):
    count = codes.shape[0]
    slot = lax.rem(lax.broadcasted_iota(jnp.int32, (count, 1), 0), SLOTS)
    lane = lax.broadcasted_iota(jnp.int32, (count, HOT), 1)
    hit = lane == KMAX * CHARS
    for q in range(KMAX):
        moved = codes if q == 0 else pltpu.roll(codes, count - q, 0)
        moved = jnp.where((moved >= 0) & (slot + q < SLOTS), moved + q * CHARS, -1)
        hit = jnp.logical_or(hit, lane == moved)
    return hit.astype(F32).astype(BF)


def conv_forward_block(filters, codes, lengths, refs, out_ref, where, kept):
    table_ref, kernel_ref, width_ref = refs
    hot_ref, window_ref, slope_ref = kept
    words = lengths.shape[0]
    hot = hot_rows(codes)
    hot_ref[...] = hot
    windows = dot(hot, table_ref[...]).astype(BF)
    window_ref[...] = windows
    chunk = 384
    for at in range(0, kernel_ref.shape[1], chunk):
        columns = slice(at, at + chunk)
        activated = jnp.tanh(dot(windows, kernel_ref[:, columns])).reshape(words, SLOTS, chunk)
        counts = jnp.maximum(lengths - width_ref[:, columns] + 1, 1)
        position = lax.broadcasted_iota(jnp.int32, (words, SLOTS, chunk), 1)
        inside = position < counts[:, None, :]
        weight = jnp.where(inside, jnp.exp(activated), 0.0)
        totals = jnp.sum(weight, axis=1)
        pooled = jnp.log(totals) - jnp.log(counts.astype(F32))
        lane = at + lax.broadcasted_iota(jnp.int32, (words, chunk), 1)
        out_ref[where, columns] = keep_feature(pooled, lane, filters)
        slope = weight * (1.0 / totals)[:, None, :] * (1.0 - activated * activated)
        slope_ref[:, columns] = slope.astype(BF).reshape(words * SLOTS, chunk)


def keep_feature(value, lane, filters):
    value = value.astype(BF).astype(F32)
    return jnp.where(lane < filters, value, jnp.where(lane == filters, 1.0, 0.0))


def conv_backward_block(kept, kernel_ref, grad_ref, where, kernel_grad_ref, hot_grad_ref):
    hot_ref, window_ref, slope_ref = kept
    words = WORD_BLOCK
    windows = window_ref[...]
    chunk = 384
    grad_windows = jnp.zeros(windows.shape, F32)
    for at in range(0, kernel_ref.shape[1], chunk):
        columns = slice(at, at + chunk)
        slope = slope_ref[:, columns].astype(F32).reshape(words, SLOTS, chunk)
        grad = (grad_ref[where, columns][:, None, :] * slope).astype(BF)
        grad = grad.reshape(words * SLOTS, chunk)
        kernel_grad_ref[:, columns] += dot_rows(windows, grad)
        grad_windows += dot_cols(grad, kernel_ref[:, columns])
    hot_grad_ref[...] += dot_rows(hot_ref[...], grad_windows.astype(BF))


WORD_BLOCK = 16


class SmallSum:
    SIB, NEAR, CROSS, LINE, BACK_LINE, BACK_CROSS, BACK_NEAR, BACK_SIB = range(0, 16, 2)

    def __init__(self, conv, mine, out, scratch):
        self.conv, self.mine, self.out = conv, mine, out
        self.by_sibling, self.by_near, self.by_cross, self.by_line, self.sems = scratch
        self.line = Line(conv.fsdp)
        self.at = at = self.line.at
        self.length = self.line.length
        self.near_at = at.first * 2 * self.length
        self.near_other = (1 - at.first) * 2 * self.length
        self.cross_at = self.near_at + at.last * self.length
        self.cross_other = self.near_at + (1 - at.last) * self.length
        self.own = self.cross_at + at.z

    @staticmethod
    def scratch(conv):
        n = conv.fsdp
        sizes = (n, n // 2, n // 4, n // 4)
        return [pltpu.VMEM((size,) + conv.block, F32) for size in sizes] + [
            pltpu.SemaphoreType.DMA((16 * (n // 4),))
        ]

    def sem(self, kind, index=0):
        return self.sems.at[kind * self.length + index]

    def message(self, kind, src, dst, target, send=0, receive=0):
        return remote(src, dst, self.sem(kind, send), self.sem(kind + 1, receive), target)

    def part(self, ref, begin, size):
        return ref.at[self.at.c, pl.ds(begin, size)]

    def sibling(self):
        return self.message(self.SIB, self.mine.at[1 - self.at.c], self.by_sibling, self.at.sibling)

    def near(self):
        size = 2 * self.length
        source = self.part(self.mine, self.near_other, size)
        return self.message(self.NEAR, source, self.by_near, self.at.partner1)

    def cross(self):
        source = self.part(self.mine, self.cross_other, self.length)
        return self.message(self.CROSS, source, self.by_cross, self.at.partner3)

    def lined(self, z, source=None):
        block = self.mine.at[self.at.c, self.cross_at + z]
        target = self.by_line.at[z if source else self.at.z]
        return self.message(
            self.LINE, block, target, self.line.peer(z), z, z if source else self.at.z
        )

    def back_line(self, z, source=None):
        here = self.out.at[self.at.c, self.cross_at + z if source else self.own]
        return self.message(
            self.BACK_LINE, here, here, self.line.peer(z), z, z if source else self.at.z
        )

    def back_cross(self, source=None):
        begin = self.cross_other if source else self.cross_at
        here = self.part(self.out, begin, self.length)
        return self.message(self.BACK_CROSS, here, here, self.at.partner3)

    def back_near(self, source=None):
        here = self.part(self.out, self.near_other if source else self.near_at, 2 * self.length)
        return self.message(self.BACK_NEAR, here, here, self.at.partner1)

    def back_sibling(self, source=None):
        here = self.out.at[1 - self.at.c if source else self.at.c]
        return self.message(self.BACK_SIB, here, here, self.at.sibling)

    def add(self, begin, source):
        size = source.shape[0]
        self.mine[self.at.c, pl.ds(begin, size)] += source[...]

    def steps(self):
        def begin():
            self.sibling().start()

        def to_near():
            self.sibling().wait_recv()
            self.add(0, self.by_sibling)
            self.near().start()

        def to_cross():
            self.near().wait_recv()
            self.add(self.near_at, self.by_near)
            self.cross().start()

        def to_line():
            self.cross().wait_recv()
            self.add(self.cross_at, self.by_cross)
            self.line.others(lambda z: self.lined(z).start())

        def total():
            self.out[self.at.c, self.own] = self.mine[self.at.c, self.own]

            def chip(z):
                self.lined(z, True).wait_recv()
                self.out[self.at.c, self.own] += self.by_line[z]

            self.line.others(chip)
            self.line.others(lambda z: self.back_line(z).start())

        def from_line():
            self.line.others(lambda z: self.back_line(z, True).wait_recv())
            self.back_cross().start()

        def from_cross():
            self.back_cross(True).wait_recv()
            self.back_near().start()

        def from_near():
            self.back_near(True).wait_recv()
            self.back_sibling().start()

        def end():
            self.back_sibling(True).wait_recv()
            for message in (
                self.sibling(),
                self.near(),
                self.cross(),
                self.back_cross(),
                self.back_near(),
                self.back_sibling(),
            ):
                message.wait_send()
            self.line.others(lambda z: self.lined(z).wait_send())
            self.line.others(lambda z: self.back_line(z).wait_send())

        return [begin, to_near, to_cross, to_line, total, from_line, from_cross, from_near, end]


def place_kernel(plans, *refs):
    for plan, shard, out in zip(plans, refs[: len(plans)], refs[len(plans) :]):
        plan.place_blocks(shard, out)


def place_all(plans, shards):
    vmem = pl.BlockSpec(memory_space=pltpu.VMEM)
    placed = pl.pallas_call(
        functools.partial(place_kernel, plans),
        out_shape=[plan.placed_shape() for plan in plans],
        in_specs=[vmem] * len(plans),
        out_specs=[vmem] * len(plans),
        compiler_params=pltpu.CompilerParams(vmem_limit_bytes=48 * 2**20),
    )(*[plan.blocks_of(shard) for plan, shard in zip(plans, shards)])
    return [plan.from_placed(each) for plan, each in zip(plans, placed)]


class Dense:
    by_rows = False
    dtype = F32

    def __init__(self, rows, columns, fsdp):
        self.fsdp = fsdp
        self.filled = rows
        self.block = (up_to(-(-rows // fsdp), 8), columns // 2)
        self.shape = (2, fsdp) + self.block

    def pick(self, ref, half, slot):
        return ref.at[half, slot]

    def fill(self, slots, source):
        slots[...] = jnp.zeros_like(slots)
        depth, half = self.block
        for block in range(self.filled // depth):
            for h in range(2):
                slots[h, block] = source[
                    block * depth : (block + 1) * depth, h * half : (h + 1) * half
                ]


def tail_kernel(plans, conv_ref, grad_ref, conv_out, total_out, conv_in, *scratch):
    conv, highway = plans
    small = SmallSum(conv, conv_in, conv_out, scratch[:5])
    work = Reduce([highway], [grad_ref], [total_out], [None], scratch[5:], [False])
    work.line.greet()
    conv.fill(conv_in, conv_ref)
    work.begin(0)
    work.legs(work.first_leg, 0, 0, work.items)
    for step in small.steps():
        step()
    work.legs(work.middle_leg, 0, 0, work.items)
    work.last_leg(0)
    work.finish(0)


def tail(plans, conv_grad, highway_grad, collective_id):
    conv, highway = plans
    vmem = pl.BlockSpec(memory_space=pltpu.VMEM)
    return pl.pallas_call(
        functools.partial(tail_kernel, plans),
        out_shape=[
            jax.ShapeDtypeStruct(conv.shape, F32),
            jax.ShapeDtypeStruct(highway.block, F32),
        ],
        in_specs=[vmem, pl.BlockSpec(memory_space=pl.ANY)],
        out_specs=[vmem] * 2,
        scratch_shapes=[pltpu.VMEM(conv.shape, F32)]
        + SmallSum.scratch(conv)
        + Reduce.scratch([highway], [False], [False]),
        compiler_params=pltpu.CompilerParams(
            collective_id=collective_id, has_side_effects=True, vmem_limit_bytes=48 * 2**20
        ),
    )(conv_grad, highway_grad)


def gate_parts(sums):
    parts = [sums[:, :HP]]
    for g in range(1, 4):
        begin = g * H // LANE * LANE
        moved = sums[:, begin : begin + HP + LANE]
        parts.append(pltpu.roll(moved, HP + LANE - (g * H - begin), 1)[:, :HP])
    return parts


def join_gates(parts, columns):
    rows = parts[0].shape[0]
    total = None
    for g, part in enumerate(parts):
        begin = g * H // LANE * LANE
        wide = jnp.concatenate([part, jnp.zeros((rows, LANE), F32)], axis=1)
        if g * H - begin:
            wide = pltpu.roll(wide, g * H - begin, 1)
        pieces = [wide]
        if begin:
            pieces = [jnp.zeros((rows, begin), F32)] + pieces
        if columns - begin - HP - LANE > 0:
            pieces = pieces + [jnp.zeros((rows, columns - begin - HP - LANE), F32)]
        placed = jnp.concatenate(pieces, axis=1)[:, :columns]
        total = placed if total is None else total + placed
    return total


HIDDEN_CHUNKS = ((0, 48), (48, 96), (96, 128), (128, 144))


def hidden_chunks(rows):
    return [(a, min(b, rows)) for a, b in HIDDEN_CHUNKS if a < rows] + (
        [(HIDDEN_CHUNKS[-1][1], rows)] if rows > HIDDEN_CHUNKS[-1][1] else []
    )


def lstm_forward_kernel(
    batch, n, x_ref, w_ref, h0_ref, c0_ref, keep_ref, extra_ref, own_ref, *refs
):
    hp_ref, cp_ref, i_ref, f_ref, u_ref, o_ref, t_ref, hall_ref, part_ref = refs[:9]
    hidden, soft_sems, hidden_sems = refs[9:]
    line = Line(n)
    at, length = line.at, line.length
    rows_all = x_ref.shape[0]
    chunks = hidden_chunks(rows_all)
    RECV, TO_LINE, TO_NEAR, TO_LAST, LOCAL = range(5)
    sem = Semaphores(soft_sems, n)
    H_RECV, H_LINE, H_SIB = range(3)
    hsem = Semaphores(hidden_sems, 2 * length * len(chunks))

    def column(z):
        return at.f + 4 * (z - at.z)

    def to_line(z):
        return remote(
            own_ref.at[2 * z + at.c],
            part_ref.at[at.f],
            sem(TO_LINE, z),
            sem(RECV, at.f),
            line.peer(z),
        )

    def pass_on(kind, index, slot, target, own=False):
        return remote(
            own_ref.at[line.me] if own else part_ref.at[slot],
            part_ref.at[slot],
            sem(kind, index),
            sem(RECV, slot),
            target,
        )

    def landed(slot):
        pass_on(TO_NEAR, 0, slot, at.partner1).wait_recv()

    local = pltpu.make_async_copy(own_ref.at[line.me], part_ref.at[at.f], sem(LOCAL, 0))

    def event_begin():
        line.others(lambda z: to_line(z).start())
        pass_on(TO_NEAR, at.z, at.f, at.partner1, True).start()
        pass_on(TO_LAST, at.z, at.f, at.partner3, True).start()
        local.start()

    def event_line():
        def chip(z):
            landed(column(z))
            pass_on(TO_NEAR, z, column(z), at.partner1).start()
            pass_on(TO_LAST, z, column(z), at.partner3).start()

        line.others(chip)

    def event_near():
        def chip(z):
            slot = column(z) + at.flip1
            landed(slot)
            pass_on(TO_LAST, length + z, slot, at.partner3).start()

        line.chips(chip)

    def event_end():
        def chip(z):
            landed(column(z) + at.flip3)
            landed(column(z) + at.flip1 + at.flip3)
            pass_on(TO_NEAR, z, column(z), at.partner1).wait_send()
            pass_on(TO_LAST, z, column(z), at.partner3).wait_send()
            pass_on(TO_LAST, length + z, column(z), at.partner3).wait_send()

        line.chips(chip)
        line.others(lambda z: to_line(z).wait_send())
        local.wait()

    def chunk_copy(k, member, kind, index, target):
        begin, end = chunks[k]
        here = hall_ref.at[member, pl.ds(begin, end - begin), :]
        return remote(
            here,
            here,
            hsem(kind, index * len(chunks) + k),
            hsem(H_RECV, member * len(chunks) + k),
            target,
        )

    def chunk_out(k):
        begin, end = chunks[k]
        hall_ref[line.me, begin:end, :] = hidden[begin:end, :].astype(BF)
        line.others(lambda z: chunk_copy(k, line.me, H_LINE, z, line.peer(z)).start())
        chunk_copy(k, line.me, H_SIB, at.z, at.sibling).start()

    def chunk_pass(k):
        def chip(z):
            member = 2 * z + at.c
            chunk_copy(k, member, H_SIB, z, at.sibling).wait_recv()
            chunk_copy(k, member, H_SIB, z, at.sibling).start()

        line.others(chip)

    def chunk_end(k):
        def chip(z):
            chunk_copy(k, 2 * z + 1 - at.c, H_SIB, z, at.sibling).wait_recv()
            chunk_copy(k, 2 * z + at.c, H_SIB, z, at.sibling).wait_send()

        line.chips(chip)
        line.others(lambda z: chunk_copy(k, line.me, H_LINE, z, line.peer(z)).wait_send())

    line.greet(True, False)
    event_begin()
    per_tile = 8 // batch
    tiles = rows_all // 8
    row = lax.broadcasted_iota(jnp.int32, (8, HP), 0)
    lane = lax.broadcasted_iota(jnp.int32, (8, LANE), 1)
    last = HP - LANE

    def tile(step, carried):
        h, c = carried
        rows = pl.ds(pl.multiple_of(step * 8, 8), 8)
        x = x_ref[rows, :]
        keep = keep_ref[rows, :]
        saved = None
        for part in range(per_tile):
            hp, cp = h * keep, c * keep
            sums = x + dot(hp.astype(BF), w_ref[...])
            i, f, u, o = gate_parts(sums)
            i, f, u, o = jax.nn.sigmoid(i), jax.nn.sigmoid(f), jnp.tanh(u), jax.nn.sigmoid(o)
            c = f * cp + i * u
            t = jnp.tanh(c)
            h = (o * t).astype(BF).astype(F32)
            now = (hp, cp, i, f, u, o, t, h)
            if saved is None:
                saved = now
            else:
                saved = tuple(jnp.where(row >= part * batch, b, a) for a, b in zip(saved, now))
            h, c = pltpu.roll(h, batch, 0), pltpu.roll(c, batch, 0)
        for ref, value in zip((hp_ref, cp_ref, i_ref, f_ref, u_ref, o_ref, t_ref), saved):
            ref[rows, :] = value
        hidden[rows, :last] = saved[-1][:, :last]
        hidden[rows, last:] = jnp.where(lane < H - last, saved[-1][:, last:], extra_ref[rows, :])

        pl.when(step == tiles // 3)(event_line)
        pl.when(step == tiles * 2 // 3)(event_near)
        for k, (_, end) in enumerate(chunks):
            pl.when(step == end // 8 - 1)(functools.partial(chunk_out, k))
        return h, c

    lax.fori_loop(0, tiles, tile, (h0_ref[...], c0_ref[...]))
    for k in range(len(chunks)):
        chunk_pass(k)
    event_end()
    for k in range(len(chunks)):
        chunk_end(k)


def lstm_forward(batch, plan, x, recur, h0, c0, keep, extra, own, collective_id):
    rows, n = x.shape[0], plan.fsdp
    members = plan.parts
    chunks = len(hidden_chunks(rows))
    vmem = pl.BlockSpec(memory_space=pltpu.VMEM)
    anywhere = pl.BlockSpec(memory_space=pl.ANY)
    return pl.pallas_call(
        functools.partial(lstm_forward_kernel, batch, n),
        out_shape=[jax.ShapeDtypeStruct((rows, HP), F32)] * 7
        + [
            jax.ShapeDtypeStruct((members, rows, HP), BF),
            jax.ShapeDtypeStruct((n,) + plan.block, BF),
        ],
        in_specs=[vmem] * 6 + [anywhere],
        out_specs=[vmem] * 8 + [anywhere],
        scratch_shapes=[
            pltpu.VMEM((rows, HP), F32),
            pltpu.SemaphoreType.DMA((5 * n,)),
            pltpu.SemaphoreType.DMA((3 * members * chunks,)),
        ],
        compiler_params=pltpu.CompilerParams(
            collective_id=collective_id, has_side_effects=True, vmem_limit_bytes=48 * 2**20
        ),
    )(x, recur, h0, c0, keep, extra, own)


def lstm_backward_kernel(
    batch,
    n,
    dh_ref,
    w_ref,
    keep_ref,
    cp_ref,
    i_ref,
    f_ref,
    u_ref,
    o_ref,
    t_ref,
    grad_ref,
    dz_ref,
    out_ref,
    held_near,
    held_line,
    from_last,
    from_near,
    sems,
):
    line = Line(n)
    at, length = line.at, line.length
    LAST, LAST_RECV, NEAR, NEAR_RECV, TO_LINE, LINE_RECV, SIB, SIB_RECV = range(8)
    sem = Semaphores(sems, 2 * length)

    def slot(z, b1, b3):
        return 4 * z + at.stride1 * b1 + at.stride3 * b3

    def to_last(z, b1):
        return remote(
            grad_ref.at[slot(z, b1, 1 - at.last)],
            from_last.at[2 * z + b1],
            sem(LAST, 2 * z + b1),
            sem(LAST_RECV, 2 * z + b1),
            at.partner3,
        )

    def to_near(z):
        return remote(
            held_near.at[z], from_near.at[z], sem(NEAR, z), sem(NEAR_RECV, z), at.partner1
        )

    def to_line(z):
        return remote(
            held_line.at[z], out_ref.at[line.me], sem(TO_LINE, z), sem(LINE_RECV, at.z), line.peer(z)
        )

    def line_arrived(z):
        here = out_ref.at[2 * z + at.c]
        remote(here, here, sem(TO_LINE, z), sem(LINE_RECV, z), line.peer(z)).wait_recv()

    def to_sibling(z, other=False):
        here = out_ref.at[2 * z + (1 - at.c if other else at.c)]
        return remote(here, here, sem(SIB, z), sem(SIB_RECV, z), at.sibling)

    def event_begin():
        def chip(z):
            to_last(z, 1 - at.first).start()

        line.chips(chip)

        def chip_own(z):
            to_last(z, at.first).start()

        line.chips(chip_own)

    def event_last():
        def chip(z):
            b1 = 1 - at.first
            to_last(z, b1).wait_recv()
            held_near[z] = (
                grad_ref[slot(z, b1, at.last)].astype(F32) + from_last[2 * z + b1].astype(F32)
            ).astype(BF)
            to_near(z).start()

        line.chips(chip)

    def event_near():
        def chip(z):
            to_last(z, at.first).wait_recv()
            to_near(z).wait_recv()
            total = (
                grad_ref[slot(z, at.first, at.last)].astype(F32)
                + from_last[2 * z + at.first].astype(F32)
                + from_near[z].astype(F32)
            ).astype(BF)
            held_line[z] = total

            @pl.when(z == at.z)
            def _():
                out_ref[line.me] = total

            @pl.when(z != at.z)
            def _():
                to_line(z).start()

        line.chips(chip)
        to_sibling(at.z).start()

    def event_line():
        def chip(z):
            line_arrived(z)
            to_sibling(z).start()

        line.others(chip)

    def event_end():
        def chip(z):
            to_sibling(z, True).wait_recv()
            to_sibling(z).wait_send()
            to_near(z).wait_send()
            to_last(z, 0).wait_send()
            to_last(z, 1).wait_send()

        line.chips(chip)
        line.others(lambda z: to_line(z).wait_send())

    line.greet(True, False)
    event_begin()
    per_tile = 8 // batch
    tiles = dh_ref.shape[0] // 8
    row = lax.broadcasted_iota(jnp.int32, (8, dz_ref.shape[1]), 0)
    real = lax.broadcasted_iota(jnp.int32, (8, HP), 1) < H

    def tile(step, carried):
        dh_carry, dc_carry = carried
        rows = pl.ds(pl.multiple_of((tiles - 1 - step) * 8, 8), 8)
        keep = keep_ref[rows, :]
        i, f, u, o, t = (r[rows, :] for r in (i_ref, f_ref, u_ref, o_ref, t_ref))
        soft = dh_ref[rows, :]
        to_c = o * (1.0 - t * t)
        to_i = jnp.where(real, u * i * (1.0 - i), 0.0)
        to_f = jnp.where(real, cp_ref[rows, :] * f * (1.0 - f), 0.0)
        to_u = jnp.where(real, i * (1.0 - u * u), 0.0)
        to_o = jnp.where(real, t * o * (1.0 - o), 0.0)
        back = f * keep
        saved = None
        for part in reversed(range(per_tile)):
            dh = jnp.where(real, soft + dh_carry, 0.0)
            dc = dc_carry + dh * to_c
            dz = join_gates([dc * to_i, dc * to_f, dc * to_u, dh * to_o], dz_ref.shape[1])
            saved = dz if saved is None else jnp.where(row >= (part + 1) * batch, saved, dz)
            dh_carry = dot(dz.astype(BF), w_ref[...]) * keep
            dc_carry = dc * back
            dh_carry, dc_carry = (
                pltpu.roll(dh_carry, 8 - batch, 0),
                pltpu.roll(dc_carry, 8 - batch, 0),
            )
        dz_ref[rows, :] = saved
        pl.when(step == tiles // 3)(event_last)
        pl.when(step == tiles * 2 // 3)(event_near)
        pl.when(step == tiles - 2)(event_line)
        return dh_carry, dc_carry

    zero = jnp.zeros((8, HP), F32)
    lax.fori_loop(0, tiles, tile, (zero, zero))
    event_end()


def lstm_backward(batch, plan, columns, dh, recur_t, keep, states, grad, collective_id):
    rows, n = dh.shape[0], plan.fsdp
    length = n // 4
    vmem = pl.BlockSpec(memory_space=pltpu.VMEM)
    return pl.pallas_call(
        functools.partial(lstm_backward_kernel, batch, n),
        out_shape=[
            jax.ShapeDtypeStruct((rows, columns), F32),
            jax.ShapeDtypeStruct((plan.parts,) + plan.block, BF),
        ],
        in_specs=[vmem] * 10,
        out_specs=[vmem] * 2,
        scratch_shapes=[
            pltpu.VMEM((length,) + plan.block, BF),
            pltpu.VMEM((length,) + plan.block, BF),
            pltpu.VMEM((2 * length,) + plan.block, BF),
            pltpu.VMEM((length,) + plan.block, BF),
            pltpu.SemaphoreType.DMA((8 * 2 * length,)),
        ],
        compiler_params=pltpu.CompilerParams(
            collective_id=collective_id, has_side_effects=True, vmem_limit_bytes=48 * 2**20
        ),
    )(dh, recur_t, keep, *states, grad)


def turned(value, lanes):
    rows = value.shape[0]
    if rows < lanes:
        value = jnp.concatenate([value, jnp.zeros((lanes - rows, value.shape[1]), F32)], axis=0)
    return value.T


def copy_windows(plan, source, target, base, found, place):
    target[...] = jnp.zeros_like(target)
    for o, first, last in found:
        start, to = plan.starts[o] - base, place(o) * plan.rows
        target[to + first : to + last, :] = source[start + first : start + last, :]


def add_windows(plan, source, target, base, found, begin):
    for o, first, last in found:
        start, at = plan.starts[o] - base, o * plan.rows - begin
        target[start + first : start + last, :] += source[at + first : at + last, :]


def matrices_of(plan, filters):
    result = []
    for m in range(4):
        base = m * (filters + 1)
        found = plan.meeting(base, base + filters + 1)
        result.append((base, found, found[0][0] * plan.rows, (found[-1][0] + 1) * plan.rows))
    return result


def head_kernel(plans, soft, filters, blocks, *refs):
    highway, lstm = plans
    owns = refs[:2]
    codes_ref, length_ref, table_ref, kernel_ref, width_ref, soft_ref = refs[2:8]
    highway_out, lstm_out, x_ref, recur_ref, soft_out = refs[8:13]
    kept_outs, wide_out = refs[13:16], refs[16]
    features, trans_refs, gate_refs = refs[17:20], refs[20:22], refs[22:24]
    highway_w, lstm_w, turned_ref, wide, recur_sum = refs[24:29]
    kept_stages, wide_stage, gather_sems, out_sems, keep_sems = refs[29:32], *refs[32:]
    rows, fp = features[0].shape
    words = turned_ref.shape[1]
    work = Gather(plans, owns, (highway_w, lstm_w), gather_sems, True)
    work.line.greet()

    def conv(begin, end):
        def block(i, _):
            at = pl.ds(pl.multiple_of(i * WORD_BLOCK, WORD_BLOCK), WORD_BLOCK)
            slots = pl.ds(
                pl.multiple_of(i * WORD_BLOCK * SLOTS, WORD_BLOCK * SLOTS), WORD_BLOCK * SLOTS
            )
            pl.when(i >= 2)(lambda: wait_kept(i - 2))
            k = lax.rem(i, 2)
            conv_forward_block(
                filters,
                codes_ref[slots, :],
                length_ref[at, :],
                (table_ref, kernel_ref, width_ref),
                features[0],
                at,
                [stage.at[k] for stage in kept_stages],
            )
            for copy in keep_copies(i):
                copy.start()
            return 0

        lax.fori_loop(begin, end, block, 0)

    def keep_copies(i):
        k = lax.rem(i, 2)
        size = WORD_BLOCK * SLOTS
        to = pl.ds(pl.multiple_of(i * size, size), size)
        return [
            pltpu.make_async_copy(stage.at[k], out.at[to], keep_sems.at[2 * j + k])
            for j, (stage, out) in enumerate(zip(kept_stages, kept_outs))
        ]

    def wait_kept(i):
        for copy in keep_copies(i):
            copy.wait()

    def wide_copy(m):
        return pltpu.make_async_copy(wide_stage.at[m % 2], wide_out.at[m], keep_sems.at[6 + m % 2])

    chunk = 384

    def layer_sum(m, wide=wide):
        base, found, begin, end = matrices[m]
        copy_windows(
            highway, turned_ref, wide.at[: end - begin], base, found, lambda o: o - found[0][0]
        )
        target = (trans_refs if m % 2 == 0 else gate_refs)[m // 2]
        if m >= 2:
            wide_copy(m - 2).wait()
        wide_stage[m % 2, : end - begin, :] = wide[: end - begin, :].astype(BF)
        wide_copy(m).start()

        def columns(j, _):
            where = pl.ds(pl.multiple_of(j * chunk, chunk), chunk)
            left = wide[: end - begin, :].astype(BF)
            target[:, where] = dot_rows(left, highway_w[begin:end, where])[:rows]
            return 0

        lax.fori_loop(0, fp // chunk, columns, 0)

    def layer(l):
        turned_ref[:fp, :] = turned(features[l][...], words)
        layer_sum(2 * l)

    def layer_end(l):
        layer_sum(2 * l + 1)
        trans, gate = trans_refs[l][...], jax.nn.sigmoid(gate_refs[l][...])
        gate_refs[l][...] = gate
        value = gate * trans * jax.nn.sigmoid(trans) + (1.0 - gate) * features[l][...]
        lane = lax.broadcasted_iota(jnp.int32, (rows, fp), 1)
        features[l + 1][...] = keep_feature(value, lane, filters)

    matrices = matrices_of(highway, filters)
    work.begin(0)
    of_highway, of_lstm = work.steps(0), work.steps(1)
    passing = len(of_highway) - 2 * work.line.length
    third = -(-blocks // 3)
    conv(0, third)
    work.run(of_highway[: passing // 2])
    conv(third, 2 * third)
    work.run(of_highway[passing // 2 : passing])
    work.begin(1)
    conv(2 * third, blocks)
    soft.place_blocks(soft_ref, soft_out)
    work.run(of_lstm[: passing // 2])
    work.run(of_highway[passing:])
    work.from_sibling(0)
    out_copies = [
        pltpu.make_async_copy(highway_w, highway_out, out_sems.at[0]),
        pltpu.make_async_copy(lstm_w, lstm_out, out_sems.at[1]),
    ]
    out_copies[0].start()
    layer(0)
    work.run(of_lstm[passing // 2 : passing - 1])
    layer_end(0)
    work.run(of_lstm[passing - 1 : passing])
    layer(1)
    layer_end(1)

    turned_ref[...] = jnp.zeros_like(turned_ref)
    sub = lax.broadcasted_iota(jnp.int32, (fp, words), 0)
    turned_ref[:fp, :] = jnp.where(sub < filters, turned(features[2][...], words), 0.0)
    turned_ref[lstm.used - 1 : lstm.used, :] = jnp.ones((1, words), F32)
    wide = wide.at[: lstm.total]
    copy_windows(lstm, turned_ref, wide, 0, lstm.meeting(0, lstm.used), lambda o: o)
    work.run(of_lstm[passing:])
    work.from_sibling(1)
    out_copies[1].start()
    left = wide[...].astype(BF)
    half = lstm.block[1]
    for h in range(2):
        x_ref[:, h * half : (h + 1) * half] = dot_rows(left, lstm_w[h])[:rows]

    recur_sum[...] = jnp.zeros_like(recur_sum)
    depth = lstm.block[0]
    for h in range(2):
        for slot in sorted({o // lstm.dp for o, _, _ in lstm.meeting(filters, filters + H)}):
            piece = lstm_w[h, slot * depth : (slot + 1) * depth, :].astype(F32)
            for o, first, last in lstm.meeting(filters, filters + H):
                if o // lstm.dp == slot:
                    start, at = lstm.starts[o] - filters, (o % lstm.dp) * lstm.rows
                    recur_sum[start + first : start + last, h * half : (h + 1) * half] += piece[
                        at + first : at + last
                    ]
    recur_ref[...] = recur_sum[...].astype(BF)
    for a in range(2):
        work.finish(a)
    for copy in out_copies:
        copy.wait()
    for m in (2, 3):
        wide_copy(m).wait()
    for i in range(max(blocks - 2, 0), blocks):
        wait_kept(i)


def head(plans, soft, filters, own, conv_inputs, soft_flat, rows, fp, collective_id):
    highway, lstm = plans
    words = up_to(rows, 2 * LANE)
    vmem = pl.BlockSpec(memory_space=pltpu.VMEM)
    anywhere = pl.BlockSpec(memory_space=pl.ANY)
    feature = jax.ShapeDtypeStruct((rows, fp), F32)
    matrices = matrices_of(highway, filters)
    longest_matrix = max(end - begin for _, _, begin, end in matrices)
    longest = max(lstm.total, longest_matrix)
    kept_widths = (HOT, LANE, fp)
    return pl.pallas_call(
        functools.partial(head_kernel, plans, soft, filters, rows // WORD_BLOCK),
        out_shape=[
            jax.ShapeDtypeStruct(highway.shape, BF),
            jax.ShapeDtypeStruct(lstm.shape, BF),
            jax.ShapeDtypeStruct((rows, lstm.columns), F32),
            jax.ShapeDtypeStruct((HP, lstm.columns), BF),
            soft.placed_shape(),
        ]
        + [jax.ShapeDtypeStruct((rows * SLOTS, width), BF) for width in kept_widths]
        + [jax.ShapeDtypeStruct((4, longest_matrix, words), BF)]
        + [feature] * 7,
        in_specs=[anywhere] * 2 + [vmem] * 6,
        out_specs=[anywhere] * 2 + [vmem] * 3 + [anywhere] * 4 + [vmem] * 7,
        scratch_shapes=[
            pltpu.VMEM(highway.shape, BF),
            pltpu.VMEM(lstm.shape, BF),
            pltpu.VMEM((up_to(max(lstm.used, fp), LANE), words), F32),
            pltpu.VMEM((longest, words), F32),
            pltpu.VMEM((HP, lstm.columns), F32),
        ]
        + [pltpu.VMEM((2, WORD_BLOCK * SLOTS, width), BF) for width in kept_widths]
        + [
            pltpu.VMEM((2, longest_matrix, words), BF),
            Gather.semaphores(plans),
            pltpu.SemaphoreType.DMA((2,)),
            pltpu.SemaphoreType.DMA((8,)),
        ],
        compiler_params=pltpu.CompilerParams(
            collective_id=collective_id, has_side_effects=True, vmem_limit_bytes=62 * 2**20
        ),
    )(*own, *conv_inputs, soft.blocks_of(soft_flat))


def highway_backward_kernel(plans, conv, filters, blocks, *refs):
    highway, lstm = plans
    dz_ref, hp_ref = refs[:2]
    features, trans_refs, gate_refs = refs[2:5], refs[5:7], refs[7:9]
    kernel_ref, mask_ref, fold_ref = refs[9:12]
    highway_all, lstm_all, kept_all, wide_all = refs[12], refs[13], refs[14:17], refs[17]
    lstm_landed, grad_out, kernel_grad, total_out = refs[18:22]
    refs = refs[22:]
    if conv:
        highway_landed, highway_total, conv_out = refs[:3]
        conv_in, refs = refs[3], refs[4:]
        small = SmallSum(conv, conv_in, conv_out, refs[:5])
        refs = refs[5:]
    lstm_grad, highway_w, lstm_w, turned_ref, wide, back, dz, pairs = refs[:8]
    carry, feature_grad, hot_grad, load_sems, pair_sems, out_sems = refs[8:14]
    kept, wide_low, kept_sems, refs = refs[14:17], refs[17], refs[18], refs[19:]
    rows, fp = features[0].shape
    words = turned_ref.shape[1]
    at = Place()
    total = total_out.at[at.c]
    if conv:
        work = Reduce(
            [lstm, highway],
            [lstm_grad, grad_out],
            [total, highway_total],
            [lstm_landed, highway_landed],
            refs,
            [True, False],
        )
    else:
        work = Reduce([lstm], [lstm_grad], [total], [lstm_landed], refs, [True])
    length, items = work.line.length, work.items
    matrices = matrices_of(highway, filters)
    half = lstm.block[1]
    of_input = lstm.meeting(0, filters)
    input_rows = lstm_w.shape[0]

    def layer_rows(l):
        begin, end = matrices[2 * l][2], matrices[2 * l + 1][3]
        return begin, end

    def load_layer(l):
        begin, end = layer_rows(l)
        return pltpu.make_async_copy(
            highway_all.at[pl.ds(begin, end - begin)],
            highway_w.at[pl.ds(0, end - begin)],
            load_sems.at[l],
        )

    def load_lstm(h):
        return pltpu.make_async_copy(
            lstm_all.at[h, pl.ds(0, input_rows)], lstm_w, load_sems.at[2 + h]
        )

    def load_kept(i):
        k = lax.rem(i, 2)
        size = WORD_BLOCK * SLOTS
        at = pl.ds(pl.multiple_of(i * size, size), size)
        return [
            pltpu.make_async_copy(source.at[at], to.at[k], kept_sems.at[2 * j + k])
            for j, (source, to) in enumerate(zip(kept_all, kept))
        ]

    def load_wide(m):
        return pltpu.make_async_copy(wide_all.at[m], wide_low.at[m % 2], kept_sems.at[6 + m % 2])

    load_layer(1).start()
    load_lstm(0).start()
    for i in range(min(2, blocks)):
        for copy in load_kept(jnp.int32(i)):
            copy.start()
    for m in range(2):
        load_wide(m).start()
    work.line.greet()

    dz[...] = jnp.zeros_like(dz)
    dz[:rows, :] = dz_ref[...].astype(BF)
    lane = lax.broadcasted_iota(jnp.int32, (rows, HP), 1)
    hidden = jnp.where(lane < H, hp_ref[...], jnp.where(lane == H, 1.0, 0.0))
    sub = lax.broadcasted_iota(jnp.int32, (fp, words), 0)
    turned_ref[:fp, :] = jnp.where(sub < filters, turned(features[2][...], words), 0.0)
    depth = up_to(H + 1, 8)
    turned_ref[filters : filters + depth, :] = turned(hidden, words)[:depth]
    copy_windows(
        lstm,
        turned_ref,
        wide.at[: lstm.total],
        0,
        lstm.meeting(0, lstm.used),
        lambda o: lstm.position[o],
    )
    unit = lstm.total // (2 * length)

    def lstm_weights(i, _):
        where = pl.ds(pl.multiple_of(i * unit, unit), unit)
        left = wide[where, :].astype(BF)
        for h in range(2):
            lstm_grad[h, where, :] = dot(left, dz[:, h * half : (h + 1) * half]).astype(BF)
        return 0

    lax.fori_loop(0, 2 * length, lstm_weights, 0)
    work.begin(0)

    lane = lax.broadcasted_iota(jnp.int32, (rows, fp), 1)
    back[...] = jnp.zeros_like(back)
    for h in range(2):
        load_lstm(h).wait()
        wide[:input_rows, :] = dot_cols(lstm_w[...], dz[:, h * half : (h + 1) * half])
        if h == 0:
            load_lstm(1).start()
        add_windows(lstm, wide, back, 0, of_input, 0)
    grad = jnp.where(lane < filters, back[...].T[:rows], 0.0)

    def lead(k):
        work.legs(work.first_leg, 0, k * items // 4, (k + 1) * items // 4)

    lead(0)
    pairs[...] = jnp.zeros_like(pairs)
    for l in (1, 0):
        trans, gate = trans_refs[l][...], gate_refs[l][...]
        sig = jax.nn.sigmoid(trans)
        pairs[2 * l, :rows, :] = (grad * gate * sig * (1.0 + trans * (1.0 - sig))).astype(BF)
        pairs[2 * l + 1, :rows, :] = (
            grad * (trans * sig - features[l][...]) * gate * (1.0 - gate)
        ).astype(BF)
        load_layer(l).wait()
        back[...] = jnp.zeros_like(back)
        begin = layer_rows(l)[0]
        for m in (2 * l, 2 * l + 1):
            base, found, low, high = matrices[m]
            result = dot_cols(highway_w[low - begin : high - begin, :], pairs[m])
            add_windows(highway, result, back, base, found, low)
            if m % 2 and l:
                load_layer(0).start()
            if m > 0:
                lead(4 - m)
        grad = grad * (1.0 - gate) + back[...].T[:rows]
        grad = jnp.where(lane < filters, grad, 0.0)
    feature_grad[...] = grad

    kernel_grad[...] = jnp.zeros_like(kernel_grad)
    hot_grad[...] = jnp.zeros_like(hot_grad)

    def conv_block(i, _):
        where = pl.ds(pl.multiple_of(i * WORD_BLOCK, WORD_BLOCK), WORD_BLOCK)
        for copy in load_kept(i):
            copy.wait()
        k = lax.rem(i, 2)
        conv_backward_block(
            [ref.at[k] for ref in kept], kernel_ref, feature_grad, where, kernel_grad, hot_grad
        )

        @pl.when(i + 2 < blocks)
        def _():
            for copy in load_kept(i + 2):
                copy.start()


        @pl.when(i >= blocks - 4)
        def _():
            k = i - (blocks - 4)
            work.legs(work.middle_leg, 0, k * length // 4, (k + 1) * length // 4)

        return 0

    lax.fori_loop(0, blocks, conv_block, 0)
    kernel_grad[:, fp:] = jnp.dot(
        fold_ref[...],
        hot_grad[...] * mask_ref[...],
        precision=lax.Precision.HIGHEST,
        preferred_element_type=F32,
    )
    steps = []
    if conv:
        conv.fill(conv_in, kernel_grad)
        steps = small.steps()
        steps[0]()

    staged = highway_w
    chunk = 384
    size = highway.rows
    pending, shared = [], None
    empty = [o for o in range(len(highway.starts)) if all(o != f[0] for m in matrices for f in m[1])]
    for m in range(4):
        base, found, low, high = matrices[m]
        load_wide(m).wait()
        for copy in pending:
            copy.wait()
        adds = shared == found[0][0]
        shares = m < 3 and matrices[m + 1][1][0][0] == found[-1][0]
        count = len(found)

        def columns(j, _):
            where = pl.ds(pl.multiple_of(j * chunk, chunk), chunk)
            result = dot(wide_low[m % 2, : high - low, :], pairs[m, :, where])
            if adds:
                first = result[:size] + carry[:, where]
                staged[:size, where] = first.astype(BF)
                staged[size : high - low, where] = result[size:].astype(BF)
            else:
                staged[: high - low, where] = result.astype(BF)
            if shares:
                carry[:, where] = result[(count - 1) * size :]
            return 0

        lax.fori_loop(0, fp // chunk, columns, 0)
        if m < 2:
            load_wide(m + 2).start()
        shared = found[-1][0] if shares else None
        sent = found[:-1] if shares else found
        pending = [
            pltpu.make_async_copy(
                staged.at[pl.ds(k * size, size)],
                grad_out.at[pl.ds(highway.position[o] * size, size)],
                out_sems.at[k],
            )
            for k, (o, _, _) in enumerate(sent)
        ]
        for copy in pending:
            copy.start()
        if conv and m == 2:
            steps[1]()
        work.legs(
            work.middle_leg, 0, length + m * length // 4, length + (m + 1) * length // 4
        )
    for copy in pending:
        copy.wait()
    if empty:
        staged[:size, :] = jnp.zeros((size, fp), BF)
        for o in empty:
            copy = pltpu.make_async_copy(
                staged.at[pl.ds(0, size)],
                grad_out.at[pl.ds(highway.position[o] * size, size)],
                out_sems.at[0],
            )
            copy.start()
            copy.wait()
    copy = remote(total, total, pair_sems.at[0], pair_sems.at[1], at.sibling)
    if not conv:
        work.last_leg(0)
        copy.start()
    else:
        work.begin(1)
        work.legs(work.first_leg, 1, 0, length)
        steps[2]()
        work.legs(work.first_leg, 1, length, items)
        late = steps[3:-1]
        for k, step in enumerate(late):
            work.legs(
                work.middle_leg, 1, k * items // len(late), (k + 1) * items // len(late)
            )
            step()
            if k == 1:
                work.last_leg(0)
                copy.start()
        work.last_leg(1)
        steps[-1]()
    for a in range(2 if conv else 1):
        work.finish(a)
    copy.wait()


def conv_columns(fp):
    return up_to(fp + LANE, 2 * LANE)


def highway_backward(
    plans, conv, filters, dz, hp, features, trans, gates, conv_inputs, everywhere, collective_id
):
    highway, lstm = plans
    rows, fp = features[0].shape
    words = up_to(rows, 2 * LANE)
    vmem = pl.BlockSpec(memory_space=pltpu.VMEM)
    anywhere = pl.BlockSpec(memory_space=pl.ANY)
    matrices = matrices_of(highway, filters)
    longest = max([lstm.total] + [end - begin for _, _, begin, end in matrices])
    layer = max(matrices[2 * l + 1][3] - matrices[2 * l][2] for l in range(2))
    input_rows = up_to((lstm.meeting(0, filters)[-1][0] + 1) * lstm.rows, 16)
    return pl.pallas_call(
        functools.partial(highway_backward_kernel, plans, conv, filters, rows // WORD_BLOCK),
        out_shape=[
            jax.ShapeDtypeStruct((lstm.fsdp,) + lstm.block, BF),
            jax.ShapeDtypeStruct(highway.shape, BF),
            jax.ShapeDtypeStruct((LANE, conv_columns(fp)), F32),
            jax.ShapeDtypeStruct((2,) + lstm.block, F32),
        ]
        + (
            [
                jax.ShapeDtypeStruct((highway.fsdp,) + highway.block, BF),
                jax.ShapeDtypeStruct(highway.block, F32),
                jax.ShapeDtypeStruct(conv.shape, F32),
            ]
            if conv
            else []
        ),
        in_specs=[vmem] * 12 + [anywhere] * 6,
        out_specs=[anywhere] * 2 + [vmem] * 2 + ([anywhere, vmem, vmem] if conv else []),
        scratch_shapes=(
            [pltpu.VMEM(conv.shape, F32)] + SmallSum.scratch(conv) if conv else []
        )
        + [
            pltpu.VMEM(lstm.shape, BF),
            pltpu.VMEM((layer, highway.columns), BF),
            pltpu.VMEM((input_rows, lstm.block[1]), BF),
            pltpu.VMEM((up_to(max(lstm.used + 8, fp), LANE), words), F32),
            pltpu.VMEM((longest, words), F32),
            pltpu.VMEM((fp, words), F32),
            pltpu.VMEM((words, lstm.columns), BF),
            pltpu.VMEM((4, words, fp), BF),
            pltpu.VMEM((highway.rows, fp), F32),
            pltpu.VMEM((rows, fp), F32),
            pltpu.VMEM((HOT, LANE), F32),
            pltpu.SemaphoreType.DMA((4,)),
            pltpu.SemaphoreType.DMA((2,)),
            pltpu.SemaphoreType.DMA((max(len(found) for _, found, _, _ in matrices),)),
        ]
        + [pltpu.VMEM((2, WORD_BLOCK * SLOTS, width), BF) for width in (HOT, LANE, fp)]
        + [pltpu.VMEM((2,) + everywhere[-1].shape[1:], BF), pltpu.SemaphoreType.DMA((8,))]
        + (
            Reduce.scratch([lstm, highway], [True, False], [True, True])
            if conv
            else Reduce.scratch([lstm], [True], [True])
        ),
        compiler_params=pltpu.CompilerParams(
            collective_id=collective_id, has_side_effects=True, vmem_limit_bytes=255 * 2**18
        ),
    )(dz, hp, *features, *trans, *gates, *conv_inputs, *everywhere)


def softmax_kernel(
    vocab,
    n,
    h_ref,
    w_ref,
    map_ref,
    map_back_ref,
    loss_ref,
    grad_h_ref,
    grad_w_ref,
    spread_back,
    logits,
    grads,
    stats,
    for_sibling,
    from_sibling,
    for_line,
    from_line,
    own_total,
    sems,
):
    line = Line(n)
    at, length, me = line.at, line.length, line.me
    members, rows, _ = h_ref.shape
    width = w_ref.shape[-1]
    w = w_ref[...].reshape(-1, width)
    STAT, STAT_RECV, SIB, SIB_RECV, TO_LINE, LINE_RECV = range(6)
    sem = Semaphores(sems, members)
    column = me * width + lax.broadcasted_iota(jnp.int32, (rows, width), 1)
    real_column = column.astype(F32)
    words = up_to(rows, LANE)
    lane = lax.broadcasted_iota(jnp.int32, (rows, LANE), 1)
    aside = HP - LANE

    def pieces(b):
        tail = h_ref[b, :, aside:].astype(F32)
        first = H + 1 - aside
        target = tail[:, first : first + 1] * 256.0 + tail[:, first + 1 : first + 2]
        scale = (
            tail[:, first + 2 : first + 3]
            + tail[:, first + 3 : first + 4]
            + tail[:, first + 4 : first + 5]
        )
        return target, scale

    line.greet(False, True)

    def forward(b, _):
        h = h_ref[b]
        wide = dot(h, map_ref[...]).astype(BF)
        spread_back[b] = dot(h, map_back_ref[...]).astype(BF)
        now = jnp.where(column < vocab, dot(wide, w), -1e30)
        logits[b] = now
        target, _ = pieces(b)
        top = jnp.max(now, axis=1, keepdims=True)
        log_sum = top + jnp.log(jnp.sum(jnp.exp(now - top), axis=1, keepdims=True))
        picked = jnp.sum(jnp.where(real_column == target, now, 0.0), axis=1, keepdims=True)
        both = jnp.where(lane == 0, log_sum, jnp.where(lane == 1, picked, 0.0))
        both = jnp.concatenate([both, jnp.zeros((words - rows, LANE), F32)], axis=0).T
        stats[me, 0, pl.ds(b, 1), :] = both[0:1, :]
        stats[me, 1, pl.ds(b, 1), :] = both[1:2, :]
        return 0

    lax.fori_loop(0, members, forward, 0)

    def stat(member, target):
        here = stats.at[member]
        return remote(here, here, sem(STAT, member), sem(STAT_RECV, member), target)

    def stat_out(z):
        return [
            remote(
                stats.at[me], stats.at[me], sem(STAT, 2 * z + core), sem(STAT_RECV, me), target
            )
            for core, target in ((at.c, line.peer(z)), (1 - at.c, line.peer(z, True)))
        ]

    def send_stats(z):
        for copy in stat_out(z):
            copy.start()

    line.others(send_stats)
    to_pair = remote(
        stats.at[me], stats.at[me], sem(STAT, 2 * at.z + 1 - at.c), sem(STAT_RECV, me), at.sibling
    )
    to_pair.start()

    def stats_in(z):
        for core in (at.c, 1 - at.c):
            stat(2 * z + core, at.sibling).wait_recv()

    line.others(stats_in)
    stat(2 * at.z + 1 - at.c, at.sibling).wait_recv()
    top = stats[0, 0]
    for q in range(1, members):
        top = jnp.maximum(top, stats[q, 0])
    total = jnp.zeros_like(top)
    picked = jnp.zeros_like(top)
    for q in range(members):
        total += jnp.exp(stats[q, 0] - top)
        picked += stats[q, 1]
    log_total = top + jnp.log(total)
    loss_ref[...] = log_total - picked
    log_columns = jnp.concatenate(
        [log_total, jnp.zeros((LANE - members, words), F32)], axis=0
    ).T[:rows]

    def to_sibling(z):
        return remote(
            for_sibling.at[z], from_sibling.at[z], sem(SIB, z), sem(SIB_RECV, z), at.sibling
        )

    def to_line(z):
        return remote(
            for_line.at[z], from_line.at[at.z], sem(TO_LINE, z), sem(LINE_RECV, at.z), line.peer(z)
        )

    def backward(k, _):
        z = lax.rem(k, length)
        mine = k >= length
        b = 2 * z + jnp.where(mine, at.c, 1 - at.c)
        target, scale = pieces(b)
        log_sum = jnp.sum(jnp.where(lane == b, log_columns, 0.0), axis=1, keepdims=True)
        share = jnp.exp(logits[b] - log_sum)
        grad = ((share - (real_column == target).astype(F32)) * scale).astype(BF)
        grads[b] = grad
        back = dot_cols(grad, w)

        @pl.when(jnp.logical_not(mine))
        def _():
            for_sibling[z] = back.astype(BF)
            to_sibling(z).start()

        @pl.when(mine)
        def _():
            to_sibling(z).wait_recv()
            total = back + from_sibling[z].astype(F32)

            @pl.when(z == at.z)
            def _():
                own_total[...] = total

            @pl.when(z != at.z)
            def _():
                for_line[z] = total.astype(BF)
                to_line(z).start()

        return 0

    lax.fori_loop(0, 2 * length, backward, 0)

    depth = map_ref.shape[1]
    unit = 256
    everything = grads[...].reshape(members * rows, width)

    def weight_grad(m, _):
        left = spread_back[:, :, pl.ds(pl.multiple_of(m * unit, unit), unit)]
        result = dot_rows(left.reshape(members * rows, unit), everything).astype(BF)
        grad_w_ref[pl.ds(m * unit, unit), :] = result
        return 0

    lax.fori_loop(0, depth // unit, weight_grad, 0)

    def arrived(z):
        remote(
            from_line.at[z], from_line.at[z], sem(TO_LINE, z), sem(LINE_RECV, z), line.peer(z)
        ).wait_recv()
        own_total[...] += from_line[z].astype(F32)

    line.others(arrived)
    spread_grad = own_total[...]
    high = spread_grad.astype(BF)
    low = (spread_grad - high.astype(F32)).astype(BF)
    grad_h_ref[...] = dot_cols(high, map_ref[...]) + dot_cols(low, map_ref[...])

    def finish(z):
        for copy in stat_out(z):
            copy.wait_send()
        to_line(z).wait_send()

    line.others(finish)
    line.chips(lambda z: to_sibling(z).wait_send())
    to_pair.wait_send()


def word_softmax(plan, h, weights, mapping, mapping_back, collective_id):
    members, rows, depth = h.shape
    n = plan.fsdp
    spread = mapping.shape[1]
    per_slot, width = plan.block
    words = up_to(rows, LANE)
    length = members // 2
    vmem = pl.BlockSpec(memory_space=pltpu.VMEM)
    loss, grad_h, grad_w = pl.pallas_call(
        functools.partial(softmax_kernel, plan.width, n),
        out_shape=[
            jax.ShapeDtypeStruct((members, words), F32),
            jax.ShapeDtypeStruct((rows, depth), F32),
            jax.ShapeDtypeStruct((spread, width), BF),
        ],
        in_specs=[vmem] * 4,
        out_specs=[vmem] * 3,
        scratch_shapes=[
            pltpu.VMEM((members, rows, spread), BF),
            pltpu.VMEM((members, rows, width), F32),
            pltpu.VMEM((members, rows, width), BF),
            pltpu.VMEM((members, 2, members, words), F32),
            pltpu.VMEM((length, rows, spread), BF),
            pltpu.VMEM((length, rows, spread), BF),
            pltpu.VMEM((length, rows, spread), BF),
            pltpu.VMEM((length, rows, spread), BF),
            pltpu.VMEM((rows, spread), F32),
            pltpu.SemaphoreType.DMA((6 * members,)),
        ],
        compiler_params=pltpu.CompilerParams(
            collective_id=collective_id, has_side_effects=True, vmem_limit_bytes=62 * 2**20
        ),
    )(h, weights, mapping, mapping_back)
    return loss, grad_h, grad_w.reshape((n,) + plan.block)


def shards(
    fsdp_count,
    dp_count,
    chars,
    lengths,
    targets,
    resets,
    init_state,
    window_grad,
    char_table,
    conv_weight,
    conv_bias,
    highway_flat,
    lstm_flat,
    soft_flat,
):
    micro_count, streams, step_count, letters = chars.shape
    char_count, embed_dim = char_table.shape
    filters = conv_weight.shape[1]
    batch = micro_count * streams
    words = step_count * batch
    rows = up_to(words, 16)
    fp = up_to(filters + 1, LANE)
    dp_at, fsdp_at = lax.axis_index("dp"), lax.axis_index("fsdp")
    highway = Windows(
        highway_flat.shape[0] * fsdp_count, filters, 4 * (filters + 1), fsdp_count, dp_count, True
    )
    lstm = Windows(
        lstm_flat.shape[0] * fsdp_count, 4 * H, filters + H + 1, fsdp_count, dp_count, False
    )
    soft = Windows(
        soft_flat.shape[0] * fsdp_count, V, H + 1, fsdp_count, dp_count, False, fsdp_count // 2
    )
    member = 2 * (fsdp_at // 4) + lax.rem(dp_at, 2)

    def by_step(array):
        return jnp.moveaxis(array.reshape((batch, step_count) + array.shape[3:]), 1, 0).reshape(
            (words,) + array.shape[3:]
        )

    def pad_rows(array, value=0):
        return jnp.pad(
            array,
            [(0, rows - words)] + [(0, 0)] * (array.ndim - 1),
            constant_values=value,
        )

    word_chars = pad_rows(by_step(chars))
    word_lengths = pad_rows(by_step(lengths))[:, None]
    position = jnp.arange(letters, dtype=jnp.int32)[None, :]
    codes = jnp.where(position < word_lengths, word_chars, -1)
    codes = jnp.pad(codes, ((0, 0), (0, SLOTS - letters)), constant_values=-1)
    codes = codes.reshape(rows * SLOTS, 1)
    column = np.arange(fp)
    widths = np.ones((fp,), np.int32)
    for cut_at in FILTER_CUTS:
        widths = widths + ((column >= filters * cut_at // 22) & (column < filters))
    widths = widths.astype(np.int32)
    kernel_mask = jnp.asarray(
        np.arange(KMAX * embed_dim)[:, None] // embed_dim < widths[None, :filters]
    )
    ones_row = KMAX * embed_dim
    kernel = jnp.concatenate(
        [jnp.where(kernel_mask, conv_weight, jnp.zeros_like(conv_weight)), conv_bias[None, :]], axis=0
    )
    kernel = jnp.pad(kernel, ((0, LANE - ones_row - 1), (0, fp - filters)))
    spread_table = jnp.concatenate(
        [
            jnp.pad(char_table, ((0, 0), (q * embed_dim, LANE - (q + 1) * embed_dim)))
            for q in range(KMAX)
        ]
        + [jnp.asarray((np.arange(LANE) == ones_row)[None, :].astype(np.float32)).astype(BF)],
        axis=0,
    )
    spread_table = jnp.pad(spread_table, ((0, HOT - KMAX * char_count - 1), (0, 0)))
    conv_inputs = (codes, word_lengths, spread_table, kernel, jnp.asarray(widths)[None, :])

    highway_all, lstm_all, from_input, recur, soft_placed, *kept = head(
        [highway, lstm],
        soft,
        filters,
        place_all([highway, lstm], [highway_flat, lstm_flat]),
        conv_inputs,
        soft_flat,
        rows,
        fp,
        1,
    )
    kept_parts, kept = kept[:4], kept[4:]
    features, trans, gates = kept[:3], kept[3:5], kept[5:7]

    soft_own = soft.from_placed(soft_placed)
    recur_t = recur.T
    keep = pad_rows(by_step(1 - resets).astype(F32))[:, None]
    start = init_state.reshape(batch, 2, H)
    start = jnp.pad(start, ((0, 8 - batch), (0, 0), (0, HP - H)))
    row_scale = jnp.broadcast_to(
        window_grad.reshape(1, batch) / step_count, (step_count, batch)
    ).reshape(words)
    goal = by_step(targets)
    scale_high = lax.reduce_precision(row_scale, 8, 7)
    scale_mid = lax.reduce_precision(row_scale - scale_high, 8, 7)
    extra = jnp.stack(
        [
            jnp.ones((words,), F32),
            (goal // 256).astype(F32),
            (goal % 256).astype(F32),
            scale_high,
            scale_mid,
            row_scale - scale_high - scale_mid,
        ],
        axis=1,
    )
    aside = H - (HP - LANE)
    extra = jnp.pad(extra, ((0, rows - words), (aside, LANE - aside - extra.shape[1])))
    *states, hidden_all, soft_part = lstm_forward(
        batch,
        soft,
        from_input,
        recur,
        start[:, 0].astype(BF).astype(F32),
        start[:, 1],
        keep,
        extra,
        soft_own,
        4,
    )
    hp = states[0]

    word_loss, grad_hidden, soft_grad = word_softmax(
        soft,
        hidden_all,
        soft_part,
        one_hot_map(HP, soft.gathered),
        one_hot_map(HP, soft.reduced),
        5,
    )
    word_loss = lax.dynamic_index_in_dim(word_loss, member, 0, keepdims=False)
    window_loss = jnp.mean(word_loss[:words].reshape(step_count, batch), axis=0).reshape(
        micro_count, streams
    )

    dz, soft_part = lstm_backward(
        batch, soft, lstm.columns, grad_hidden, recur_t, keep, states[1:], soft_grad, 6
    )
    hot_row, hot_lane = np.arange(HOT), np.arange(LANE)
    hot_mask = (hot_row[:, None] // char_count == hot_lane[None, :] // embed_dim) & (
        hot_row[:, None] < KMAX * char_count
    )
    hot_fold = (hot_row[None, :] % char_count == np.arange(LANE)[:, None]) & (
        hot_row[None, :] < KMAX * char_count
    )
    conv = Dense(LANE, conv_columns(fp), fsdp_count)
    at_once = 2 * fsdp_count * highway.block[0] * highway.block[1] * 2 <= 12 * 2**20
    _, highway_grad, conv_grad, lstm_part, *rest = highway_backward(
        [highway, lstm],
        conv if at_once else None,
        filters,
        dz,
        hp,
        features,
        trans,
        gates,
        (
            kernel,
            jnp.asarray(hot_mask.astype(np.float32)),
            jnp.asarray(hot_fold.astype(np.float32)),
        ),
        (highway_all, lstm_all, *kept_parts),
        7,
    )
    if at_once:
        _, highway_part, conv_grad = rest
    else:
        conv_grad, highway_part = tail([conv, highway], conv_grad, highway_grad, 3)
    conv_grad = jnp.concatenate(
        [conv_grad[h].reshape(-1, conv.block[1])[:LANE] for h in range(2)], axis=1
    )
    conv_weight_grad = jnp.where(kernel_mask, conv_grad[:ones_row, :filters], 0.0)
    conv_bias_grad = conv_grad[ones_row, :filters]
    table_grad = jnp.sum(
        conv_grad[:char_count, fp : fp + KMAX * embed_dim].reshape(char_count, KMAX, embed_dim), axis=1
    )

    def own_window(plan, part):
        if dp_count > 2:
            groups = [list(range(h, dp_count, 2)) for h in range(2)]
            part = lax.psum(part.astype(F32), "dp", axis_index_groups=groups)
        if plan.by_rows:
            at = dp_at // 2
        else:
            at = dp_at
            part = jnp.concatenate(
                [
                    lax.dynamic_slice_in_dim(part[p], at * plan.rows, plan.rows, 0)
                    for p in range(plan.parts)
                ],
                axis=1,
            ).astype(F32)
            return plan.to_flat(part, dp_at, fsdp_at)
        window = lax.dynamic_slice_in_dim(part, at * plan.rows, plan.rows, 0)
        return plan.to_flat(window, dp_at, fsdp_at)

    return (
        window_loss,
        table_grad,
        conv_weight_grad,
        conv_bias_grad,
        own_window(highway, highway_part),
        own_window(lstm, lstm_part),
        own_window(soft, soft_part),
    )


def solution(mesh):
    in_specs = (
        P(None, ("dp", "fsdp"), None, None),
        P(None, ("dp", "fsdp"), None),
        P(None, ("dp", "fsdp"), None),
        P(None, ("dp", "fsdp"), None),
        P(None, ("dp", "fsdp"), None, None),
        P(None, ("dp", "fsdp")),
        P(),
        P(),
        P(),
        P("fsdp", None),
        P("fsdp", None),
        P("fsdp", None),
    )
    out_specs = (
        P(None, ("dp", "fsdp")),
        P(),
        P(),
        P(),
        P(("dp", "fsdp"), None),
        P(("dp", "fsdp"), None),
        P(("dp", "fsdp"), None),
    )
    return jax.shard_map(
        functools.partial(shards, mesh.shape["fsdp"], mesh.shape["dp"]),
        mesh=mesh,
        in_specs=in_specs,
        out_specs=out_specs,
        check_vma=False,
    )
```

```python
import functools

import jax
import jax.numpy as jnp
import ml_dtypes
import numpy as np
from jax import lax
from jax.experimental import pallas as pl
from jax.experimental.pallas import tpu as pltpu
from jax.sharding import PartitionSpec as P

H = 650
V = 10000
KMAX = 7
LANE = 128
HP = 768
SLOTS = 24
CHARS = 51
HOT = 384
FILTER_CUTS = (1, 3, 6, 10, 14, 18)
MESH = pl.DeviceIdType.MESH
BF = jnp.bfloat16
F32 = jnp.float32


def up_to(value, unit):
    return -(-value // unit) * unit


def dot(left, right):
    return jnp.dot(left, right, preferred_element_type=F32)


def dot_rows(left, right):
    return lax.dot_general(left, right, (((0,), (0,)), ((), ())), preferred_element_type=F32)


def dot_cols(left, right):
    return lax.dot_general(left, right, (((1,), (1,)), ((), ())), preferred_element_type=F32)


class Windows:
    dtype = BF

    def __init__(self, flat_rows, width, used, fsdp, dp, by_rows, parts=2):
        owners = fsdp * dp
        self.parts = parts
        self.width, self.by_rows, self.fsdp, self.dp, self.used = width, by_rows, fsdp, dp, used
        self.entries = flat_rows * LANE // owners
        self.starts = [o * self.entries // width for o in range(owners)]
        self.spans = [
            (o * self.entries % width + self.entries - 1) // width + 1 for o in range(owners)
        ]
        unit = 16 if by_rows else 8
        rows = up_to(max(self.spans), unit)
        while (dp * rows) % 16:
            rows += unit
        self.rows = rows
        self.total = owners * rows
        self.columns = up_to(width, LANE) if by_rows else parts * up_to(-(-width // parts), LANE)
        self.block = (
            (dp // 2 * rows, self.columns) if by_rows else (dp * rows, self.columns // parts)
        )
        self.shape = (
            (self.total, self.columns)
            if by_rows
            else (parts, self.total, self.columns // parts)
        )
        if by_rows:
            order = [
                (2 * jj + h) * fsdp + f
                for f in range(fsdp)
                for h in range(2)
                for jj in range(dp // 2)
            ]
        else:
            order = [d * fsdp + f for f in range(fsdp) for d in range(dp)]
        self.position = [order.index(o) for o in range(owners)]
        self.gathered = self.row_map(range(owners))
        self.reduced = self.row_map(order)

    def row_map(self, order):
        rows_of = [
            [
                self.starts[o] + i if i < self.spans[o] and self.starts[o] + i < self.used else -1
                for i in range(self.rows)
            ]
            for o in order
        ]
        return np.array(rows_of, np.int32).reshape(-1)

    def pick(self, ref, half, slot):
        depth = self.block[0]
        if self.by_rows:
            return ref.at[pl.ds(pl.multiple_of((2 * slot + half) * depth, 16), depth)]
        return ref.at[half, pl.ds(pl.multiple_of(slot * depth, 16), depth)]

    def meeting(self, begin, end):
        found = []
        for o, (start, span) in enumerate(zip(self.starts, self.spans)):
            first, last = max(0, begin - start), min(span, end - start)
            if first < last:
                found.append((o, first, last))
        return found

    @property
    def lines(self):
        return up_to(-(-self.rows * self.width // LANE), 16) + 32

    def place_blocks(self, shard_ref, out_ref):
        fsdp_at = lax.axis_index("fsdp")
        count = self.entries // LANE
        out_ref[...] = jnp.zeros_like(out_ref)
        for j in range(self.dp):
            shift = lax.rem((fsdp_at * self.dp + j) * self.entries, self.width)
            lanes, lines = lax.rem(shift, LANE), lax.rem(shift // LANE, 16)
            block = shard_ref[j].astype(F32)
            extra = up_to(count, 16) + 16 - count
            block = jnp.concatenate([block, jnp.zeros((extra, LANE), F32)], axis=0)
            block = pltpu.roll(block, lanes, 1)
            lane = lax.broadcasted_iota(jnp.int32, block.shape, 1)
            block = jnp.where(lane < lanes, pltpu.roll(block, 1, 0), block)
            for step in (1, 2, 4, 8):
                moved = lax.rem(lines // step, 2) == 1
                block = jnp.where(moved, pltpu.roll(block, step, 0), block)
            begin = pl.multiple_of(shift // (16 * LANE) * 16, 16)
            out_ref[j, pl.ds(begin, count + extra), :] = block.astype(BF)

    def placed_shape(self):
        return jax.ShapeDtypeStruct((self.dp, self.lines, LANE), BF)

    def blocks_of(self, shard):
        return shard.reshape(self.dp, self.entries // LANE, LANE)

    def from_placed(self, placed):
        size = self.rows * self.width
        joined = jnp.concatenate(
            [
                jnp.pad(
                    placed[j].reshape(-1)[:size].reshape(self.rows, self.width),
                    ((0, 0), (0, self.columns - self.width)),
                )
                for j in range(self.dp)
            ],
            axis=0,
        )
        if self.by_rows:
            return joined.reshape((2,) + self.block)
        part = self.columns // self.parts
        return jnp.stack([joined[:, p * part : (p + 1) * part] for p in range(self.parts)])

    def to_flat(self, window, dp_at, fsdp_at):
        shift = lax.rem((dp_at * self.fsdp + fsdp_at) * self.entries, self.width)
        flat = window[:, : self.width].reshape(-1)
        return lax.dynamic_slice(flat, (shift,), (self.entries,)).reshape(-1, LANE)


def one_hot_map(rows, row_map):
    return jnp.asarray((np.arange(rows)[:, None] == row_map[None, :]).astype(ml_dtypes.bfloat16))


class Place:
    def __init__(self):
        self.d, self.f = lax.axis_index("dp"), lax.axis_index("fsdp")
        self.c = lax.rem(self.d, 2)
        x, y, self.z = lax.rem(self.f, 2), lax.rem(self.f // 2, 2), self.f // 4
        self.first = x + self.c * (y - x)
        self.last = y + self.c * (x - y)
        self.stride1, self.stride3 = 1 + self.c, 2 - self.c
        self.flip1 = self.stride1 * (1 - 2 * self.first)
        self.flip3 = self.stride3 * (1 - 2 * self.last)
        self.partner1 = (self.d, self.f + self.flip1)
        self.partner3 = (self.d, self.f + self.flip3)
        self.sibling = (self.d + 1 - 2 * self.c, self.f)

    def last_bit(self, block):
        bit_x, bit_y = lax.rem(block, 2), lax.rem(block // 2, 2)
        return bit_y + self.c * (bit_x - bit_y)


def remote(src, dst, send, recv, target):
    return pltpu.make_async_remote_copy(
        src_ref=src,
        dst_ref=dst,
        send_sem=send,
        recv_sem=recv,
        device_id=target,
        device_id_type=MESH,
    )


class Line:
    def __init__(self, n):
        self.at = Place()
        self.length = n // 4
        self.me = 2 * self.at.z + self.at.c

    def peer(self, z, other_core=False):
        at = self.at
        return (at.d + (1 - 2 * at.c if other_core else 0), at.f + 4 * (z - at.z))

    def column(self, z):
        return self.at.f + 4 * (z - self.at.z)

    def others(self, body):
        def step(z, _):
            pl.when(z != self.at.z)(functools.partial(body, z))
            return 0

        lax.fori_loop(0, self.length, step, 0)

    def chips(self, body):
        def step(z, _):
            body(z)
            return 0

        lax.fori_loop(0, self.length, step, 0)

    def far(self, k):
        z = jnp.int32(0)
        for here in range(self.length):
            order = sorted(range(self.length), key=lambda there: (-abs(there - here), there))
            for i, there in enumerate(order):
                z = jnp.where((self.at.z == here) & (k == i), there, z)
        return z

    def greet(self, across=True, both_cores=False):
        barrier = pltpu.get_barrier_semaphore()

        def signal(target):
            pl.semaphore_signal(barrier, inc=1, device_id=target, device_id_type=MESH)

        signal(self.at.sibling)
        count = 1
        if across:
            signal(self.at.partner1)
            signal(self.at.partner3)
            count += 2

        def chip(z):
            signal(self.peer(z))
            if both_cores:
                signal(self.peer(z, True))

        self.others(chip)
        pl.semaphore_wait(barrier, count + (self.length - 1) * (2 if both_cores else 1))


class Semaphores:
    def __init__(self, ref, size):
        self.ref, self.size = ref, size

    def __call__(self, kind, index):
        return self.ref.at[kind * self.size + index]


class Gather:
    RECV, SIB_RECV, LINE, NEAR, LAST, SIB, LOCAL = range(7)

    def __init__(self, plans, own, outs, sems, shared):
        self.plans, self.own, self.outs, self.sems, self.shared = plans, own, outs, sems, shared
        self.n = plans[0].fsdp
        self.line = Line(self.n)
        self.at = self.line.at

    @staticmethod
    def semaphores(plans):
        return pltpu.SemaphoreType.DMA((7 * len(plans) * plans[0].fsdp,))

    def sem(self, kind, a, index):
        return self.sems.at[(kind * len(self.plans) + a) * self.n + index]

    def source(self, a, half):
        return self.own[a].at[half] if self.shared else self.own[a]

    def copy(self, kind, a, index, block, target, own=False):
        here = self.plans[a].pick(self.outs[a], self.at.c, block)
        return remote(
            self.source(a, self.at.c) if own else here,
            here,
            self.sem(kind, a, index),
            self.sem(self.SIB_RECV if kind == self.SIB else self.RECV, a, block),
            target,
        )

    def arrived(self, a, block, kind=RECV):
        c = self.at.c
        here = self.plans[a].pick(self.outs[a], 1 - c if kind == self.SIB_RECV else c, block)
        remote(
            here, here, self.sem(self.SIB, a, block), self.sem(kind, a, block), self.at.sibling
        ).wait_recv()

    def local(self, a, half):
        return pltpu.make_async_copy(
            self.source(a, half),
            self.plans[a].pick(self.outs[a], half, self.at.f),
            self.sem(self.LOCAL, a, half if self.shared else 0),
        )

    def to_sibling(self, a, block, own=False):
        return self.copy(self.SIB, a, block, block, self.at.sibling, own)

    def close_by(self, k):
        return self.line.far(self.line.length - 1 - k)

    def begin(self, a):
        at, line = self.at, self.line
        self.copy(self.NEAR, a, at.z, at.f, at.partner1, True).start()
        self.copy(self.LAST, a, at.z, at.f, at.partner3, True).start()

        def chip(k, _):
            z = self.close_by(k)
            self.copy(self.LINE, a, z, at.f, line.peer(z), True).start()
            return 0

        lax.fori_loop(1, line.length, chip, 0)
        if self.shared:
            for half in (0, 1):
                self.local(a, half).start()
        else:
            self.to_sibling(a, at.f, True).start()
            self.local(a, at.c).start()

    def from_line(self, a, k):
        z = self.close_by(k)
        block = self.line.column(z)
        self.arrived(a, block)
        self.copy(self.NEAR, a, z, block, self.at.partner1).start()
        self.copy(self.LAST, a, z, block, self.at.partner3).start()
        self.to_sibling(a, block).start()

    def from_near(self, a, k):
        z = self.close_by(k)
        block = self.line.column(z) + self.at.flip1
        self.arrived(a, block)
        self.copy(self.LAST, a, self.line.length + z, block, self.at.partner3).start()
        self.to_sibling(a, block).start()

    def from_last(self, a, k):
        length = self.line.length
        block = (
            self.line.column(self.close_by(lax.rem(k, length)))
            + self.at.flip3
            + self.at.flip1 * (k // length)
        )
        self.arrived(a, block)
        self.to_sibling(a, block).start()

    def steps(self, a):
        length = self.line.length
        order = [(self.from_near, 0), (self.from_line, 1)]
        for k in range(2, length):
            order += [(self.from_line, k), (self.from_near, k - 1)]
        order += [(self.from_near, length - 1)] if length > 1 else []
        order += [(self.from_last, k) for k in range(2 * length)]
        return [functools.partial(step, a, k) for step, k in order]

    def run(self, steps):
        for step in steps:
            step()

    def from_sibling(self, a):
        def block_in(block, _):
            if self.shared:

                @pl.when(jnp.logical_not(block == self.at.f))
                def _():
                    self.arrived(a, block, self.SIB_RECV)

            else:
                self.arrived(a, block, self.SIB_RECV)
            return 0

        lax.fori_loop(0, self.n, block_in, 0)
        if self.shared:
            for half in (0, 1):
                self.local(a, half).wait()
        else:
            self.local(a, self.at.c).wait()

    def finish(self, a):
        at, line = self.at, self.line

        def sent(kind, index):
            self.copy(kind, a, index, at.f, at.sibling).wait_send()

        def chip(z):
            sent(self.NEAR, z)
            sent(self.LAST, z)
            sent(self.LAST, line.length + z)

        line.chips(chip)
        line.others(lambda z: sent(self.LINE, z))

        def block_done(block, _):
            if self.shared:
                pl.when(jnp.logical_not(block == at.f))(lambda: sent(self.SIB, block))
            else:
                sent(self.SIB, block)
            return 0

        lax.fori_loop(0, self.n, block_done, 0)


class MiddleGather(Gather):
    RECV, SIB_RECV, ONE, UP, DOWN, LAST, SIB, LOCAL = range(8)

    @staticmethod
    def semaphores(plans):
        return pltpu.SemaphoreType.DMA((8 * len(plans) * plans[0].fsdp,))

    def send(self, kind, a, block, own=False):
        up = kind == self.UP
        target = (self.at.d, self.at.f + (4 if up else -4))

        @pl.when(self.at.z < self.line.length - 1 if up else self.at.z > 0)
        def _():
            self.copy(kind, a, block, block, target, own).start()

    def begin(self, a):
        at = self.at
        self.copy(self.ONE, a, at.f, at.f, at.partner1, True).start()
        self.send(self.UP, a, at.f, True)
        self.send(self.DOWN, a, at.f, True)
        self.copy(self.LAST, a, at.f, at.f, at.partner3, True).start()
        for half in (0, 1):
            self.local(a, half).start()

    def near(self, a):
        block = self.at.f + self.at.flip1
        self.arrived(a, block)
        self.send(self.UP, a, block)
        self.send(self.DOWN, a, block)
        self.copy(self.LAST, a, block, block, self.at.partner3).start()
        self.to_sibling(a, block).start()

    def along(self, a, distance):
        for sign in (1, -1):
            z = self.at.z - sign * distance

            def take(sign=sign):
                for flip in (0, 1):
                    block = self.at.f - 4 * sign * distance + flip * self.at.flip1
                    self.arrived(a, block)
                    self.send(self.UP if sign == 1 else self.DOWN, a, block)
                    self.copy(self.LAST, a, block, block, self.at.partner3).start()
                    self.to_sibling(a, block).start()

            pl.when((z >= 0) & (z < self.line.length))(take)

    def across(self, a, distance):
        for sign in (1,) if distance == 0 else (1, -1):
            z = self.at.z - sign * distance

            def take(sign=sign):
                for flip in (0, 1):
                    block = (
                        self.at.f - 4 * sign * distance + flip * self.at.flip1 + self.at.flip3
                    )
                    self.arrived(a, block)
                    self.to_sibling(a, block).start()

            pl.when((z >= 0) & (z < self.line.length))(take)

    def steps(self, a):
        steps = [functools.partial(self.near, a)]
        for distance in range(1, self.line.length):
            steps += [functools.partial(self.along, a, distance)]
            steps += [functools.partial(self.across, a, distance - 1)]
        return steps + [functools.partial(self.across, a, self.line.length - 1)]

    def finish(self, a):
        at, length = self.at, self.line.length

        def sent(kind, block):
            self.copy(kind, a, block, block, at.sibling).wait_send()

        def block_done(block, _):
            z = block // 4
            pl.when(jnp.logical_not(block == at.f))(lambda: sent(self.SIB, block))

            @pl.when(at.last_bit(block) == at.last)
            def _():
                sent(self.LAST, block)
                pl.when((z <= at.z) & (at.z < length - 1))(lambda: sent(self.UP, block))
                pl.when((z >= at.z) & (at.z > 0))(lambda: sent(self.DOWN, block))

            return 0

        lax.fori_loop(0, self.n, block_done, 0)
        sent(self.ONE, at.f)


STAGES = 4


class Reduce:
    SIB, SIB_RECV, LOAD, NEAR, NEAR_RECV, CROSS, CROSS_RECV, LINE, LINE_RECV, STAGE = range(10)

    def __init__(self, plans, ins, totals, landed, scratch, in_place):
        count = len(plans)
        self.plans, self.ins, self.totals, self.in_place = plans, ins, totals, in_place
        scratch = list(scratch)
        self.held = [None if here else scratch.pop(0) for here in in_place]
        self.staged = [ref is not None for ref in landed]
        self.stage = [scratch.pop(0) if far else None for far in self.staged]
        self.landed = [scratch.pop(0) if ref is None else ref for ref in landed]
        self.close, self.cross, self.lined = (
            scratch[k * count : (k + 1) * count] for k in range(3)
        )
        self.sems = scratch[3 * count]
        self.n = plans[0].fsdp
        self.line = Line(self.n)
        self.at = self.line.at
        self.items = 2 * self.line.length

    @staticmethod
    def scratch(plans, in_place, staged):
        def buffers(size, kept=None):
            return [
                pltpu.VMEM((size,) + plan.block, plan.dtype)
                for a, plan in enumerate(plans)
                if kept is None or kept[a]
            ]

        n = plans[0].fsdp
        return (
            buffers(n, [not here for here in in_place])
            + buffers(STAGES, staged)
            + buffers(n, [not far for far in staged])
            + buffers(n // 2)
            + buffers(n // 4) * 2
            + [pltpu.SemaphoreType.DMA((10 * len(plans) * n,))]
        )

    def sem(self, kind, a, index):
        return self.sems.at[(kind * len(self.plans) + a) * self.n + index]

    def slot(self, z, b1, b3):
        return 4 * z + self.at.stride1 * b1 + self.at.stride3 * b3

    def item(self, t):
        ours = lax.rem(t, 2)
        return self.line.far(t // 2), (1 - self.at.last) + ours * (2 * self.at.last - 1)

    def turn(self, m):
        swapped = jnp.where(lax.rem(m, 2) == 0, m - 1, m + 1)
        return jnp.where((m == 0) | (m == self.items - 1), m, swapped)

    def hold(self, a, block):
        if self.in_place[a]:
            return self.plans[a].pick(self.ins[a], self.at.c, block)
        return self.held[a].at[block]

    def to_sibling(self, a, block):
        return remote(
            self.plans[a].pick(self.ins[a], 1 - self.at.c, block),
            self.landed[a].at[block],
            self.sem(self.SIB, a, block),
            self.sem(self.SIB_RECV, a, block),
            self.at.sibling,
        )

    def load(self, a, block):
        return pltpu.make_async_copy(
            self.plans[a].pick(self.ins[a], self.at.c, block),
            self.held[a].at[block],
            self.sem(self.LOAD, a, block),
        )

    def to_near(self, a, z, b3):
        return remote(
            self.hold(a, self.slot(z, 1 - self.at.first, b3)),
            self.close[a].at[2 * z + b3],
            self.sem(self.NEAR, a, 2 * z + b3),
            self.sem(self.NEAR_RECV, a, 2 * z + b3),
            self.at.partner1,
        )

    def to_cross(self, a, z):
        return remote(
            self.hold(a, self.slot(z, self.at.first, 1 - self.at.last)),
            self.cross[a].at[z],
            self.sem(self.CROSS, a, z),
            self.sem(self.CROSS_RECV, a, z),
            self.at.partner3,
        )

    def to_line(self, a, z):
        return remote(
            self.hold(a, self.slot(z, self.at.first, self.at.last)),
            self.lined[a].at[self.at.z],
            self.sem(self.LINE, a, z),
            self.sem(self.LINE_RECV, a, self.at.z),
            self.line.peer(z),
        )

    def line_arrived(self, a, z):
        here = self.lined[a].at[z]
        remote(
            here, here, self.sem(self.LINE, a, z), self.sem(self.LINE_RECV, a, z), self.line.peer(z)
        ).wait_recv()

    def rows(self, a, body):
        unit = 16

        def step(i, _):
            body(pl.ds(pl.multiple_of(i * unit, unit), unit))
            return 0

        if self.plans[a].block[0] < unit:
            body(slice(None))
        else:
            lax.fori_loop(0, self.plans[a].block[0] // unit, step, 0)

    def add(self, a, block, sources):
        held = self.hold(a, block)

        def body(where):
            total = held[where, :].astype(F32)
            for ref, at in sources:
                total += ref[at, where, :].astype(F32)
            held[where, :] = total.astype(held.dtype)

        self.rows(a, body)

    def begin(self, a):
        for flip in (1, 0):
            b1 = self.at.first + flip * (1 - 2 * self.at.first)

            def start(t, _, b1=b1):
                z, b3 = self.item(t)
                block = self.slot(z, b1, b3)
                self.to_sibling(a, block).start()
                if not self.in_place[a]:
                    self.load(a, block).start()
                return 0

            lax.fori_loop(0, self.items, start, 0)

    def in_order(self, q):
        late = jnp.int32(q >= self.items)
        z, b3 = self.item(jnp.where(q >= self.items, self.turn(q - self.items), q))
        return self.slot(z, (1 - self.at.first) + late * (2 * self.at.first - 1), b3)

    def to_stage(self, a, q):
        k = lax.rem(q, STAGES)
        return pltpu.make_async_copy(
            self.landed[a].at[self.in_order(q)], self.stage[a].at[k], self.sem(self.STAGE, a, k)
        )

    def fetch(self, a, q):
        self.to_sibling(a, self.in_order(q)).wait_recv()
        self.to_stage(a, q).start()

    def ready(self, a, block, q):
        if not self.in_place[a]:
            self.load(a, block).wait()
        if not self.staged[a]:
            self.to_sibling(a, block).wait_recv()
            return self.landed[a], block

        @pl.when(q == 0)
        def _():
            for k in range(STAGES):
                self.fetch(a, jnp.int32(k))

        self.to_stage(a, q).wait()
        return self.stage[a], lax.rem(q, STAGES)

    def used(self, a, q):
        if self.staged[a]:
            pl.when(q + STAGES < 2 * self.items)(lambda: self.fetch(a, q + STAGES))

    def first_leg(self, a, t):
        z, b3 = self.item(t)
        block = self.slot(z, 1 - self.at.first, b3)
        self.add(a, block, [self.ready(a, block, t)])
        self.to_near(a, z, b3).start()
        self.used(a, t)

    def middle_leg(self, a, m):
        t = self.turn(m)
        z, b3 = self.item(t)
        block = self.slot(z, self.at.first, b3)
        sources = [self.ready(a, block, self.items + m), (self.close[a], 2 * z + b3)]
        self.to_near(a, z, b3).wait_recv()

        @pl.when(lax.rem(t, 2) == 0)
        def _():
            self.add(a, block, sources)
            self.to_cross(a, z).start()

        @pl.when(lax.rem(t, 2) == 1)
        def _():
            self.to_cross(a, z).wait_recv()
            self.add(a, block, sources + [(self.cross[a], z)])

            @pl.when(z != self.at.z)
            def _():
                self.to_line(a, z).start()

        self.used(a, self.items + m)

    def legs(self, body, a, begin, end):
        def step(t, _):
            body(a, t)
            return 0

        lax.fori_loop(begin, end, step, 0)

    def last_leg(self, a):
        block = self.slot(self.at.z, self.at.first, self.at.last)

        def body(where):
            self.totals[a][where, :] = self.hold(a, block)[where, :].astype(F32)

        self.rows(a, body)

        def chip(z):
            self.line_arrived(a, z)

            def body(where):
                self.totals[a][where, :] += self.lined[a][z, where, :].astype(F32)

            self.rows(a, body)

        self.line.others(chip)

    def finish(self, a):
        def done(t, _):
            z, b3 = self.item(t)
            for b1 in (self.at.first, 1 - self.at.first):
                self.to_sibling(a, self.slot(z, b1, b3)).wait_send()
            self.to_near(a, z, b3).wait_send()
            return 0

        lax.fori_loop(0, self.items, done, 0)
        self.line.chips(lambda z: self.to_cross(a, z).wait_send())
        self.line.others(lambda z: self.to_line(a, z).wait_send())


def reduce_out(plan):
    return jax.ShapeDtypeStruct(plan.block if plan.by_rows else (2,) + plan.block, F32)


def hot_rows(codes):
    count = codes.shape[0]
    slot = lax.rem(lax.broadcasted_iota(jnp.int32, (count, 1), 0), SLOTS)
    lane = lax.broadcasted_iota(jnp.int32, (count, HOT), 1)
    hit = lane == KMAX * CHARS
    for q in range(KMAX):
        moved = codes if q == 0 else pltpu.roll(codes, count - q, 0)
        moved = jnp.where((moved >= 0) & (slot + q < SLOTS), moved + q * CHARS, -1)
        hit = jnp.logical_or(hit, lane == moved)
    return hit.astype(F32).astype(BF)


def conv_forward_block(filters, codes, lengths, refs, out_ref, where, kept):
    table_ref, kernel_ref, width_ref = refs
    hot_ref, window_ref, slope_ref = kept
    words = lengths.shape[0]
    hot = hot_rows(codes)
    hot_ref[...] = hot
    windows = dot(hot, table_ref[...]).astype(BF)
    window_ref[...] = windows
    chunk = 384
    for at in range(0, kernel_ref.shape[1], chunk):
        columns = slice(at, at + chunk)
        activated = jnp.tanh(dot(windows, kernel_ref[:, columns])).reshape(words, SLOTS, chunk)
        counts = jnp.maximum(lengths - width_ref[:, columns] + 1, 1)
        position = lax.broadcasted_iota(jnp.int32, (words, SLOTS, chunk), 1)
        inside = position < counts[:, None, :]
        weight = jnp.where(inside, jnp.exp(activated), 0.0)
        totals = jnp.sum(weight, axis=1)
        pooled = jnp.log(totals) - jnp.log(counts.astype(F32))
        lane = at + lax.broadcasted_iota(jnp.int32, (words, chunk), 1)
        out_ref[where, columns] = keep_feature(pooled, lane, filters)
        slope = weight * (1.0 / totals)[:, None, :] * (1.0 - activated * activated)
        slope_ref[:, columns] = slope.astype(BF).reshape(words * SLOTS, chunk)


def keep_feature(value, lane, filters):
    value = value.astype(BF).astype(F32)
    return jnp.where(lane < filters, value, jnp.where(lane == filters, 1.0, 0.0))


def conv_backward_block(kept, kernel_ref, grad_ref, where, kernel_grad_ref, hot_grad_ref):
    hot_ref, window_ref, slope_ref = kept
    words = WORD_BLOCK
    windows = window_ref[...]
    chunk = 384
    grad_windows = jnp.zeros(windows.shape, F32)
    for at in range(0, kernel_ref.shape[1], chunk):
        columns = slice(at, at + chunk)
        slope = slope_ref[:, columns].astype(F32).reshape(words, SLOTS, chunk)
        grad = (grad_ref[where, columns][:, None, :] * slope).astype(BF)
        grad = grad.reshape(words * SLOTS, chunk)
        kernel_grad_ref[:, columns] += dot_rows(windows, grad)
        grad_windows += dot_cols(grad, kernel_ref[:, columns])
    hot_grad_ref[...] += dot_rows(hot_ref[...], grad_windows.astype(BF))


WORD_BLOCK = 16


class SmallSum:
    SIB, NEAR, CROSS, LINE, BACK_LINE, BACK_CROSS, BACK_NEAR, BACK_SIB = range(0, 16, 2)

    def __init__(self, conv, mine, out, scratch):
        self.conv, self.mine, self.out = conv, mine, out
        self.by_sibling, self.by_near, self.by_cross, self.by_line, self.sems = scratch
        self.line = Line(conv.fsdp)
        self.at = at = self.line.at
        self.length = self.line.length
        self.near_at = at.first * 2 * self.length
        self.near_other = (1 - at.first) * 2 * self.length
        self.cross_at = self.near_at + at.last * self.length
        self.cross_other = self.near_at + (1 - at.last) * self.length
        self.own = self.cross_at + at.z

    @staticmethod
    def scratch(conv):
        n = conv.fsdp
        sizes = (n, n // 2, n // 4, n // 4)
        return [pltpu.VMEM((size,) + conv.block, F32) for size in sizes] + [
            pltpu.SemaphoreType.DMA((16 * (n // 4),))
        ]

    def sem(self, kind, index=0):
        return self.sems.at[kind * self.length + index]

    def message(self, kind, src, dst, target, send=0, receive=0):
        return remote(src, dst, self.sem(kind, send), self.sem(kind + 1, receive), target)

    def part(self, ref, begin, size):
        return ref.at[self.at.c, pl.ds(begin, size)]

    def sibling(self):
        return self.message(self.SIB, self.mine.at[1 - self.at.c], self.by_sibling, self.at.sibling)

    def near(self):
        size = 2 * self.length
        source = self.part(self.mine, self.near_other, size)
        return self.message(self.NEAR, source, self.by_near, self.at.partner1)

    def cross(self):
        source = self.part(self.mine, self.cross_other, self.length)
        return self.message(self.CROSS, source, self.by_cross, self.at.partner3)

    def lined(self, z, source=None):
        block = self.mine.at[self.at.c, self.cross_at + z]
        target = self.by_line.at[z if source else self.at.z]
        return self.message(
            self.LINE, block, target, self.line.peer(z), z, z if source else self.at.z
        )

    def back_line(self, z, source=None):
        here = self.out.at[self.at.c, self.cross_at + z if source else self.own]
        return self.message(
            self.BACK_LINE, here, here, self.line.peer(z), z, z if source else self.at.z
        )

    def back_cross(self, source=None):
        begin = self.cross_other if source else self.cross_at
        here = self.part(self.out, begin, self.length)
        return self.message(self.BACK_CROSS, here, here, self.at.partner3)

    def back_near(self, source=None):
        here = self.part(self.out, self.near_other if source else self.near_at, 2 * self.length)
        return self.message(self.BACK_NEAR, here, here, self.at.partner1)

    def back_sibling(self, source=None):
        here = self.out.at[1 - self.at.c if source else self.at.c]
        return self.message(self.BACK_SIB, here, here, self.at.sibling)

    def add(self, begin, source):
        size = source.shape[0]
        self.mine[self.at.c, pl.ds(begin, size)] += source[...]

    def steps(self):
        def begin():
            self.sibling().start()

        def to_near():
            self.sibling().wait_recv()
            self.add(0, self.by_sibling)
            self.near().start()

        def to_cross():
            self.near().wait_recv()
            self.add(self.near_at, self.by_near)
            self.cross().start()

        def to_line():
            self.cross().wait_recv()
            self.add(self.cross_at, self.by_cross)
            self.line.others(lambda z: self.lined(z).start())

        def total():
            self.out[self.at.c, self.own] = self.mine[self.at.c, self.own]

            def chip(z):
                self.lined(z, True).wait_recv()
                self.out[self.at.c, self.own] += self.by_line[z]

            self.line.others(chip)
            self.line.others(lambda z: self.back_line(z).start())

        def from_line():
            self.line.others(lambda z: self.back_line(z, True).wait_recv())
            self.back_cross().start()

        def from_cross():
            self.back_cross(True).wait_recv()
            self.back_near().start()

        def from_near():
            self.back_near(True).wait_recv()
            self.back_sibling().start()

        def end():
            self.back_sibling(True).wait_recv()
            for message in (
                self.sibling(),
                self.near(),
                self.cross(),
                self.back_cross(),
                self.back_near(),
                self.back_sibling(),
            ):
                message.wait_send()
            self.line.others(lambda z: self.lined(z).wait_send())
            self.line.others(lambda z: self.back_line(z).wait_send())

        return [begin, to_near, to_cross, to_line, total, from_line, from_cross, from_near, end]


def place_kernel(plans, *refs):
    for plan, shard, out in zip(plans, refs[: len(plans)], refs[len(plans) :]):
        plan.place_blocks(shard, out)


def place_all(plans, shards):
    vmem = pl.BlockSpec(memory_space=pltpu.VMEM)
    placed = pl.pallas_call(
        functools.partial(place_kernel, plans),
        out_shape=[plan.placed_shape() for plan in plans],
        in_specs=[vmem] * len(plans),
        out_specs=[vmem] * len(plans),
        compiler_params=pltpu.CompilerParams(vmem_limit_bytes=48 * 2**20),
    )(*[plan.blocks_of(shard) for plan, shard in zip(plans, shards)])
    return [plan.from_placed(each) for plan, each in zip(plans, placed)]


class Dense:
    by_rows = False
    dtype = F32

    def __init__(self, rows, columns, fsdp):
        self.fsdp = fsdp
        self.filled = rows
        self.block = (up_to(-(-rows // fsdp), 8), columns // 2)
        self.shape = (2, fsdp) + self.block

    def pick(self, ref, half, slot):
        return ref.at[half, slot]

    def fill(self, slots, source):
        slots[...] = jnp.zeros_like(slots)
        depth, half = self.block
        for block in range(self.filled // depth):
            for h in range(2):
                slots[h, block] = source[
                    block * depth : (block + 1) * depth, h * half : (h + 1) * half
                ]


def tail_kernel(plans, conv_ref, grad_ref, conv_out, total_out, conv_in, *scratch):
    conv, highway = plans
    small = SmallSum(conv, conv_in, conv_out, scratch[:5])
    work = Reduce([highway], [grad_ref], [total_out], [None], scratch[5:], [False])
    work.line.greet()
    conv.fill(conv_in, conv_ref)
    work.begin(0)
    work.legs(work.first_leg, 0, 0, work.items)
    for step in small.steps():
        step()
    work.legs(work.middle_leg, 0, 0, work.items)
    work.last_leg(0)
    work.finish(0)


def tail(plans, conv_grad, highway_grad, collective_id):
    conv, highway = plans
    vmem = pl.BlockSpec(memory_space=pltpu.VMEM)
    return pl.pallas_call(
        functools.partial(tail_kernel, plans),
        out_shape=[
            jax.ShapeDtypeStruct(conv.shape, F32),
            jax.ShapeDtypeStruct(highway.block, F32),
        ],
        in_specs=[vmem, pl.BlockSpec(memory_space=pl.ANY)],
        out_specs=[vmem] * 2,
        scratch_shapes=[pltpu.VMEM(conv.shape, F32)]
        + SmallSum.scratch(conv)
        + Reduce.scratch([highway], [False], [False]),
        compiler_params=pltpu.CompilerParams(
            collective_id=collective_id, has_side_effects=True, vmem_limit_bytes=62 * 2**20
        ),
    )(conv_grad, highway_grad)


def gate_parts(sums):
    parts = [sums[:, :HP]]
    for g in range(1, 4):
        begin = g * H // LANE * LANE
        moved = sums[:, begin : begin + HP + LANE]
        parts.append(pltpu.roll(moved, HP + LANE - (g * H - begin), 1)[:, :HP])
    return parts


def join_gates(parts, columns):
    rows = parts[0].shape[0]
    total = None
    for g, part in enumerate(parts):
        begin = g * H // LANE * LANE
        wide = jnp.concatenate([part, jnp.zeros((rows, LANE), F32)], axis=1)
        if g * H - begin:
            wide = pltpu.roll(wide, g * H - begin, 1)
        pieces = [wide]
        if begin:
            pieces = [jnp.zeros((rows, begin), F32)] + pieces
        if columns - begin - HP - LANE > 0:
            pieces = pieces + [jnp.zeros((rows, columns - begin - HP - LANE), F32)]
        placed = jnp.concatenate(pieces, axis=1)[:, :columns]
        total = placed if total is None else total + placed
    return total


HIDDEN_CHUNKS = ((0, 48), (48, 96), (96, 128), (128, 144))


def hidden_chunks(rows):
    return [(a, min(b, rows)) for a, b in HIDDEN_CHUNKS if a < rows] + (
        [(HIDDEN_CHUNKS[-1][1], rows)] if rows > HIDDEN_CHUNKS[-1][1] else []
    )


def lstm_forward_kernel(
    batch, n, x_ref, w_ref, h0_ref, c0_ref, keep_ref, extra_ref, own_ref, *refs
):
    hp_ref, cp_ref, i_ref, f_ref, u_ref, o_ref, t_ref, hall_ref, part_ref = refs[:9]
    hidden, soft_sems, hidden_sems = refs[9:]
    line = Line(n)
    at, length = line.at, line.length
    rows_all = x_ref.shape[0]
    chunks = hidden_chunks(rows_all)
    RECV, TO_LINE, TO_NEAR, TO_LAST, LOCAL = range(5)
    sem = Semaphores(soft_sems, n)
    H_RECV, H_LINE, H_SIB = range(3)
    hsem = Semaphores(hidden_sems, 2 * length * len(chunks))

    def column(z):
        return at.f + 4 * (z - at.z)

    def to_line(z):
        return remote(
            own_ref.at[2 * z + at.c],
            part_ref.at[at.f],
            sem(TO_LINE, z),
            sem(RECV, at.f),
            line.peer(z),
        )

    def pass_on(kind, index, slot, target, own=False):
        return remote(
            own_ref.at[line.me] if own else part_ref.at[slot],
            part_ref.at[slot],
            sem(kind, index),
            sem(RECV, slot),
            target,
        )

    def landed(slot):
        pass_on(TO_NEAR, 0, slot, at.partner1).wait_recv()

    local = pltpu.make_async_copy(own_ref.at[line.me], part_ref.at[at.f], sem(LOCAL, 0))

    def event_begin():
        line.others(lambda z: to_line(z).start())
        pass_on(TO_NEAR, at.z, at.f, at.partner1, True).start()
        pass_on(TO_LAST, at.z, at.f, at.partner3, True).start()
        local.start()

    def event_line():
        def chip(z):
            landed(column(z))
            pass_on(TO_NEAR, z, column(z), at.partner1).start()
            pass_on(TO_LAST, z, column(z), at.partner3).start()

        line.others(chip)

    def event_near():
        def chip(z):
            slot = column(z) + at.flip1
            landed(slot)
            pass_on(TO_LAST, length + z, slot, at.partner3).start()

        line.chips(chip)

    def event_end():
        def chip(z):
            landed(column(z) + at.flip3)
            landed(column(z) + at.flip1 + at.flip3)
            pass_on(TO_NEAR, z, column(z), at.partner1).wait_send()
            pass_on(TO_LAST, z, column(z), at.partner3).wait_send()
            pass_on(TO_LAST, length + z, column(z), at.partner3).wait_send()

        line.chips(chip)
        line.others(lambda z: to_line(z).wait_send())
        local.wait()

    def chunk_copy(k, member, kind, index, target):
        begin, end = chunks[k]
        here = hall_ref.at[member, pl.ds(begin, end - begin), :]
        return remote(
            here,
            here,
            hsem(kind, index * len(chunks) + k),
            hsem(H_RECV, member * len(chunks) + k),
            target,
        )

    def chunk_out(k):
        begin, end = chunks[k]
        hall_ref[line.me, begin:end, :] = hidden[begin:end, :].astype(BF)
        line.others(lambda z: chunk_copy(k, line.me, H_LINE, z, line.peer(z)).start())
        chunk_copy(k, line.me, H_SIB, at.z, at.sibling).start()

    def chunk_pass(k):
        def chip(z):
            member = 2 * z + at.c
            chunk_copy(k, member, H_SIB, z, at.sibling).wait_recv()
            chunk_copy(k, member, H_SIB, z, at.sibling).start()

        line.others(chip)

    def chunk_end(k):
        def chip(z):
            chunk_copy(k, 2 * z + 1 - at.c, H_SIB, z, at.sibling).wait_recv()
            chunk_copy(k, 2 * z + at.c, H_SIB, z, at.sibling).wait_send()

        line.chips(chip)
        line.others(lambda z: chunk_copy(k, line.me, H_LINE, z, line.peer(z)).wait_send())

    line.greet(True, False)
    event_begin()
    per_tile = 8 // batch
    tiles = rows_all // 8
    row = lax.broadcasted_iota(jnp.int32, (8, HP), 0)
    lane = lax.broadcasted_iota(jnp.int32, (8, LANE), 1)
    last = HP - LANE
    used = up_to(H, 16)

    def tile(step, carried):
        h, c = carried
        rows = pl.ds(pl.multiple_of(step * 8, 8), 8)
        x = x_ref[rows, :]
        keep = keep_ref[rows, :]
        saved = None
        for part in range(per_tile):
            hp, cp = h * keep, c * keep
            sums = x + dot(hp[:, :used].astype(BF), w_ref[:used, :])
            i, f, u, o = gate_parts(sums)
            i, f, u, o = jax.nn.sigmoid(i), jax.nn.sigmoid(f), jnp.tanh(u), jax.nn.sigmoid(o)
            c = f * cp + i * u
            t = jnp.tanh(c)
            h = (o * t).astype(BF).astype(F32)
            now = (hp, cp, i, f, u, o, t, h)
            if saved is None:
                saved = now
            else:
                saved = tuple(jnp.where(row >= part * batch, b, a) for a, b in zip(saved, now))
            h, c = pltpu.roll(h, batch, 0), pltpu.roll(c, batch, 0)
        for ref, value in zip((hp_ref, cp_ref, i_ref, f_ref, u_ref, o_ref, t_ref), saved):
            ref[rows, :] = value
        hidden[rows, :last] = saved[-1][:, :last]
        hidden[rows, last:] = jnp.where(lane < H - last, saved[-1][:, last:], extra_ref[rows, :])

        pl.when(step == tiles // 3)(event_line)
        pl.when(step == tiles * 2 // 3)(event_near)
        for k, (_, end) in enumerate(chunks):
            pl.when(step == end // 8 - 1)(functools.partial(chunk_out, k))
            if end // 8 + 4 < tiles:
                pl.when(step == end // 8 + 4)(functools.partial(chunk_pass, k))
        return h, c

    lax.fori_loop(0, tiles, tile, (h0_ref[...], c0_ref[...]))
    for k, (_, end) in enumerate(chunks):
        if end // 8 + 4 >= tiles:
            chunk_pass(k)
    event_end()
    for k in range(len(chunks)):
        chunk_end(k)


def lstm_forward(batch, plan, x, recur, h0, c0, keep, extra, own, collective_id):
    rows, n = x.shape[0], plan.fsdp
    members = plan.parts
    chunks = len(hidden_chunks(rows))
    vmem = pl.BlockSpec(memory_space=pltpu.VMEM)
    anywhere = pl.BlockSpec(memory_space=pl.ANY)
    return pl.pallas_call(
        functools.partial(lstm_forward_kernel, batch, n),
        out_shape=[jax.ShapeDtypeStruct((rows, HP), F32)] * 7
        + [
            jax.ShapeDtypeStruct((members, rows, HP), BF),
            jax.ShapeDtypeStruct((n,) + plan.block, BF),
        ],
        in_specs=[vmem] * 6 + [anywhere],
        out_specs=[vmem] * 8 + [anywhere],
        scratch_shapes=[
            pltpu.VMEM((rows, HP), F32),
            pltpu.SemaphoreType.DMA((5 * n,)),
            pltpu.SemaphoreType.DMA((3 * members * chunks,)),
        ],
        compiler_params=pltpu.CompilerParams(
            collective_id=collective_id, has_side_effects=True, vmem_limit_bytes=62 * 2**20
        ),
    )(x, recur, h0, c0, keep, extra, own)


def lstm_backward_kernel(
    batch,
    n,
    dh_ref,
    w_ref,
    keep_ref,
    cp_ref,
    i_ref,
    f_ref,
    u_ref,
    o_ref,
    t_ref,
    grad_ref,
    dz_ref,
    out_ref,
    held_near,
    held_line,
    from_last,
    from_near,
    sems,
):
    line = Line(n)
    at, length = line.at, line.length
    LAST, LAST_RECV, NEAR, NEAR_RECV, TO_LINE, LINE_RECV, SIB, SIB_RECV = range(8)
    sem = Semaphores(sems, 2 * length)

    def slot(z, b1, b3):
        return 4 * z + at.stride1 * b1 + at.stride3 * b3

    def to_last(z, b1):
        return remote(
            grad_ref.at[slot(z, b1, 1 - at.last)],
            from_last.at[2 * z + b1],
            sem(LAST, 2 * z + b1),
            sem(LAST_RECV, 2 * z + b1),
            at.partner3,
        )

    def to_near(z):
        return remote(
            held_near.at[z], from_near.at[z], sem(NEAR, z), sem(NEAR_RECV, z), at.partner1
        )

    def to_line(z):
        return remote(
            held_line.at[z], out_ref.at[line.me], sem(TO_LINE, z), sem(LINE_RECV, at.z), line.peer(z)
        )

    def line_arrived(z):
        here = out_ref.at[2 * z + at.c]
        remote(here, here, sem(TO_LINE, z), sem(LINE_RECV, z), line.peer(z)).wait_recv()

    def to_sibling(z, other=False):
        here = out_ref.at[2 * z + (1 - at.c if other else at.c)]
        return remote(here, here, sem(SIB, z), sem(SIB_RECV, z), at.sibling)

    def event_begin():
        def chip(z):
            to_last(z, 1 - at.first).start()

        line.chips(chip)

        def chip_own(z):
            to_last(z, at.first).start()

        line.chips(chip_own)

    def event_last():
        def chip(z):
            b1 = 1 - at.first
            to_last(z, b1).wait_recv()
            held_near[z] = (
                grad_ref[slot(z, b1, at.last)].astype(F32) + from_last[2 * z + b1].astype(F32)
            ).astype(BF)
            to_near(z).start()

        line.chips(chip)

    def event_near():
        def chip(z):
            to_last(z, at.first).wait_recv()
            to_near(z).wait_recv()
            total = (
                grad_ref[slot(z, at.first, at.last)].astype(F32)
                + from_last[2 * z + at.first].astype(F32)
                + from_near[z].astype(F32)
            ).astype(BF)
            held_line[z] = total

            @pl.when(z == at.z)
            def _():
                out_ref[line.me] = total

            @pl.when(z != at.z)
            def _():
                to_line(z).start()

        line.chips(chip)
        to_sibling(at.z).start()

    def event_line():
        def chip(z):
            line_arrived(z)
            to_sibling(z).start()

        line.others(chip)

    def event_end():
        def chip(z):
            to_sibling(z, True).wait_recv()
            to_sibling(z).wait_send()
            to_near(z).wait_send()
            to_last(z, 0).wait_send()
            to_last(z, 1).wait_send()

        line.chips(chip)
        line.others(lambda z: to_line(z).wait_send())

    line.greet(True, False)
    event_begin()
    per_tile = 8 // batch
    tiles = dh_ref.shape[0] // 8
    row = lax.broadcasted_iota(jnp.int32, (8, dz_ref.shape[1]), 0)
    real = lax.broadcasted_iota(jnp.int32, (8, HP), 1) < H
    used = up_to(4 * H, 16)

    def tile(step, carried):
        dh_carry, dc_carry = carried
        rows = pl.ds(pl.multiple_of((tiles - 1 - step) * 8, 8), 8)
        keep = keep_ref[rows, :]
        i, f, u, o, t = (r[rows, :] for r in (i_ref, f_ref, u_ref, o_ref, t_ref))
        soft = dh_ref[rows, :]
        to_c = o * (1.0 - t * t)
        to_i = jnp.where(real, u * i * (1.0 - i), 0.0)
        to_f = jnp.where(real, cp_ref[rows, :] * f * (1.0 - f), 0.0)
        to_u = jnp.where(real, i * (1.0 - u * u), 0.0)
        to_o = jnp.where(real, t * o * (1.0 - o), 0.0)
        back = f * keep
        saved = None
        for part in reversed(range(per_tile)):
            dh = jnp.where(real, soft + dh_carry, 0.0)
            dc = dc_carry + dh * to_c
            dz = join_gates([dc * to_i, dc * to_f, dc * to_u, dh * to_o], dz_ref.shape[1])
            saved = dz if saved is None else jnp.where(row >= (part + 1) * batch, saved, dz)
            dh_carry = dot(dz[:, :used].astype(BF), w_ref[:used, :]) * keep
            dc_carry = dc * back
            dh_carry, dc_carry = (
                pltpu.roll(dh_carry, 8 - batch, 0),
                pltpu.roll(dc_carry, 8 - batch, 0),
            )
        dz_ref[rows, :] = saved
        pl.when(step == tiles // 3)(event_last)
        pl.when(step == tiles * 2 // 3)(event_near)
        pl.when(step == tiles - 2)(event_line)
        return dh_carry, dc_carry

    zero = jnp.zeros((8, HP), F32)
    lax.fori_loop(0, tiles, tile, (zero, zero))
    event_end()


def lstm_backward(batch, plan, columns, dh, recur_t, keep, states, grad, collective_id):
    rows, n = dh.shape[0], plan.fsdp
    length = n // 4
    vmem = pl.BlockSpec(memory_space=pltpu.VMEM)
    return pl.pallas_call(
        functools.partial(lstm_backward_kernel, batch, n),
        out_shape=[
            jax.ShapeDtypeStruct((rows, columns), F32),
            jax.ShapeDtypeStruct((plan.parts,) + plan.block, BF),
        ],
        in_specs=[vmem] * 10,
        out_specs=[vmem] * 2,
        scratch_shapes=[
            pltpu.VMEM((length,) + plan.block, BF),
            pltpu.VMEM((length,) + plan.block, BF),
            pltpu.VMEM((2 * length,) + plan.block, BF),
            pltpu.VMEM((length,) + plan.block, BF),
            pltpu.SemaphoreType.DMA((8 * 2 * length,)),
        ],
        compiler_params=pltpu.CompilerParams(
            collective_id=collective_id, has_side_effects=True, vmem_limit_bytes=62 * 2**20
        ),
    )(dh, recur_t, keep, *states, grad)


def turned(value, lanes):
    rows = value.shape[0]
    if rows < lanes:
        value = jnp.concatenate([value, jnp.zeros((lanes - rows, value.shape[1]), F32)], axis=0)
    return value.T


def copy_windows(plan, source, target, base, found, place):
    target[...] = jnp.zeros_like(target)
    for o, first, last in found:
        start, to = plan.starts[o] - base, place(o) * plan.rows
        target[to + first : to + last, :] = source[start + first : start + last, :]


def add_windows(plan, source, target, base, found, begin):
    for o, first, last in found:
        start, at = plan.starts[o] - base, o * plan.rows - begin
        target[start + first : start + last, :] += source[at + first : at + last, :]


def matrices_of(plan, filters):
    result = []
    for m in range(4):
        base = m * (filters + 1)
        found = plan.meeting(base, base + filters + 1)
        result.append((base, found, found[0][0] * plan.rows, (found[-1][0] + 1) * plan.rows))
    return result


def head_kernel(plans, soft, filters, blocks, *refs):
    highway, lstm = plans
    owns = refs[:2]
    codes_ref, length_ref, table_ref, kernel_ref, width_ref, soft_ref = refs[2:8]
    highway_out, lstm_out, x_ref, recur_ref, soft_out = refs[8:13]
    kept_outs, wide_out = refs[13:16], refs[16]
    features, trans_refs, gate_refs = refs[17:20], refs[20:22], refs[22:24]
    highway_w, lstm_w, turned_ref, wide, recur_sum = refs[24:29]
    kept_stages, wide_stage, highway_sems, lstm_sems, out_sems, keep_sems = refs[29:32], *refs[32:]
    rows, fp = features[0].shape
    words = turned_ref.shape[1]
    gather_h = MiddleGather([highway], owns[:1], [highway_w], highway_sems, True)
    gather_l = Gather([lstm], owns[1:], [lstm_w], lstm_sems, True)
    gather_h.line.greet()

    def conv(begin, end):
        def block(i, _):
            at = pl.ds(pl.multiple_of(i * WORD_BLOCK, WORD_BLOCK), WORD_BLOCK)
            slots = pl.ds(
                pl.multiple_of(i * WORD_BLOCK * SLOTS, WORD_BLOCK * SLOTS), WORD_BLOCK * SLOTS
            )
            pl.when(i >= 2)(lambda: wait_kept(i - 2))
            k = lax.rem(i, 2)
            conv_forward_block(
                filters,
                codes_ref[slots, :],
                length_ref[at, :],
                (table_ref, kernel_ref, width_ref),
                features[0],
                at,
                [stage.at[k] for stage in kept_stages],
            )
            for copy in keep_copies(i):
                copy.start()
            return 0

        lax.fori_loop(begin, end, block, 0)

    def keep_copies(i):
        k = lax.rem(i, 2)
        size = WORD_BLOCK * SLOTS
        to = pl.ds(pl.multiple_of(i * size, size), size)
        return [
            pltpu.make_async_copy(stage.at[k], out.at[to], keep_sems.at[2 * j + k])
            for j, (stage, out) in enumerate(zip(kept_stages, kept_outs))
        ]

    def wait_kept(i):
        for copy in keep_copies(i):
            copy.wait()

    def wide_copy(m):
        return pltpu.make_async_copy(wide_stage.at[m % 2], wide_out.at[m], keep_sems.at[6 + m % 2])

    chunk = 384

    def layer_sum(m, wide=wide):
        base, found, begin, end = matrices[m]
        copy_windows(
            highway, turned_ref, wide.at[: end - begin], base, found, lambda o: o - found[0][0]
        )
        target = (trans_refs if m % 2 == 0 else gate_refs)[m // 2]
        if m >= 2:
            wide_copy(m - 2).wait()
        wide_stage[m % 2, : end - begin, :] = wide[: end - begin, :].astype(BF)
        wide_copy(m).start()

        def columns(j, _):
            where = pl.ds(pl.multiple_of(j * chunk, chunk), chunk)
            left = wide[: end - begin, :].astype(BF)
            target[:, where] = dot_rows(left, highway_w[begin:end, where])[:rows]
            return 0

        lax.fori_loop(0, fp // chunk, columns, 0)

    def layer(l):
        turned_ref[:fp, :] = turned(features[l][...], words)
        layer_sum(2 * l)

    def layer_end(l):
        layer_sum(2 * l + 1)
        trans, gate = trans_refs[l][...], jax.nn.sigmoid(gate_refs[l][...])
        gate_refs[l][...] = gate
        value = gate * trans * jax.nn.sigmoid(trans) + (1.0 - gate) * features[l][...]
        lane = lax.broadcasted_iota(jnp.int32, (rows, fp), 1)
        features[l + 1][...] = keep_feature(value, lane, filters)

    matrices = matrices_of(highway, filters)
    gather_h.begin(0)
    of_highway, of_lstm = gather_h.steps(0), gather_l.steps(0)
    passing = len(of_lstm) - 2 * gather_l.line.length
    third = -(-blocks // 3)
    conv(0, third)
    gather_h.run(of_highway[:1])
    conv(third, 2 * third)
    gather_h.run(of_highway[1:3])
    gather_l.begin(0)
    conv(2 * third, blocks)
    soft.place_blocks(soft_ref, soft_out)
    gather_h.run(of_highway[3:5])
    gather_l.run(of_lstm[: passing // 2])
    gather_h.run(of_highway[5:-1])
    gather_l.run(of_lstm[passing // 2 : passing // 2 + 1])
    gather_h.run(of_highway[-1:])
    gather_h.from_sibling(0)
    out_copies = [
        pltpu.make_async_copy(highway_w, highway_out, out_sems.at[0]),
        pltpu.make_async_copy(lstm_w, lstm_out, out_sems.at[1]),
    ]
    out_copies[0].start()
    layer(0)
    gather_l.run(of_lstm[passing // 2 + 1 : passing - 1])
    layer_end(0)
    gather_l.run(of_lstm[passing - 1 : passing])
    layer(1)
    layer_end(1)

    turned_ref[...] = jnp.zeros_like(turned_ref)
    sub = lax.broadcasted_iota(jnp.int32, (fp, words), 0)
    turned_ref[:fp, :] = jnp.where(sub < filters, turned(features[2][...], words), 0.0)
    turned_ref[lstm.used - 1 : lstm.used, :] = jnp.ones((1, words), F32)
    wide = wide.at[: lstm.total]
    copy_windows(lstm, turned_ref, wide, 0, lstm.meeting(0, lstm.used), lambda o: o)
    gather_l.run(of_lstm[passing:])
    gather_l.from_sibling(0)
    out_copies[1].start()
    left = wide[...].astype(BF)
    half = lstm.block[1]
    for h in range(2):
        x_ref[:, h * half : (h + 1) * half] = dot_rows(left, lstm_w[h])[:rows]

    recur_sum[...] = jnp.zeros_like(recur_sum)
    depth = lstm.block[0]
    for h in range(2):
        for slot in sorted({o // lstm.dp for o, _, _ in lstm.meeting(filters, filters + H)}):
            piece = lstm_w[h, slot * depth : (slot + 1) * depth, :].astype(F32)
            for o, first, last in lstm.meeting(filters, filters + H):
                if o // lstm.dp == slot:
                    start, at = lstm.starts[o] - filters, (o % lstm.dp) * lstm.rows
                    recur_sum[start + first : start + last, h * half : (h + 1) * half] += piece[
                        at + first : at + last
                    ]
    recur_ref[...] = recur_sum[...].astype(BF)
    gather_h.finish(0)
    gather_l.finish(0)
    for copy in out_copies:
        copy.wait()
    for m in (2, 3):
        wide_copy(m).wait()
    for i in range(max(blocks - 2, 0), blocks):
        wait_kept(i)


def head(plans, soft, filters, own, conv_inputs, soft_flat, rows, fp, collective_id):
    highway, lstm = plans
    words = up_to(rows, 2 * LANE)
    vmem = pl.BlockSpec(memory_space=pltpu.VMEM)
    anywhere = pl.BlockSpec(memory_space=pl.ANY)
    feature = jax.ShapeDtypeStruct((rows, fp), F32)
    matrices = matrices_of(highway, filters)
    longest_matrix = max(end - begin for _, _, begin, end in matrices)
    longest = max(lstm.total, longest_matrix)
    kept_widths = (HOT, LANE, fp)
    return pl.pallas_call(
        functools.partial(head_kernel, plans, soft, filters, rows // WORD_BLOCK),
        out_shape=[
            jax.ShapeDtypeStruct(highway.shape, BF),
            jax.ShapeDtypeStruct(lstm.shape, BF),
            jax.ShapeDtypeStruct((rows, lstm.columns), F32),
            jax.ShapeDtypeStruct((HP, lstm.columns), BF),
            soft.placed_shape(),
        ]
        + [jax.ShapeDtypeStruct((rows * SLOTS, width), BF) for width in kept_widths]
        + [jax.ShapeDtypeStruct((4, longest_matrix, words), BF)]
        + [feature] * 7,
        in_specs=[anywhere] * 2 + [vmem] * 6,
        out_specs=[anywhere] * 2 + [vmem] * 3 + [anywhere] * 4 + [vmem] * 7,
        scratch_shapes=[
            pltpu.VMEM(highway.shape, BF),
            pltpu.VMEM(lstm.shape, BF),
            pltpu.VMEM((up_to(max(lstm.used, fp), LANE), words), F32),
            pltpu.VMEM((longest, words), F32),
            pltpu.VMEM((HP, lstm.columns), F32),
        ]
        + [pltpu.VMEM((2, WORD_BLOCK * SLOTS, width), BF) for width in kept_widths]
        + [
            pltpu.VMEM((2, longest_matrix, words), BF),
            MiddleGather.semaphores([highway]),
            Gather.semaphores([lstm]),
            pltpu.SemaphoreType.DMA((2,)),
            pltpu.SemaphoreType.DMA((8,)),
        ],
        compiler_params=pltpu.CompilerParams(
            collective_id=collective_id, has_side_effects=True, vmem_limit_bytes=62 * 2**20
        ),
    )(*own, *conv_inputs, soft.blocks_of(soft_flat))


def highway_backward_kernel(plans, conv, filters, blocks, *refs):
    highway, lstm = plans
    dz_ref, hp_ref = refs[:2]
    features, trans_refs, gate_refs = refs[2:5], refs[5:7], refs[7:9]
    kernel_ref, mask_ref, fold_ref = refs[9:12]
    highway_all, lstm_all, kept_all, wide_all = refs[12], refs[13], refs[14:17], refs[17]
    lstm_landed, grad_out, kernel_grad, total_out = refs[18:22]
    refs = refs[22:]
    if conv:
        highway_landed, highway_total, conv_out = refs[:3]
        conv_in, refs = refs[3], refs[4:]
        small = SmallSum(conv, conv_in, conv_out, refs[:5])
        refs = refs[5:]
    lstm_grad, highway_w, lstm_w, turned_ref, wide, back, dz, pairs = refs[:8]
    carry, feature_grad, hot_grad, load_sems, pair_sems, out_sems = refs[8:14]
    kept, wide_low, kept_sems, refs = refs[14:17], refs[17], refs[18], refs[19:]
    rows, fp = features[0].shape
    words = turned_ref.shape[1]
    at = Place()
    total = total_out.at[at.c]
    if conv:
        work = Reduce(
            [lstm, highway],
            [lstm_grad, grad_out],
            [total, highway_total],
            [lstm_landed, highway_landed],
            refs,
            [True, False],
        )
    else:
        work = Reduce([lstm], [lstm_grad], [total], [lstm_landed], refs, [True])
    length, items = work.line.length, work.items
    matrices = matrices_of(highway, filters)
    half = lstm.block[1]
    of_input = lstm.meeting(0, filters)
    input_rows = lstm_w.shape[0]

    def layer_rows(l):
        begin, end = matrices[2 * l][2], matrices[2 * l + 1][3]
        return begin, end

    def load_layer(l):
        begin, end = layer_rows(l)
        return pltpu.make_async_copy(
            highway_all.at[pl.ds(begin, end - begin)],
            highway_w.at[pl.ds(0, end - begin)],
            load_sems.at[l],
        )

    def load_lstm(h):
        return pltpu.make_async_copy(
            lstm_all.at[h, pl.ds(0, input_rows)], lstm_w, load_sems.at[2 + h]
        )

    def load_kept(i):
        k = lax.rem(i, 2)
        size = WORD_BLOCK * SLOTS
        at = pl.ds(pl.multiple_of(i * size, size), size)
        return [
            pltpu.make_async_copy(source.at[at], to.at[k], kept_sems.at[2 * j + k])
            for j, (source, to) in enumerate(zip(kept_all, kept))
        ]

    def load_wide(m):
        return pltpu.make_async_copy(wide_all.at[m], wide_low.at[m % 2], kept_sems.at[6 + m % 2])

    load_layer(1).start()
    load_lstm(0).start()
    for i in range(min(2, blocks)):
        for copy in load_kept(jnp.int32(i)):
            copy.start()
    for m in range(2):
        load_wide(m).start()
    work.line.greet()

    dz[...] = jnp.zeros_like(dz)
    dz[:rows, :] = dz_ref[...].astype(BF)
    lane = lax.broadcasted_iota(jnp.int32, (rows, HP), 1)
    hidden = jnp.where(lane < H, hp_ref[...], jnp.where(lane == H, 1.0, 0.0))
    sub = lax.broadcasted_iota(jnp.int32, (fp, words), 0)
    turned_ref[:fp, :] = jnp.where(sub < filters, turned(features[2][...], words), 0.0)
    depth = up_to(H + 1, 8)
    turned_ref[filters : filters + depth, :] = turned(hidden, words)[:depth]
    copy_windows(
        lstm,
        turned_ref,
        wide.at[: lstm.total],
        0,
        lstm.meeting(0, lstm.used),
        lambda o: lstm.position[o],
    )
    unit = lstm.total // (2 * length)

    def lstm_weights(i, _):
        where = pl.ds(pl.multiple_of(i * unit, unit), unit)
        left = wide[where, :].astype(BF)
        for h in range(2):
            lstm_grad[h, where, :] = dot(left, dz[:, h * half : (h + 1) * half]).astype(BF)
        return 0

    lax.fori_loop(0, 2 * length, lstm_weights, 0)
    work.begin(0)

    lane = lax.broadcasted_iota(jnp.int32, (rows, fp), 1)
    back[...] = jnp.zeros_like(back)
    for h in range(2):
        load_lstm(h).wait()
        wide[:input_rows, :] = dot_cols(lstm_w[...], dz[:, h * half : (h + 1) * half])
        if h == 0:
            load_lstm(1).start()
        add_windows(lstm, wide, back, 0, of_input, 0)
    grad = jnp.where(lane < filters, back[...].T[:rows], 0.0)

    def lead(k):
        work.legs(work.first_leg, 0, k * items // 4, (k + 1) * items // 4)

    lead(0)
    pairs[...] = jnp.zeros_like(pairs)
    for l in (1, 0):
        trans, gate = trans_refs[l][...], gate_refs[l][...]
        sig = jax.nn.sigmoid(trans)
        pairs[2 * l, :rows, :] = (grad * gate * sig * (1.0 + trans * (1.0 - sig))).astype(BF)
        pairs[2 * l + 1, :rows, :] = (
            grad * (trans * sig - features[l][...]) * gate * (1.0 - gate)
        ).astype(BF)
        load_layer(l).wait()
        back[...] = jnp.zeros_like(back)
        begin = layer_rows(l)[0]
        for m in (2 * l, 2 * l + 1):
            base, found, low, high = matrices[m]
            result = dot_cols(highway_w[low - begin : high - begin, :], pairs[m])
            add_windows(highway, result, back, base, found, low)
            if m % 2 and l:
                load_layer(0).start()
            if m > 0:
                lead(4 - m)
        grad = grad * (1.0 - gate) + back[...].T[:rows]
        grad = jnp.where(lane < filters, grad, 0.0)
    feature_grad[...] = grad

    kernel_grad[...] = jnp.zeros_like(kernel_grad)
    hot_grad[...] = jnp.zeros_like(hot_grad)

    def conv_block(i, _):
        where = pl.ds(pl.multiple_of(i * WORD_BLOCK, WORD_BLOCK), WORD_BLOCK)
        for copy in load_kept(i):
            copy.wait()
        k = lax.rem(i, 2)
        conv_backward_block(
            [ref.at[k] for ref in kept], kernel_ref, feature_grad, where, kernel_grad, hot_grad
        )

        @pl.when(i + 2 < blocks)
        def _():
            for copy in load_kept(i + 2):
                copy.start()


        @pl.when(i >= blocks - 4)
        def _():
            k = i - (blocks - 4)
            work.legs(work.middle_leg, 0, k * length // 4, (k + 1) * length // 4)

        return 0

    lax.fori_loop(0, blocks, conv_block, 0)
    kernel_grad[:, fp:] = jnp.dot(
        fold_ref[...],
        hot_grad[...] * mask_ref[...],
        precision=lax.Precision.HIGHEST,
        preferred_element_type=F32,
    )
    steps = []
    if conv:
        conv.fill(conv_in, kernel_grad)
        steps = small.steps()
        steps[0]()

    staged = highway_w
    chunk = 384
    size = highway.rows
    pending, shared = [], None
    empty = [o for o in range(len(highway.starts)) if all(o != f[0] for m in matrices for f in m[1])]
    for m in range(4):
        base, found, low, high = matrices[m]
        load_wide(m).wait()
        for copy in pending:
            copy.wait()
        adds = shared == found[0][0]
        shares = m < 3 and matrices[m + 1][1][0][0] == found[-1][0]
        count = len(found)

        def columns(j, _):
            where = pl.ds(pl.multiple_of(j * chunk, chunk), chunk)
            result = dot(wide_low[m % 2, : high - low, :], pairs[m, :, where])
            if adds:
                first = result[:size] + carry[:, where]
                staged[:size, where] = first.astype(BF)
                staged[size : high - low, where] = result[size:].astype(BF)
            else:
                staged[: high - low, where] = result.astype(BF)
            if shares:
                carry[:, where] = result[(count - 1) * size :]
            return 0

        lax.fori_loop(0, fp // chunk, columns, 0)
        if m < 2:
            load_wide(m + 2).start()
        shared = found[-1][0] if shares else None
        sent = found[:-1] if shares else found
        pending = [
            pltpu.make_async_copy(
                staged.at[pl.ds(k * size, size)],
                grad_out.at[pl.ds(highway.position[o] * size, size)],
                out_sems.at[k],
            )
            for k, (o, _, _) in enumerate(sent)
        ]
        for copy in pending:
            copy.start()
        if conv and m == 2:
            steps[1]()
        work.legs(
            work.middle_leg, 0, length + m * length // 4, length + (m + 1) * length // 4
        )
    for copy in pending:
        copy.wait()
    if empty:
        staged[:size, :] = jnp.zeros((size, fp), BF)
        for o in empty:
            copy = pltpu.make_async_copy(
                staged.at[pl.ds(0, size)],
                grad_out.at[pl.ds(highway.position[o] * size, size)],
                out_sems.at[0],
            )
            copy.start()
            copy.wait()
    copy = remote(total, total, pair_sems.at[0], pair_sems.at[1], at.sibling)
    if not conv:
        work.last_leg(0)
        copy.start()
    else:
        work.begin(1)
        work.legs(work.first_leg, 1, 0, length)
        steps[2]()
        work.legs(work.first_leg, 1, length, items)
        late = steps[3:-1]
        for k, step in enumerate(late):
            work.legs(
                work.middle_leg, 1, k * items // len(late), (k + 1) * items // len(late)
            )
            step()
            if k == 1:
                work.last_leg(0)
                copy.start()
        work.last_leg(1)
        steps[-1]()
    for a in range(2 if conv else 1):
        work.finish(a)
    copy.wait()


def conv_columns(fp):
    return up_to(fp + LANE, 2 * LANE)


def highway_backward(
    plans, conv, filters, dz, hp, features, trans, gates, conv_inputs, everywhere, collective_id
):
    highway, lstm = plans
    rows, fp = features[0].shape
    words = up_to(rows, 2 * LANE)
    vmem = pl.BlockSpec(memory_space=pltpu.VMEM)
    anywhere = pl.BlockSpec(memory_space=pl.ANY)
    matrices = matrices_of(highway, filters)
    longest = max([lstm.total] + [end - begin for _, _, begin, end in matrices])
    layer = max(matrices[2 * l + 1][3] - matrices[2 * l][2] for l in range(2))
    input_rows = up_to((lstm.meeting(0, filters)[-1][0] + 1) * lstm.rows, 16)
    return pl.pallas_call(
        functools.partial(highway_backward_kernel, plans, conv, filters, rows // WORD_BLOCK),
        out_shape=[
            jax.ShapeDtypeStruct((lstm.fsdp,) + lstm.block, BF),
            jax.ShapeDtypeStruct(highway.shape, BF),
            jax.ShapeDtypeStruct((LANE, conv_columns(fp)), F32),
            jax.ShapeDtypeStruct((2,) + lstm.block, F32),
        ]
        + (
            [
                jax.ShapeDtypeStruct((highway.fsdp,) + highway.block, BF),
                jax.ShapeDtypeStruct(highway.block, F32),
                jax.ShapeDtypeStruct(conv.shape, F32),
            ]
            if conv
            else []
        ),
        in_specs=[vmem] * 12 + [anywhere] * 6,
        out_specs=[anywhere] * 2 + [vmem] * 2 + ([anywhere, vmem, vmem] if conv else []),
        scratch_shapes=(
            [pltpu.VMEM(conv.shape, F32)] + SmallSum.scratch(conv) if conv else []
        )
        + [
            pltpu.VMEM(lstm.shape, BF),
            pltpu.VMEM((layer, highway.columns), BF),
            pltpu.VMEM((input_rows, lstm.block[1]), BF),
            pltpu.VMEM((up_to(max(lstm.used + 8, fp), LANE), words), F32),
            pltpu.VMEM((longest, words), F32),
            pltpu.VMEM((fp, words), F32),
            pltpu.VMEM((words, lstm.columns), BF),
            pltpu.VMEM((4, words, fp), BF),
            pltpu.VMEM((highway.rows, fp), F32),
            pltpu.VMEM((rows, fp), F32),
            pltpu.VMEM((HOT, LANE), F32),
            pltpu.SemaphoreType.DMA((4,)),
            pltpu.SemaphoreType.DMA((2,)),
            pltpu.SemaphoreType.DMA((max(len(found) for _, found, _, _ in matrices),)),
        ]
        + [pltpu.VMEM((2, WORD_BLOCK * SLOTS, width), BF) for width in (HOT, LANE, fp)]
        + [pltpu.VMEM((2,) + everywhere[-1].shape[1:], BF), pltpu.SemaphoreType.DMA((8,))]
        + (
            Reduce.scratch([lstm, highway], [True, False], [True, True])
            if conv
            else Reduce.scratch([lstm], [True], [True])
        ),
        compiler_params=pltpu.CompilerParams(
            collective_id=collective_id, has_side_effects=True, vmem_limit_bytes=255 * 2**18
        ),
    )(dz, hp, *features, *trans, *gates, *conv_inputs, *everywhere)


def softmax_kernel(
    vocab,
    n,
    h_ref,
    w_ref,
    map_ref,
    map_back_ref,
    recur_ref,
    loss_ref,
    grad_h_ref,
    grad_w_ref,
    turned_out,
    turn_in,
    turn_out,
    turn_sems,
    spread_back,
    logits,
    grads,
    stats,
    for_sibling,
    from_sibling,
    for_line,
    from_line,
    own_total,
    sems,
):
    line = Line(n)
    at, length, me = line.at, line.length, line.me
    members, rows, _ = h_ref.shape
    width = w_ref.shape[-1]
    w = w_ref[...].reshape(-1, width)
    STAT, STAT_RECV, SIB, SIB_RECV, TO_LINE, LINE_RECV = range(6)
    sem = Semaphores(sems, members)
    column = me * width + lax.broadcasted_iota(jnp.int32, (rows, width), 1)
    real_column = column.astype(F32)
    words = up_to(rows, LANE)
    lane = lax.broadcasted_iota(jnp.int32, (rows, LANE), 1)
    aside = HP - LANE

    def pieces(b):
        tail = h_ref[b, :, aside:].astype(F32)
        first = H + 1 - aside
        target = tail[:, first : first + 1] * 256.0 + tail[:, first + 1 : first + 2]
        scale = (
            tail[:, first + 2 : first + 3]
            + tail[:, first + 3 : first + 4]
            + tail[:, first + 4 : first + 5]
        )
        return target, scale

    piece = turn_in.shape[2]
    pieces_of = recur_ref.shape[1] // piece

    def turn_load(j):
        return pltpu.make_async_copy(
            recur_ref.at[:, pl.ds(j * piece, piece)], turn_in.at[j % 2], turn_sems.at[j % 2]
        )

    def turn_store(j):
        return pltpu.make_async_copy(
            turn_out.at[j % 2], turned_out.at[pl.ds(j * piece, piece)], turn_sems.at[2 + j % 2]
        )

    turn_load(0).start()
    line.greet(False, True)

    def forward(b, _):
        h = h_ref[b]
        wide = dot(h, map_ref[...]).astype(BF)
        spread_back[b] = dot(h, map_back_ref[...]).astype(BF)
        now = jnp.where(column < vocab, dot(wide, w), -1e30)
        logits[b] = now
        target, _ = pieces(b)
        top = jnp.max(now, axis=1, keepdims=True)
        log_sum = top + jnp.log(jnp.sum(jnp.exp(now - top), axis=1, keepdims=True))
        picked = jnp.sum(jnp.where(real_column == target, now, 0.0), axis=1, keepdims=True)
        both = jnp.where(lane == 0, log_sum, jnp.where(lane == 1, picked, 0.0))
        both = jnp.concatenate([both, jnp.zeros((words - rows, LANE), F32)], axis=0).T
        stats[me, 0, pl.ds(b, 1), :] = both[0:1, :]
        stats[me, 1, pl.ds(b, 1), :] = both[1:2, :]
        return 0

    lax.fori_loop(0, members, forward, 0)

    def stat(member, target):
        here = stats.at[member]
        return remote(here, here, sem(STAT, member), sem(STAT_RECV, member), target)

    def stat_out(z):
        return [
            remote(
                stats.at[me], stats.at[me], sem(STAT, 2 * z + core), sem(STAT_RECV, me), target
            )
            for core, target in ((at.c, line.peer(z)), (1 - at.c, line.peer(z, True)))
        ]

    def send_stats(z):
        for copy in stat_out(z):
            copy.start()

    line.others(send_stats)
    to_pair = remote(
        stats.at[me], stats.at[me], sem(STAT, 2 * at.z + 1 - at.c), sem(STAT_RECV, me), at.sibling
    )
    to_pair.start()

    def stats_in(z):
        for core in (at.c, 1 - at.c):
            stat(2 * z + core, at.sibling).wait_recv()

    line.others(stats_in)
    stat(2 * at.z + 1 - at.c, at.sibling).wait_recv()
    top = stats[0, 0]
    for q in range(1, members):
        top = jnp.maximum(top, stats[q, 0])
    total = jnp.zeros_like(top)
    picked = jnp.zeros_like(top)
    for q in range(members):
        total += jnp.exp(stats[q, 0] - top)
        picked += stats[q, 1]
    log_total = top + jnp.log(total)
    loss_ref[...] = log_total - picked
    log_columns = jnp.concatenate(
        [log_total, jnp.zeros((LANE - members, words), F32)], axis=0
    ).T[:rows]

    def to_sibling(z):
        return remote(
            for_sibling.at[z], from_sibling.at[z], sem(SIB, z), sem(SIB_RECV, z), at.sibling
        )

    def to_line(z):
        return remote(
            for_line.at[z], from_line.at[at.z], sem(TO_LINE, z), sem(LINE_RECV, at.z), line.peer(z)
        )

    def backward(k, _):
        z = lax.rem(k, length)
        mine = k >= length
        b = 2 * z + jnp.where(mine, at.c, 1 - at.c)
        target, scale = pieces(b)
        log_sum = jnp.sum(jnp.where(lane == b, log_columns, 0.0), axis=1, keepdims=True)
        share = jnp.exp(logits[b] - log_sum)
        grad = ((share - (real_column == target).astype(F32)) * scale).astype(BF)
        grads[b] = grad
        back = dot_cols(grad, w)

        @pl.when(jnp.logical_not(mine))
        def _():
            for_sibling[z] = back.astype(BF)
            to_sibling(z).start()

        @pl.when(mine)
        def _():
            to_sibling(z).wait_recv()
            total = back + from_sibling[z].astype(F32)

            @pl.when(z == at.z)
            def _():
                own_total[...] = total

            @pl.when(z != at.z)
            def _():
                for_line[z] = total.astype(BF)
                to_line(z).start()

        return 0

    lax.fori_loop(0, 2 * length, backward, 0)

    depth = map_ref.shape[1]
    unit = 256
    everything = grads[...].reshape(members * rows, width)

    def weight_grad(m, _):
        left = spread_back[:, :, pl.ds(pl.multiple_of(m * unit, unit), unit)]
        result = dot_rows(left.reshape(members * rows, unit), everything).astype(BF)
        grad_w_ref[pl.ds(m * unit, unit), :] = result
        return 0

    lax.fori_loop(0, depth // unit, weight_grad, 0)

    for j in range(pieces_of):
        turn_load(j).wait()
        if j + 1 < pieces_of:
            turn_load(j + 1).start()
        if j >= 2:
            turn_store(j - 2).wait()
        turn_out[j % 2] = turn_in[j % 2].astype(F32).T.astype(BF)
        turn_store(j).start()
    for j in range(max(pieces_of - 2, 0), pieces_of):
        turn_store(j).wait()

    def arrived(z):
        remote(
            from_line.at[z], from_line.at[z], sem(TO_LINE, z), sem(LINE_RECV, z), line.peer(z)
        ).wait_recv()
        own_total[...] += from_line[z].astype(F32)

    line.others(arrived)
    spread_grad = own_total[...]
    high = spread_grad.astype(BF)
    low = (spread_grad - high.astype(F32)).astype(BF)
    grad_h_ref[...] = dot_cols(high, map_ref[...]) + dot_cols(low, map_ref[...])

    def finish(z):
        for copy in stat_out(z):
            copy.wait_send()
        to_line(z).wait_send()

    line.others(finish)
    line.chips(lambda z: to_sibling(z).wait_send())
    to_pair.wait_send()


def word_softmax(plan, h, weights, mapping, mapping_back, recur, collective_id):
    members, rows, depth = h.shape
    n = plan.fsdp
    spread = mapping.shape[1]
    per_slot, width = plan.block
    words = up_to(rows, LANE)
    length = members // 2
    vmem = pl.BlockSpec(memory_space=pltpu.VMEM)
    piece = 2 * LANE
    anywhere = pl.BlockSpec(memory_space=pl.ANY)
    loss, grad_h, grad_w, turned_recur = pl.pallas_call(
        functools.partial(softmax_kernel, plan.width, n),
        out_shape=[
            jax.ShapeDtypeStruct((members, words), F32),
            jax.ShapeDtypeStruct((rows, depth), F32),
            jax.ShapeDtypeStruct((spread, width), BF),
            jax.ShapeDtypeStruct(recur.shape[::-1], BF),
        ],
        in_specs=[vmem] * 4 + [anywhere],
        out_specs=[vmem] * 3 + [anywhere],
        scratch_shapes=[
            pltpu.VMEM((2, recur.shape[0], piece), BF),
            pltpu.VMEM((2, piece, recur.shape[0]), BF),
            pltpu.SemaphoreType.DMA((4,)),
            pltpu.VMEM((members, rows, spread), BF),
            pltpu.VMEM((members, rows, width), F32),
            pltpu.VMEM((members, rows, width), BF),
            pltpu.VMEM((members, 2, members, words), F32),
            pltpu.VMEM((length, rows, spread), BF),
            pltpu.VMEM((length, rows, spread), BF),
            pltpu.VMEM((length, rows, spread), BF),
            pltpu.VMEM((length, rows, spread), BF),
            pltpu.VMEM((rows, spread), F32),
            pltpu.SemaphoreType.DMA((6 * members,)),
        ],
        compiler_params=pltpu.CompilerParams(
            collective_id=collective_id, has_side_effects=True, vmem_limit_bytes=62 * 2**20
        ),
    )(h, weights, mapping, mapping_back, recur)
    return loss, grad_h, grad_w.reshape((n,) + plan.block), turned_recur


def shards(
    fsdp_count,
    dp_count,
    chars,
    lengths,
    targets,
    resets,
    init_state,
    window_grad,
    char_table,
    conv_weight,
    conv_bias,
    highway_flat,
    lstm_flat,
    soft_flat,
):
    micro_count, streams, step_count, letters = chars.shape
    char_count, embed_dim = char_table.shape
    filters = conv_weight.shape[1]
    batch = micro_count * streams
    words = step_count * batch
    rows = up_to(words, 16)
    fp = up_to(filters + 1, LANE)
    dp_at, fsdp_at = lax.axis_index("dp"), lax.axis_index("fsdp")
    highway = Windows(
        highway_flat.shape[0] * fsdp_count, filters, 4 * (filters + 1), fsdp_count, dp_count, True
    )
    lstm = Windows(
        lstm_flat.shape[0] * fsdp_count, 4 * H, filters + H + 1, fsdp_count, dp_count, False
    )
    soft = Windows(
        soft_flat.shape[0] * fsdp_count, V, H + 1, fsdp_count, dp_count, False, fsdp_count // 2
    )
    member = 2 * (fsdp_at // 4) + lax.rem(dp_at, 2)

    def by_step(array):
        return jnp.moveaxis(array.reshape((batch, step_count) + array.shape[3:]), 1, 0).reshape(
            (words,) + array.shape[3:]
        )

    def pad_rows(array, value=0):
        return jnp.pad(
            array,
            [(0, rows - words)] + [(0, 0)] * (array.ndim - 1),
            constant_values=value,
        )

    word_chars = pad_rows(by_step(chars))
    word_lengths = pad_rows(by_step(lengths))[:, None]
    position = jnp.arange(letters, dtype=jnp.int32)[None, :]
    codes = jnp.where(position < word_lengths, word_chars, -1)
    codes = jnp.pad(codes, ((0, 0), (0, SLOTS - letters)), constant_values=-1)
    codes = codes.reshape(rows * SLOTS, 1)
    column = np.arange(fp)
    widths = np.ones((fp,), np.int32)
    for cut_at in FILTER_CUTS:
        widths = widths + ((column >= filters * cut_at // 22) & (column < filters))
    widths = widths.astype(np.int32)
    kernel_mask = jnp.asarray(
        np.arange(KMAX * embed_dim)[:, None] // embed_dim < widths[None, :filters]
    )
    ones_row = KMAX * embed_dim
    kernel = jnp.concatenate(
        [jnp.where(kernel_mask, conv_weight, jnp.zeros_like(conv_weight)), conv_bias[None, :]], axis=0
    )
    kernel = jnp.pad(kernel, ((0, LANE - ones_row - 1), (0, fp - filters)))
    spread_table = jnp.concatenate(
        [
            jnp.pad(char_table, ((0, 0), (q * embed_dim, LANE - (q + 1) * embed_dim)))
            for q in range(KMAX)
        ]
        + [jnp.asarray((np.arange(LANE) == ones_row)[None, :].astype(np.float32)).astype(BF)],
        axis=0,
    )
    spread_table = jnp.pad(spread_table, ((0, HOT - KMAX * char_count - 1), (0, 0)))
    conv_inputs = (codes, word_lengths, spread_table, kernel, jnp.asarray(widths)[None, :])

    highway_all, lstm_all, from_input, recur, soft_placed, *kept = head(
        [highway, lstm],
        soft,
        filters,
        place_all([highway, lstm], [highway_flat, lstm_flat]),
        conv_inputs,
        soft_flat,
        rows,
        fp,
        1,
    )
    kept_parts, kept = kept[:4], kept[4:]
    features, trans, gates = kept[:3], kept[3:5], kept[5:7]

    soft_own = soft.from_placed(soft_placed)
    keep = pad_rows(by_step(1 - resets).astype(F32))[:, None]
    start = init_state.reshape(batch, 2, H)
    start = jnp.pad(start, ((0, 8 - batch), (0, 0), (0, HP - H)))
    row_scale = jnp.broadcast_to(
        window_grad.reshape(1, batch) / step_count, (step_count, batch)
    ).reshape(words)
    goal = by_step(targets)
    scale_high = lax.reduce_precision(row_scale, 8, 7)
    scale_mid = lax.reduce_precision(row_scale - scale_high, 8, 7)
    extra = jnp.stack(
        [
            jnp.ones((words,), F32),
            (goal // 256).astype(F32),
            (goal % 256).astype(F32),
            scale_high,
            scale_mid,
            row_scale - scale_high - scale_mid,
        ],
        axis=1,
    )
    aside = H - (HP - LANE)
    extra = jnp.pad(extra, ((0, rows - words), (aside, LANE - aside - extra.shape[1])))
    *states, hidden_all, soft_part = lstm_forward(
        batch,
        soft,
        from_input,
        recur,
        start[:, 0].astype(BF).astype(F32),
        start[:, 1],
        keep,
        extra,
        soft_own,
        4,
    )
    hp = states[0]

    word_loss, grad_hidden, soft_grad, recur_t = word_softmax(
        soft,
        hidden_all,
        soft_part,
        one_hot_map(HP, soft.gathered),
        one_hot_map(HP, soft.reduced),
        recur,
        5,
    )
    word_loss = lax.dynamic_index_in_dim(word_loss, member, 0, keepdims=False)
    window_loss = jnp.mean(word_loss[:words].reshape(step_count, batch), axis=0).reshape(
        micro_count, streams
    )

    dz, soft_part = lstm_backward(
        batch, soft, lstm.columns, grad_hidden, recur_t, keep, states[1:], soft_grad, 6
    )
    hot_row, hot_lane = np.arange(HOT), np.arange(LANE)
    hot_mask = (hot_row[:, None] // char_count == hot_lane[None, :] // embed_dim) & (
        hot_row[:, None] < KMAX * char_count
    )
    hot_fold = (hot_row[None, :] % char_count == np.arange(LANE)[:, None]) & (
        hot_row[None, :] < KMAX * char_count
    )
    conv = Dense(LANE, conv_columns(fp), fsdp_count)
    at_once = 2 * fsdp_count * highway.block[0] * highway.block[1] * 2 <= 12 * 2**20
    _, highway_grad, conv_grad, lstm_part, *rest = highway_backward(
        [highway, lstm],
        conv if at_once else None,
        filters,
        dz,
        hp,
        features,
        trans,
        gates,
        (
            kernel,
            jnp.asarray(hot_mask.astype(np.float32)),
            jnp.asarray(hot_fold.astype(np.float32)),
        ),
        (highway_all, lstm_all, *kept_parts),
        7,
    )
    if at_once:
        _, highway_part, conv_grad = rest
    else:
        conv_grad, highway_part = tail([conv, highway], conv_grad, highway_grad, 3)
    conv_grad = jnp.concatenate(
        [conv_grad[h].reshape(-1, conv.block[1])[:LANE] for h in range(2)], axis=1
    )
    conv_weight_grad = jnp.where(kernel_mask, conv_grad[:ones_row, :filters], 0.0)
    conv_bias_grad = conv_grad[ones_row, :filters]
    table_grad = jnp.sum(
        conv_grad[:char_count, fp : fp + KMAX * embed_dim].reshape(char_count, KMAX, embed_dim), axis=1
    )

    def own_window(plan, part):
        if dp_count > 2:
            groups = [list(range(h, dp_count, 2)) for h in range(2)]
            part = lax.psum(part.astype(F32), "dp", axis_index_groups=groups)
        if plan.by_rows:
            at = dp_at // 2
        else:
            at = dp_at
            part = jnp.concatenate(
                [
                    lax.dynamic_slice_in_dim(part[p], at * plan.rows, plan.rows, 0)
                    for p in range(plan.parts)
                ],
                axis=1,
            ).astype(F32)
            return plan.to_flat(part, dp_at, fsdp_at)
        window = lax.dynamic_slice_in_dim(part, at * plan.rows, plan.rows, 0)
        return plan.to_flat(window, dp_at, fsdp_at)

    return (
        window_loss,
        table_grad,
        conv_weight_grad,
        conv_bias_grad,
        own_window(highway, highway_part),
        own_window(lstm, lstm_part),
        own_window(soft, soft_part),
    )


def solution(mesh):
    in_specs = (
        P(None, ("dp", "fsdp"), None, None),
        P(None, ("dp", "fsdp"), None),
        P(None, ("dp", "fsdp"), None),
        P(None, ("dp", "fsdp"), None),
        P(None, ("dp", "fsdp"), None, None),
        P(None, ("dp", "fsdp")),
        P(),
        P(),
        P(),
        P("fsdp", None),
        P("fsdp", None),
        P("fsdp", None),
    )
    out_specs = (
        P(None, ("dp", "fsdp")),
        P(),
        P(),
        P(),
        P(("dp", "fsdp"), None),
        P(("dp", "fsdp"), None),
        P(("dp", "fsdp"), None),
    )
    return jax.shard_map(
        functools.partial(shards, mesh.shape["fsdp"], mesh.shape["dp"]),
        mesh=mesh,
        in_specs=in_specs,
        out_specs=out_specs,
        check_vma=False,
    )
```

```python
import functools

import jax
import jax.numpy as jnp
import ml_dtypes
import numpy as np
from jax import lax
from jax.experimental import pallas as pl
from jax.experimental.pallas import tpu as pltpu
from jax.sharding import PartitionSpec as P

H = 650
V = 10000
KMAX = 7
LANE = 128
HP = 768
SLOTS = 24
CHARS = 51
HOT = 384
FILTER_CUTS = (1, 3, 6, 10, 14, 18)
MESH = pl.DeviceIdType.MESH
BF = jnp.bfloat16
F32 = jnp.float32


def up_to(value, unit):
    return -(-value // unit) * unit


def dot(left, right):
    return jnp.dot(left, right, preferred_element_type=F32)


def dot_rows(left, right):
    return lax.dot_general(left, right, (((0,), (0,)), ((), ())), preferred_element_type=F32)


def dot_cols(left, right):
    return lax.dot_general(left, right, (((1,), (1,)), ((), ())), preferred_element_type=F32)


class Windows:
    dtype = BF

    def __init__(self, flat_rows, width, used, fsdp, dp, by_rows, parts=2):
        owners = fsdp * dp
        self.parts = parts
        self.width, self.by_rows, self.fsdp, self.dp, self.used = width, by_rows, fsdp, dp, used
        self.entries = flat_rows * LANE // owners
        self.starts = [o * self.entries // width for o in range(owners)]
        self.spans = [
            (o * self.entries % width + self.entries - 1) // width + 1 for o in range(owners)
        ]
        unit = 16 if by_rows else 8
        rows = up_to(max(self.spans), unit)
        while (dp * rows) % 16:
            rows += unit
        self.rows = rows
        self.total = owners * rows
        self.columns = up_to(width, LANE) if by_rows else parts * up_to(-(-width // parts), LANE)
        self.block = (
            (dp // 2 * rows, self.columns) if by_rows else (dp * rows, self.columns // parts)
        )
        self.shape = (
            (self.total, self.columns)
            if by_rows
            else (parts, self.total, self.columns // parts)
        )
        if by_rows:
            order = [
                (2 * jj + h) * fsdp + f
                for f in range(fsdp)
                for h in range(2)
                for jj in range(dp // 2)
            ]
        else:
            order = [d * fsdp + f for f in range(fsdp) for d in range(dp)]
        self.position = [order.index(o) for o in range(owners)]
        self.gathered = self.row_map(range(owners))
        self.reduced = self.row_map(order)

    def row_map(self, order):
        rows_of = [
            [
                self.starts[o] + i if i < self.spans[o] and self.starts[o] + i < self.used else -1
                for i in range(self.rows)
            ]
            for o in order
        ]
        return np.array(rows_of, np.int32).reshape(-1)

    def pick(self, ref, half, slot):
        depth = self.block[0]
        if self.by_rows:
            return ref.at[pl.ds(pl.multiple_of((2 * slot + half) * depth, 16), depth)]
        return ref.at[half, pl.ds(pl.multiple_of(slot * depth, 16), depth)]

    def meeting(self, begin, end):
        found = []
        for o, (start, span) in enumerate(zip(self.starts, self.spans)):
            first, last = max(0, begin - start), min(span, end - start)
            if first < last:
                found.append((o, first, last))
        return found

    @property
    def lines(self):
        return up_to(-(-self.rows * self.width // LANE), 16) + 32

    def place_blocks(self, shard_ref, out_ref):
        fsdp_at = lax.axis_index("fsdp")
        count = self.entries // LANE
        out_ref[...] = jnp.zeros_like(out_ref)
        for j in range(self.dp):
            shift = lax.rem((fsdp_at * self.dp + j) * self.entries, self.width)
            lanes, lines = lax.rem(shift, LANE), lax.rem(shift // LANE, 16)
            block = shard_ref[j].astype(F32)
            extra = up_to(count, 16) + 16 - count
            block = jnp.concatenate([block, jnp.zeros((extra, LANE), F32)], axis=0)
            block = pltpu.roll(block, lanes, 1)
            lane = lax.broadcasted_iota(jnp.int32, block.shape, 1)
            block = jnp.where(lane < lanes, pltpu.roll(block, 1, 0), block)
            for step in (1, 2, 4, 8):
                moved = lax.rem(lines // step, 2) == 1
                block = jnp.where(moved, pltpu.roll(block, step, 0), block)
            begin = pl.multiple_of(shift // (16 * LANE) * 16, 16)
            out_ref[j, pl.ds(begin, count + extra), :] = block.astype(BF)

    def placed_shape(self):
        return jax.ShapeDtypeStruct((self.dp, self.lines, LANE), BF)

    def blocks_of(self, shard):
        return shard.reshape(self.dp, self.entries // LANE, LANE)

    def from_placed(self, placed):
        size = self.rows * self.width
        joined = jnp.concatenate(
            [
                jnp.pad(
                    placed[j].reshape(-1)[:size].reshape(self.rows, self.width),
                    ((0, 0), (0, self.columns - self.width)),
                )
                for j in range(self.dp)
            ],
            axis=0,
        )
        if self.by_rows:
            return joined.reshape((2,) + self.block)
        part = self.columns // self.parts
        return jnp.stack([joined[:, p * part : (p + 1) * part] for p in range(self.parts)])

    def to_flat(self, window, dp_at, fsdp_at):
        shift = lax.rem((dp_at * self.fsdp + fsdp_at) * self.entries, self.width)
        flat = window[:, : self.width].reshape(-1)
        return lax.dynamic_slice(flat, (shift,), (self.entries,)).reshape(-1, LANE)


def one_hot_map(rows, row_map):
    return jnp.asarray((np.arange(rows)[:, None] == row_map[None, :]).astype(ml_dtypes.bfloat16))


class Place:
    def __init__(self):
        self.d, self.f = lax.axis_index("dp"), lax.axis_index("fsdp")
        self.c = lax.rem(self.d, 2)
        x, y, self.z = lax.rem(self.f, 2), lax.rem(self.f // 2, 2), self.f // 4
        self.first = x + self.c * (y - x)
        self.last = y + self.c * (x - y)
        self.stride1, self.stride3 = 1 + self.c, 2 - self.c
        self.flip1 = self.stride1 * (1 - 2 * self.first)
        self.flip3 = self.stride3 * (1 - 2 * self.last)
        self.partner1 = (self.d, self.f + self.flip1)
        self.partner3 = (self.d, self.f + self.flip3)
        self.sibling = (self.d + 1 - 2 * self.c, self.f)

    def last_bit(self, block):
        bit_x, bit_y = lax.rem(block, 2), lax.rem(block // 2, 2)
        return bit_y + self.c * (bit_x - bit_y)


def remote(src, dst, send, recv, target):
    return pltpu.make_async_remote_copy(
        src_ref=src,
        dst_ref=dst,
        send_sem=send,
        recv_sem=recv,
        device_id=target,
        device_id_type=MESH,
    )


class Line:
    def __init__(self, n):
        self.at = Place()
        self.length = n // 4
        self.me = 2 * self.at.z + self.at.c

    def peer(self, z, other_core=False):
        at = self.at
        return (at.d + (1 - 2 * at.c if other_core else 0), at.f + 4 * (z - at.z))

    def column(self, z):
        return self.at.f + 4 * (z - self.at.z)

    def others(self, body):
        def step(z, _):
            pl.when(z != self.at.z)(functools.partial(body, z))
            return 0

        lax.fori_loop(0, self.length, step, 0)

    def chips(self, body):
        def step(z, _):
            body(z)
            return 0

        lax.fori_loop(0, self.length, step, 0)

    def far(self, k):
        z = jnp.int32(0)
        for here in range(self.length):
            order = sorted(range(self.length), key=lambda there: (-abs(there - here), there))
            for i, there in enumerate(order):
                z = jnp.where((self.at.z == here) & (k == i), there, z)
        return z

    def greet(self, across=True, both_cores=False):
        barrier = pltpu.get_barrier_semaphore()

        def signal(target):
            pl.semaphore_signal(barrier, inc=1, device_id=target, device_id_type=MESH)

        signal(self.at.sibling)
        count = 1
        if across:
            signal(self.at.partner1)
            signal(self.at.partner3)
            count += 2

        def chip(z):
            signal(self.peer(z))
            if both_cores:
                signal(self.peer(z, True))

        self.others(chip)
        pl.semaphore_wait(barrier, count + (self.length - 1) * (2 if both_cores else 1))


class Semaphores:
    def __init__(self, ref, size):
        self.ref, self.size = ref, size

    def __call__(self, kind, index):
        return self.ref.at[kind * self.size + index]


class Gather:
    RECV, SIB_RECV, LINE, NEAR, LAST, SIB, LOCAL = range(7)

    def __init__(self, plans, own, outs, sems, shared):
        self.plans, self.own, self.outs, self.sems, self.shared = plans, own, outs, sems, shared
        self.n = plans[0].fsdp
        self.line = Line(self.n)
        self.at = self.line.at

    @staticmethod
    def semaphores(plans):
        return pltpu.SemaphoreType.DMA((7 * len(plans) * plans[0].fsdp,))

    def sem(self, kind, a, index):
        return self.sems.at[(kind * len(self.plans) + a) * self.n + index]

    def source(self, a, half):
        return self.own[a].at[half] if self.shared else self.own[a]

    def copy(self, kind, a, index, block, target, own=False):
        here = self.plans[a].pick(self.outs[a], self.at.c, block)
        return remote(
            self.source(a, self.at.c) if own else here,
            here,
            self.sem(kind, a, index),
            self.sem(self.SIB_RECV if kind == self.SIB else self.RECV, a, block),
            target,
        )

    def arrived(self, a, block, kind=RECV):
        c = self.at.c
        here = self.plans[a].pick(self.outs[a], 1 - c if kind == self.SIB_RECV else c, block)
        remote(
            here, here, self.sem(self.SIB, a, block), self.sem(kind, a, block), self.at.sibling
        ).wait_recv()

    def local(self, a, half):
        return pltpu.make_async_copy(
            self.source(a, half),
            self.plans[a].pick(self.outs[a], half, self.at.f),
            self.sem(self.LOCAL, a, half if self.shared else 0),
        )

    def to_sibling(self, a, block, own=False):
        return self.copy(self.SIB, a, block, block, self.at.sibling, own)

    def close_by(self, k):
        return self.line.far(self.line.length - 1 - k)

    def begin(self, a):
        at, line = self.at, self.line
        self.copy(self.NEAR, a, at.z, at.f, at.partner1, True).start()
        self.copy(self.LAST, a, at.z, at.f, at.partner3, True).start()

        def chip(k, _):
            z = self.close_by(k)
            self.copy(self.LINE, a, z, at.f, line.peer(z), True).start()
            return 0

        lax.fori_loop(1, line.length, chip, 0)
        if self.shared:
            for half in (0, 1):
                self.local(a, half).start()
        else:
            self.to_sibling(a, at.f, True).start()
            self.local(a, at.c).start()

    def from_line(self, a, k):
        z = self.close_by(k)
        block = self.line.column(z)
        self.arrived(a, block)
        self.copy(self.NEAR, a, z, block, self.at.partner1).start()
        self.copy(self.LAST, a, z, block, self.at.partner3).start()
        self.to_sibling(a, block).start()

    def from_near(self, a, k):
        z = self.close_by(k)
        block = self.line.column(z) + self.at.flip1
        self.arrived(a, block)
        self.copy(self.LAST, a, self.line.length + z, block, self.at.partner3).start()
        self.to_sibling(a, block).start()

    def from_last(self, a, k):
        length = self.line.length
        block = (
            self.line.column(self.close_by(lax.rem(k, length)))
            + self.at.flip3
            + self.at.flip1 * (k // length)
        )
        self.arrived(a, block)
        self.to_sibling(a, block).start()

    def steps(self, a):
        length = self.line.length
        order = [(self.from_near, 0), (self.from_line, 1)]
        for k in range(2, length):
            order += [(self.from_line, k), (self.from_near, k - 1)]
        order += [(self.from_near, length - 1)] if length > 1 else []
        order += [(self.from_last, k) for k in range(2 * length)]
        return [functools.partial(step, a, k) for step, k in order]

    def run(self, steps):
        for step in steps:
            step()

    def from_sibling(self, a):
        def block_in(block, _):
            if self.shared:

                @pl.when(jnp.logical_not(block == self.at.f))
                def _():
                    self.arrived(a, block, self.SIB_RECV)

            else:
                self.arrived(a, block, self.SIB_RECV)
            return 0

        lax.fori_loop(0, self.n, block_in, 0)
        if self.shared:
            for half in (0, 1):
                self.local(a, half).wait()
        else:
            self.local(a, self.at.c).wait()

    def finish(self, a):
        at, line = self.at, self.line

        def sent(kind, index):
            self.copy(kind, a, index, at.f, at.sibling).wait_send()

        def chip(z):
            sent(self.NEAR, z)
            sent(self.LAST, z)
            sent(self.LAST, line.length + z)

        line.chips(chip)
        line.others(lambda z: sent(self.LINE, z))

        def block_done(block, _):
            if self.shared:
                pl.when(jnp.logical_not(block == at.f))(lambda: sent(self.SIB, block))
            else:
                sent(self.SIB, block)
            return 0

        lax.fori_loop(0, self.n, block_done, 0)


class MiddleGather(Gather):
    RECV, SIB_RECV, ONE, UP, DOWN, LAST, SIB, LOCAL = range(8)

    @staticmethod
    def semaphores(plans):
        return pltpu.SemaphoreType.DMA((8 * len(plans) * plans[0].fsdp,))

    def send(self, kind, a, block, own=False):
        up = kind == self.UP
        target = (self.at.d, self.at.f + (4 if up else -4))

        @pl.when(self.at.z < self.line.length - 1 if up else self.at.z > 0)
        def _():
            self.copy(kind, a, block, block, target, own).start()

    def begin(self, a):
        at = self.at
        self.copy(self.ONE, a, at.f, at.f, at.partner1, True).start()
        self.send(self.UP, a, at.f, True)
        self.send(self.DOWN, a, at.f, True)
        self.copy(self.LAST, a, at.f, at.f, at.partner3, True).start()
        for half in (0, 1):
            self.local(a, half).start()

    def near(self, a):
        block = self.at.f + self.at.flip1
        self.arrived(a, block)
        self.send(self.UP, a, block)
        self.send(self.DOWN, a, block)
        self.copy(self.LAST, a, block, block, self.at.partner3).start()
        self.to_sibling(a, block).start()

    def along(self, a, distance):
        for sign in (1, -1):
            z = self.at.z - sign * distance

            def take(sign=sign):
                for flip in (0, 1):
                    block = self.at.f - 4 * sign * distance + flip * self.at.flip1
                    self.arrived(a, block)
                    self.send(self.UP if sign == 1 else self.DOWN, a, block)
                    self.copy(self.LAST, a, block, block, self.at.partner3).start()
                    self.to_sibling(a, block).start()

            pl.when((z >= 0) & (z < self.line.length))(take)

    def across(self, a, distance):
        for sign in (1,) if distance == 0 else (1, -1):
            z = self.at.z - sign * distance

            def take(sign=sign):
                for flip in (0, 1):
                    block = (
                        self.at.f - 4 * sign * distance + flip * self.at.flip1 + self.at.flip3
                    )
                    self.arrived(a, block)
                    self.to_sibling(a, block).start()

            pl.when((z >= 0) & (z < self.line.length))(take)

    def steps(self, a):
        steps = [functools.partial(self.near, a)]
        for distance in range(1, self.line.length):
            steps += [functools.partial(self.along, a, distance)]
            steps += [functools.partial(self.across, a, distance - 1)]
        return steps + [functools.partial(self.across, a, self.line.length - 1)]

    def finish(self, a):
        at, length = self.at, self.line.length

        def sent(kind, block):
            self.copy(kind, a, block, block, at.sibling).wait_send()

        def block_done(block, _):
            z = block // 4
            pl.when(jnp.logical_not(block == at.f))(lambda: sent(self.SIB, block))

            @pl.when(at.last_bit(block) == at.last)
            def _():
                sent(self.LAST, block)
                pl.when((z <= at.z) & (at.z < length - 1))(lambda: sent(self.UP, block))
                pl.when((z >= at.z) & (at.z > 0))(lambda: sent(self.DOWN, block))

            return 0

        lax.fori_loop(0, self.n, block_done, 0)
        sent(self.ONE, at.f)


STAGES = 4


class Reduce:
    SIB, SIB_RECV, LOAD, NEAR, NEAR_RECV, CROSS, CROSS_RECV, LINE, LINE_RECV, STAGE = range(10)

    def __init__(self, plans, ins, totals, landed, scratch, in_place):
        count = len(plans)
        self.plans, self.ins, self.totals, self.in_place = plans, ins, totals, in_place
        scratch = list(scratch)
        self.held = [None if here else scratch.pop(0) for here in in_place]
        self.staged = [ref is not None for ref in landed]
        self.stage = [scratch.pop(0) if far else None for far in self.staged]
        self.landed = [scratch.pop(0) if ref is None else ref for ref in landed]
        self.close, self.cross, self.lined = (
            scratch[k * count : (k + 1) * count] for k in range(3)
        )
        self.sems = scratch[3 * count]
        self.n = plans[0].fsdp
        self.line = Line(self.n)
        self.at = self.line.at
        self.items = 2 * self.line.length

    @staticmethod
    def scratch(plans, in_place, staged):
        def buffers(size, kept=None):
            return [
                pltpu.VMEM((size,) + plan.block, plan.dtype)
                for a, plan in enumerate(plans)
                if kept is None or kept[a]
            ]

        n = plans[0].fsdp
        return (
            buffers(n, [not here for here in in_place])
            + buffers(STAGES, staged)
            + buffers(n, [not far for far in staged])
            + buffers(n // 2)
            + buffers(n // 4) * 2
            + [pltpu.SemaphoreType.DMA((10 * len(plans) * n,))]
        )

    def sem(self, kind, a, index):
        return self.sems.at[(kind * len(self.plans) + a) * self.n + index]

    def slot(self, z, b1, b3):
        return 4 * z + self.at.stride1 * b1 + self.at.stride3 * b3

    def item(self, t):
        ours = lax.rem(t, 2)
        return self.line.far(t // 2), (1 - self.at.last) + ours * (2 * self.at.last - 1)

    def turn(self, m):
        swapped = jnp.where(lax.rem(m, 2) == 0, m - 1, m + 1)
        return jnp.where((m == 0) | (m == self.items - 1), m, swapped)

    def hold(self, a, block):
        if self.in_place[a]:
            return self.plans[a].pick(self.ins[a], self.at.c, block)
        return self.held[a].at[block]

    def to_sibling(self, a, block):
        return remote(
            self.plans[a].pick(self.ins[a], 1 - self.at.c, block),
            self.landed[a].at[block],
            self.sem(self.SIB, a, block),
            self.sem(self.SIB_RECV, a, block),
            self.at.sibling,
        )

    def load(self, a, block):
        return pltpu.make_async_copy(
            self.plans[a].pick(self.ins[a], self.at.c, block),
            self.held[a].at[block],
            self.sem(self.LOAD, a, block),
        )

    def to_near(self, a, z, b3):
        return remote(
            self.hold(a, self.slot(z, 1 - self.at.first, b3)),
            self.close[a].at[2 * z + b3],
            self.sem(self.NEAR, a, 2 * z + b3),
            self.sem(self.NEAR_RECV, a, 2 * z + b3),
            self.at.partner1,
        )

    def to_cross(self, a, z):
        return remote(
            self.hold(a, self.slot(z, self.at.first, 1 - self.at.last)),
            self.cross[a].at[z],
            self.sem(self.CROSS, a, z),
            self.sem(self.CROSS_RECV, a, z),
            self.at.partner3,
        )

    def to_line(self, a, z):
        return remote(
            self.hold(a, self.slot(z, self.at.first, self.at.last)),
            self.lined[a].at[self.at.z],
            self.sem(self.LINE, a, z),
            self.sem(self.LINE_RECV, a, self.at.z),
            self.line.peer(z),
        )

    def line_arrived(self, a, z):
        here = self.lined[a].at[z]
        remote(
            here, here, self.sem(self.LINE, a, z), self.sem(self.LINE_RECV, a, z), self.line.peer(z)
        ).wait_recv()

    def rows(self, a, body):
        unit = 16

        def step(i, _):
            body(pl.ds(pl.multiple_of(i * unit, unit), unit))
            return 0

        if self.plans[a].block[0] < unit:
            body(slice(None))
        else:
            lax.fori_loop(0, self.plans[a].block[0] // unit, step, 0)

    def add(self, a, block, sources):
        held = self.hold(a, block)

        def body(where):
            total = held[where, :].astype(F32)
            for ref, at in sources:
                total += ref[at, where, :].astype(F32)
            held[where, :] = total.astype(held.dtype)

        self.rows(a, body)

    def begin(self, a):
        for flip in (1, 0):
            b1 = self.at.first + flip * (1 - 2 * self.at.first)

            def start(t, _, b1=b1):
                z, b3 = self.item(t)
                block = self.slot(z, b1, b3)
                self.to_sibling(a, block).start()
                if not self.in_place[a]:
                    self.load(a, block).start()
                return 0

            lax.fori_loop(0, self.items, start, 0)

    def in_order(self, q):
        late = jnp.int32(q >= self.items)
        z, b3 = self.item(jnp.where(q >= self.items, self.turn(q - self.items), q))
        return self.slot(z, (1 - self.at.first) + late * (2 * self.at.first - 1), b3)

    def to_stage(self, a, q):
        k = lax.rem(q, STAGES)
        return pltpu.make_async_copy(
            self.landed[a].at[self.in_order(q)], self.stage[a].at[k], self.sem(self.STAGE, a, k)
        )

    def fetch(self, a, q):
        self.to_sibling(a, self.in_order(q)).wait_recv()
        self.to_stage(a, q).start()

    def ready(self, a, block, q):
        if not self.in_place[a]:
            self.load(a, block).wait()
        if not self.staged[a]:
            self.to_sibling(a, block).wait_recv()
            return self.landed[a], block

        @pl.when(q == 0)
        def _():
            for k in range(STAGES):
                self.fetch(a, jnp.int32(k))

        self.to_stage(a, q).wait()
        return self.stage[a], lax.rem(q, STAGES)

    def used(self, a, q):
        if self.staged[a]:
            pl.when(q + STAGES < 2 * self.items)(lambda: self.fetch(a, q + STAGES))

    def first_leg(self, a, t):
        z, b3 = self.item(t)
        block = self.slot(z, 1 - self.at.first, b3)
        self.add(a, block, [self.ready(a, block, t)])
        self.to_near(a, z, b3).start()
        self.used(a, t)

    def middle_leg(self, a, m):
        t = self.turn(m)
        z, b3 = self.item(t)
        block = self.slot(z, self.at.first, b3)
        sources = [self.ready(a, block, self.items + m), (self.close[a], 2 * z + b3)]
        self.to_near(a, z, b3).wait_recv()

        @pl.when(lax.rem(t, 2) == 0)
        def _():
            self.add(a, block, sources)
            self.to_cross(a, z).start()

        @pl.when(lax.rem(t, 2) == 1)
        def _():
            self.to_cross(a, z).wait_recv()
            self.add(a, block, sources + [(self.cross[a], z)])

            @pl.when(z != self.at.z)
            def _():
                self.to_line(a, z).start()

        self.used(a, self.items + m)

    def legs(self, body, a, begin, end):
        def step(t, _):
            body(a, t)
            return 0

        lax.fori_loop(begin, end, step, 0)

    def last_leg(self, a):
        block = self.slot(self.at.z, self.at.first, self.at.last)

        def body(where):
            self.totals[a][where, :] = self.hold(a, block)[where, :].astype(F32)

        self.rows(a, body)

        def chip(z):
            self.line_arrived(a, z)

            def body(where):
                self.totals[a][where, :] += self.lined[a][z, where, :].astype(F32)

            self.rows(a, body)

        self.line.others(chip)

    def finish(self, a):
        def done(t, _):
            z, b3 = self.item(t)
            for b1 in (self.at.first, 1 - self.at.first):
                self.to_sibling(a, self.slot(z, b1, b3)).wait_send()
            self.to_near(a, z, b3).wait_send()
            return 0

        lax.fori_loop(0, self.items, done, 0)
        self.line.chips(lambda z: self.to_cross(a, z).wait_send())
        self.line.others(lambda z: self.to_line(a, z).wait_send())


def reduce_out(plan):
    return jax.ShapeDtypeStruct(plan.block if plan.by_rows else (2,) + plan.block, F32)


def hot_rows(codes):
    count = codes.shape[0]
    slot = lax.rem(lax.broadcasted_iota(jnp.int32, (count, 1), 0), SLOTS)
    lane = lax.broadcasted_iota(jnp.int32, (count, HOT), 1)
    hit = lane == KMAX * CHARS
    for q in range(KMAX):
        moved = codes if q == 0 else pltpu.roll(codes, count - q, 0)
        moved = jnp.where((moved >= 0) & (slot + q < SLOTS), moved + q * CHARS, -1)
        hit = jnp.logical_or(hit, lane == moved)
    return hit.astype(F32).astype(BF)


def conv_forward_block(filters, codes, lengths, refs, out_ref, where, kept):
    table_ref, kernel_ref, width_ref = refs
    hot_ref, window_ref, slope_ref = kept
    words = lengths.shape[0]
    hot = hot_rows(codes)
    hot_ref[...] = hot
    windows = dot(hot, table_ref[...]).astype(BF)
    window_ref[...] = windows
    chunk = 384
    for at in range(0, kernel_ref.shape[1], chunk):
        columns = slice(at, at + chunk)
        activated = jnp.tanh(dot(windows, kernel_ref[:, columns])).reshape(words, SLOTS, chunk)
        counts = jnp.maximum(lengths - width_ref[:, columns] + 1, 1)
        position = lax.broadcasted_iota(jnp.int32, (words, SLOTS, chunk), 1)
        inside = position < counts[:, None, :]
        weight = jnp.where(inside, jnp.exp(activated), 0.0)
        totals = jnp.sum(weight, axis=1)
        pooled = jnp.log(totals) - jnp.log(counts.astype(F32))
        lane = at + lax.broadcasted_iota(jnp.int32, (words, chunk), 1)
        out_ref[where, columns] = keep_feature(pooled, lane, filters)
        slope = weight * (1.0 / totals)[:, None, :] * (1.0 - activated * activated)
        slope_ref[:, columns] = slope.astype(BF).reshape(words * SLOTS, chunk)


def keep_feature(value, lane, filters):
    value = value.astype(BF).astype(F32)
    return jnp.where(lane < filters, value, jnp.where(lane == filters, 1.0, 0.0))


def conv_backward_block(kept, kernel_ref, grad_ref, where, kernel_grad_ref, hot_grad_ref):
    hot_ref, window_ref, slope_ref = kept
    words = WORD_BLOCK
    windows = window_ref[...]
    chunk = 384
    grad_windows = jnp.zeros(windows.shape, F32)
    for at in range(0, kernel_ref.shape[1], chunk):
        columns = slice(at, at + chunk)
        slope = slope_ref[:, columns].astype(F32).reshape(words, SLOTS, chunk)
        grad = (grad_ref[where, columns][:, None, :] * slope).astype(BF)
        grad = grad.reshape(words * SLOTS, chunk)
        kernel_grad_ref[:, columns] += dot_rows(windows, grad)
        grad_windows += dot_cols(grad, kernel_ref[:, columns])
    hot_grad_ref[...] += dot_rows(hot_ref[...], grad_windows.astype(BF))


WORD_BLOCK = 16


class SmallSum:
    SIB, NEAR, CROSS, LINE, BACK_LINE, BACK_CROSS, BACK_NEAR, BACK_SIB = range(0, 16, 2)

    def __init__(self, conv, mine, out, scratch):
        self.conv, self.mine, self.out = conv, mine, out
        self.by_sibling, self.by_near, self.by_cross, self.by_line, self.sems = scratch
        self.line = Line(conv.fsdp)
        self.at = at = self.line.at
        self.length = self.line.length
        self.near_at = at.first * 2 * self.length
        self.near_other = (1 - at.first) * 2 * self.length
        self.cross_at = self.near_at + at.last * self.length
        self.cross_other = self.near_at + (1 - at.last) * self.length
        self.own = self.cross_at + at.z

    @staticmethod
    def scratch(conv):
        n = conv.fsdp
        sizes = (n, n // 2, n // 4, n // 4)
        return [pltpu.VMEM((size,) + conv.block, F32) for size in sizes] + [
            pltpu.SemaphoreType.DMA((16 * (n // 4),))
        ]

    def sem(self, kind, index=0):
        return self.sems.at[kind * self.length + index]

    def message(self, kind, src, dst, target, send=0, receive=0):
        return remote(src, dst, self.sem(kind, send), self.sem(kind + 1, receive), target)

    def part(self, ref, begin, size):
        return ref.at[self.at.c, pl.ds(begin, size)]

    def sibling(self):
        return self.message(self.SIB, self.mine.at[1 - self.at.c], self.by_sibling, self.at.sibling)

    def near(self):
        size = 2 * self.length
        source = self.part(self.mine, self.near_other, size)
        return self.message(self.NEAR, source, self.by_near, self.at.partner1)

    def cross(self):
        source = self.part(self.mine, self.cross_other, self.length)
        return self.message(self.CROSS, source, self.by_cross, self.at.partner3)

    def lined(self, z, source=None):
        block = self.mine.at[self.at.c, self.cross_at + z]
        target = self.by_line.at[z if source else self.at.z]
        return self.message(
            self.LINE, block, target, self.line.peer(z), z, z if source else self.at.z
        )

    def back_line(self, z, source=None):
        here = self.out.at[self.at.c, self.cross_at + z if source else self.own]
        return self.message(
            self.BACK_LINE, here, here, self.line.peer(z), z, z if source else self.at.z
        )

    def back_cross(self, source=None):
        begin = self.cross_other if source else self.cross_at
        here = self.part(self.out, begin, self.length)
        return self.message(self.BACK_CROSS, here, here, self.at.partner3)

    def back_near(self, source=None):
        here = self.part(self.out, self.near_other if source else self.near_at, 2 * self.length)
        return self.message(self.BACK_NEAR, here, here, self.at.partner1)

    def back_sibling(self, source=None):
        here = self.out.at[1 - self.at.c if source else self.at.c]
        return self.message(self.BACK_SIB, here, here, self.at.sibling)

    def add(self, begin, source):
        size = source.shape[0]
        self.mine[self.at.c, pl.ds(begin, size)] += source[...]

    def steps(self):
        def begin():
            self.sibling().start()

        def to_near():
            self.sibling().wait_recv()
            self.add(0, self.by_sibling)
            self.near().start()

        def to_cross():
            self.near().wait_recv()
            self.add(self.near_at, self.by_near)
            self.cross().start()

        def to_line():
            self.cross().wait_recv()
            self.add(self.cross_at, self.by_cross)
            self.line.others(lambda z: self.lined(z).start())

        def total():
            self.out[self.at.c, self.own] = self.mine[self.at.c, self.own]

            def chip(z):
                self.lined(z, True).wait_recv()
                self.out[self.at.c, self.own] += self.by_line[z]

            self.line.others(chip)
            self.line.others(lambda z: self.back_line(z).start())

        def from_line():
            self.line.others(lambda z: self.back_line(z, True).wait_recv())
            self.back_cross().start()

        def from_cross():
            self.back_cross(True).wait_recv()
            self.back_near().start()

        def from_near():
            self.back_near(True).wait_recv()
            self.back_sibling().start()

        def end():
            self.back_sibling(True).wait_recv()
            for message in (
                self.sibling(),
                self.near(),
                self.cross(),
                self.back_cross(),
                self.back_near(),
                self.back_sibling(),
            ):
                message.wait_send()
            self.line.others(lambda z: self.lined(z).wait_send())
            self.line.others(lambda z: self.back_line(z).wait_send())

        return [begin, to_near, to_cross, to_line, total, from_line, from_cross, from_near, end]


def place_kernel(plans, *refs):
    for plan, shard, out in zip(plans, refs[: len(plans)], refs[len(plans) :]):
        plan.place_blocks(shard, out)


def place_all(plans, shards):
    vmem = pl.BlockSpec(memory_space=pltpu.VMEM)
    placed = pl.pallas_call(
        functools.partial(place_kernel, plans),
        out_shape=[plan.placed_shape() for plan in plans],
        in_specs=[vmem] * len(plans),
        out_specs=[vmem] * len(plans),
        compiler_params=pltpu.CompilerParams(vmem_limit_bytes=48 * 2**20),
    )(*[plan.blocks_of(shard) for plan, shard in zip(plans, shards)])
    return [plan.from_placed(each) for plan, each in zip(plans, placed)]


class Dense:
    by_rows = False
    dtype = F32

    def __init__(self, rows, columns, fsdp):
        self.fsdp = fsdp
        self.filled = rows
        self.block = (up_to(-(-rows // fsdp), 8), columns // 2)
        self.shape = (2, fsdp) + self.block

    def pick(self, ref, half, slot):
        return ref.at[half, slot]

    def fill(self, slots, source):
        slots[...] = jnp.zeros_like(slots)
        depth, half = self.block
        for block in range(self.filled // depth):
            for h in range(2):
                slots[h, block] = source[
                    block * depth : (block + 1) * depth, h * half : (h + 1) * half
                ]


def tail_kernel(plans, conv_ref, grad_ref, conv_out, total_out, conv_in, *scratch):
    conv, highway = plans
    small = SmallSum(conv, conv_in, conv_out, scratch[:5])
    work = Reduce([highway], [grad_ref], [total_out], [None], scratch[5:], [False])
    work.line.greet()
    conv.fill(conv_in, conv_ref)
    work.begin(0)
    work.legs(work.first_leg, 0, 0, work.items)
    for step in small.steps():
        step()
    work.legs(work.middle_leg, 0, 0, work.items)
    work.last_leg(0)
    work.finish(0)


def tail(plans, conv_grad, highway_grad, collective_id):
    conv, highway = plans
    vmem = pl.BlockSpec(memory_space=pltpu.VMEM)
    return pl.pallas_call(
        functools.partial(tail_kernel, plans),
        out_shape=[
            jax.ShapeDtypeStruct(conv.shape, F32),
            jax.ShapeDtypeStruct(highway.block, F32),
        ],
        in_specs=[vmem, pl.BlockSpec(memory_space=pl.ANY)],
        out_specs=[vmem] * 2,
        scratch_shapes=[pltpu.VMEM(conv.shape, F32)]
        + SmallSum.scratch(conv)
        + Reduce.scratch([highway], [False], [False]),
        compiler_params=pltpu.CompilerParams(
            collective_id=collective_id, has_side_effects=True, vmem_limit_bytes=62 * 2**20
        ),
    )(conv_grad, highway_grad)


def gate_parts(sums):
    parts = [sums[:, :HP]]
    for g in range(1, 4):
        begin = g * H // LANE * LANE
        moved = sums[:, begin : begin + HP + LANE]
        parts.append(pltpu.roll(moved, HP + LANE - (g * H - begin), 1)[:, :HP])
    return parts


def join_gates(parts, columns):
    rows = parts[0].shape[0]
    total = None
    for g, part in enumerate(parts):
        begin = g * H // LANE * LANE
        wide = jnp.concatenate([part, jnp.zeros((rows, LANE), F32)], axis=1)
        if g * H - begin:
            wide = pltpu.roll(wide, g * H - begin, 1)
        pieces = [wide]
        if begin:
            pieces = [jnp.zeros((rows, begin), F32)] + pieces
        if columns - begin - HP - LANE > 0:
            pieces = pieces + [jnp.zeros((rows, columns - begin - HP - LANE), F32)]
        placed = jnp.concatenate(pieces, axis=1)[:, :columns]
        total = placed if total is None else total + placed
    return total


HIDDEN_CHUNKS = ((0, 48), (48, 96), (96, 128), (128, 144))


def hidden_chunks(rows):
    return [(a, min(b, rows)) for a, b in HIDDEN_CHUNKS if a < rows] + (
        [(HIDDEN_CHUNKS[-1][1], rows)] if rows > HIDDEN_CHUNKS[-1][1] else []
    )


def lstm_forward_kernel(
    batch, n, x_ref, w_ref, h0_ref, c0_ref, keep_ref, extra_ref, own_ref, *refs
):
    hp_ref, cp_ref, i_ref, f_ref, u_ref, o_ref, t_ref, hall_ref, part_ref = refs[:9]
    hidden, soft_sems, hidden_sems = refs[9:]
    line = Line(n)
    at, length = line.at, line.length
    rows_all = x_ref.shape[0]
    chunks = hidden_chunks(rows_all)
    RECV, TO_LINE, TO_NEAR, TO_LAST, LOCAL = range(5)
    sem = Semaphores(soft_sems, n)
    H_RECV, H_LINE, H_SIB = range(3)
    hsem = Semaphores(hidden_sems, 2 * length * len(chunks))

    def column(z):
        return at.f + 4 * (z - at.z)

    def to_line(z):
        return remote(
            own_ref.at[2 * z + at.c],
            part_ref.at[at.f],
            sem(TO_LINE, z),
            sem(RECV, at.f),
            line.peer(z),
        )

    def pass_on(kind, index, slot, target, own=False):
        return remote(
            own_ref.at[line.me] if own else part_ref.at[slot],
            part_ref.at[slot],
            sem(kind, index),
            sem(RECV, slot),
            target,
        )

    def landed(slot):
        pass_on(TO_NEAR, 0, slot, at.partner1).wait_recv()

    local = pltpu.make_async_copy(own_ref.at[line.me], part_ref.at[at.f], sem(LOCAL, 0))

    def event_begin():
        line.others(lambda z: to_line(z).start())
        pass_on(TO_NEAR, at.z, at.f, at.partner1, True).start()
        pass_on(TO_LAST, at.z, at.f, at.partner3, True).start()
        local.start()

    def event_line():
        def chip(z):
            landed(column(z))
            pass_on(TO_NEAR, z, column(z), at.partner1).start()
            pass_on(TO_LAST, z, column(z), at.partner3).start()

        line.others(chip)

    def event_near():
        def chip(z):
            slot = column(z) + at.flip1
            landed(slot)
            pass_on(TO_LAST, length + z, slot, at.partner3).start()

        line.chips(chip)

    def event_end():
        def chip(z):
            landed(column(z) + at.flip3)
            landed(column(z) + at.flip1 + at.flip3)
            pass_on(TO_NEAR, z, column(z), at.partner1).wait_send()
            pass_on(TO_LAST, z, column(z), at.partner3).wait_send()
            pass_on(TO_LAST, length + z, column(z), at.partner3).wait_send()

        line.chips(chip)
        line.others(lambda z: to_line(z).wait_send())
        local.wait()

    def chunk_copy(k, member, kind, index, target):
        begin, end = chunks[k]
        here = hall_ref.at[member, pl.ds(begin, end - begin), :]
        return remote(
            here,
            here,
            hsem(kind, index * len(chunks) + k),
            hsem(H_RECV, member * len(chunks) + k),
            target,
        )

    def chunk_out(k):
        begin, end = chunks[k]
        hall_ref[line.me, begin:end, :] = hidden[begin:end, :].astype(BF)
        line.others(lambda z: chunk_copy(k, line.me, H_LINE, z, line.peer(z)).start())
        chunk_copy(k, line.me, H_SIB, at.z, at.sibling).start()

    def chunk_pass(k):
        def chip(z):
            member = 2 * z + at.c
            chunk_copy(k, member, H_SIB, z, at.sibling).wait_recv()
            chunk_copy(k, member, H_SIB, z, at.sibling).start()

        line.others(chip)

    def chunk_end(k):
        def chip(z):
            chunk_copy(k, 2 * z + 1 - at.c, H_SIB, z, at.sibling).wait_recv()
            chunk_copy(k, 2 * z + at.c, H_SIB, z, at.sibling).wait_send()

        line.chips(chip)
        line.others(lambda z: chunk_copy(k, line.me, H_LINE, z, line.peer(z)).wait_send())

    line.greet(True, False)
    event_begin()
    per_tile = 8 // batch
    tiles = rows_all // 8
    row = lax.broadcasted_iota(jnp.int32, (8, HP), 0)
    lane = lax.broadcasted_iota(jnp.int32, (8, LANE), 1)
    last = HP - LANE
    used = up_to(H, 16)

    def tile(step, carried):
        h, c = carried
        rows = pl.ds(pl.multiple_of(step * 8, 8), 8)
        x = x_ref[rows, :]
        keep = keep_ref[rows, :]
        saved = None
        for part in range(per_tile):
            hp, cp = h * keep, c * keep
            sums = x + dot(hp[:, :used].astype(BF), w_ref[:used, :])
            i, f, u, o = gate_parts(sums)
            i, f, u, o = jax.nn.sigmoid(i), jax.nn.sigmoid(f), jnp.tanh(u), jax.nn.sigmoid(o)
            c = f * cp + i * u
            t = jnp.tanh(c)
            h = (o * t).astype(BF).astype(F32)
            now = (hp, cp, i, f, u, o, t, h)
            if saved is None:
                saved = now
            else:
                saved = tuple(jnp.where(row >= part * batch, b, a) for a, b in zip(saved, now))
            h, c = pltpu.roll(h, batch, 0), pltpu.roll(c, batch, 0)
        for ref, value in zip((hp_ref, cp_ref, i_ref, f_ref, u_ref, o_ref, t_ref), saved):
            ref[rows, :] = value
        hidden[rows, :last] = saved[-1][:, :last]
        hidden[rows, last:] = jnp.where(lane < H - last, saved[-1][:, last:], extra_ref[rows, :])

        pl.when(step == tiles // 3)(event_line)
        pl.when(step == tiles * 2 // 3)(event_near)
        for k, (_, end) in enumerate(chunks):
            pl.when(step == end // 8 - 1)(functools.partial(chunk_out, k))
            if end // 8 + 4 < tiles:
                pl.when(step == end // 8 + 4)(functools.partial(chunk_pass, k))
        return h, c

    lax.fori_loop(0, tiles, tile, (h0_ref[...], c0_ref[...]))
    for k, (_, end) in enumerate(chunks):
        if end // 8 + 4 >= tiles:
            chunk_pass(k)
    event_end()
    for k in range(len(chunks)):
        chunk_end(k)


def lstm_forward(batch, plan, x, recur, h0, c0, keep, extra, own, collective_id):
    rows, n = x.shape[0], plan.fsdp
    members = plan.parts
    chunks = len(hidden_chunks(rows))
    vmem = pl.BlockSpec(memory_space=pltpu.VMEM)
    anywhere = pl.BlockSpec(memory_space=pl.ANY)
    return pl.pallas_call(
        functools.partial(lstm_forward_kernel, batch, n),
        out_shape=[jax.ShapeDtypeStruct((rows, HP), F32)] * 7
        + [
            jax.ShapeDtypeStruct((members, rows, HP), BF),
            jax.ShapeDtypeStruct((n,) + plan.block, BF),
        ],
        in_specs=[vmem] * 6 + [anywhere],
        out_specs=[vmem] * 8 + [anywhere],
        scratch_shapes=[
            pltpu.VMEM((rows, HP), F32),
            pltpu.SemaphoreType.DMA((5 * n,)),
            pltpu.SemaphoreType.DMA((3 * members * chunks,)),
        ],
        compiler_params=pltpu.CompilerParams(
            collective_id=collective_id, has_side_effects=True, vmem_limit_bytes=62 * 2**20
        ),
    )(x, recur, h0, c0, keep, extra, own)


def lstm_backward_kernel(
    batch,
    n,
    dh_ref,
    w_ref,
    keep_ref,
    cp_ref,
    i_ref,
    f_ref,
    u_ref,
    o_ref,
    t_ref,
    grad_ref,
    dz_ref,
    out_ref,
    held_near,
    held_line,
    from_last,
    from_near,
    sems,
):
    line = Line(n)
    at, length = line.at, line.length
    LAST, LAST_RECV, NEAR, NEAR_RECV, TO_LINE, LINE_RECV, SIB, SIB_RECV = range(8)
    sem = Semaphores(sems, 2 * length)

    def slot(z, b1, b3):
        return 4 * z + at.stride1 * b1 + at.stride3 * b3

    def to_last(z, b1):
        return remote(
            grad_ref.at[slot(z, b1, 1 - at.last)],
            from_last.at[2 * z + b1],
            sem(LAST, 2 * z + b1),
            sem(LAST_RECV, 2 * z + b1),
            at.partner3,
        )

    def to_near(z):
        return remote(
            held_near.at[z], from_near.at[z], sem(NEAR, z), sem(NEAR_RECV, z), at.partner1
        )

    def to_line(z):
        return remote(
            held_line.at[z], out_ref.at[line.me], sem(TO_LINE, z), sem(LINE_RECV, at.z), line.peer(z)
        )

    def line_arrived(z):
        here = out_ref.at[2 * z + at.c]
        remote(here, here, sem(TO_LINE, z), sem(LINE_RECV, z), line.peer(z)).wait_recv()

    def to_sibling(z, other=False):
        here = out_ref.at[2 * z + (1 - at.c if other else at.c)]
        return remote(here, here, sem(SIB, z), sem(SIB_RECV, z), at.sibling)

    def event_begin():
        def chip(z):
            to_last(z, 1 - at.first).start()

        line.chips(chip)

        def chip_own(z):
            to_last(z, at.first).start()

        line.chips(chip_own)

    def event_last():
        def chip(z):
            b1 = 1 - at.first
            to_last(z, b1).wait_recv()
            held_near[z] = (
                grad_ref[slot(z, b1, at.last)].astype(F32) + from_last[2 * z + b1].astype(F32)
            ).astype(BF)
            to_near(z).start()

        line.chips(chip)

    def event_near():
        def chip(z):
            to_last(z, at.first).wait_recv()
            to_near(z).wait_recv()
            total = (
                grad_ref[slot(z, at.first, at.last)].astype(F32)
                + from_last[2 * z + at.first].astype(F32)
                + from_near[z].astype(F32)
            ).astype(BF)
            held_line[z] = total

            @pl.when(z == at.z)
            def _():
                out_ref[line.me] = total

            @pl.when(z != at.z)
            def _():
                to_line(z).start()

        line.chips(chip)
        to_sibling(at.z).start()

    def event_line():
        def chip(z):
            line_arrived(z)
            to_sibling(z).start()

        line.others(chip)

    def event_end():
        def chip(z):
            to_sibling(z, True).wait_recv()
            to_sibling(z).wait_send()
            to_near(z).wait_send()
            to_last(z, 0).wait_send()
            to_last(z, 1).wait_send()

        line.chips(chip)
        line.others(lambda z: to_line(z).wait_send())

    line.greet(True, False)
    event_begin()
    per_tile = 8 // batch
    tiles = dh_ref.shape[0] // 8
    row = lax.broadcasted_iota(jnp.int32, (8, dz_ref.shape[1]), 0)
    real = lax.broadcasted_iota(jnp.int32, (8, HP), 1) < H
    used = up_to(4 * H, 16)

    def tile(step, carried):
        dh_carry, dc_carry = carried
        rows = pl.ds(pl.multiple_of((tiles - 1 - step) * 8, 8), 8)
        keep = keep_ref[rows, :]
        i, f, u, o, t = (r[rows, :] for r in (i_ref, f_ref, u_ref, o_ref, t_ref))
        soft = dh_ref[rows, :]
        to_c = o * (1.0 - t * t)
        to_i = jnp.where(real, u * i * (1.0 - i), 0.0)
        to_f = jnp.where(real, cp_ref[rows, :] * f * (1.0 - f), 0.0)
        to_u = jnp.where(real, i * (1.0 - u * u), 0.0)
        to_o = jnp.where(real, t * o * (1.0 - o), 0.0)
        back = f * keep
        saved = None
        for part in reversed(range(per_tile)):
            dh = jnp.where(real, soft + dh_carry, 0.0)
            dc = dc_carry + dh * to_c
            dz = join_gates([dc * to_i, dc * to_f, dc * to_u, dh * to_o], dz_ref.shape[1])
            saved = dz if saved is None else jnp.where(row >= (part + 1) * batch, saved, dz)
            dh_carry = dot(dz[:, :used].astype(BF), w_ref[:used, :]) * keep
            dc_carry = dc * back
            dh_carry, dc_carry = (
                pltpu.roll(dh_carry, 8 - batch, 0),
                pltpu.roll(dc_carry, 8 - batch, 0),
            )
        dz_ref[rows, :] = saved
        pl.when(step == tiles // 3)(event_last)
        pl.when(step == tiles * 2 // 3)(event_near)
        pl.when(step == tiles - 2)(event_line)
        return dh_carry, dc_carry

    zero = jnp.zeros((8, HP), F32)
    lax.fori_loop(0, tiles, tile, (zero, zero))
    event_end()


def lstm_backward(batch, plan, columns, dh, recur_t, keep, states, grad, collective_id):
    rows, n = dh.shape[0], plan.fsdp
    length = n // 4
    vmem = pl.BlockSpec(memory_space=pltpu.VMEM)
    return pl.pallas_call(
        functools.partial(lstm_backward_kernel, batch, n),
        out_shape=[
            jax.ShapeDtypeStruct((rows, columns), F32),
            jax.ShapeDtypeStruct((plan.parts,) + plan.block, BF),
        ],
        in_specs=[vmem] * 10,
        out_specs=[vmem] * 2,
        scratch_shapes=[
            pltpu.VMEM((length,) + plan.block, BF),
            pltpu.VMEM((length,) + plan.block, BF),
            pltpu.VMEM((2 * length,) + plan.block, BF),
            pltpu.VMEM((length,) + plan.block, BF),
            pltpu.SemaphoreType.DMA((8 * 2 * length,)),
        ],
        compiler_params=pltpu.CompilerParams(
            collective_id=collective_id, has_side_effects=True, vmem_limit_bytes=62 * 2**20
        ),
    )(dh, recur_t, keep, *states, grad)


def turned(value, lanes):
    rows = value.shape[0]
    if rows < lanes:
        value = jnp.concatenate([value, jnp.zeros((lanes - rows, value.shape[1]), F32)], axis=0)
    return value.T


def copy_windows(plan, source, target, base, found, place):
    target[...] = jnp.zeros_like(target)
    for o, first, last in found:
        start, to = plan.starts[o] - base, place(o) * plan.rows
        target[to + first : to + last, :] = source[start + first : start + last, :]


def add_windows(plan, source, target, base, found, begin):
    for o, first, last in found:
        start, at = plan.starts[o] - base, o * plan.rows - begin
        target[start + first : start + last, :] += source[at + first : at + last, :]


def matrices_of(plan, filters):
    result = []
    for m in range(4):
        base = m * (filters + 1)
        found = plan.meeting(base, base + filters + 1)
        result.append((base, found, found[0][0] * plan.rows, (found[-1][0] + 1) * plan.rows))
    return result


def head_kernel(plans, soft, filters, blocks, *refs):
    highway, lstm = plans
    owns = refs[:2]
    codes_ref, length_ref, table_ref, kernel_ref, width_ref, soft_ref = refs[2:8]
    highway_out, lstm_out, x_ref, recur_ref, soft_out = refs[8:13]
    kept_outs, wide_out = refs[13:16], refs[16]
    features, trans_refs, gate_refs = refs[17:20], refs[20:22], refs[22:24]
    highway_w, lstm_w, turned_ref, wide, recur_sum = refs[24:29]
    kept_stages, wide_stage, highway_sems, lstm_sems, out_sems, keep_sems = refs[29:32], *refs[32:]
    rows, fp = features[0].shape
    words = turned_ref.shape[1]
    gather_h = MiddleGather([highway], owns[:1], [highway_w], highway_sems, True)
    gather_l = Gather([lstm], owns[1:], [lstm_w], lstm_sems, True)
    gather_h.line.greet()

    def conv(begin, end):
        def block(i, _):
            at = pl.ds(pl.multiple_of(i * WORD_BLOCK, WORD_BLOCK), WORD_BLOCK)
            slots = pl.ds(
                pl.multiple_of(i * WORD_BLOCK * SLOTS, WORD_BLOCK * SLOTS), WORD_BLOCK * SLOTS
            )
            pl.when(i >= 2)(lambda: wait_kept(i - 2))
            k = lax.rem(i, 2)
            conv_forward_block(
                filters,
                codes_ref[slots, :],
                length_ref[at, :],
                (table_ref, kernel_ref, width_ref),
                features[0],
                at,
                [stage.at[k] for stage in kept_stages],
            )
            for copy in keep_copies(i):
                copy.start()
            return 0

        lax.fori_loop(begin, end, block, 0)

    def keep_copies(i):
        k = lax.rem(i, 2)
        size = WORD_BLOCK * SLOTS
        to = pl.ds(pl.multiple_of(i * size, size), size)
        return [
            pltpu.make_async_copy(stage.at[k], out.at[to], keep_sems.at[2 * j + k])
            for j, (stage, out) in enumerate(zip(kept_stages, kept_outs))
        ]

    def wait_kept(i):
        for copy in keep_copies(i):
            copy.wait()

    def wide_copy(m):
        return pltpu.make_async_copy(wide_stage.at[m % 2], wide_out.at[m], keep_sems.at[6 + m % 2])

    chunk = 384

    def layer_sum(m, wide=wide):
        base, found, begin, end = matrices[m]
        copy_windows(
            highway, turned_ref, wide.at[: end - begin], base, found, lambda o: o - found[0][0]
        )
        target = (trans_refs if m % 2 == 0 else gate_refs)[m // 2]
        if m >= 2:
            wide_copy(m - 2).wait()
        wide_stage[m % 2, : end - begin, :] = wide[: end - begin, :].astype(BF)
        wide_copy(m).start()

        def columns(j, _):
            where = pl.ds(pl.multiple_of(j * chunk, chunk), chunk)
            left = wide[: end - begin, :].astype(BF)
            target[:, where] = dot_rows(left, highway_w[begin:end, where])[:rows]
            return 0

        lax.fori_loop(0, fp // chunk, columns, 0)

    def layer(l):
        turned_ref[:fp, :] = turned(features[l][...], words)
        layer_sum(2 * l)

    def layer_end(l):
        layer_sum(2 * l + 1)
        trans, gate = trans_refs[l][...], jax.nn.sigmoid(gate_refs[l][...])
        gate_refs[l][...] = gate
        value = gate * trans * jax.nn.sigmoid(trans) + (1.0 - gate) * features[l][...]
        lane = lax.broadcasted_iota(jnp.int32, (rows, fp), 1)
        features[l + 1][...] = keep_feature(value, lane, filters)

    matrices = matrices_of(highway, filters)
    gather_h.begin(0)
    of_highway, of_lstm = gather_h.steps(0), gather_l.steps(0)
    passing = len(of_lstm) - 2 * gather_l.line.length
    third = -(-blocks // 3)
    conv(0, third)
    gather_h.run(of_highway[:1])
    conv(third, 2 * third)
    gather_h.run(of_highway[1:3])
    gather_l.begin(0)
    conv(2 * third, blocks)
    soft.place_blocks(soft_ref, soft_out)
    gather_h.run(of_highway[3:5])
    gather_l.run(of_lstm[: passing // 2])
    gather_h.run(of_highway[5:-1])
    gather_l.run(of_lstm[passing // 2 : passing - 1])
    gather_h.run(of_highway[-1:])
    gather_h.from_sibling(0)
    out_copies = [
        pltpu.make_async_copy(highway_w, highway_out, out_sems.at[0]),
        pltpu.make_async_copy(lstm_w, lstm_out, out_sems.at[1]),
    ]
    out_copies[0].start()
    layer(0)
    layer_end(0)
    gather_l.run(of_lstm[passing - 1 : passing])
    layer(1)
    layer_end(1)

    turned_ref[...] = jnp.zeros_like(turned_ref)
    sub = lax.broadcasted_iota(jnp.int32, (fp, words), 0)
    turned_ref[:fp, :] = jnp.where(sub < filters, turned(features[2][...], words), 0.0)
    turned_ref[lstm.used - 1 : lstm.used, :] = jnp.ones((1, words), F32)
    wide = wide.at[: lstm.total]
    copy_windows(lstm, turned_ref, wide, 0, lstm.meeting(0, lstm.used), lambda o: o)
    gather_l.run(of_lstm[passing:])
    gather_l.from_sibling(0)
    out_copies[1].start()
    left = wide[...].astype(BF)
    half = lstm.block[1]
    for h in range(2):
        x_ref[:, h * half : (h + 1) * half] = dot_rows(left, lstm_w[h])[:rows]

    recur_sum[...] = jnp.zeros_like(recur_sum)
    depth = lstm.block[0]
    for h in range(2):
        for slot in sorted({o // lstm.dp for o, _, _ in lstm.meeting(filters, filters + H)}):
            piece = lstm_w[h, slot * depth : (slot + 1) * depth, :].astype(F32)
            for o, first, last in lstm.meeting(filters, filters + H):
                if o // lstm.dp == slot:
                    start, at = lstm.starts[o] - filters, (o % lstm.dp) * lstm.rows
                    recur_sum[start + first : start + last, h * half : (h + 1) * half] += piece[
                        at + first : at + last
                    ]
    recur_ref[...] = recur_sum[...].astype(BF)
    gather_h.finish(0)
    gather_l.finish(0)
    for copy in out_copies:
        copy.wait()
    for m in (2, 3):
        wide_copy(m).wait()
    for i in range(max(blocks - 2, 0), blocks):
        wait_kept(i)


def head(plans, soft, filters, own, conv_inputs, soft_flat, rows, fp, collective_id):
    highway, lstm = plans
    words = up_to(rows, 2 * LANE)
    vmem = pl.BlockSpec(memory_space=pltpu.VMEM)
    anywhere = pl.BlockSpec(memory_space=pl.ANY)
    feature = jax.ShapeDtypeStruct((rows, fp), F32)
    matrices = matrices_of(highway, filters)
    longest_matrix = max(end - begin for _, _, begin, end in matrices)
    longest = max(lstm.total, longest_matrix)
    kept_widths = (HOT, LANE, fp)
    return pl.pallas_call(
        functools.partial(head_kernel, plans, soft, filters, rows // WORD_BLOCK),
        out_shape=[
            jax.ShapeDtypeStruct(highway.shape, BF),
            jax.ShapeDtypeStruct(lstm.shape, BF),
            jax.ShapeDtypeStruct((rows, lstm.columns), F32),
            jax.ShapeDtypeStruct((HP, lstm.columns), BF),
            soft.placed_shape(),
        ]
        + [jax.ShapeDtypeStruct((rows * SLOTS, width), BF) for width in kept_widths]
        + [jax.ShapeDtypeStruct((4, longest_matrix, words), BF)]
        + [feature] * 7,
        in_specs=[anywhere] * 2 + [vmem] * 6,
        out_specs=[anywhere] * 2 + [vmem] * 3 + [anywhere] * 4 + [vmem] * 7,
        scratch_shapes=[
            pltpu.VMEM(highway.shape, BF),
            pltpu.VMEM(lstm.shape, BF),
            pltpu.VMEM((up_to(max(lstm.used, fp), LANE), words), F32),
            pltpu.VMEM((longest, words), F32),
            pltpu.VMEM((HP, lstm.columns), F32),
        ]
        + [pltpu.VMEM((2, WORD_BLOCK * SLOTS, width), BF) for width in kept_widths]
        + [
            pltpu.VMEM((2, longest_matrix, words), BF),
            MiddleGather.semaphores([highway]),
            Gather.semaphores([lstm]),
            pltpu.SemaphoreType.DMA((2,)),
            pltpu.SemaphoreType.DMA((8,)),
        ],
        compiler_params=pltpu.CompilerParams(
            collective_id=collective_id, has_side_effects=True, vmem_limit_bytes=62 * 2**20
        ),
    )(*own, *conv_inputs, soft.blocks_of(soft_flat))


def highway_backward_kernel(plans, conv, filters, blocks, *refs):
    highway, lstm = plans
    dz_ref, hp_ref = refs[:2]
    features, trans_refs, gate_refs = refs[2:5], refs[5:7], refs[7:9]
    kernel_ref, mask_ref, fold_ref = refs[9:12]
    highway_all, lstm_all, kept_all, wide_all = refs[12], refs[13], refs[14:17], refs[17]
    lstm_landed, grad_out, kernel_grad, total_out = refs[18:22]
    refs = refs[22:]
    if conv:
        highway_landed, highway_total, conv_out = refs[:3]
        conv_in, refs = refs[3], refs[4:]
        small = SmallSum(conv, conv_in, conv_out, refs[:5])
        refs = refs[5:]
    lstm_grad, highway_w, lstm_w, turned_ref, wide, back, dz, pairs = refs[:8]
    carry, feature_grad, hot_grad, load_sems, pair_sems, out_sems = refs[8:14]
    kept, wide_low, kept_sems, refs = refs[14:17], refs[17], refs[18], refs[19:]
    rows, fp = features[0].shape
    words = turned_ref.shape[1]
    at = Place()
    total = total_out.at[at.c]
    if conv:
        work = Reduce(
            [lstm, highway],
            [lstm_grad, grad_out],
            [total, highway_total],
            [lstm_landed, highway_landed],
            refs,
            [True, False],
        )
    else:
        work = Reduce([lstm], [lstm_grad], [total], [lstm_landed], refs, [True])
    length, items = work.line.length, work.items
    matrices = matrices_of(highway, filters)
    half = lstm.block[1]
    of_input = lstm.meeting(0, filters)
    input_rows = lstm_w.shape[0]

    def layer_rows(l):
        begin, end = matrices[2 * l][2], matrices[2 * l + 1][3]
        return begin, end

    def load_layer(l):
        begin, end = layer_rows(l)
        return pltpu.make_async_copy(
            highway_all.at[pl.ds(begin, end - begin)],
            highway_w.at[pl.ds(0, end - begin)],
            load_sems.at[l],
        )

    def load_lstm(h):
        return pltpu.make_async_copy(
            lstm_all.at[h, pl.ds(0, input_rows)], lstm_w, load_sems.at[2 + h]
        )

    def load_kept(i):
        k = lax.rem(i, 2)
        size = WORD_BLOCK * SLOTS
        at = pl.ds(pl.multiple_of(i * size, size), size)
        return [
            pltpu.make_async_copy(source.at[at], to.at[k], kept_sems.at[2 * j + k])
            for j, (source, to) in enumerate(zip(kept_all, kept))
        ]

    def load_wide(m):
        return pltpu.make_async_copy(wide_all.at[m], wide_low.at[m % 2], kept_sems.at[6 + m % 2])

    load_layer(1).start()
    load_lstm(0).start()
    for i in range(min(2, blocks)):
        for copy in load_kept(jnp.int32(i)):
            copy.start()
    for m in range(2):
        load_wide(m).start()
    work.line.greet()

    dz[...] = jnp.zeros_like(dz)
    dz[:rows, :] = dz_ref[...].astype(BF)
    lane = lax.broadcasted_iota(jnp.int32, (rows, HP), 1)
    hidden = jnp.where(lane < H, hp_ref[...], jnp.where(lane == H, 1.0, 0.0))
    sub = lax.broadcasted_iota(jnp.int32, (fp, words), 0)
    turned_ref[:fp, :] = jnp.where(sub < filters, turned(features[2][...], words), 0.0)
    depth = up_to(H + 1, 8)
    turned_ref[filters : filters + depth, :] = turned(hidden, words)[:depth]
    copy_windows(
        lstm,
        turned_ref,
        wide.at[: lstm.total],
        0,
        lstm.meeting(0, lstm.used),
        lambda o: lstm.position[o],
    )
    unit = lstm.total // (2 * length)

    def lstm_weights(i, _):
        where = pl.ds(pl.multiple_of(i * unit, unit), unit)
        left = wide[where, :].astype(BF)
        for h in range(2):
            lstm_grad[h, where, :] = dot(left, dz[:, h * half : (h + 1) * half]).astype(BF)
        return 0

    lax.fori_loop(0, 2 * length, lstm_weights, 0)
    work.begin(0)

    lane = lax.broadcasted_iota(jnp.int32, (rows, fp), 1)
    back[...] = jnp.zeros_like(back)
    for h in range(2):
        load_lstm(h).wait()
        wide[:input_rows, :] = dot_cols(lstm_w[...], dz[:, h * half : (h + 1) * half])
        if h == 0:
            load_lstm(1).start()
        add_windows(lstm, wide, back, 0, of_input, 0)
    grad = jnp.where(lane < filters, back[...].T[:rows], 0.0)

    def lead(k):
        work.legs(work.first_leg, 0, k * items // 4, (k + 1) * items // 4)

    lead(0)
    pairs[...] = jnp.zeros_like(pairs)
    for l in (1, 0):
        trans, gate = trans_refs[l][...], gate_refs[l][...]
        sig = jax.nn.sigmoid(trans)
        pairs[2 * l, :rows, :] = (grad * gate * sig * (1.0 + trans * (1.0 - sig))).astype(BF)
        pairs[2 * l + 1, :rows, :] = (
            grad * (trans * sig - features[l][...]) * gate * (1.0 - gate)
        ).astype(BF)
        load_layer(l).wait()
        back[...] = jnp.zeros_like(back)
        begin = layer_rows(l)[0]
        for m in (2 * l, 2 * l + 1):
            base, found, low, high = matrices[m]
            result = dot_cols(highway_w[low - begin : high - begin, :], pairs[m])
            add_windows(highway, result, back, base, found, low)
            if m % 2 and l:
                load_layer(0).start()
            if m > 0:
                lead(4 - m)
        grad = grad * (1.0 - gate) + back[...].T[:rows]
        grad = jnp.where(lane < filters, grad, 0.0)
    feature_grad[...] = grad

    kernel_grad[...] = jnp.zeros_like(kernel_grad)
    hot_grad[...] = jnp.zeros_like(hot_grad)

    def conv_block(i, _):
        where = pl.ds(pl.multiple_of(i * WORD_BLOCK, WORD_BLOCK), WORD_BLOCK)
        for copy in load_kept(i):
            copy.wait()
        k = lax.rem(i, 2)
        conv_backward_block(
            [ref.at[k] for ref in kept], kernel_ref, feature_grad, where, kernel_grad, hot_grad
        )

        @pl.when(i + 2 < blocks)
        def _():
            for copy in load_kept(i + 2):
                copy.start()


        @pl.when(i >= blocks - 4)
        def _():
            k = i - (blocks - 4)
            work.legs(work.middle_leg, 0, k * length // 4, (k + 1) * length // 4)

        return 0

    lax.fori_loop(0, blocks, conv_block, 0)
    kernel_grad[:, fp:] = jnp.dot(
        fold_ref[...],
        hot_grad[...] * mask_ref[...],
        precision=lax.Precision.HIGHEST,
        preferred_element_type=F32,
    )
    steps = []
    if conv:
        conv.fill(conv_in, kernel_grad)
        steps = small.steps()
        steps[0]()

    staged = highway_w
    chunk = 384
    size = highway.rows
    pending, shared = [], None
    empty = [o for o in range(len(highway.starts)) if all(o != f[0] for m in matrices for f in m[1])]
    for m in range(4):
        base, found, low, high = matrices[m]
        load_wide(m).wait()
        for copy in pending:
            copy.wait()
        adds = shared == found[0][0]
        shares = m < 3 and matrices[m + 1][1][0][0] == found[-1][0]
        count = len(found)

        def columns(j, _):
            where = pl.ds(pl.multiple_of(j * chunk, chunk), chunk)
            result = dot(wide_low[m % 2, : high - low, :], pairs[m, :, where])
            if adds:
                first = result[:size] + carry[:, where]
                staged[:size, where] = first.astype(BF)
                staged[size : high - low, where] = result[size:].astype(BF)
            else:
                staged[: high - low, where] = result.astype(BF)
            if shares:
                carry[:, where] = result[(count - 1) * size :]
            return 0

        lax.fori_loop(0, fp // chunk, columns, 0)
        if m < 2:
            load_wide(m + 2).start()
        shared = found[-1][0] if shares else None
        sent = found[:-1] if shares else found
        pending = [
            pltpu.make_async_copy(
                staged.at[pl.ds(k * size, size)],
                grad_out.at[pl.ds(highway.position[o] * size, size)],
                out_sems.at[k],
            )
            for k, (o, _, _) in enumerate(sent)
        ]
        for copy in pending:
            copy.start()
        if conv and m == 2:
            steps[1]()
        work.legs(
            work.middle_leg, 0, length + m * length // 4, length + (m + 1) * length // 4
        )
    for copy in pending:
        copy.wait()
    if empty:
        staged[:size, :] = jnp.zeros((size, fp), BF)
        for o in empty:
            copy = pltpu.make_async_copy(
                staged.at[pl.ds(0, size)],
                grad_out.at[pl.ds(highway.position[o] * size, size)],
                out_sems.at[0],
            )
            copy.start()
            copy.wait()
    copy = remote(total, total, pair_sems.at[0], pair_sems.at[1], at.sibling)
    if not conv:
        work.last_leg(0)
        copy.start()
    else:
        work.begin(1)
        work.legs(work.first_leg, 1, 0, length)
        steps[2]()
        work.legs(work.first_leg, 1, length, items)
        late = steps[3:-1]
        for k, step in enumerate(late):
            work.legs(
                work.middle_leg, 1, k * items // len(late), (k + 1) * items // len(late)
            )
            step()
            if k == 1:
                work.last_leg(0)
                copy.start()
        work.last_leg(1)
        steps[-1]()
    for a in range(2 if conv else 1):
        work.finish(a)
    copy.wait()


def conv_columns(fp):
    return up_to(fp + LANE, 2 * LANE)


def highway_backward(
    plans, conv, filters, dz, hp, features, trans, gates, conv_inputs, everywhere, collective_id
):
    highway, lstm = plans
    rows, fp = features[0].shape
    words = up_to(rows, 2 * LANE)
    vmem = pl.BlockSpec(memory_space=pltpu.VMEM)
    anywhere = pl.BlockSpec(memory_space=pl.ANY)
    matrices = matrices_of(highway, filters)
    longest = max([lstm.total] + [end - begin for _, _, begin, end in matrices])
    layer = max(matrices[2 * l + 1][3] - matrices[2 * l][2] for l in range(2))
    input_rows = up_to((lstm.meeting(0, filters)[-1][0] + 1) * lstm.rows, 16)
    return pl.pallas_call(
        functools.partial(highway_backward_kernel, plans, conv, filters, rows // WORD_BLOCK),
        out_shape=[
            jax.ShapeDtypeStruct((lstm.fsdp,) + lstm.block, BF),
            jax.ShapeDtypeStruct(highway.shape, BF),
            jax.ShapeDtypeStruct((LANE, conv_columns(fp)), F32),
            jax.ShapeDtypeStruct((2,) + lstm.block, F32),
        ]
        + (
            [
                jax.ShapeDtypeStruct((highway.fsdp,) + highway.block, BF),
                jax.ShapeDtypeStruct(highway.block, F32),
                jax.ShapeDtypeStruct(conv.shape, F32),
            ]
            if conv
            else []
        ),
        in_specs=[vmem] * 12 + [anywhere] * 6,
        out_specs=[anywhere] * 2 + [vmem] * 2 + ([anywhere, vmem, vmem] if conv else []),
        scratch_shapes=(
            [pltpu.VMEM(conv.shape, F32)] + SmallSum.scratch(conv) if conv else []
        )
        + [
            pltpu.VMEM(lstm.shape, BF),
            pltpu.VMEM((layer, highway.columns), BF),
            pltpu.VMEM((input_rows, lstm.block[1]), BF),
            pltpu.VMEM((up_to(max(lstm.used + 8, fp), LANE), words), F32),
            pltpu.VMEM((longest, words), F32),
            pltpu.VMEM((fp, words), F32),
            pltpu.VMEM((words, lstm.columns), BF),
            pltpu.VMEM((4, words, fp), BF),
            pltpu.VMEM((highway.rows, fp), F32),
            pltpu.VMEM((rows, fp), F32),
            pltpu.VMEM((HOT, LANE), F32),
            pltpu.SemaphoreType.DMA((4,)),
            pltpu.SemaphoreType.DMA((2,)),
            pltpu.SemaphoreType.DMA((max(len(found) for _, found, _, _ in matrices),)),
        ]
        + [pltpu.VMEM((2, WORD_BLOCK * SLOTS, width), BF) for width in (HOT, LANE, fp)]
        + [pltpu.VMEM((2,) + everywhere[-1].shape[1:], BF), pltpu.SemaphoreType.DMA((8,))]
        + (
            Reduce.scratch([lstm, highway], [True, False], [True, True])
            if conv
            else Reduce.scratch([lstm], [True], [True])
        ),
        compiler_params=pltpu.CompilerParams(
            collective_id=collective_id, has_side_effects=True, vmem_limit_bytes=255 * 2**18
        ),
    )(dz, hp, *features, *trans, *gates, *conv_inputs, *everywhere)


def softmax_kernel(
    vocab,
    n,
    h_ref,
    w_ref,
    map_ref,
    map_back_ref,
    recur_ref,
    loss_ref,
    grad_h_ref,
    grad_w_ref,
    turned_out,
    turn_in,
    turn_out,
    turn_sems,
    spread_back,
    logits,
    grads,
    stats,
    for_sibling,
    from_sibling,
    for_line,
    from_line,
    own_total,
    sems,
):
    line = Line(n)
    at, length, me = line.at, line.length, line.me
    members, rows, _ = h_ref.shape
    width = w_ref.shape[-1]
    w = w_ref[...].reshape(-1, width)
    STAT, STAT_RECV, SIB, SIB_RECV, TO_LINE, LINE_RECV = range(6)
    sem = Semaphores(sems, members)
    column = me * width + lax.broadcasted_iota(jnp.int32, (rows, width), 1)
    real_column = column.astype(F32)
    words = up_to(rows, LANE)
    lane = lax.broadcasted_iota(jnp.int32, (rows, LANE), 1)
    aside = HP - LANE

    def pieces(b):
        tail = h_ref[b, :, aside:].astype(F32)
        first = H + 1 - aside
        target = tail[:, first : first + 1] * 256.0 + tail[:, first + 1 : first + 2]
        scale = (
            tail[:, first + 2 : first + 3]
            + tail[:, first + 3 : first + 4]
            + tail[:, first + 4 : first + 5]
        )
        return target, scale

    piece = turn_in.shape[2]
    pieces_of = recur_ref.shape[1] // piece

    def turn_load(j):
        return pltpu.make_async_copy(
            recur_ref.at[:, pl.ds(j * piece, piece)], turn_in.at[j % 2], turn_sems.at[j % 2]
        )

    def turn_store(j):
        return pltpu.make_async_copy(
            turn_out.at[j % 2], turned_out.at[pl.ds(j * piece, piece)], turn_sems.at[2 + j % 2]
        )

    turn_load(0).start()
    line.greet(False, True)

    def forward(b, _):
        h = h_ref[b]
        wide = dot(h, map_ref[...]).astype(BF)
        spread_back[b] = dot(h, map_back_ref[...]).astype(BF)
        now = jnp.where(column < vocab, dot(wide, w), -1e30)
        logits[b] = now
        target, _ = pieces(b)
        top = jnp.max(now, axis=1, keepdims=True)
        log_sum = top + jnp.log(jnp.sum(jnp.exp(now - top), axis=1, keepdims=True))
        picked = jnp.sum(jnp.where(real_column == target, now, 0.0), axis=1, keepdims=True)
        both = jnp.where(lane == 0, log_sum, jnp.where(lane == 1, picked, 0.0))
        both = jnp.concatenate([both, jnp.zeros((words - rows, LANE), F32)], axis=0).T
        stats[me, 0, pl.ds(b, 1), :] = both[0:1, :]
        stats[me, 1, pl.ds(b, 1), :] = both[1:2, :]
        return 0

    lax.fori_loop(0, members, forward, 0)

    def stat(member, target):
        here = stats.at[member]
        return remote(here, here, sem(STAT, member), sem(STAT_RECV, member), target)

    def stat_out(z):
        return [
            remote(
                stats.at[me], stats.at[me], sem(STAT, 2 * z + core), sem(STAT_RECV, me), target
            )
            for core, target in ((at.c, line.peer(z)), (1 - at.c, line.peer(z, True)))
        ]

    def send_stats(z):
        for copy in stat_out(z):
            copy.start()

    line.others(send_stats)
    to_pair = remote(
        stats.at[me], stats.at[me], sem(STAT, 2 * at.z + 1 - at.c), sem(STAT_RECV, me), at.sibling
    )
    to_pair.start()

    def stats_in(z):
        for core in (at.c, 1 - at.c):
            stat(2 * z + core, at.sibling).wait_recv()

    line.others(stats_in)
    stat(2 * at.z + 1 - at.c, at.sibling).wait_recv()
    top = stats[0, 0]
    for q in range(1, members):
        top = jnp.maximum(top, stats[q, 0])
    total = jnp.zeros_like(top)
    picked = jnp.zeros_like(top)
    for q in range(members):
        total += jnp.exp(stats[q, 0] - top)
        picked += stats[q, 1]
    log_total = top + jnp.log(total)
    loss_ref[...] = log_total - picked
    log_columns = jnp.concatenate(
        [log_total, jnp.zeros((LANE - members, words), F32)], axis=0
    ).T[:rows]

    def to_sibling(z):
        return remote(
            for_sibling.at[z], from_sibling.at[z], sem(SIB, z), sem(SIB_RECV, z), at.sibling
        )

    def to_line(z):
        return remote(
            for_line.at[z], from_line.at[at.z], sem(TO_LINE, z), sem(LINE_RECV, at.z), line.peer(z)
        )

    def backward(k, _):
        z = line.far(lax.rem(k, length))
        mine = k >= length
        b = 2 * z + jnp.where(mine, at.c, 1 - at.c)
        target, scale = pieces(b)
        log_sum = jnp.sum(jnp.where(lane == b, log_columns, 0.0), axis=1, keepdims=True)
        share = jnp.exp(logits[b] - log_sum)
        grad = ((share - (real_column == target).astype(F32)) * scale).astype(BF)
        grads[b] = grad
        back = dot_cols(grad, w)

        @pl.when(jnp.logical_not(mine))
        def _():
            for_sibling[z] = back.astype(BF)
            to_sibling(z).start()

        @pl.when(mine)
        def _():
            to_sibling(z).wait_recv()
            total = back + from_sibling[z].astype(F32)

            @pl.when(z == at.z)
            def _():
                own_total[...] = total

            @pl.when(z != at.z)
            def _():
                for_line[z] = total.astype(BF)
                to_line(z).start()

        return 0

    lax.fori_loop(0, 2 * length, backward, 0)

    depth = map_ref.shape[1]
    unit = 256
    everything = grads[...].reshape(members * rows, width)

    def weight_grad(m, _):
        left = spread_back[:, :, pl.ds(pl.multiple_of(m * unit, unit), unit)]
        result = dot_rows(left.reshape(members * rows, unit), everything).astype(BF)
        grad_w_ref[pl.ds(m * unit, unit), :] = result
        return 0

    lax.fori_loop(0, depth // unit, weight_grad, 0)

    for j in range(pieces_of):
        turn_load(j).wait()
        if j + 1 < pieces_of:
            turn_load(j + 1).start()
        if j >= 2:
            turn_store(j - 2).wait()
        turn_out[j % 2] = turn_in[j % 2].astype(F32).T.astype(BF)
        turn_store(j).start()
    for j in range(max(pieces_of - 2, 0), pieces_of):
        turn_store(j).wait()

    def arrived(z):
        remote(
            from_line.at[z], from_line.at[z], sem(TO_LINE, z), sem(LINE_RECV, z), line.peer(z)
        ).wait_recv()
        own_total[...] += from_line[z].astype(F32)

    line.others(arrived)
    spread_grad = own_total[...]
    high = spread_grad.astype(BF)
    low = (spread_grad - high.astype(F32)).astype(BF)
    grad_h_ref[...] = dot_cols(high, map_ref[...]) + dot_cols(low, map_ref[...])

    def finish(z):
        for copy in stat_out(z):
            copy.wait_send()
        to_line(z).wait_send()

    line.others(finish)
    line.chips(lambda z: to_sibling(z).wait_send())
    to_pair.wait_send()


def word_softmax(plan, h, weights, mapping, mapping_back, recur, collective_id):
    members, rows, depth = h.shape
    n = plan.fsdp
    spread = mapping.shape[1]
    per_slot, width = plan.block
    words = up_to(rows, LANE)
    length = members // 2
    vmem = pl.BlockSpec(memory_space=pltpu.VMEM)
    piece = 2 * LANE
    anywhere = pl.BlockSpec(memory_space=pl.ANY)
    loss, grad_h, grad_w, turned_recur = pl.pallas_call(
        functools.partial(softmax_kernel, plan.width, n),
        out_shape=[
            jax.ShapeDtypeStruct((members, words), F32),
            jax.ShapeDtypeStruct((rows, depth), F32),
            jax.ShapeDtypeStruct((spread, width), BF),
            jax.ShapeDtypeStruct(recur.shape[::-1], BF),
        ],
        in_specs=[vmem] * 4 + [anywhere],
        out_specs=[vmem] * 3 + [anywhere],
        scratch_shapes=[
            pltpu.VMEM((2, recur.shape[0], piece), BF),
            pltpu.VMEM((2, piece, recur.shape[0]), BF),
            pltpu.SemaphoreType.DMA((4,)),
            pltpu.VMEM((members, rows, spread), BF),
            pltpu.VMEM((members, rows, width), F32),
            pltpu.VMEM((members, rows, width), BF),
            pltpu.VMEM((members, 2, members, words), F32),
            pltpu.VMEM((length, rows, spread), BF),
            pltpu.VMEM((length, rows, spread), BF),
            pltpu.VMEM((length, rows, spread), BF),
            pltpu.VMEM((length, rows, spread), BF),
            pltpu.VMEM((rows, spread), F32),
            pltpu.SemaphoreType.DMA((6 * members,)),
        ],
        compiler_params=pltpu.CompilerParams(
            collective_id=collective_id, has_side_effects=True, vmem_limit_bytes=62 * 2**20
        ),
    )(h, weights, mapping, mapping_back, recur)
    return loss, grad_h, grad_w.reshape((n,) + plan.block), turned_recur


def shards(
    fsdp_count,
    dp_count,
    chars,
    lengths,
    targets,
    resets,
    init_state,
    window_grad,
    char_table,
    conv_weight,
    conv_bias,
    highway_flat,
    lstm_flat,
    soft_flat,
):
    micro_count, streams, step_count, letters = chars.shape
    char_count, embed_dim = char_table.shape
    filters = conv_weight.shape[1]
    batch = micro_count * streams
    words = step_count * batch
    rows = up_to(words, 16)
    fp = up_to(filters + 1, LANE)
    dp_at, fsdp_at = lax.axis_index("dp"), lax.axis_index("fsdp")
    highway = Windows(
        highway_flat.shape[0] * fsdp_count, filters, 4 * (filters + 1), fsdp_count, dp_count, True
    )
    lstm = Windows(
        lstm_flat.shape[0] * fsdp_count, 4 * H, filters + H + 1, fsdp_count, dp_count, False
    )
    soft = Windows(
        soft_flat.shape[0] * fsdp_count, V, H + 1, fsdp_count, dp_count, False, fsdp_count // 2
    )
    member = 2 * (fsdp_at // 4) + lax.rem(dp_at, 2)

    def by_step(array):
        return jnp.moveaxis(array.reshape((batch, step_count) + array.shape[3:]), 1, 0).reshape(
            (words,) + array.shape[3:]
        )

    def pad_rows(array, value=0):
        return jnp.pad(
            array,
            [(0, rows - words)] + [(0, 0)] * (array.ndim - 1),
            constant_values=value,
        )

    word_chars = pad_rows(by_step(chars))
    word_lengths = pad_rows(by_step(lengths))[:, None]
    position = jnp.arange(letters, dtype=jnp.int32)[None, :]
    codes = jnp.where(position < word_lengths, word_chars, -1)
    codes = jnp.pad(codes, ((0, 0), (0, SLOTS - letters)), constant_values=-1)
    codes = codes.reshape(rows * SLOTS, 1)
    column = np.arange(fp)
    widths = np.ones((fp,), np.int32)
    for cut_at in FILTER_CUTS:
        widths = widths + ((column >= filters * cut_at // 22) & (column < filters))
    widths = widths.astype(np.int32)
    kernel_mask = jnp.asarray(
        np.arange(KMAX * embed_dim)[:, None] // embed_dim < widths[None, :filters]
    )
    ones_row = KMAX * embed_dim
    kernel = jnp.concatenate(
        [jnp.where(kernel_mask, conv_weight, jnp.zeros_like(conv_weight)), conv_bias[None, :]], axis=0
    )
    kernel = jnp.pad(kernel, ((0, LANE - ones_row - 1), (0, fp - filters)))
    spread_table = jnp.concatenate(
        [
            jnp.pad(char_table, ((0, 0), (q * embed_dim, LANE - (q + 1) * embed_dim)))
            for q in range(KMAX)
        ]
        + [jnp.asarray((np.arange(LANE) == ones_row)[None, :].astype(np.float32)).astype(BF)],
        axis=0,
    )
    spread_table = jnp.pad(spread_table, ((0, HOT - KMAX * char_count - 1), (0, 0)))
    conv_inputs = (codes, word_lengths, spread_table, kernel, jnp.asarray(widths)[None, :])

    highway_all, lstm_all, from_input, recur, soft_placed, *kept = head(
        [highway, lstm],
        soft,
        filters,
        place_all([highway, lstm], [highway_flat, lstm_flat]),
        conv_inputs,
        soft_flat,
        rows,
        fp,
        1,
    )
    kept_parts, kept = kept[:4], kept[4:]
    features, trans, gates = kept[:3], kept[3:5], kept[5:7]

    soft_own = soft.from_placed(soft_placed)
    keep = pad_rows(by_step(1 - resets).astype(F32))[:, None]
    start = init_state.reshape(batch, 2, H)
    start = jnp.pad(start, ((0, 8 - batch), (0, 0), (0, HP - H)))
    row_scale = jnp.broadcast_to(
        window_grad.reshape(1, batch) / step_count, (step_count, batch)
    ).reshape(words)
    goal = by_step(targets)
    scale_high = lax.reduce_precision(row_scale, 8, 7)
    scale_mid = lax.reduce_precision(row_scale - scale_high, 8, 7)
    extra = jnp.stack(
        [
            jnp.ones((words,), F32),
            (goal // 256).astype(F32),
            (goal % 256).astype(F32),
            scale_high,
            scale_mid,
            row_scale - scale_high - scale_mid,
        ],
        axis=1,
    )
    aside = H - (HP - LANE)
    extra = jnp.pad(extra, ((0, rows - words), (aside, LANE - aside - extra.shape[1])))
    *states, hidden_all, soft_part = lstm_forward(
        batch,
        soft,
        from_input,
        recur,
        start[:, 0].astype(BF).astype(F32),
        start[:, 1],
        keep,
        extra,
        soft_own,
        4,
    )
    hp = states[0]

    word_loss, grad_hidden, soft_grad, recur_t = word_softmax(
        soft,
        hidden_all,
        soft_part,
        one_hot_map(HP, soft.gathered),
        one_hot_map(HP, soft.reduced),
        recur,
        5,
    )
    word_loss = lax.dynamic_index_in_dim(word_loss, member, 0, keepdims=False)
    window_loss = jnp.mean(word_loss[:words].reshape(step_count, batch), axis=0).reshape(
        micro_count, streams
    )

    dz, soft_part = lstm_backward(
        batch, soft, lstm.columns, grad_hidden, recur_t, keep, states[1:], soft_grad, 6
    )
    hot_row, hot_lane = np.arange(HOT), np.arange(LANE)
    hot_mask = (hot_row[:, None] // char_count == hot_lane[None, :] // embed_dim) & (
        hot_row[:, None] < KMAX * char_count
    )
    hot_fold = (hot_row[None, :] % char_count == np.arange(LANE)[:, None]) & (
        hot_row[None, :] < KMAX * char_count
    )
    conv = Dense(LANE, conv_columns(fp), fsdp_count)
    at_once = 2 * fsdp_count * highway.block[0] * highway.block[1] * 2 <= 12 * 2**20
    _, highway_grad, conv_grad, lstm_part, *rest = highway_backward(
        [highway, lstm],
        conv if at_once else None,
        filters,
        dz,
        hp,
        features,
        trans,
        gates,
        (
            kernel,
            jnp.asarray(hot_mask.astype(np.float32)),
            jnp.asarray(hot_fold.astype(np.float32)),
        ),
        (highway_all, lstm_all, *kept_parts),
        7,
    )
    if at_once:
        _, highway_part, conv_grad = rest
    else:
        conv_grad, highway_part = tail([conv, highway], conv_grad, highway_grad, 3)
    conv_grad = jnp.concatenate(
        [conv_grad[h].reshape(-1, conv.block[1])[:LANE] for h in range(2)], axis=1
    )
    conv_weight_grad = jnp.where(kernel_mask, conv_grad[:ones_row, :filters], 0.0)
    conv_bias_grad = conv_grad[ones_row, :filters]
    table_grad = jnp.sum(
        conv_grad[:char_count, fp : fp + KMAX * embed_dim].reshape(char_count, KMAX, embed_dim), axis=1
    )

    def own_window(plan, part):
        if dp_count > 2:
            groups = [list(range(h, dp_count, 2)) for h in range(2)]
            part = lax.psum(part.astype(F32), "dp", axis_index_groups=groups)
        if plan.by_rows:
            at = dp_at // 2
        else:
            at = dp_at
            part = jnp.concatenate(
                [
                    lax.dynamic_slice_in_dim(part[p], at * plan.rows, plan.rows, 0)
                    for p in range(plan.parts)
                ],
                axis=1,
            ).astype(F32)
            return plan.to_flat(part, dp_at, fsdp_at)
        window = lax.dynamic_slice_in_dim(part, at * plan.rows, plan.rows, 0)
        return plan.to_flat(window, dp_at, fsdp_at)

    return (
        window_loss,
        table_grad,
        conv_weight_grad,
        conv_bias_grad,
        own_window(highway, highway_part),
        own_window(lstm, lstm_part),
        own_window(soft, soft_part),
    )


def solution(mesh):
    in_specs = (
        P(None, ("dp", "fsdp"), None, None),
        P(None, ("dp", "fsdp"), None),
        P(None, ("dp", "fsdp"), None),
        P(None, ("dp", "fsdp"), None),
        P(None, ("dp", "fsdp"), None, None),
        P(None, ("dp", "fsdp")),
        P(),
        P(),
        P(),
        P("fsdp", None),
        P("fsdp", None),
        P("fsdp", None),
    )
    out_specs = (
        P(None, ("dp", "fsdp")),
        P(),
        P(),
        P(),
        P(("dp", "fsdp"), None),
        P(("dp", "fsdp"), None),
        P(("dp", "fsdp"), None),
    )
    return jax.shard_map(
        functools.partial(shards, mesh.shape["fsdp"], mesh.shape["dp"]),
        mesh=mesh,
        in_specs=in_specs,
        out_specs=out_specs,
        check_vma=False,
    )
```
